32 devices in a mesh: harm: 2 (over y), gx: 4 (over z), gz: 4 (over x, core).
Axes of the slice: x: 2, y: 2, z: 4, core: 2. Of those that a mesh axis runs over, the one named last changes fastest.
Arguments:
- perturbation: bfloat16 [8, 2, 4, 128, 24, 128], P('harm', None, None, 'gx', 'gz'), may hold values from -6 to 6
- base_mean: bfloat16 [3, 128, 24, 128], P(None, 'gx', 'gz'), may hold values from -6 to 6
- base_modes: bfloat16 [2, 2, 3, 128, 24, 128], P(None, None, None, 'gx', 'gz'), may hold values from -3 to 3
- solid_mask: int32 [128, 24, 128], P('gx', 'gz'), may hold values from 0 to 1, as said below
Outputs:
- residual_harmonics: float32 [8, 2, 4, 128, 24, 128], P('harm', None, None, 'gx', 'gz')
The draws below stay inside these ranges and needn't reach their ends.
Inputs may be any that keep to these rules, and one draw needn't show every extreme that they name: `solid_mask`: 1 on the cells of one circular cylinder of radius 2 or more cells in the x-y plane, the same at every spanwise position, 0 elsewhere.
All inputs are finite; a program needn't handle non-finite values.
Results may differ from the reference program's by a relative error of at most 0.0003.
Values may be sent and summed in bfloat16 or wider, within the bound.
No kernel may reach another device: no remote copies, remote signals or barrier semaphores. Data moves between devices by JAX's collectives and lax.ppermute only.
A program may use at most 128 MiB of HBM per device.

```python
import jax
import jax.numpy as jnp
from jax import lax

MODES = 2
NY = 128
HARMS = 8
NX = 128
NZ = 24


def draw_solid_mask(key, part):
    key_x, key_y, key_r = jax.random.split(jax.random.fold_in(key, 17), 3)
    centre_x = jax.random.randint(key_x, (), 0, NX)
    centre_y = jax.random.randint(key_y, (), NY // 4, 3 * NY // 4)
    radius = jax.random.randint(key_r, (), 2, max(3, NY // 8) + 1)
    spots_x = jnp.arange(NX, dtype=jnp.int32)[:, None]
    spots_y = jnp.arange(NY, dtype=jnp.int32)[None, :]
    inside = (spots_x - centre_x) ** 2 + (spots_y - centre_y) ** 2 <= radius * radius
    plane = jnp.where(inside, 1, 0).astype(jnp.int32)
    return jnp.broadcast_to(plane[:, None, :], (NX, NZ, NY)).astype(jnp.int32)


def block_levels(rng, shape, pieces, smallest, largest):
    level, own = 1.0, jax.random.fold_in(rng, 6)
    for position, shards_of in pieces:
        heights = jnp.exp(jax.random.uniform(jax.random.fold_in(own, position), (shards_of,), jnp.float32, smallest / len(pieces), largest / len(pieces)))
        level = level * jnp.repeat(heights, shape[position] // shards_of).reshape([-1 if axis == position else 1 for axis in range(len(shape))])
    return level


def centred(own_key, shape, deviation, reach, pieces=(), kind=jnp.bfloat16):
    drawn = deviation * jax.random.normal(own_key, shape, jnp.float32)
    if pieces:
        drawn = drawn * block_levels(own_key, shape, pieces, -0.22, 0.18)
    return jnp.clip(drawn, -reach, reach).astype(kind)


def setup_inputs(seed: int = 0) -> dict:
    keys = jax.random.split(jax.random.key(seed), 5)
    return {
        "perturbation": centred(keys[0], (HARMS, 2, 4, NX, NZ, NY), 1.0, 6.0, ((0, 2), (3, 4), (4, 4))),
        "base_mean": centred(keys[1], (3, NX, NZ, NY), 1.0, 6.0, ((1, 4), (2, 4))),
        "base_modes": centred(keys[2], (MODES, 2, 3, NX, NZ, NY), 0.5, 3.0, ((3, 4), (4, 4))),
        "solid_mask": draw_solid_mask(jax.random.fold_in(keys[4], 71), 0),
    }


FREQUENCY_STEP = 0.2
VISCOSITY = 0.05
PENALTY = 4.0


def wall_shift(values, offset):
    dims_count = values.ndim
    length_y = values.shape[-1]
    widths = [(0, 0)] * (dims_count - 1) + [(2, 2)]
    return lax.slice_in_dim(jnp.pad(values, widths), 2 + offset, 2 + offset + length_y, axis=dims_count - 1)


def moved(values, direction, offset):
    if direction == 0:
        return jnp.roll(values, -offset, axis=values.ndim - 3)
    if direction == 2:
        return jnp.roll(values, -offset, axis=values.ndim - 2)
    return wall_shift(values, offset)


def first_deriv(values, direction):
    near = moved(values, direction, 1) - moved(values, direction, -1)
    far = moved(values, direction, 2) - moved(values, direction, -2)
    return (8.0 * near - far) / 12.0


def second_deriv(values, direction):
    near = moved(values, direction, 1) + moved(values, direction, -1)
    far = moved(values, direction, 2) + moved(values, direction, -2)
    return (16.0 * near - far - 30.0 * values) / 12.0


def base_pair(mean_part, mode_part, mode_shift):
    if mode_shift == 0:
        return mean_part, jnp.zeros_like(mean_part)
    if mode_shift > 0:
        return mode_part[mode_shift - 1, 0], mode_part[mode_shift - 1, 1]
    return mode_part[-mode_shift - 1, 0], -mode_part[-mode_shift - 1, 1]


def reference(perturbation, base_mean, base_modes, solid_mask):
    values = perturbation.astype(jnp.float32)
    velocity = values[:, :, :3]
    pressure = values[:, :, 3]
    count_h = values.shape[0]
    blank = jnp.zeros((MODES,) + velocity.shape[1:], jnp.float32)
    extended = jnp.concatenate([blank, velocity, blank], 0)
    mean_flow = base_mean.astype(jnp.float32)
    mode_flow = base_modes.astype(jnp.float32)
    solid_field = solid_mask.astype(jnp.float32)
    harmonic = jnp.arange(count_h, dtype=jnp.int32) - count_h // 2
    frequency = (FREQUENCY_STEP * harmonic.astype(jnp.float32))[:, None, None, None, None]
    accum_real = -frequency * velocity[:, 1] + PENALTY * solid_field * velocity[:, 0]
    accum_imag = frequency * velocity[:, 0] + PENALTY * solid_field * velocity[:, 1]
    diverge_real = jnp.zeros(pressure[:, 0].shape, jnp.float32)
    diverge_imag = jnp.zeros(pressure[:, 0].shape, jnp.float32)
    for direction in range(3):
        gradient = first_deriv(extended, direction)
        mean_grad = first_deriv(mean_flow, direction)
        mode_grad = first_deriv(mode_flow, direction)
        press_grad = first_deriv(pressure, direction)
        laplace_term = second_deriv(velocity, direction)
        selector = (jnp.arange(3, dtype=jnp.int32) == direction).astype(jnp.float32)[:, None, None, None]
        accum_real = accum_real + press_grad[:, 0][:, None] * selector - VISCOSITY * laplace_term[:, 0]
        accum_imag = accum_imag + press_grad[:, 1][:, None] * selector - VISCOSITY * laplace_term[:, 1]
        diverge_real = diverge_real + gradient[MODES:MODES + count_h, 0, direction]
        diverge_imag = diverge_imag + gradient[MODES:MODES + count_h, 1, direction]
        for mode_shift in range(-MODES, MODES + 1):
            flow_real, flow_imag = base_pair(mean_flow, mode_flow, mode_shift)
            slope_real, slope_imag = base_pair(mean_grad, mode_grad, mode_shift)
            grad_src = gradient[MODES - mode_shift:MODES - mode_shift + count_h]
            value_src = extended[MODES - mode_shift:MODES - mode_shift + count_h]
            carry_real = flow_real[direction]
            carry_imag = flow_imag[direction]
            along_real = value_src[:, 0, direction][:, None]
            along_imag = value_src[:, 1, direction][:, None]
            accum_real = accum_real + carry_real * grad_src[:, 0] - carry_imag * grad_src[:, 1] + along_real * slope_real - along_imag * slope_imag
            accum_imag = accum_imag + carry_real * grad_src[:, 1] + carry_imag * grad_src[:, 0] + along_real * slope_imag + along_imag * slope_real
    momentum = jnp.stack([accum_real, accum_imag], 1)
    continuity = jnp.stack([diverge_real, diverge_imag], 1)[:, :, None]
    return jnp.concatenate([momentum, continuity], 2)
```

```python
import jax
import jax.numpy as jnp
import numpy as np
from jax import lax
from jax.experimental import pallas as pl
from jax.experimental.pallas import tpu as pltpu
from jax.sharding import PartitionSpec as P

FREQUENCY_STEP = 0.2
VISCOSITY = 0.05
PENALTY = 4.0
FIRST = {-2: 1.0, -1: -8.0, 1: 8.0, 2: -1.0}
SECOND = {-2: -1.0, -1: 16.0, 0: -30.0, 1: 16.0, 2: -1.0}
HALO_X = 16
VMEM_BYTES = 56 * 1024 * 1024
ANY = pl.BlockSpec(memory_space=pl.ANY)
VMEM = pl.BlockSpec(memory_space=pltpu.VMEM)
SMEM = pl.BlockSpec(memory_space=pltpu.SMEM)


def stencil_rows(nz, nx, odd):
    own = nz * nx
    at_xb, at_xa = own, own + HALO_X
    at_cross = own + 2 * HALO_X
    at_near = at_cross + 2 * nx
    depth = at_near + 2 * nx
    at_zb, at_za = (at_near, at_cross) if odd else (at_cross, at_near)
    rows = np.zeros((3, own, depth), np.float32)
    for z in range(nz):
        for x in range(nx):
            row = z * nx + x
            for table, parts in ((FIRST, (0, 1)), (SECOND, (2, 2))):
                for step, weight in table.items():
                    sx = x + step
                    if sx < 0:
                        column = at_xb + 2 * z + sx + 2
                    elif sx >= nx:
                        column = at_xa + 2 * z + sx - nx
                    else:
                        column = z * nx + sx
                    rows[parts[0], row, column] += weight
                    sz = z + step
                    if sz < 0:
                        column = at_zb + (sz + 2) * nx + x
                    elif sz >= nz:
                        column = at_za + (sz - nz) * nx + x
                    else:
                        column = sz * nx + x
                    rows[parts[1], row, column] += weight
    return rows.reshape(3 * own, depth)


def wall_columns(ny):
    out = np.zeros((ny, 2 * ny), np.float32)
    for part, table in enumerate((FIRST, SECOND)):
        for y in range(ny):
            for step, weight in table.items():
                if 0 <= y + step < ny:
                    out[y + step, part * ny + y] = weight
    return out


def edge_rows(nz, nx):
    pick = np.zeros((2 * HALO_X, nz * nx), np.float32)
    for z in range(nz):
        for j in range(2):
            pick[2 * z + j, z * nx + j] = 1.0
            pick[HALO_X + 2 * z + j, z * nx + nx - 2 + j] = 1.0
    return pick


def run_copies(copies, sems):
    started = [pltpu.make_async_copy(src, dst, sems.at[i]) for i, (src, dst) in enumerate(copies)]
    for copy in started:
        copy.start()
    for copy in started:
        copy.wait()


def shards(perturbation, base_mean, base_modes, solid_mask):
    per, modes = perturbation.shape[0], base_modes.shape[0]
    nx, nz, ny = perturbation.shape[3], perturbation.shape[4], perturbation.shape[5]
    own = nz * nx
    bf16, f32 = jnp.bfloat16, jnp.float32
    harms, size_x, size_z = (lax.axis_size(a) for a in ("harm", "gx", "gz"))
    me_h, me_z = lax.axis_index("harm"), lax.axis_index("gz")
    swap = harms == 2
    sides = 1 if swap else 2
    n_pert, n_mean, n_modes = per * 8, 3, modes * 6
    n_base = n_mean + n_modes
    n_res = n_pert + n_base
    n_nb = modes * 6
    n_all = n_res + sides * n_nb

    pert = jnp.swapaxes(perturbation, 3, 4).reshape(n_pert, nz, nx, ny)
    mean = jnp.swapaxes(base_mean, 1, 2)
    mode = jnp.swapaxes(base_modes, 3, 4).reshape(n_modes, nz, nx, ny)
    mask = jnp.swapaxes(solid_mask, 0, 1).reshape(own, ny)

    odd = lax.rem(me_z, 2)
    cross_z = odd * (nz - 2)
    near_z = (1 - odd) * (nz - 2)
    shared = jnp.where(me_h == 0, per - modes, 0) if swap else jnp.int32(0)
    scalars = jnp.stack([me_h, odd, cross_z, near_z, shared]).astype(jnp.int32)

    cross_pairs = [(i, (i + 1) % size_z if i % 2 else (i - 1) % size_z) for i in range(size_z)]
    near_pairs = [(i, i + 1 if i % 2 == 0 else i - 1) for i in range(size_z)]
    up_x = [(i, (i + 1) % size_x) for i in range(size_x)]
    down_x = [(j, i) for i, j in up_x]
    if swap:
        harm_perms = [[(0, 1), (1, 0)]]
    else:
        up_h = [(i, i + 1) for i in range(harms - 1)]
        harm_perms = [up_h, [(j, i) for i, j in up_h]]
    n_first = modes * 8 if swap else n_pert
    n_second = n_res - n_first

    def sent(s, scal):
        return scal[4] if swap else (per - modes if s == 0 else 0)

    def plan_first(refs):
        scal, pert_ref, first_ref, *nb_refs = refs
        copies = []
        at = scal[4] * 8 if swap else 0
        copies.append((pert_ref.at[pl.ds(at, n_first), pl.ds(scal[2], 2)], first_ref))
        for s, nb_ref in enumerate(nb_refs):
            for i in range(modes * 2):
                copies.append((pert_ref.at[pl.ds(sent(s, scal) * 8 + 4 * i, 3)], nb_ref.at[pl.ds(3 * i, 3)]))
        return copies

    face = lambda n: jax.ShapeDtypeStruct((n, 2, nx, ny), bf16)

    def copies_of(plan, count, outs, *args):
        def body(*refs):
            run_copies(plan(refs[:-1]), refs[-1])

        return pl.pallas_call(
            body,
            out_shape=outs,
            in_specs=[SMEM] + [ANY] * (len(args) - 1),
            out_specs=tuple(ANY for _ in outs),
            scratch_shapes=[pltpu.SemaphoreType.DMA((count,))],
        )(*args)

    with jax.named_scope("pack_first"):
        first, *nb_send = copies_of(
            plan_first,
            1 + sides * modes * 2,
            (face(n_first),) + tuple(jax.ShapeDtypeStruct((n_nb, nz, nx, ny), bf16) for _ in range(sides)),
            scalars,
            pert,
        )
    first_got = lax.ppermute(first, "gz", cross_pairs)
    nb_got = [lax.ppermute(b, "harm", p) for b, p in zip(nb_send, harm_perms)]

    def pack_second(scal, pick_ref, pert_any, mean_any, mode_any, pert_ref, mean_ref, mode_ref, second_ref, lo_ref, hi_ref, sems):
        z = pl.ds(scal[2], 2)
        copies = []
        if swap:
            rest = per - modes - scal[4]
            copies.append((pert_any.at[pl.ds(rest * 8, n_pert - n_first), z], second_ref.at[pl.ds(0, n_pert - n_first)]))
        at = n_pert - n_first
        copies.append((mean_any.at[:, z], second_ref.at[pl.ds(at, n_mean)]))
        copies.append((mode_any.at[:, z], second_ref.at[pl.ds(at + n_mean, n_modes)]))
        started = [pltpu.make_async_copy(src, dst, sems.at[i]) for i, (src, dst) in enumerate(copies)]
        for copy in started:
            copy.start()
        pick = pick_ref[...]
        at = 0
        for ref, count in ((pert_ref, n_pert), (mean_ref, n_mean), (mode_ref, n_modes)):
            for f in range(0, count, 2):
                wide = min(2, count - f)
                rows = [ref[f + i].reshape(own, ny) for i in range(wide)]
                both = jnp.concatenate(rows, axis=1) if wide == 2 else rows[0]
                got = jnp.dot(pick, both, preferred_element_type=f32).astype(bf16)
                for i in range(wide):
                    lo_ref[at + f + i] = got[:HALO_X, i * ny : (i + 1) * ny]
                    hi_ref[at + f + i] = got[HALO_X:, i * ny : (i + 1) * ny]
            at += count
        for copy in started:
            copy.wait()

    edge = jax.ShapeDtypeStruct((n_res, HALO_X, ny), bf16)
    with jax.named_scope("pack_second"):
        second, edge_lo, edge_hi = pl.pallas_call(
            pack_second,
            out_shape=(face(n_second), edge, edge),
            in_specs=[SMEM, VMEM, ANY, ANY, ANY, VMEM, VMEM, VMEM],
            out_specs=(ANY, VMEM, VMEM),
            scratch_shapes=[pltpu.SemaphoreType.DMA((3,))],
            compiler_params=pltpu.CompilerParams(vmem_limit_bytes=VMEM_BYTES // 2),
        )(scalars, jnp.asarray(edge_rows(nz, nx), bf16), pert, mean, mode, pert, mean, mode)
    second_got = lax.ppermute(second, "gz", cross_pairs)
    xb_got = lax.ppermute(edge_hi, "gx", up_x)
    xa_got = lax.ppermute(edge_lo, "gx", down_x)

    deep = 2 * nx + 2 * HALO_X
    first_rows = first_got.reshape(n_first, 2 * nx, ny)

    def plan_relay(refs):
        scal, first_ref, xb_ref, xa_ref, *outs = refs
        copies = []
        for s, out in enumerate(outs):
            for i in range(modes * 2):
                field = sent(s, scal) * 8 + 4 * i
                to = pl.ds(3 * i, 3)
                near = 4 * i if swap else field
                copies.append((first_ref.at[pl.ds(near, 3)], out.at[to, pl.ds(0, 2 * nx)]))
                copies.append((xb_ref.at[pl.ds(field, 3)], out.at[to, pl.ds(2 * nx, HALO_X)]))
                copies.append((xa_ref.at[pl.ds(field, 3)], out.at[to, pl.ds(2 * nx + HALO_X, HALO_X)]))
        return copies

    with jax.named_scope("pack_relay"):
        relay = copies_of(
            plan_relay,
            sides * modes * 6,
            tuple(jax.ShapeDtypeStruct((n_nb, deep, ny), bf16) for _ in range(sides)),
            scalars,
            first_rows,
            xb_got,
            xa_got,
        )
    relay_got = [lax.ppermute(b, "harm", p) for b, p in zip(relay, harm_perms)]

    def plan_near(refs):
        scal, pert_ref, mean_ref, mode_ref, *rest = refs
        z = pl.ds(scal[3], 2)
        out = rest[-1]
        copies = [
            (pert_ref.at[:, z], out.at[pl.ds(0, n_pert)]),
            (mean_ref.at[:, z], out.at[pl.ds(n_pert, n_mean)]),
            (mode_ref.at[:, z], out.at[pl.ds(n_pert + n_mean, n_modes)]),
        ]
        for s in range(sides):
            copies.append((rest[s].at[:, z], out.at[pl.ds(n_res + s * n_nb, n_nb)]))
        return copies

    with jax.named_scope("pack_near"):
        (near,) = copies_of(plan_near, 3 + sides, (face(n_all),), scalars, pert, mean, mode, *nb_got)
    near_got = lax.ppermute(near, "gz", near_pairs)

    at_xb, at_xa = own, own + HALO_X
    at_cross = own + 2 * HALO_X
    at_near = at_cross + 2 * nx
    depth = at_near + 2 * nx
    stencil = jnp.asarray(np.stack([stencil_rows(nz, nx, False), stencil_rows(nz, nx, True)]), bf16)
    walls = jnp.asarray(wall_columns(ny), bf16)
    n_even = n_all + n_all % 2

    def operator(scal, stencil_any, walls_ref, mask_ref, pert_ref, mean_ref, mode_ref, first_ref, second_ref, near_ref, xb_ref, xa_ref, *rest):
        nb_refs, relay_refs = rest[:sides], rest[sides : 2 * sides]
        out_ref, fields, grads, laps, plain, weights, sems = rest[2 * sides :]
        base_at = n_pert
        copies = [(stencil_any.at[scal[1]], weights)]
        copies.append((pert_ref, fields.at[pl.ds(0, n_pert), pl.ds(0, own)]))
        copies.append((mean_ref, fields.at[pl.ds(base_at, n_mean), pl.ds(0, own)]))
        copies.append((mode_ref, fields.at[pl.ds(base_at + n_mean, n_modes), pl.ds(0, own)]))
        cross = pl.ds(at_cross, 2 * nx)
        if swap:
            rest_at = per - modes - scal[4]
            copies.append((first_ref, fields.at[pl.ds(scal[4] * 8, n_first), cross]))
            copies.append((second_ref.at[pl.ds(0, n_pert - n_first)], fields.at[pl.ds(rest_at * 8, n_pert - n_first), cross]))
        else:
            copies.append((first_ref, fields.at[pl.ds(0, n_pert), cross]))
        copies.append((second_ref.at[pl.ds(n_pert - n_first, n_base)], fields.at[pl.ds(base_at, n_base), cross]))
        copies.append((near_ref, fields.at[pl.ds(0, n_all), pl.ds(at_near, 2 * nx)]))
        copies.append((xb_ref, fields.at[pl.ds(0, n_res), pl.ds(at_xb, HALO_X)]))
        copies.append((xa_ref, fields.at[pl.ds(0, n_res), pl.ds(at_xa, HALO_X)]))
        for s in range(sides):
            mine = pl.ds(n_res + s * n_nb, n_nb)
            copies.append((nb_refs[s], fields.at[mine, pl.ds(0, own)]))
            copies.append((relay_refs[s].at[:, pl.ds(0, 2 * nx)], fields.at[mine, cross]))
            copies.append((relay_refs[s].at[:, pl.ds(2 * nx, 2 * HALO_X)], fields.at[mine, pl.ds(at_xb, 2 * HALO_X)]))
        run_copies(copies, sems)
        if n_even != n_all:
            fields[n_all] = jnp.zeros((depth, ny), bf16)

        def slopes(pair, carry):
            f = 2 * pair
            both = jnp.concatenate([fields[f], fields[f + 1]], axis=1)
            got = jnp.dot(weights[...], both, preferred_element_type=f32)
            for i in range(2):
                lanes = slice(i * ny, (i + 1) * ny)
                grads[f + i, 0] = got[:own, lanes]
                grads[f + i, 2] = got[own : 2 * own, lanes]
                mine = fields[f + i, pl.ds(0, own)]
                wall = jnp.dot(mine, walls_ref[...], preferred_element_type=f32)
                grads[f + i, 1] = wall[:, :ny]
                laps[f + i] = got[2 * own :, lanes] + wall[:, ny:]
                plain[f + i] = mine.astype(f32)
            return carry

        lax.fori_loop(0, n_even // 2, slopes, 0)

        def base_at_mode(m, c):
            if m == 0:
                return base_at + c, None, 1.0
            at = base_at + n_mean + (abs(m) - 1) * 6 + c
            return at, at + 3, (1.0 if m > 0 else -1.0)

        def product(acc, flow, value):
            (fr, fi, sign), (vr, vi) = flow, value
            re, im = acc[0] + fr * vr, acc[1] + fr * vi
            if fi is not None:
                if sign > 0:
                    re, im = re - fi * vi, im + fi * vr
                else:
                    re, im = re + fi * vi, im - fi * vr
            return re, im

        def contribution(acc, pairs, rows):
            for d in range(3):
                for k, m, at in pairs:
                    fr, fi, sign = base_at_mode(m, d)
                    flow = (plain[fr, rows], None if fi is None else plain[fi, rows], sign)
                    along = (plain[at + d, rows], plain[at + d + nb_step(at), rows])
                    for c in range(3):
                        sr, si, _ = base_at_mode(m, c)
                        slope = (grads[sr, d, rows], None if si is None else grads[si, d, rows], sign)
                        grad = (grads[at + c, d, rows], grads[at + c + nb_step(at), d, rows])
                        acc[k, c] = product(acc[k, c], flow, grad)
                        acc[k, c] = product(acc[k, c], slope, along)
            return acc

        def nb_step(at):
            return 4 if at < n_pert else 3

        resident, below, above = [], [], []
        for k in range(per):
            for m in range(-modes, modes + 1):
                l = k - m
                if l < 0:
                    below.append((k, m, n_res + (l + modes) * 6))
                elif l >= per:
                    above.append((k, m, n_res + (sides - 1) * n_nb + (l - per) * 6))
                else:
                    resident.append((k, m, l * 8))
        half = per * harms // 2

        def block(b, carry):
            rows = pl.ds(pl.multiple_of(b * 8, 8), 8)
            zero = jnp.zeros((8, ny), f32)
            acc = {(k, c): (zero, zero) for k in range(per) for c in range(3)}
            acc = contribution(acc, resident, rows)
            solid = PENALTY * mask_ref[rows].astype(f32)
            for k in range(per):
                freq = FREQUENCY_STEP * (scal[0] * per + k - half).astype(f32)
                for c in range(3):
                    ur, ui = plain[k * 8 + c, rows], plain[k * 8 + 4 + c, rows]
                    re = acc[k, c][0] + grads[k * 8 + 3, c, rows] - VISCOSITY * laps[k * 8 + c, rows]
                    im = acc[k, c][1] + grads[k * 8 + 7, c, rows] - VISCOSITY * laps[k * 8 + 4 + c, rows]
                    out_ref[k * 8 + c, rows] = re * (1.0 / 12.0) + (solid * ur - freq * ui)
                    out_ref[k * 8 + 4 + c, rows] = im * (1.0 / 12.0) + (solid * ui + freq * ur)
                for i in range(2):
                    at = k * 8 + 4 * i
                    out_ref[at + 3, rows] = (grads[at, 0, rows] + grads[at + 1, 1, rows] + grads[at + 2, 2, rows]) * (1.0 / 12.0)
            return carry

        lax.fori_loop(0, own // 8, block, 0)

        def neighbours(pairs):
            def nb_block(b, carry):
                rows = pl.ds(pl.multiple_of(b * 8, 8), 8)
                zero = jnp.zeros((8, ny), f32)
                keys = sorted({k for k, _, _ in pairs})
                acc = {(k, c): (zero, zero) for k in keys for c in range(3)}
                acc = contribution(acc, pairs, rows)
                for k in keys:
                    for c in range(3):
                        for i in range(2):
                            at = k * 8 + 4 * i + c
                            out_ref[at, rows] = out_ref[at, rows] + acc[k, c][i] * (1.0 / 12.0)
                return carry

            lax.fori_loop(0, own // 8, nb_block, 0)

        pl.when(scal[0] > 0)(lambda: neighbours(below))
        pl.when(scal[0] < harms - 1)(lambda: neighbours(above))

    n_copies = 10 + 3 * sides + (1 if swap else 0)
    flat = lambda a: a.reshape(a.shape[0], -1, ny)
    with jax.named_scope("operator"):
        out = pl.pallas_call(
            operator,
            out_shape=jax.ShapeDtypeStruct((n_pert, own, ny), f32),
            in_specs=[SMEM, ANY, VMEM, VMEM] + [ANY] * (8 + 2 * sides),
            out_specs=VMEM,
            scratch_shapes=[
                pltpu.VMEM((n_even, depth, ny), bf16),
                pltpu.VMEM((n_even, 3, own, ny), f32),
                pltpu.VMEM((n_even, own, ny), f32),
                pltpu.VMEM((n_even, own, ny), f32),
                pltpu.VMEM((3 * own, depth), bf16),
                pltpu.SemaphoreType.DMA((n_copies,)),
            ],
            compiler_params=pltpu.CompilerParams(vmem_limit_bytes=VMEM_BYTES),
        )(
            scalars, stencil, walls, mask, flat(pert), flat(mean), flat(mode), flat(first_got), flat(second_got), flat(near_got),
            xb_got, xa_got, *[flat(b) for b in nb_got], *relay_got,
        )
    return jnp.swapaxes(out.reshape(per, 2, 4, nz, nx, ny), 3, 4)


def solution(mesh):
    return jax.shard_map(
        shards,
        mesh=mesh,
        in_specs=(
            P("harm", None, None, "gx", "gz", None),
            P(None, "gx", "gz", None),
            P(None, None, None, "gx", "gz", None),
            P("gx", "gz", None),
        ),
        out_specs=P("harm", None, None, "gx", "gz", None),
        check_vma=False,
    )
```

```python
import jax
import jax.numpy as jnp
import numpy as np
from jax import lax
from jax.experimental import pallas as pl
from jax.experimental.pallas import tpu as pltpu
from jax.sharding import PartitionSpec as P

FREQUENCY_STEP = 0.2
VISCOSITY = 0.05
PENALTY = 4.0
FIRST = {-2: 1.0, -1: -8.0, 1: 8.0, 2: -1.0}
SECOND = {-2: -1.0, -1: 16.0, 0: -30.0, 1: 16.0, 2: -1.0}
HALO_X = 16
VMEM_BYTES = 56 * 1024 * 1024
ANY = pl.BlockSpec(memory_space=pl.ANY)
VMEM = pl.BlockSpec(memory_space=pltpu.VMEM)


def stencil_rows(nz, nx, odd):
    own = nz * nx
    at_xb, at_xa = own, own + HALO_X
    at_cross = own + 2 * HALO_X
    at_near = at_cross + 2 * nx
    depth = at_near + 2 * nx
    at_zb, at_za = (at_near, at_cross) if odd else (at_cross, at_near)
    rows = np.zeros((3, own, depth), np.float32)
    for z in range(nz):
        for x in range(nx):
            row = z * nx + x
            for table, parts in ((FIRST, (0, 1)), (SECOND, (2, 2))):
                for step, weight in table.items():
                    sx = x + step
                    if sx < 0:
                        column = at_xb + 2 * z + sx + 2
                    elif sx >= nx:
                        column = at_xa + 2 * z + sx - nx
                    else:
                        column = z * nx + sx
                    rows[parts[0], row, column] += weight
                    sz = z + step
                    if sz < 0:
                        column = at_zb + (sz + 2) * nx + x
                    elif sz >= nz:
                        column = at_za + (sz - nz) * nx + x
                    else:
                        column = sz * nx + x
                    rows[parts[1], row, column] += weight
    return rows.reshape(3 * own, depth)


def wall_columns(ny):
    out = np.zeros((ny, 2 * ny), np.float32)
    for part, table in enumerate((FIRST, SECOND)):
        for y in range(ny):
            for step, weight in table.items():
                if 0 <= y + step < ny:
                    out[y + step, part * ny + y] = weight
    return out


def edge_rows(nz, nx):
    pick = np.zeros((2 * HALO_X, nz * nx), np.float32)
    for z in range(nz):
        for j in range(2):
            pick[2 * z + j, z * nx + j] = 1.0
            pick[HALO_X + 2 * z + j, z * nx + nx - 2 + j] = 1.0
    return pick


def run_copies(copies, sems):
    started = [pltpu.make_async_copy(src, dst, sems.at[i]) for i, (src, dst) in enumerate(copies)]
    for copy in started:
        copy.start()
    for copy in started:
        copy.wait()


def shards(perturbation, base_mean, base_modes, solid_mask):
    per, modes = perturbation.shape[0], base_modes.shape[0]
    nx, nz, ny = perturbation.shape[3], perturbation.shape[4], perturbation.shape[5]
    own = nz * nx
    bf16, f32 = jnp.bfloat16, jnp.float32
    harms, size_x, size_z = (lax.axis_size(a) for a in ("harm", "gx", "gz"))
    swap = harms == 2
    sides = 1 if swap else 2
    n_pert, n_mean, n_modes = per * 8, 3, modes * 6
    n_base = n_mean + n_modes
    n_res = n_pert + n_base
    n_nb = modes * 6
    n_all = n_res + sides * n_nb

    pert = jnp.swapaxes(perturbation, 3, 4).reshape(n_pert, nz, nx, ny)
    mean = jnp.swapaxes(base_mean, 1, 2)
    mode = jnp.swapaxes(base_modes, 3, 4).reshape(n_modes, nz, nx, ny)
    mask = jnp.swapaxes(solid_mask, 0, 1).reshape(own, ny)

    def place():
        me_h, odd = lax.axis_index("harm"), lax.rem(lax.axis_index("gz"), 2)
        shared = jnp.where(me_h == 0, per - modes, 0) if swap else 0
        return me_h, odd, odd * (nz - 2), (1 - odd) * (nz - 2), shared

    cross_pairs = [(i, (i + 1) % size_z if i % 2 else (i - 1) % size_z) for i in range(size_z)]
    near_pairs = [(i, i + 1 if i % 2 == 0 else i - 1) for i in range(size_z)]
    up_x = [(i, (i + 1) % size_x) for i in range(size_x)]
    down_x = [(j, i) for i, j in up_x]
    if swap:
        harm_perms = [[(0, 1), (1, 0)]]
    else:
        up_h = [(i, i + 1) for i in range(harms - 1)]
        harm_perms = [up_h, [(j, i) for i, j in up_h]]
    n_first = modes * 8 if swap else n_pert
    n_second = n_res - n_first

    def sent(s, scal):
        return scal[4] if swap else (per - modes if s == 0 else 0)

    face = lambda n: jax.ShapeDtypeStruct((n, 2, nx, ny), bf16)
    roomy = pltpu.CompilerParams(vmem_limit_bytes=VMEM_BYTES // 2)

    def pack_first(pert_ref, first_ref, *nb_refs):
        scal = place()
        at = scal[4] * 8 if swap else 0
        for f in range(n_first):
            first_ref[f] = pert_ref[at + f, pl.ds(scal[2], 2)]
        for s, nb_ref in enumerate(nb_refs):
            for i in range(modes * 2):
                for c in range(3):
                    nb_ref[3 * i + c] = pert_ref[sent(s, scal) * 8 + 4 * i + c]

    with jax.named_scope("pack_first"):
        first, *nb_send = pl.pallas_call(
            pack_first,
            out_shape=(face(n_first),) + tuple(jax.ShapeDtypeStruct((n_nb, nz, nx, ny), bf16) for _ in range(sides)),
            compiler_params=roomy,
        )(pert)
    first_got = lax.ppermute(first, "gz", cross_pairs)
    nb_got = [lax.ppermute(b, "harm", p) for b, p in zip(nb_send, harm_perms)]

    def pack_second(pick_ref, pert_ref, mean_ref, mode_ref, second_ref, lo_ref, hi_ref):
        scal = place()
        z = pl.ds(scal[2], 2)
        at = n_pert - n_first
        if swap:
            rest = (per - modes - scal[4]) * 8
            for f in range(at):
                second_ref[f] = pert_ref[rest + f, z]
        second_ref[at : at + n_mean] = mean_ref[:, z]
        second_ref[at + n_mean :] = mode_ref[:, z]
        pick = pick_ref[...]
        at = 0
        for ref, count in ((pert_ref, n_pert), (mean_ref, n_mean), (mode_ref, n_modes)):
            for f in range(0, count, 2):
                wide = min(2, count - f)
                rows = [ref[f + i].reshape(own, ny) for i in range(wide)]
                both = jnp.concatenate(rows, axis=1) if wide == 2 else rows[0]
                got = jnp.dot(pick, both, preferred_element_type=f32).astype(bf16)
                for i in range(wide):
                    lo_ref[at + f + i] = got[:HALO_X, i * ny : (i + 1) * ny]
                    hi_ref[at + f + i] = got[HALO_X:, i * ny : (i + 1) * ny]
            at += count

    edge = jax.ShapeDtypeStruct((n_res, HALO_X, ny), bf16)
    with jax.named_scope("pack_second"):
        second, edge_lo, edge_hi = pl.pallas_call(
            pack_second, out_shape=(face(n_second), edge, edge), compiler_params=roomy
        )(jnp.asarray(edge_rows(nz, nx), bf16), pert, mean, mode)
    second_got = lax.ppermute(second, "gz", cross_pairs)
    xb_got = lax.ppermute(edge_hi, "gx", up_x)
    xa_got = lax.ppermute(edge_lo, "gx", down_x)

    deep = 2 * nx + 2 * HALO_X

    def pack_relay(first_ref, xb_ref, xa_ref, *outs):
        scal = place()
        for s, out in enumerate(outs):
            for i in range(modes * 2):
                field = sent(s, scal) * 8 + 4 * i
                near = 4 * i if swap else field
                for c in range(3):
                    out[3 * i + c, : 2 * nx] = first_ref[near + c].reshape(2 * nx, ny)
                    out[3 * i + c, 2 * nx : 2 * nx + HALO_X] = xb_ref[field + c]
                    out[3 * i + c, 2 * nx + HALO_X :] = xa_ref[field + c]

    with jax.named_scope("pack_relay"):
        relay = pl.pallas_call(
            pack_relay,
            out_shape=tuple(jax.ShapeDtypeStruct((n_nb, deep, ny), bf16) for _ in range(sides)),
            compiler_params=roomy,
        )(first_got, xb_got, xa_got)
    relay_got = [lax.ppermute(b, "harm", p) for b, p in zip(relay, harm_perms)]

    def pack_near(pert_ref, mean_ref, mode_ref, *rest):
        out = rest[-1]
        z = pl.ds(place()[3], 2)
        out[:n_pert] = pert_ref[:, z]
        out[n_pert : n_pert + n_mean] = mean_ref[:, z]
        out[n_pert + n_mean : n_res] = mode_ref[:, z]
        for s in range(sides):
            out[n_res + s * n_nb : n_res + (s + 1) * n_nb] = rest[s][:, z]

    with jax.named_scope("pack_near"):
        near = pl.pallas_call(
            pack_near,
            out_shape=face(n_all),
            in_specs=[VMEM] * (3 + sides) + [ANY],
            compiler_params=roomy,
        )(pert, mean, mode, *nb_got, relay[0])
    near_got = lax.ppermute(near, "gz", near_pairs)

    at_xb, at_xa = own, own + HALO_X
    at_cross = own + 2 * HALO_X
    at_near = at_cross + 2 * nx
    depth = at_near + 2 * nx
    stencil = jnp.asarray(np.stack([stencil_rows(nz, nx, False), stencil_rows(nz, nx, True)]), bf16)
    walls = jnp.asarray(wall_columns(ny), bf16)
    n_even = n_all + n_all % 2

    def operator(stencil_any, walls_ref, mask_ref, pert_ref, mean_ref, mode_ref, first_ref, second_ref, near_ref, xb_ref, xa_ref, *rest):
        scal = place()
        nb_refs, relay_refs = rest[:sides], rest[sides : 2 * sides]
        out_ref, fields, grads, laps, plain, weights, sems = rest[2 * sides :]
        base_at = n_pert
        copies = [(stencil_any.at[scal[1]], weights)]
        copies.append((pert_ref, fields.at[pl.ds(0, n_pert), pl.ds(0, own)]))
        copies.append((mean_ref, fields.at[pl.ds(base_at, n_mean), pl.ds(0, own)]))
        copies.append((mode_ref, fields.at[pl.ds(base_at + n_mean, n_modes), pl.ds(0, own)]))
        cross = pl.ds(at_cross, 2 * nx)
        if swap:
            rest_at = per - modes - scal[4]
            copies.append((first_ref, fields.at[pl.ds(scal[4] * 8, n_first), cross]))
            copies.append((second_ref.at[pl.ds(0, n_pert - n_first)], fields.at[pl.ds(rest_at * 8, n_pert - n_first), cross]))
        else:
            copies.append((first_ref, fields.at[pl.ds(0, n_pert), cross]))
        copies.append((second_ref.at[pl.ds(n_pert - n_first, n_base)], fields.at[pl.ds(base_at, n_base), cross]))
        copies.append((near_ref, fields.at[pl.ds(0, n_all), pl.ds(at_near, 2 * nx)]))
        copies.append((xb_ref, fields.at[pl.ds(0, n_res), pl.ds(at_xb, HALO_X)]))
        copies.append((xa_ref, fields.at[pl.ds(0, n_res), pl.ds(at_xa, HALO_X)]))
        for s in range(sides):
            mine = pl.ds(n_res + s * n_nb, n_nb)
            copies.append((nb_refs[s], fields.at[mine, pl.ds(0, own)]))
            copies.append((relay_refs[s].at[:, pl.ds(0, 2 * nx)], fields.at[mine, cross]))
            copies.append((relay_refs[s].at[:, pl.ds(2 * nx, 2 * HALO_X)], fields.at[mine, pl.ds(at_xb, 2 * HALO_X)]))
        run_copies(copies, sems)
        if n_even != n_all:
            fields[n_all] = jnp.zeros((depth, ny), bf16)

        def slopes(pair, carry):
            f = 2 * pair
            both = jnp.concatenate([fields[f], fields[f + 1]], axis=1)
            got = jnp.dot(weights[...], both, preferred_element_type=f32)
            for i in range(2):
                lanes = slice(i * ny, (i + 1) * ny)
                grads[f + i, 0] = got[:own, lanes]
                grads[f + i, 2] = got[own : 2 * own, lanes]
                mine = fields[f + i, pl.ds(0, own)]
                wall = jnp.dot(mine, walls_ref[...], preferred_element_type=f32)
                grads[f + i, 1] = wall[:, :ny]
                laps[f + i] = got[2 * own :, lanes] + wall[:, ny:]
                plain[f + i] = mine.astype(f32)
            return carry

        lax.fori_loop(0, n_even // 2, slopes, 0)

        def base_at_mode(m, c):
            if m == 0:
                return base_at + c, None, 1.0
            at = base_at + n_mean + (abs(m) - 1) * 6 + c
            return at, at + 3, (1.0 if m > 0 else -1.0)

        def product(acc, flow, value):
            (fr, fi, sign), (vr, vi) = flow, value
            re, im = acc[0] + fr * vr, acc[1] + fr * vi
            if fi is not None:
                if sign > 0:
                    re, im = re - fi * vi, im + fi * vr
                else:
                    re, im = re + fi * vi, im - fi * vr
            return re, im

        def contribution(acc, pairs, rows):
            for d in range(3):
                for k, m, at in pairs:
                    fr, fi, sign = base_at_mode(m, d)
                    flow = (plain[fr, rows], None if fi is None else plain[fi, rows], sign)
                    along = (plain[at + d, rows], plain[at + d + nb_step(at), rows])
                    for c in range(3):
                        sr, si, _ = base_at_mode(m, c)
                        slope = (grads[sr, d, rows], None if si is None else grads[si, d, rows], sign)
                        grad = (grads[at + c, d, rows], grads[at + c + nb_step(at), d, rows])
                        acc[k, c] = product(acc[k, c], flow, grad)
                        acc[k, c] = product(acc[k, c], slope, along)
            return acc

        def nb_step(at):
            return 4 if at < n_pert else 3

        resident, below, above = [], [], []
        for k in range(per):
            for m in range(-modes, modes + 1):
                l = k - m
                if l < 0:
                    below.append((k, m, n_res + (l + modes) * 6))
                elif l >= per:
                    above.append((k, m, n_res + (sides - 1) * n_nb + (l - per) * 6))
                else:
                    resident.append((k, m, l * 8))
        half = per * harms // 2

        def block(b, carry):
            rows = pl.ds(pl.multiple_of(b * 8, 8), 8)
            zero = jnp.zeros((8, ny), f32)
            acc = {(k, c): (zero, zero) for k in range(per) for c in range(3)}
            acc = contribution(acc, resident, rows)
            solid = PENALTY * mask_ref[rows].astype(f32)
            for k in range(per):
                freq = FREQUENCY_STEP * (scal[0] * per + k - half).astype(f32)
                for c in range(3):
                    ur, ui = plain[k * 8 + c, rows], plain[k * 8 + 4 + c, rows]
                    re = acc[k, c][0] + grads[k * 8 + 3, c, rows] - VISCOSITY * laps[k * 8 + c, rows]
                    im = acc[k, c][1] + grads[k * 8 + 7, c, rows] - VISCOSITY * laps[k * 8 + 4 + c, rows]
                    out_ref[k * 8 + c, rows] = re * (1.0 / 12.0) + (solid * ur - freq * ui)
                    out_ref[k * 8 + 4 + c, rows] = im * (1.0 / 12.0) + (solid * ui + freq * ur)
                for i in range(2):
                    at = k * 8 + 4 * i
                    out_ref[at + 3, rows] = (grads[at, 0, rows] + grads[at + 1, 1, rows] + grads[at + 2, 2, rows]) * (1.0 / 12.0)
            return carry

        lax.fori_loop(0, own // 8, block, 0)

        def neighbours(pairs):
            def nb_block(b, carry):
                rows = pl.ds(pl.multiple_of(b * 8, 8), 8)
                zero = jnp.zeros((8, ny), f32)
                keys = sorted({k for k, _, _ in pairs})
                acc = {(k, c): (zero, zero) for k in keys for c in range(3)}
                acc = contribution(acc, pairs, rows)
                for k in keys:
                    for c in range(3):
                        for i in range(2):
                            at = k * 8 + 4 * i + c
                            out_ref[at, rows] = out_ref[at, rows] + acc[k, c][i] * (1.0 / 12.0)
                return carry

            lax.fori_loop(0, own // 8, nb_block, 0)

        pl.when(scal[0] > 0)(lambda: neighbours(below))
        pl.when(scal[0] < harms - 1)(lambda: neighbours(above))

    n_copies = 10 + 3 * sides + (1 if swap else 0)
    flat = lambda a: a.reshape(a.shape[0], -1, ny)
    with jax.named_scope("operator"):
        out = pl.pallas_call(
            operator,
            out_shape=jax.ShapeDtypeStruct((n_pert, own, ny), f32),
            in_specs=[ANY, VMEM, VMEM] + [ANY] * (8 + 2 * sides),
            out_specs=VMEM,
            scratch_shapes=[
                pltpu.VMEM((n_even, depth, ny), bf16),
                pltpu.VMEM((n_even, 3, own, ny), f32),
                pltpu.VMEM((n_even, own, ny), f32),
                pltpu.VMEM((n_even, own, ny), f32),
                pltpu.VMEM((3 * own, depth), bf16),
                pltpu.SemaphoreType.DMA((n_copies,)),
            ],
            compiler_params=pltpu.CompilerParams(vmem_limit_bytes=VMEM_BYTES),
        )(
            stencil, walls, mask, flat(pert), flat(mean), flat(mode), flat(first_got), flat(second_got), flat(near_got),
            xb_got, xa_got, *[flat(b) for b in nb_got], *relay_got,
        )
    return jnp.swapaxes(out.reshape(per, 2, 4, nz, nx, ny), 3, 4)


def solution(mesh):
    return jax.shard_map(
        shards,
        mesh=mesh,
        in_specs=(
            P("harm", None, None, "gx", "gz", None),
            P(None, "gx", "gz", None),
            P(None, None, None, "gx", "gz", None),
            P("gx", "gz", None),
        ),
        out_specs=P("harm", None, None, "gx", "gz", None),
        check_vma=False,
    )
```

```python
import jax
import jax.numpy as jnp
import numpy as np
from jax import lax
from jax.experimental import pallas as pl
from jax.experimental.pallas import tpu as pltpu
from jax.sharding import PartitionSpec as P

FREQUENCY_STEP = 0.2
VISCOSITY = 0.05
PENALTY = 4.0
FIRST = {-2: 1.0, -1: -8.0, 1: 8.0, 2: -1.0}
SECOND = {-2: -1.0, -1: 16.0, 0: -30.0, 1: 16.0, 2: -1.0}
HALO_X = 16
VMEM_BYTES = 56 * 1024 * 1024
ANY = pl.BlockSpec(memory_space=pl.ANY)
VMEM = pl.BlockSpec(memory_space=pltpu.VMEM)


def stencil_rows(nz, nx, odd):
    own = nz * nx
    at_xb, at_xa = own, own + HALO_X
    at_cross = own + 2 * HALO_X
    at_near = at_cross + 2 * nx
    depth = at_near + 2 * nx
    at_zb, at_za = (at_near, at_cross) if odd else (at_cross, at_near)
    rows = np.zeros((3, own, depth), np.float32)
    for z in range(nz):
        for x in range(nx):
            row = z * nx + x
            for table, parts in ((FIRST, (0, 1)), (SECOND, (2, 2))):
                for step, weight in table.items():
                    sx = x + step
                    if sx < 0:
                        column = at_xb + 2 * z + sx + 2
                    elif sx >= nx:
                        column = at_xa + 2 * z + sx - nx
                    else:
                        column = z * nx + sx
                    rows[parts[0], row, column] += weight
                    sz = z + step
                    if sz < 0:
                        column = at_zb + (sz + 2) * nx + x
                    elif sz >= nz:
                        column = at_za + (sz - nz) * nx + x
                    else:
                        column = sz * nx + x
                    rows[parts[1], row, column] += weight
    return rows.reshape(3 * own, depth)


def wall_columns(ny):
    out = np.zeros((ny, 2 * ny), np.float32)
    for part, table in enumerate((FIRST, SECOND)):
        for y in range(ny):
            for step, weight in table.items():
                if 0 <= y + step < ny:
                    out[y + step, part * ny + y] = weight
    return out


def wall_pairs(ny):
    first, second = np.split(wall_columns(ny), 2, axis=1)
    return np.block([[first, first, second, second], [first, -first, second, -second]])


def edge_rows(nz, nx):
    pick = np.zeros((2 * HALO_X, nz * nx), np.float32)
    for z in range(nz):
        for j in range(2):
            pick[2 * z + j, z * nx + j] = 1.0
            pick[HALO_X + 2 * z + j, z * nx + nx - 2 + j] = 1.0
    return pick


def run_copies(copies, sems):
    started = [pltpu.make_async_copy(src, dst, sems.at[i]) for i, (src, dst) in enumerate(copies)]
    for copy in started:
        copy.start()
    for copy in started:
        copy.wait()


def shards(perturbation, base_mean, base_modes, solid_mask):
    per, modes = perturbation.shape[0], base_modes.shape[0]
    nx, nz, ny = perturbation.shape[3], perturbation.shape[4], perturbation.shape[5]
    own = nz * nx
    bf16, f32 = jnp.bfloat16, jnp.float32
    harms, size_x, size_z = (lax.axis_size(a) for a in ("harm", "gx", "gz"))
    swap = harms == 2
    sides = 1 if swap else 2
    n_pert, n_mean, n_modes = per * 8, 3, modes * 6
    n_base = n_mean + n_modes
    n_res = n_pert + n_base
    n_nb = modes * 6
    n_all = n_res + sides * n_nb

    pert = jnp.swapaxes(perturbation, 3, 4).reshape(n_pert, nz, nx, ny)
    mean = jnp.swapaxes(base_mean, 1, 2)
    mode = jnp.swapaxes(base_modes, 3, 4).reshape(n_modes, nz, nx, ny)
    mask = jnp.swapaxes(solid_mask, 0, 1).reshape(own, ny)

    def place():
        me_h, odd = lax.axis_index("harm"), lax.rem(lax.axis_index("gz"), 2)
        shared = jnp.where(me_h == 0, per - modes, 0) if swap else 0
        return me_h, odd, odd * (nz - 2), (1 - odd) * (nz - 2), shared

    cross_pairs = [(i, (i + 1) % size_z if i % 2 else (i - 1) % size_z) for i in range(size_z)]
    near_pairs = [(i, i + 1 if i % 2 == 0 else i - 1) for i in range(size_z)]
    up_x = [(i, (i + 1) % size_x) for i in range(size_x)]
    down_x = [(j, i) for i, j in up_x]
    if swap:
        harm_perms = [[(0, 1), (1, 0)]]
    else:
        up_h = [(i, i + 1) for i in range(harms - 1)]
        harm_perms = [up_h, [(j, i) for i, j in up_h]]
    n_first = modes * 8 if swap else n_pert
    n_second = n_res - n_first

    def sent(s, scal):
        return scal[4] if swap else (per - modes if s == 0 else 0)

    face = lambda n: jax.ShapeDtypeStruct((n, 2, nx, ny), bf16)
    roomy = pltpu.CompilerParams(vmem_limit_bytes=VMEM_BYTES // 2)

    def pack_first(pert_ref, first_ref, *nb_refs):
        scal = place()
        at = scal[4] * 8 if swap else 0
        for f in range(n_first):
            first_ref[f] = pert_ref[at + f, pl.ds(scal[2], 2)]
        for s, nb_ref in enumerate(nb_refs):
            for i in range(modes * 2):
                for c in range(3):
                    nb_ref[3 * i + c] = pert_ref[sent(s, scal) * 8 + 4 * i + c]

    with jax.named_scope("pack_first"):
        first, *nb_send = pl.pallas_call(
            pack_first,
            out_shape=(face(n_first),) + tuple(jax.ShapeDtypeStruct((n_nb, nz, nx, ny), bf16) for _ in range(sides)),
            compiler_params=roomy,
        )(pert)
    first_got = lax.ppermute(first, "gz", cross_pairs)
    nb_got = [lax.ppermute(b, "harm", p) for b, p in zip(nb_send, harm_perms)]

    def pack_second(pick_ref, pert_ref, mean_ref, mode_ref, second_ref, lo_ref, hi_ref):
        scal = place()
        z = pl.ds(scal[2], 2)
        at = n_pert - n_first
        if swap:
            rest = (per - modes - scal[4]) * 8
            for f in range(at):
                second_ref[f] = pert_ref[rest + f, z]
        second_ref[at : at + n_mean] = mean_ref[:, z]
        second_ref[at + n_mean :] = mode_ref[:, z]
        pick = pick_ref[...]
        at = 0
        for ref, count in ((pert_ref, n_pert), (mean_ref, n_mean), (mode_ref, n_modes)):
            for f in range(0, count, 2):
                wide = min(2, count - f)
                rows = [ref[f + i].reshape(own, ny) for i in range(wide)]
                both = jnp.concatenate(rows, axis=1) if wide == 2 else rows[0]
                got = jnp.dot(pick, both, preferred_element_type=f32).astype(bf16)
                for i in range(wide):
                    lo_ref[at + f + i] = got[:HALO_X, i * ny : (i + 1) * ny]
                    hi_ref[at + f + i] = got[HALO_X:, i * ny : (i + 1) * ny]
            at += count

    edge = jax.ShapeDtypeStruct((n_res, HALO_X, ny), bf16)
    with jax.named_scope("pack_second"):
        second, edge_lo, edge_hi = pl.pallas_call(
            pack_second, out_shape=(face(n_second), edge, edge), compiler_params=roomy
        )(jnp.asarray(edge_rows(nz, nx), bf16), pert, mean, mode)
    second_got = lax.ppermute(second, "gz", cross_pairs)
    xb_got = lax.ppermute(edge_hi, "gx", up_x)
    xa_got = lax.ppermute(edge_lo, "gx", down_x)

    quarter = nx // 4
    part = own // 2
    walls_pair = jnp.asarray(wall_pairs(ny), bf16)
    table = stencil_rows(nz, nx, False).reshape(3, nz, nx, -1)
    PAIRS = ((0, 3), (1, 2))
    DRIFT = (-1.5 * FREQUENCY_STEP, -0.5 * FREQUENCY_STEP)

    def entries(t, p, q, r, s):
        return t, q, p + r, p - r, q + s, s - q, t + p, t - p

    def couple(acc, ent, vec):
        t, q, pr, pmr, qs, sq, tp, tmp = ent
        out = []
        for i in range(2):
            a, e, b, g = (vec[j][i] for j in range(4))
            out.append(
                (
                    acc[0][i] + t * a + pr * b + sq * g,
                    acc[1][i] + t * e + qs * b + pmr * g,
                    acc[2][i] + pr * a + qs * e + tp * b + q * g,
                    acc[3][i] + sq * a + pmr * e + q * b + tmp * g,
                )
            )
        return [(out[0][j], out[1][j]) for j in range(4)]

    def harmonics_of(acc, scale):
        out = [None] * 4
        for at, (lo, hi) in enumerate(PAIRS):
            (ar, ai), (er, ei) = acc[2 * at], acc[2 * at + 1]
            out[lo] = ((ar + ei) * scale, (ai - er) * scale)
            out[hi] = ((ar - ei) * scale, (ai + er) * scale)
        return out

    def basis_of(values):
        out = []
        for lo, hi in PAIRS:
            (lr, li), (hr, hi_) = values[lo], values[hi]
            out += [(lr + hr, li + hi_), (hi_ - li, lr - hr)]
        return out

    def resident_kernel(edge):
        def pick(x):
            x = x.reshape(nz, nx, ny)
            if edge:
                x = jnp.concatenate([x[:, :quarter], x[:, nx - quarter :]], axis=1)
            else:
                x = x[:, quarter : nx - quarter]
            return x.reshape(part, ny)

        cells = table[:, :, [*range(quarter), *range(nx - quarter, nx)]] if edge else table[:, :, quarter : nx - quarter]
        depth = own + 2 * HALO_X if edge else own
        rows_of = jnp.asarray(cells[..., :depth].reshape(3 * part, depth), bf16)

        def body(rows_ref, walls_ref, mask_ref, pert_ref, mean_ref, mode_ref, *rest):
            if edge:
                xb_ref, xa_ref = rest[:2]
            out_ref, grads, plain, ents, lin = rest[-5:]
            me_h = place()[0]
            mean_freq = 12.0 * FREQUENCY_STEP * (me_h * per + 1.5 - per * harms / 2).astype(f32)

            def rhs(ref, at, fields):
                cols = []
                for f in fields:
                    mine = ref[f]
                    if edge:
                        mine = jnp.concatenate([mine, xb_ref[at + f], xa_ref[at + f]], axis=0)
                    cols.append(mine)
                return cols[0] if len(cols) == 1 else jnp.concatenate(cols, axis=1)

            def dot(a, b):
                return jnp.dot(a, b, preferred_element_type=f32)

            for at, (lo, hi) in enumerate(PAIRS):
                for i in range(2):
                    fl, fr = lo * 8 + i * 4 + 3, hi * 8 + i * 4 + 3
                    got = dot(rows_ref[: 2 * part], rhs(pert_ref, 0, (fl, fr)))
                    wall = dot(jnp.concatenate([pick(pert_ref[fl].astype(f32)), pick(pert_ref[fr].astype(f32))], axis=1).astype(bf16), walls_ref[:, : 2 * ny])
                    for d in range(3):
                        if d == 1:
                            total, diff = wall[:, :ny], wall[:, ny:]
                        else:
                            span = slice(0, part) if d == 0 else slice(part, 2 * part)
                            total, diff = got[span, :ny] + got[span, ny:], got[span, :ny] - got[span, ny:]
                        lin[2 * at, i, d] = total
                        lin[2 * at + 1, 1 - i, d] = diff if i == 0 else -diff
            for at, (lo, hi) in enumerate(PAIRS):
                for c in range(3):
                    for i in range(2):
                        sign = 1.0 if i == 0 else -1.0
                        fl, fr = lo * 8 + i * 4 + c, hi * 8 + i * 4 + c
                        got = dot(rows_ref[...], rhs(pert_ref, 0, (fl, fr)))
                        xl, xr = pick(pert_ref[fl].astype(f32)), pick(pert_ref[fr].astype(f32))
                        wall = dot(jnp.concatenate([xl, xr], axis=1).astype(bf16), walls_ref[...])
                        total, diff = xl + xr, xl - xr
                        plain[2 * at, i, c] = total
                        plain[2 * at + 1, 1 - i, c] = sign * diff
                        for d in range(3):
                            if d == 1:
                                gt, gd = wall[:, :ny], wall[:, ny : 2 * ny]
                            else:
                                span = slice(0, part) if d == 0 else slice(part, 2 * part)
                                gt, gd = got[span, :ny] + got[span, ny:], got[span, :ny] - got[span, ny:]
                            gd = sign * gd
                            grads[2 * at, i, c, d] = gt
                            grads[2 * at + 1, 1 - i, c, d] = gd
                            if d == c:
                                if c == 0:
                                    lin[2 * at, i, 3] = gt
                                    lin[2 * at + 1, 1 - i, 3] = gd
                                else:
                                    lin[2 * at, i, 3] = lin[2 * at, i, 3] + gt
                                    lin[2 * at + 1, 1 - i, 3] = lin[2 * at + 1, 1 - i, 3] + gd
                        lt = got[2 * part :, :ny] + got[2 * part :, ny:] + wall[:, 2 * ny : 3 * ny]
                        ld = got[2 * part :, :ny] - got[2 * part :, ny:] + wall[:, 3 * ny :]
                        solid = (12.0 * PENALTY) * pick(mask_ref[...].astype(f32))
                        drift = 12.0 * DRIFT[at]
                        lin[2 * at, i, c] = lin[2 * at, i, c] - VISCOSITY * lt + solid * total
                        lin[2 * at + 1, 1 - i, c] = lin[2 * at + 1, 1 - i, c] + sign * (solid * diff - VISCOSITY * ld)
                        lin[2 * at, 1 - i, c] = lin[2 * at, 1 - i, c] + sign * (mean_freq * total + drift * diff)
                        lin[2 * at + 1, i, c] = lin[2 * at + 1, i, c] - (mean_freq * diff + drift * total)
            for c in range(3):
                picked = [pick(mean_ref[c].astype(f32))] + [pick(mode_ref[3 * i + c].astype(f32)) for i in range(4)]
                for n, ent in enumerate(entries(*picked)):
                    ents[c, n] = ent
                mean_at = dot(rows_ref[: 2 * part], rhs(mean_ref, n_pert, (c,)))
                mean_wall = dot(picked[0].astype(bf16), walls_ref[:ny, :ny])
                at = n_pert + n_mean
                real = dot(rows_ref[: 2 * part], rhs(mode_ref, at, (c, 6 + c)))
                imag = dot(rows_ref[: 2 * part], rhs(mode_ref, at, (3 + c, 9 + c)))
                wall_real = dot(jnp.concatenate([picked[1], picked[3]], axis=1).astype(bf16), walls_ref[:, : 2 * ny])
                wall_imag = dot(jnp.concatenate([picked[2], picked[4]], axis=1).astype(bf16), walls_ref[:, : 2 * ny])
                for d in range(3):
                    if d == 1:
                        pr, pmr = wall_real[:, :ny], wall_real[:, ny:]
                        qs, qms = wall_imag[:, :ny], wall_imag[:, ny:]
                        t, p, q = mean_wall, 0.5 * (pr + pmr), 0.5 * (qs + qms)
                        values = (t, q, pr, pmr, qs, -qms, t + p, t - p)
                    else:
                        span = slice(0, part) if d == 0 else slice(part, 2 * part)
                        values = entries(mean_at[span], real[span, :ny], imag[span, :ny], real[span, ny:], imag[span, ny:])
                    for n, ent in enumerate(values):
                        ents[3 + 3 * d + c, n] = ent

            def block(b, carry):
                rows = pl.ds(pl.multiple_of(b * 8, 8), 8)
                for c in range(4):
                    acc = [(lin[j, 0, c, rows], lin[j, 1, c, rows]) for j in range(4)]
                    if c < 3:
                        for d in range(3):
                            flow = [ents[d, n, rows] for n in range(8)]
                            acc = couple(acc, flow, [(grads[j, 0, c, d, rows], grads[j, 1, c, d, rows]) for j in range(4)])
                            slope = [ents[3 + 3 * d + c, n, rows] for n in range(8)]
                            acc = couple(acc, slope, [(plain[j, 0, d, rows], plain[j, 1, d, rows]) for j in range(4)])
                    for k, (re, im) in enumerate(harmonics_of(acc, 1.0 / 24.0)):
                        out_ref[k * 8 + c, rows] = re
                        out_ref[k * 8 + 4 + c, rows] = im
                return carry

            lax.fori_loop(0, part // 8, block, 0)

        def call(*extra):
            return pl.pallas_call(
                body,
                out_shape=jax.ShapeDtypeStruct((n_pert, part, ny), f32),
                in_specs=[VMEM] * 6 + ([VMEM, VMEM] if edge else [ANY]) + [ANY] * (len(extra) - (2 if edge else 1)),
                out_specs=VMEM,
                scratch_shapes=[
                    pltpu.VMEM((4, 2, 3, 3, part, ny), f32),
                    pltpu.VMEM((4, 2, 3, part, ny), f32),
                    pltpu.VMEM((12, 8, part, ny), f32),
                    pltpu.VMEM((4, 2, 4, part, ny), f32),
                ],
                compiler_params=roomy,
                cost_estimate=pl.CostEstimate(flops=40_000_000, bytes_accessed=20_000_000, transcendentals=0),
            )(rows_of, walls_pair, mask, flat(pert), flat(mean), flat(mode), *extra)

        return call

    flat = lambda a: a.reshape(a.shape[0], -1, ny)
    with jax.named_scope("resident_middle"):
        middle = resident_kernel(False)(edge_lo)

    deep = 2 * nx + 2 * HALO_X

    def pack_relay(first_ref, xb_ref, xa_ref, _, *outs):
        scal = place()
        for s, out in enumerate(outs):
            for i in range(modes * 2):
                field = sent(s, scal) * 8 + 4 * i
                near = 4 * i if swap else field
                for c in range(3):
                    out[3 * i + c, : 2 * nx] = first_ref[near + c].reshape(2 * nx, ny)
                    out[3 * i + c, 2 * nx : 2 * nx + HALO_X] = xb_ref[field + c]
                    out[3 * i + c, 2 * nx + HALO_X :] = xa_ref[field + c]

    with jax.named_scope("pack_relay"):
        relay = pl.pallas_call(
            pack_relay,
            out_shape=tuple(jax.ShapeDtypeStruct((n_nb, deep, ny), bf16) for _ in range(sides)),
            in_specs=[VMEM] * 3 + [ANY],
            compiler_params=roomy,
        )(first_got, xb_got, xa_got, middle)
    relay_got = [lax.ppermute(b, "harm", p) for b, p in zip(relay, harm_perms)]

    def pack_near(pert_ref, mean_ref, mode_ref, *rest):
        out = rest[-1]
        z = pl.ds(place()[3], 2)
        out[:n_pert] = pert_ref[:, z]
        out[n_pert : n_pert + n_mean] = mean_ref[:, z]
        out[n_pert + n_mean : n_res] = mode_ref[:, z]
        for s in range(sides):
            out[n_res + s * n_nb : n_res + (s + 1) * n_nb] = rest[s][:, z]

    with jax.named_scope("pack_near"):
        near = pl.pallas_call(
            pack_near,
            out_shape=face(n_all),
            in_specs=[VMEM] * (3 + sides) + [ANY],
            compiler_params=roomy,
        )(pert, mean, mode, *nb_got, relay[0])
    near_got = lax.ppermute(near, "gz", near_pairs)

    with jax.named_scope("resident_edge"):
        edges = resident_kernel(True)(xb_got, xa_got, relay[0], near)

    at_xb, at_cross = own, own + 2 * HALO_X
    at_near = at_cross + 2 * nx
    depth = at_near + 2 * nx
    both_stencils = np.stack([stencil_rows(nz, nx, odd)[: 2 * own] for odd in (False, True)])
    n_ext = n_modes + sides * n_nb

    def finish(stencil_any, walls_ref, pert_ref, mean_ref, mode_ref, middle_any, edges_any, mode_any, first_any, second_any, near_any, second_flat, near_flat, xb_any, xa_any, *rest):
        scal = place()
        nb_any, relay_any = rest[:sides], rest[sides : 2 * sides]
        out_ref, fields, halo, grads, plain, weights, sems = rest[2 * sides :]
        copies = [(stencil_any.at[scal[1]], weights)]
        cross, close = pl.ds(at_cross, 2 * nx), pl.ds(at_near, 2 * nx)
        mine = pl.ds(0, n_modes)
        base_modes_at = n_pert + n_mean
        second_at = n_pert - n_first
        copies.append((mode_any, fields.at[mine, pl.ds(0, own)]))
        copies.append((second_flat.at[pl.ds(second_at + n_mean, n_modes)], fields.at[mine, cross]))
        copies.append((near_flat.at[pl.ds(base_modes_at, n_modes)], fields.at[mine, close]))
        copies.append((xb_any.at[pl.ds(base_modes_at, n_modes)], fields.at[mine, pl.ds(at_xb, HALO_X)]))
        copies.append((xa_any.at[pl.ds(base_modes_at, n_modes)], fields.at[mine, pl.ds(at_xb + HALO_X, HALO_X)]))
        for s in range(sides):
            mine = pl.ds(n_modes + s * n_nb, n_nb)
            copies.append((nb_any[s], fields.at[mine, pl.ds(0, own)]))
            copies.append((relay_any[s].at[:, pl.ds(0, 2 * nx)], fields.at[mine, cross]))
            copies.append((relay_any[s].at[:, pl.ds(2 * nx, 2 * HALO_X)], fields.at[mine, pl.ds(at_xb, 2 * HALO_X)]))
            copies.append((near_flat.at[pl.ds(n_res + s * n_nb, n_nb)], fields.at[mine, close]))
        if swap:
            rest_at = per - modes - scal[4]
            copies.append((first_any, halo.at[0, pl.ds(scal[4] * 8, n_first)]))
            copies.append((second_any.at[pl.ds(0, second_at)], halo.at[0, pl.ds(rest_at * 8, second_at)]))
        else:
            copies.append((first_any, halo.at[0, pl.ds(0, n_pert)]))
        copies.append((second_any.at[pl.ds(second_at, n_base)], halo.at[0, pl.ds(n_pert, n_base)]))
        copies.append((near_any.at[pl.ds(0, n_res)], halo.at[1]))
        for z in range(nz):
            half = nx // 2
            copies.append((middle_any.at[:, pl.ds(z * half, half)], out_ref.at[:, pl.ds(z * nx + quarter, half)]))
            copies.append((edges_any.at[:, pl.ds(z * half, quarter)], out_ref.at[:, pl.ds(z * nx, quarter)]))
            copies.append((edges_any.at[:, pl.ds(z * half + quarter, quarter)], out_ref.at[:, pl.ds(z * nx + nx - quarter, quarter)]))
        run_copies(copies, sems)

        def slopes(pair, carry):
            f = 2 * pair
            both = jnp.concatenate([fields[f], fields[f + 1]], axis=1)
            got = jnp.dot(weights[...], both, preferred_element_type=f32)
            for i in range(2):
                lanes = slice(i * ny, (i + 1) * ny)
                grads[f + i, 0] = got[:own, lanes]
                grads[f + i, 2] = got[own:, lanes]
                own_rows = fields[f + i, pl.ds(0, own)]
                grads[f + i, 1] = jnp.dot(own_rows, walls_ref[:ny, :ny], preferred_element_type=f32)
                plain[f + i] = own_rows.astype(f32)
            return carry

        lax.fori_loop(0, n_ext // 2, slopes, 0)

        def product(acc, flow, value, sign):
            (fr, fi), (vr, vi) = flow, value
            if sign > 0:
                return acc[0] + fr * vr - fi * vi, acc[1] + fr * vi + fi * vr
            return acc[0] + fr * vr + fi * vi, acc[1] + fr * vi - fi * vr

        below, above = [], []
        for k in range(per):
            for m in range(-modes, modes + 1):
                l = k - m
                if l < 0:
                    below.append((k, m, n_modes + (l + modes) * 6))
                elif l >= per:
                    above.append((k, m, n_modes + (sides - 1) * n_nb + (l - per) * 6))

        def neighbours(pairs):
            def block(b, carry):
                rows = pl.ds(pl.multiple_of(b * 8, 8), 8)
                for k in sorted({p[0] for p in pairs}):
                    zero = jnp.zeros((8, ny), f32)
                    acc = [(zero, zero)] * 3
                    for _, m, at in [p for p in pairs if p[0] == k]:
                        base = (abs(m) - 1) * 6
                        for d in range(3):
                            flow = plain[base + d, rows], plain[base + 3 + d, rows]
                            along = plain[at + d, rows], plain[at + 3 + d, rows]
                            for c in range(3):
                                slope = grads[base + c, d, rows], grads[base + 3 + c, d, rows]
                                grad = grads[at + c, d, rows], grads[at + 3 + c, d, rows]
                                acc[c] = product(acc[c], flow, grad, m)
                                acc[c] = product(acc[c], slope, along, m)
                    for c in range(3):
                        for i in range(2):
                            at = k * 8 + 4 * i + c
                            out_ref[at, rows] = out_ref[at, rows] + acc[c][i] * (1.0 / 12.0)
                return carry

            lax.fori_loop(0, own // 8, block, 0)

        pl.when(scal[0] > 0)(lambda: neighbours(below))
        pl.when(scal[0] < harms - 1)(lambda: neighbours(above))

        def face_block(n, carry):
            side, step, chunk = n // 4, (n // 2) % 2, n % 2
            before = side == scal[1]
            near_at = jnp.where(before, 1, 0)
            layer = jnp.where(before, step, nz - 1 - step)
            turn = jnp.where(before, 1.0, -1.0)
            first_step = step == 0
            cn, cf = turn * jnp.where(first_step, -8.0, 1.0), turn * jnp.where(first_step, 1.0, 0.0)
            ln, lf = jnp.where(first_step, 16.0, -1.0), jnp.where(first_step, -1.0, 0.0)
            rows = pl.ds(pl.multiple_of(layer * nx + chunk * 16, 16), 16)
            strip = pl.ds(pl.multiple_of(chunk * 16, 16), 16)

            def halos(f):
                return halo[side, f, near_at, strip].astype(f32), halo[side, f, 1 - near_at, strip].astype(f32)

            def slope(f):
                a, b = halos(f)
                return cn * a + cf * b

            def slope_lap(f):
                a, b = halos(f)
                return cn * a + cf * b, ln * a + lf * b

            flow = entries(mean_ref[2, rows].astype(f32), *[mode_ref[3 * i + 2, rows].astype(f32) for i in range(4)])
            along = basis_of([(pert_ref[l * 8 + 2, rows].astype(f32), pert_ref[l * 8 + 6, rows].astype(f32)) for l in range(per)])
            for c in range(4):
                if c < 3:
                    got = [[slope_lap(l * 8 + 4 * i + c) for i in range(2)] for l in range(per)]
                    vec = basis_of([(g[0][0], g[1][0]) for g in got])
                    lap = basis_of([(g[0][1], g[1][1]) for g in got])
                    acc = [tuple(-VISCOSITY * v for v in pair) for pair in lap]
                    if c == 2:
                        press = basis_of([(slope(l * 8 + 3), slope(l * 8 + 7)) for l in range(per)])
                        acc = [(a[0] + p[0], a[1] + p[1]) for a, p in zip(acc, press)]
                    acc = couple(acc, flow, vec)
                    bend = entries(slope(n_pert + c), *[slope(n_pert + n_mean + 3 * i + c) for i in range(4)])
                    acc = couple(acc, bend, along)
                else:
                    acc = vec
                for k, parts in enumerate(harmonics_of(acc, 1.0 / 24.0)):
                    for i in range(2):
                        at = k * 8 + 4 * i + c
                        out_ref[at, rows] = out_ref[at, rows] + parts[i]
            return carry

        lax.fori_loop(0, 8, face_block, 0)

    n_copies = 6 + 4 * sides + (2 if swap else 1) + 2 + 3 * nz
    with jax.named_scope("finish"):
        out = pl.pallas_call(
            finish,
            out_shape=jax.ShapeDtypeStruct((n_pert, own, ny), f32),
            in_specs=[ANY] + [VMEM] * 4 + [ANY] * (10 + 2 * sides),
            out_specs=VMEM,
            scratch_shapes=[
                pltpu.VMEM((n_ext, depth, ny), bf16),
                pltpu.VMEM((2, n_res, 2, nx, ny), bf16),
                pltpu.VMEM((n_ext, 3, own, ny), f32),
                pltpu.VMEM((n_ext, own, ny), f32),
                pltpu.VMEM((2 * own, depth), bf16),
                pltpu.SemaphoreType.DMA((n_copies,)),
            ],
            compiler_params=roomy,
            cost_estimate=pl.CostEstimate(flops=40_000_000, bytes_accessed=20_000_000, transcendentals=0),
        )(
            jnp.asarray(both_stencils, bf16), walls_pair, flat(pert), flat(mean), flat(mode), middle, edges, flat(mode),
            first_got, second_got, near_got, flat(second_got), flat(near_got), xb_got, xa_got, *[flat(b) for b in nb_got], *relay_got,
        )
    return jnp.swapaxes(out.reshape(per, 2, 4, nz, nx, ny), 3, 4)


def solution(mesh):
    return jax.shard_map(
        shards,
        mesh=mesh,
        in_specs=(
            P("harm", None, None, "gx", "gz", None),
            P(None, "gx", "gz", None),
            P(None, None, None, "gx", "gz", None),
            P("gx", "gz", None),
        ),
        out_specs=P("harm", None, None, "gx", "gz", None),
        check_vma=False,
    )
```

```python
import jax
import jax.numpy as jnp
import numpy as np
from jax import lax
from jax.experimental import pallas as pl
from jax.experimental.pallas import tpu as pltpu
from jax.sharding import PartitionSpec as P

FREQUENCY_STEP = 0.2
VISCOSITY = 0.05
PENALTY = 4.0
FIRST = {-2: 1.0, -1: -8.0, 1: 8.0, 2: -1.0}
SECOND = {-2: -1.0, -1: 16.0, 0: -30.0, 1: 16.0, 2: -1.0}
HALO_X = 16
VMEM_BYTES = 58 * 1024 * 1024
ANY = pl.BlockSpec(memory_space=pl.ANY)
VMEM = pl.BlockSpec(memory_space=pltpu.VMEM)
HBM = pl.BlockSpec(memory_space=pltpu.HBM)


def stencil_rows(nz, nx, odd):
    own = nz * nx
    at_xb, at_xa = own, own + HALO_X
    at_cross = own + 2 * HALO_X
    at_near = at_cross + 2 * nx
    depth = at_near + 2 * nx
    at_zb, at_za = (at_near, at_cross) if odd else (at_cross, at_near)
    rows = np.zeros((3, own, depth), np.float32)
    for z in range(nz):
        for x in range(nx):
            row = z * nx + x
            for table, parts in ((FIRST, (0, 1)), (SECOND, (2, 2))):
                for step, weight in table.items():
                    sx = x + step
                    if sx < 0:
                        column = at_xb + 2 * z + sx + 2
                    elif sx >= nx:
                        column = at_xa + 2 * z + sx - nx
                    else:
                        column = z * nx + sx
                    rows[parts[0], row, column] += weight
                    sz = z + step
                    if sz < 0:
                        column = at_zb + (sz + 2) * nx + x
                    elif sz >= nz:
                        column = at_za + (sz - nz) * nx + x
                    else:
                        column = sz * nx + x
                    rows[parts[1], row, column] += weight
    return rows.reshape(3 * own, depth)


def wall_columns(ny):
    out = np.zeros((ny, 2 * ny), np.float32)
    for part, table in enumerate((FIRST, SECOND)):
        for y in range(ny):
            for step, weight in table.items():
                if 0 <= y + step < ny:
                    out[y + step, part * ny + y] = weight
    return out


def wall_pairs(ny):
    first, second = np.split(wall_columns(ny), 2, axis=1)
    return np.block([[first, first, second, second], [first, -first, second, -second]])


def edge_stencil(nz):
    out = np.zeros((2, nz, 8, 2 * HALO_X), np.float32)
    for z in range(nz):
        xb, xa = 2 * z, HALO_X + 2 * z
        out[0, z, 0, xb], out[0, z, 0, xb + 1], out[0, z, 1, xb + 1] = 1.0, -8.0, 1.0
        out[1, z, 6, xa], out[1, z, 7, xa], out[1, z, 7, xa + 1] = -1.0, 8.0, -1.0
    return out.reshape(16 * nz, 2 * HALO_X)


def edge_rows(nz, nx):
    pick = np.zeros((2 * HALO_X, nz * nx), np.float32)
    for z in range(nz):
        for j in range(2):
            pick[2 * z + j, z * nx + j] = 1.0
            pick[HALO_X + 2 * z + j, z * nx + nx - 2 + j] = 1.0
    return pick


def run_copies(copies, sems):
    started = [pltpu.make_async_copy(src, dst, sems.at[i]) for i, (src, dst) in enumerate(copies)]
    for copy in started:
        copy.start()
    for copy in started:
        copy.wait()


def shards(perturbation, base_mean, base_modes, solid_mask):
    per, modes = perturbation.shape[0], base_modes.shape[0]
    nx, nz, ny = perturbation.shape[3], perturbation.shape[4], perturbation.shape[5]
    own = nz * nx
    bf16, f32 = jnp.bfloat16, jnp.float32
    harms, size_x, size_z = (lax.axis_size(a) for a in ("harm", "gx", "gz"))
    swap = harms == 2
    sides = 1 if swap else 2
    n_pert, n_mean, n_modes = per * 8, 3, modes * 6
    n_base = n_mean + n_modes
    n_res = n_pert + n_base
    n_nb = modes * 6
    n_all = n_res + sides * n_nb

    pert = jnp.swapaxes(perturbation, 3, 4).reshape(n_pert, nz, nx, ny)
    mean = jnp.swapaxes(base_mean, 1, 2)
    mode = jnp.swapaxes(base_modes, 3, 4).reshape(n_modes, nz, nx, ny)
    mask = jnp.swapaxes(solid_mask, 0, 1).reshape(own, ny)

    def place():
        me_h, odd = lax.axis_index("harm"), lax.rem(lax.axis_index("gz"), 2)
        shared = jnp.where(me_h == 0, per - modes, 0) if swap else 0
        return me_h, odd, odd * (nz - 2), (1 - odd) * (nz - 2), shared

    cross_pairs = [(i, (i + 1) % size_z if i % 2 else (i - 1) % size_z) for i in range(size_z)]
    near_pairs = [(i, i + 1 if i % 2 == 0 else i - 1) for i in range(size_z)]
    up_x = [(i, (i + 1) % size_x) for i in range(size_x)]
    down_x = [(j, i) for i, j in up_x]
    if swap:
        harm_perms = [[(0, 1), (1, 0)]]
    else:
        up_h = [(i, i + 1) for i in range(harms - 1)]
        harm_perms = [up_h, [(j, i) for i, j in up_h]]
    def sent(s, scal):
        return scal[4] if swap else (per - modes if s == 0 else 0)

    face = lambda n: jax.ShapeDtypeStruct((n, 2, nx, ny), bf16)
    roomy = pltpu.CompilerParams(vmem_limit_bytes=28 * 1024 * 1024)

    chunks = [(at, 8) for at in range(0, n_pert, 8)]

    def pack(pick_any, pert_any, mean_any, mode_any, first_ref, second_ref, lo_ref, hi_ref, *rest):
        nb_refs = rest[:sides]
        pick_ref, pert_ref, mean_ref, mode_ref, sems = rest[sides:]
        scal = place()
        loads = [(pert_any.at[pl.ds(*c)], pert_ref.at[pl.ds(*c)]) for c in chunks]
        loads += [(mean_any, mean_ref), (mode_any, mode_ref), (pick_any, pick_ref)]
        run_copies(loads, sems)
        z = pl.ds(scal[2], 2)
        for f in range(n_pert):
            first_ref[f] = pert_ref[f, z]
        for f in range(n_mean):
            second_ref[f] = mean_ref[f, z]
        for f in range(n_modes):
            second_ref[n_mean + f] = mode_ref[f, z]
        for s, nb_ref in enumerate(nb_refs):
            for i in range(modes * 2):
                for c in range(3):
                    nb_ref[3 * i + c] = pert_ref[sent(s, scal) * 8 + 4 * i + c]
        pick = pick_ref[...]
        at = 0
        for ref, count in ((pert_ref, n_pert), (mean_ref, n_mean), (mode_ref, n_modes)):
            for f in range(0, count, 2):
                wide = min(2, count - f)
                rows = [ref[f + i].reshape(own, ny) for i in range(wide)]
                both = jnp.concatenate(rows, axis=1) if wide == 2 else rows[0]
                got = jnp.dot(pick, both, preferred_element_type=f32).astype(bf16)
                for i in range(wide):
                    lo_ref[at + f + i] = got[:HALO_X, i * ny : (i + 1) * ny]
                    hi_ref[at + f + i] = got[HALO_X:, i * ny : (i + 1) * ny]
            at += count

    edge = jax.ShapeDtypeStruct((n_res, HALO_X, ny), bf16)
    with jax.named_scope("pack"):
        first, second, edge_lo, edge_hi, *nb_send = pl.pallas_call(
            pack,
            out_shape=(face(n_pert), face(n_base), edge, edge) + tuple(jax.ShapeDtypeStruct((n_nb, nz, nx, ny), bf16) for _ in range(sides)),
            in_specs=[HBM] * 4,
            scratch_shapes=[
                pltpu.VMEM((2 * HALO_X, own), bf16),
                pltpu.VMEM((n_pert, nz, nx, ny), bf16),
                pltpu.VMEM((n_mean, nz, nx, ny), bf16),
                pltpu.VMEM((n_modes, nz, nx, ny), bf16),
                pltpu.SemaphoreType.DMA((len(chunks) + 3,)),
            ],
            compiler_params=pltpu.CompilerParams(vmem_limit_bytes=VMEM_BYTES),
        )(jnp.asarray(edge_rows(nz, nx), bf16), pert, mean, mode)
    first_got = lax.ppermute(first, "gz", cross_pairs)
    nb_got = [lax.ppermute(b, "harm", p) for b, p in zip(nb_send, harm_perms)]
    xb_got = lax.ppermute(edge_hi, "gx", up_x)
    xa_got = lax.ppermute(edge_lo, "gx", down_x)
    second_got = lax.ppermute(second, "gz", cross_pairs)

    quarter = nx // 4
    part = own // 2
    walls_pair = jnp.asarray(wall_pairs(ny), bf16)
    table = stencil_rows(nz, nx, False).reshape(3, nz, nx, -1)
    PAIRS = ((0, 3), (1, 2))
    DRIFT = (-1.5 * FREQUENCY_STEP, -0.5 * FREQUENCY_STEP)

    def entries(t, p, q, r, s):
        return t, q, p + r, p - r, q + s, s - q, t + p, t - p

    def couple(acc, ent, vec):
        t, q, pr, pmr, qs, sq, tp, tmp = ent
        out = []
        for i in range(2):
            a, e, b, g = (vec[j][i] for j in range(4))
            out.append(
                (
                    acc[0][i] + t * a + pr * b + sq * g,
                    acc[1][i] + t * e + qs * b + pmr * g,
                    acc[2][i] + pr * a + qs * e + tp * b + q * g,
                    acc[3][i] + sq * a + pmr * e + q * b + tmp * g,
                )
            )
        return [(out[0][j], out[1][j]) for j in range(4)]

    def harmonics_of(acc, scale):
        out = [None] * 4
        for at, (lo, hi) in enumerate(PAIRS):
            (ar, ai), (er, ei) = acc[2 * at], acc[2 * at + 1]
            out[lo] = ((ar + ei) * scale, (ai - er) * scale)
            out[hi] = ((ar - ei) * scale, (ai + er) * scale)
        return out

    def basis_of(values):
        out = []
        for lo, hi in PAIRS:
            (lr, li), (hr, hi_) = values[lo], values[hi]
            out += [(lr + hr, li + hi_), (hi_ - li, lr - hr)]
        return out

    def resident_kernel(edge):
        def pick(x):
            x = x.reshape(nz, nx, ny)
            if edge:
                x = jnp.concatenate([x[:, :quarter], x[:, nx - quarter :]], axis=1)
            else:
                x = x[:, quarter : nx - quarter]
            return x.reshape(part, ny)

        cells = table[:, :, [*range(quarter), *range(nx - quarter, nx)]] if edge else table[:, :, quarter : nx - quarter]
        depth = own + 2 * HALO_X if edge else own
        rows_of = jnp.asarray(cells[..., :depth].reshape(3 * part, depth), bf16)

        def body(rows_ref, walls_ref, mask_ref, pert_ref, mean_ref, mode_ref, *rest):
            if edge:
                xb_ref, xa_ref = rest[:2]
            out_ref, grads, plain, ents, lin = rest[-5:]
            me_h = place()[0]
            mean_freq = 12.0 * FREQUENCY_STEP * (me_h * per + 1.5 - per * harms / 2).astype(f32)

            def rhs(ref, at, fields):
                cols = []
                for f in fields:
                    mine = ref[f]
                    if edge:
                        mine = jnp.concatenate([mine, xb_ref[at + f], xa_ref[at + f]], axis=0)
                    cols.append(mine)
                return cols[0] if len(cols) == 1 else jnp.concatenate(cols, axis=1)

            def dot(a, b):
                return jnp.dot(a, b, preferred_element_type=f32)

            for at, (lo, hi) in enumerate(PAIRS):
                for i in range(2):
                    fl, fr = lo * 8 + i * 4 + 3, hi * 8 + i * 4 + 3
                    got = dot(rows_ref[: 2 * part], rhs(pert_ref, 0, (fl, fr)))
                    wall = dot(jnp.concatenate([pick(pert_ref[fl].astype(f32)), pick(pert_ref[fr].astype(f32))], axis=1).astype(bf16), walls_ref[:, : 2 * ny])
                    for d in range(3):
                        if d == 1:
                            total, diff = wall[:, :ny], wall[:, ny:]
                        else:
                            span = slice(0, part) if d == 0 else slice(part, 2 * part)
                            total, diff = got[span, :ny] + got[span, ny:], got[span, :ny] - got[span, ny:]
                        lin[2 * at, i, d] = total
                        lin[2 * at + 1, 1 - i, d] = diff if i == 0 else -diff
            for at, (lo, hi) in enumerate(PAIRS):
                for c in range(3):
                    for i in range(2):
                        sign = 1.0 if i == 0 else -1.0
                        fl, fr = lo * 8 + i * 4 + c, hi * 8 + i * 4 + c
                        got = dot(rows_ref[...], rhs(pert_ref, 0, (fl, fr)))
                        xl, xr = pick(pert_ref[fl].astype(f32)), pick(pert_ref[fr].astype(f32))
                        wall = dot(jnp.concatenate([xl, xr], axis=1).astype(bf16), walls_ref[...])
                        total, diff = xl + xr, xl - xr
                        plain[2 * at, i, c] = total
                        plain[2 * at + 1, 1 - i, c] = sign * diff
                        for d in range(3):
                            if d == 1:
                                gt, gd = wall[:, :ny], wall[:, ny : 2 * ny]
                            else:
                                span = slice(0, part) if d == 0 else slice(part, 2 * part)
                                gt, gd = got[span, :ny] + got[span, ny:], got[span, :ny] - got[span, ny:]
                            gd = sign * gd
                            grads[2 * at, i, c, d] = gt
                            grads[2 * at + 1, 1 - i, c, d] = gd
                            if d == c:
                                if c == 0:
                                    lin[2 * at, i, 3] = gt
                                    lin[2 * at + 1, 1 - i, 3] = gd
                                else:
                                    lin[2 * at, i, 3] = lin[2 * at, i, 3] + gt
                                    lin[2 * at + 1, 1 - i, 3] = lin[2 * at + 1, 1 - i, 3] + gd
                        lt = got[2 * part :, :ny] + got[2 * part :, ny:] + wall[:, 2 * ny : 3 * ny]
                        ld = got[2 * part :, :ny] - got[2 * part :, ny:] + wall[:, 3 * ny :]
                        solid = (12.0 * PENALTY) * pick(mask_ref[...].astype(f32))
                        drift = 12.0 * DRIFT[at]
                        lin[2 * at, i, c] = lin[2 * at, i, c] - VISCOSITY * lt + solid * total
                        lin[2 * at + 1, 1 - i, c] = lin[2 * at + 1, 1 - i, c] + sign * (solid * diff - VISCOSITY * ld)
                        lin[2 * at, 1 - i, c] = lin[2 * at, 1 - i, c] + sign * (mean_freq * total + drift * diff)
                        lin[2 * at + 1, i, c] = lin[2 * at + 1, i, c] - (mean_freq * diff + drift * total)
            for c in range(3):
                picked = [pick(mean_ref[c].astype(f32))] + [pick(mode_ref[3 * i + c].astype(f32)) for i in range(4)]
                for n, ent in enumerate(entries(*picked)):
                    ents[c, n] = ent
                mean_at = dot(rows_ref[: 2 * part], rhs(mean_ref, n_pert, (c,)))
                mean_wall = dot(picked[0].astype(bf16), walls_ref[:ny, :ny])
                at = n_pert + n_mean
                real = dot(rows_ref[: 2 * part], rhs(mode_ref, at, (c, 6 + c)))
                imag = dot(rows_ref[: 2 * part], rhs(mode_ref, at, (3 + c, 9 + c)))
                wall_real = dot(jnp.concatenate([picked[1], picked[3]], axis=1).astype(bf16), walls_ref[:, : 2 * ny])
                wall_imag = dot(jnp.concatenate([picked[2], picked[4]], axis=1).astype(bf16), walls_ref[:, : 2 * ny])
                for d in range(3):
                    if d == 1:
                        pr, pmr = wall_real[:, :ny], wall_real[:, ny:]
                        qs, qms = wall_imag[:, :ny], wall_imag[:, ny:]
                        t, p, q = mean_wall, 0.5 * (pr + pmr), 0.5 * (qs + qms)
                        values = (t, q, pr, pmr, qs, -qms, t + p, t - p)
                    else:
                        span = slice(0, part) if d == 0 else slice(part, 2 * part)
                        values = entries(mean_at[span], real[span, :ny], imag[span, :ny], real[span, ny:], imag[span, ny:])
                    for n, ent in enumerate(values):
                        ents[3 + 3 * d + c, n] = ent

            def block(b, carry):
                rows = pl.ds(pl.multiple_of(b * 8, 8), 8)
                for c in range(4):
                    acc = [(lin[j, 0, c, rows], lin[j, 1, c, rows]) for j in range(4)]
                    if c < 3:
                        for d in range(3):
                            flow = [ents[d, n, rows] for n in range(8)]
                            acc = couple(acc, flow, [(grads[j, 0, c, d, rows], grads[j, 1, c, d, rows]) for j in range(4)])
                            slope = [ents[3 + 3 * d + c, n, rows] for n in range(8)]
                            acc = couple(acc, slope, [(plain[j, 0, d, rows], plain[j, 1, d, rows]) for j in range(4)])
                    for k, (re, im) in enumerate(harmonics_of(acc, 1.0 / 24.0)):
                        out_ref[k * 8 + c, rows] = re
                        out_ref[k * 8 + 4 + c, rows] = im
                return carry

            lax.fori_loop(0, part // 8, block, 0)

        def call(*extra):
            return pl.pallas_call(
                body,
                out_shape=jax.ShapeDtypeStruct((n_pert, part, ny), f32),
                in_specs=[VMEM] * 6 + ([VMEM, VMEM] if edge else [ANY]) + [ANY] * (len(extra) - (2 if edge else 1)),
                out_specs=VMEM,
                scratch_shapes=[
                    pltpu.VMEM((4, 2, 3, 3, part, ny), f32),
                    pltpu.VMEM((4, 2, 3, part, ny), f32),
                    pltpu.VMEM((12, 8, part, ny), f32),
                    pltpu.VMEM((4, 2, 4, part, ny), f32),
                ],
                compiler_params=roomy,
                cost_estimate=pl.CostEstimate(flops=40_000_000, bytes_accessed=20_000_000, transcendentals=0),
            )(rows_of, walls_pair, mask, flat(pert), flat(mean), flat(mode), *extra)

        return call

    flat = lambda a: a.reshape(a.shape[0], -1, ny)
    with jax.named_scope("resident_middle"):
        middle = resident_kernel(False)(edge_lo)

    deep = 2 * nx + 2 * HALO_X

    def pack_relay(first_ref, xb_ref, xa_ref, _, *outs):
        scal = place()
        for s, out in enumerate(outs):
            for i in range(modes * 2):
                field = sent(s, scal) * 8 + 4 * i
                for c in range(3):
                    out[3 * i + c, : 2 * nx] = first_ref[field + c].reshape(2 * nx, ny)
                    out[3 * i + c, 2 * nx : 2 * nx + HALO_X] = xb_ref[field + c]
                    out[3 * i + c, 2 * nx + HALO_X :] = xa_ref[field + c]

    with jax.named_scope("pack_relay"):
        relay = pl.pallas_call(
            pack_relay,
            out_shape=tuple(jax.ShapeDtypeStruct((n_nb, deep, ny), bf16) for _ in range(sides)),
            in_specs=[VMEM] * 3 + [ANY],
            compiler_params=roomy,
        )(first_got, xb_got, xa_got, middle)
    relay_got = [lax.ppermute(b, "harm", p) for b, p in zip(relay, harm_perms)]

    def pack_near(pert_ref, mean_ref, mode_ref, *rest):
        out = rest[-1]
        z = pl.ds(place()[3], 2)
        out[:n_pert] = pert_ref[:, z]
        out[n_pert : n_pert + n_mean] = mean_ref[:, z]
        out[n_pert + n_mean : n_res] = mode_ref[:, z]
        for s in range(sides):
            out[n_res + s * n_nb : n_res + (s + 1) * n_nb] = rest[s][:, z]

    with jax.named_scope("pack_near"):
        near = pl.pallas_call(
            pack_near,
            out_shape=face(n_all),
            in_specs=[VMEM] * (3 + sides) + [ANY],
            compiler_params=roomy,
        )(pert, mean, mode, *nb_got, relay[0])
    near_got = lax.ppermute(near, "gz", near_pairs)

    with jax.named_scope("resident_edge"):
        edges = resident_kernel(True)(xb_got, xa_got, relay[0], near)

    below, above = [], []
    for k in range(per):
        for m in range(-modes, modes + 1):
            l = k - m
            if l < 0:
                below.append((k, m, 0, (l + modes) * 6))
            elif l >= per:
                above.append((k, m, sides - 1, (l - per) * 6))

    def on_sides(work):
        me_h = lax.axis_index("harm")
        pl.when(me_h > 0)(lambda: work(below))
        pl.when(me_h < harms - 1)(lambda: work(above))

    def product(acc, flow, value, m):
        (fr, fi), (vr, vi) = flow, value
        if m > 0:
            return acc[0] + fr * vr - fi * vi, acc[1] + fr * vi + fi * vr
        return acc[0] + fr * vr + fi * vi, acc[1] + fr * vi - fi * vr

    own_stencil = stencil_rows(nz, nx, False)[: 2 * own, : own + 2 * HALO_X]
    base_modes_at = n_pert + n_mean

    def neighbours(stencil_ref, walls_ref, mode_ref, xb_ref, xa_ref, middle_ref, edges_ref, *rest):
        nb_refs = rest[:sides]
        out_ref, grads, plain = rest[-3:]

        def slopes(at, mine, halo):
            both = jnp.concatenate(mine, axis=1)
            rows = both if halo is None else jnp.concatenate([both, halo], axis=0)
            got = jnp.dot(stencil_ref[:, : rows.shape[0]], rows, preferred_element_type=f32)
            wall = [jnp.dot(x, walls_ref[:ny, :ny], preferred_element_type=f32) for x in mine]
            for i in range(2):
                lanes = slice(i * ny, (i + 1) * ny)
                grads[at + i, 0] = got[:own, lanes]
                grads[at + i, 2] = got[own:, lanes]
                grads[at + i, 1] = wall[i]
                plain[at + i] = mine[i].astype(f32)

        for f in range(0, n_modes, 2):
            at = base_modes_at + f
            halo = [jnp.concatenate([ref[at], ref[at + 1]], axis=1) for ref in (xb_ref, xa_ref)]
            slopes(f, [mode_ref[f], mode_ref[f + 1]], jnp.concatenate(halo, axis=0))
        for s in range(sides):
            for f in range(0, n_nb, 2):
                slopes(n_modes + s * n_nb + f, [nb_refs[s][f], nb_refs[s][f + 1]], None)

        for z in range(nz):
            half, at = nx // 2, z * nx
            out_ref[:, at : at + quarter] = edges_ref[:, z * half : z * half + quarter]
            out_ref[:, at + quarter : at + quarter + half] = middle_ref[:, z * half : (z + 1) * half]
            out_ref[:, at + quarter + half : at + nx] = edges_ref[:, z * half + quarter : (z + 1) * half]

        def work(pairs):
            def block(b, carry):
                rows = pl.ds(pl.multiple_of(b * 8, 8), 8)
                for k in sorted({p[0] for p in pairs}):
                    zero = jnp.zeros((8, ny), f32)
                    acc = [(zero, zero)] * 3
                    for _, m, s, f in [p for p in pairs if p[0] == k]:
                        at, base = n_modes + s * n_nb + f, (abs(m) - 1) * 6
                        for d in range(3):
                            flow = plain[base + d, rows], plain[base + 3 + d, rows]
                            along = plain[at + d, rows], plain[at + 3 + d, rows]
                            for c in range(3):
                                slope = grads[base + c, d, rows], grads[base + 3 + c, d, rows]
                                grad = grads[at + c, d, rows], grads[at + 3 + c, d, rows]
                                acc[c] = product(acc[c], flow, grad, m)
                                acc[c] = product(acc[c], slope, along, m)
                    for c in range(3):
                        for i in range(2):
                            at = k * 8 + 4 * i + c
                            out_ref[at, rows] = out_ref[at, rows] + acc[c][i] * (1.0 / 12.0)
                return carry

            lax.fori_loop(0, own // 8, block, 0)

        on_sides(work)

    n_ext = n_modes + sides * n_nb
    with jax.named_scope("neighbours"):
        inner = pl.pallas_call(
            neighbours,
            out_shape=jax.ShapeDtypeStruct((n_pert, own, ny), f32),
            scratch_shapes=[pltpu.VMEM((n_ext, 3, own, ny), f32), pltpu.VMEM((n_ext, own, ny), f32)],
            compiler_params=roomy,
        )(jnp.asarray(own_stencil, bf16), walls_pair, flat(mode), xb_got, xa_got, middle, edges, *[flat(b) for b in nb_got])

    def finish(edge_ref, pert_ref, mean_ref, mode_ref, inner_ref, first_ref, second_ref, near_ref, *rest):
        relay_refs, nb_refs = rest[:sides], rest[sides : 2 * sides]
        out_any, done, bends, sems = rest[2 * sides :]
        odd = place()[1]
        half = nx // 2
        done[...] = inner_ref[...]

        def send(layer):
            rows = pl.ds(pl.multiple_of(layer * nx, nx), nx)
            return pltpu.make_async_copy(done.at[:, rows], out_any.at[:, rows], sems.at[layer])

        for s in range(sides):
            for f in range(0, n_nb, 2):
                both = jnp.concatenate([relay_refs[s][f + i, 2 * nx :] for i in range(2)], axis=1)
                got = jnp.dot(edge_ref[...], both, preferred_element_type=f32)
                for i in range(2):
                    bends[s * n_nb + f + i] = got[:, i * ny : (i + 1) * ny]

        def edge_work(pairs):
            def layer_edges(z, carry):
                for end in range(2):
                    strip = pl.ds(pl.multiple_of(z * nx + end * half, 16), 16)
                    keep = slice(8 * end, 8 * end + 8)
                    rows = pl.ds(pl.multiple_of(z * nx + end * (nx - 8), 8), 8)
                    bent = pl.ds(pl.multiple_of((end * nz + z) * 8, 8), 8)
                    for k in sorted({p[0] for p in pairs}):
                        zero = jnp.zeros((8, ny), f32)
                        acc = [(zero, zero)] * 3
                        for _, m, s, f in [p for p in pairs if p[0] == k]:
                            base = (abs(m) - 1) * 6
                            flow = tuple(mode_ref[base + 3 * i, strip].astype(f32)[keep] for i in range(2))
                            for c in range(3):
                                at = s * n_nb + f + c
                                acc[c] = product(acc[c], flow, (bends[at, bent], bends[at + 3, bent]), m)
                        for c in range(3):
                            for i in range(2):
                                at = k * 8 + 4 * i + c
                                done[at, rows] = done[at, rows] + acc[c][i] * (1.0 / 12.0)
                return carry

            lax.fori_loop(0, nz, layer_edges, 0)

        on_sides(edge_work)
        for layer in range(2, nz - 2):
            send(layer).start()

        def face_layer(cross, step):
            before = (odd == 0) if cross else (odd == 1)
            near_at = jnp.where(before, 1, 0)
            layer = jnp.where(before, step, nz - 1 - step)
            turn = jnp.where(before, 1.0, -1.0)
            first_step = step == 0
            cn, cf = turn * jnp.where(first_step, -8.0, 1.0), turn * jnp.where(first_step, 1.0, 0.0)
            ln, lf = jnp.where(first_step, 16.0, -1.0), jnp.where(first_step, -1.0, 0.0)

            def chunk_work(chunk):
                rows = pl.ds(pl.multiple_of(layer * nx + chunk * 16, 16), 16)
                strip = pl.ds(chunk * 16, 16)

                def halos(f):
                    if not cross:
                        ref, at = near_ref, f
                    elif f < n_pert:
                        ref, at = first_ref, f
                    else:
                        ref, at = second_ref, f - n_pert
                    return ref[at, near_at, strip].astype(f32), ref[at, 1 - near_at, strip].astype(f32)

                def nb_halos(s, f):
                    if not cross:
                        return halos(n_res + s * n_nb + f)
                    at = [pl.ds(pl.multiple_of(j * nx + chunk * 16, 16), 16) for j in (near_at, 1 - near_at)]
                    return tuple(relay_refs[s][f, r].astype(f32) for r in at)

                def mix(pair):
                    return cn * pair[0] + cf * pair[1]

                def slope_lap(f):
                    a, b = halos(f)
                    return cn * a + cf * b, ln * a + lf * b

                flows = [mean_ref[2, rows].astype(f32)] + [mode_ref[3 * i + 2, rows].astype(f32) for i in range(4)]
                flow = entries(*flows)
                along = basis_of([(pert_ref[l * 8 + 2, rows].astype(f32), pert_ref[l * 8 + 6, rows].astype(f32)) for l in range(per)])
                for c in range(4):
                    if c < 3:
                        got = [[slope_lap(l * 8 + 4 * i + c) for i in range(2)] for l in range(per)]
                        vec = basis_of([(g[0][0], g[1][0]) for g in got])
                        lap = basis_of([(g[0][1], g[1][1]) for g in got])
                        acc = [tuple(-VISCOSITY * v for v in pair) for pair in lap]
                        if c == 2:
                            press = basis_of([(mix(halos(l * 8 + 3)), mix(halos(l * 8 + 7))) for l in range(per)])
                            acc = [(a[0] + p[0], a[1] + p[1]) for a, p in zip(acc, press)]
                        acc = couple(acc, flow, vec)
                        bend = entries(mix(halos(n_pert + c)), *[mix(halos(base_modes_at + 3 * i + c)) for i in range(4)])
                        acc = couple(acc, bend, along)
                    else:
                        acc = vec
                    for k, parts in enumerate(harmonics_of(acc, 1.0 / 24.0)):
                        for i in range(2):
                            at = k * 8 + 4 * i + c
                            done[at, rows] = done[at, rows] + parts[i]

                def nb_work(pairs):
                    for k in sorted({p[0] for p in pairs}):
                        zero = jnp.zeros((16, ny), f32)
                        for c in range(3):
                            acc = (zero, zero)
                            for _, m, s, f in [p for p in pairs if p[0] == k]:
                                base = (abs(m) - 1) * 6
                                mine = tuple(mode_ref[base + 3 * i + 2, rows].astype(f32) for i in range(2))
                                acc = product(acc, mine, tuple(mix(nb_halos(s, f + 3 * i + c)) for i in range(2)), m)
                                bent = tuple(mix(halos(base_modes_at + base + 3 * i + c)) for i in range(2))
                                carried = tuple(nb_refs[s][f + 3 * i + 2, rows].astype(f32) for i in range(2))
                                acc = product(acc, bent, carried, m)
                            for i in range(2):
                                at = k * 8 + 4 * i + c
                                done[at, rows] = done[at, rows] + acc[i] * (1.0 / 12.0)

                on_sides(nb_work)

            for chunk in range(nx // 16):
                chunk_work(chunk)
            send(layer).start()

        for cross in (False, True):
            lax.fori_loop(0, 2, lambda step, carry: (face_layer(cross, step), carry)[1], 0)
        for layer in range(nz):
            send(layer).wait()

    with jax.named_scope("finish"):
        out = pl.pallas_call(
            finish,
            out_shape=jax.ShapeDtypeStruct((n_pert, own, ny), f32),
            out_specs=HBM,
            scratch_shapes=[
                pltpu.VMEM((n_pert, own, ny), f32),
                pltpu.VMEM((sides * n_nb, 16 * nz, ny), f32),
                pltpu.SemaphoreType.DMA((nz,)),
            ],
            compiler_params=roomy,
        )(
            jnp.asarray(edge_stencil(nz), bf16), flat(pert), flat(mean), flat(mode), inner, first_got, second_got, near_got,
            *relay_got, *[flat(b) for b in nb_got],
        )
    return jnp.swapaxes(out.reshape(per, 2, 4, nz, nx, ny), 3, 4)


def solution(mesh):
    return jax.shard_map(
        shards,
        mesh=mesh,
        in_specs=(
            P("harm", None, None, "gx", "gz", None),
            P(None, "gx", "gz", None),
            P(None, None, None, "gx", "gz", None),
            P("gx", "gz", None),
        ),
        out_specs=P("harm", None, None, "gx", "gz", None),
        check_vma=False,
    )
```

```python
import jax
import jax.numpy as jnp
from jax import lax
from jax.experimental import pallas as pl
from jax.experimental.pallas import tpu as pltpu
from jax.sharding import PartitionSpec as P

FREQUENCY_STEP = 0.2
VISCOSITY = 0.05
PENALTY = 4.0
FIRST = {-2: 1.0, -1: -8.0, 1: 8.0, 2: -1.0}
SECOND = {-2: -1.0, -1: 16.0, 0: -30.0, 1: 16.0, 2: -1.0}
HALO_X = 16
VMEM_BYTES = 58 * 1024 * 1024
ANY = pl.BlockSpec(memory_space=pl.ANY)
VMEM = pl.BlockSpec(memory_space=pltpu.VMEM)
HBM = pl.BlockSpec(memory_space=pltpu.HBM)


def taps(delta, table):
    out = jnp.zeros(delta.shape, jnp.float32)
    for step, weight in table.items():
        out = jnp.where(delta == step, weight, out)
    return out


def iotas(rows, columns):
    return lax.broadcasted_iota(jnp.int32, (rows, 1), 0), lax.broadcasted_iota(jnp.int32, (1, columns), 1)


def column_cells(column, nz, nx):
    shift, own = nx.bit_length() - 1, nz * nx
    halo = column - own
    after = halo >= HALO_X
    edge = jnp.where(after, halo - HALO_X, halo)
    inside = column < own
    z = jnp.where(inside, column >> shift, edge >> 1)
    x = jnp.where(inside, column & (nx - 1), (edge & 1) + jnp.where(after, nx, -2))
    return z, x


def slope_matrix(part, z, x, to_z, to_x):
    dz, dx = to_z - z, to_x - x
    if part == 0:
        return jnp.where(dz == 0, taps(dx, FIRST), 0.0)
    if part == 1:
        return jnp.where(dx == 0, taps(dz, FIRST), 0.0)
    return jnp.where(dz == 0, taps(dx, SECOND), 0.0) + jnp.where(dx == 0, taps(dz, SECOND), 0.0)


def store_walls(walls_ref, ny):
    row, column = iotas(ny, ny)
    first, second = (taps(row - column, table).astype(jnp.bfloat16) for table in (FIRST, SECOND))
    for i, (block, sign) in enumerate(((first, 1), (first, -1), (second, 1), (second, -1))):
        if i * ny < walls_ref.shape[1]:
            walls_ref[:ny, i * ny : (i + 1) * ny] = block
            if walls_ref.shape[0] > ny:
                walls_ref[ny:, i * ny : (i + 1) * ny] = block if sign > 0 else -block


def run_copies(copies, sems):
    started = [pltpu.make_async_copy(src, dst, sems.at[i]) for i, (src, dst) in enumerate(copies)]
    for copy in started:
        copy.start()
    for copy in started:
        copy.wait()


def shards(perturbation, base_mean, base_modes, solid_mask):
    per, modes = perturbation.shape[0], base_modes.shape[0]
    nx, nz, ny = perturbation.shape[3], perturbation.shape[4], perturbation.shape[5]
    own = nz * nx
    bf16, f32 = jnp.bfloat16, jnp.float32
    harms, size_x, size_z = (lax.axis_size(a) for a in ("harm", "gx", "gz"))
    swap = harms == 2
    sides = 1 if swap else 2
    n_pert, n_mean, n_modes = per * 8, 3, modes * 6
    n_base = n_mean + n_modes
    n_res = n_pert + n_base
    n_nb = modes * 6
    n_all = n_res + sides * n_nb

    pert = jnp.swapaxes(perturbation, 3, 4).reshape(n_pert, nz, nx, ny)
    mean = jnp.swapaxes(base_mean, 1, 2)
    mode = jnp.swapaxes(base_modes, 3, 4).reshape(n_modes, nz, nx, ny)
    mask = jnp.swapaxes(solid_mask, 0, 1).reshape(own, ny)

    def place():
        me_h, odd = lax.axis_index("harm"), lax.rem(lax.axis_index("gz"), 2)
        shared = jnp.where(me_h == 0, per - modes, 0) if swap else 0
        return me_h, odd, odd * (nz - 2), (1 - odd) * (nz - 2), shared

    cross_pairs = [(i, (i + 1) % size_z if i % 2 else (i - 1) % size_z) for i in range(size_z)]
    near_pairs = [(i, i + 1 if i % 2 == 0 else i - 1) for i in range(size_z)]
    up_x = [(i, (i + 1) % size_x) for i in range(size_x)]
    down_x = [(j, i) for i, j in up_x]
    if swap:
        harm_perms = [[(0, 1), (1, 0)]]
    else:
        up_h = [(i, i + 1) for i in range(harms - 1)]
        harm_perms = [up_h, [(j, i) for i, j in up_h]]
    def sent(s, scal):
        return scal[4] if swap else (per - modes if s == 0 else 0)

    face = lambda n: jax.ShapeDtypeStruct((n, 2, nx, ny), bf16)
    roomy = pltpu.CompilerParams(vmem_limit_bytes=32 * 1024 * 1024)

    used = 2 * nz
    spare = HALO_X - used
    tiles = 3 * (-(-n_res // 4))

    def edge_tile(ref, f):
        group, i = divmod(f, 4)
        if i < 3:
            return ref[3 * group + i]
        parts = [ref[3 * group + j].astype(f32)[used:] for j in range(3)]
        return jnp.concatenate(parts + [jnp.zeros((spare, ny), f32)], axis=0).astype(bf16)

    def pack(pert_any, mean_any, mode_any, first_any, second_any, lo_any, hi_any, *rest):
        nb_anys = rest[:sides]
        pert_ref, mean_ref, mode_ref, lo_ref, hi_ref, in_sems, out_sems = rest[sides:]
        scal = place()
        z = pl.ds(scal[2], 2)
        loads = [(pert_any.at[pl.ds(8 * l, 8)], pert_ref.at[pl.ds(8 * l, 8)]) for l in range(per)]
        loads += [(mean_any, mean_ref), (mode_any, mode_ref)]
        loads = [pltpu.make_async_copy(src, dst, in_sems.at[i]) for i, (src, dst) in enumerate(loads)]
        for copy in loads:
            copy.start()
        out = []

        def send(src, dst):
            out.append(pltpu.make_async_copy(src, dst, out_sems.at[len(out)]))
            out[-1].start()

        row, column = iotas(2 * HALO_X, own)
        low = row < HALO_X
        row = jnp.where(low, row, row - HALO_X)
        target = (row >> 1) * nx + (row & 1) + jnp.where(low, 0, nx - 2)
        pick = jnp.where(column == target, 1.0, 0.0).astype(bf16)
        where = [(pert_ref, f) for f in range(n_pert)] + [(mean_ref, f) for f in range(n_mean)] + [(mode_ref, f) for f in range(n_modes)]

        def edges(group):
            got = []
            for f in range(4 * group, min(4 * group + 4, n_res), 2):
                mine = [ref[i].reshape(own, ny) for ref, i in where[f : min(f + 2, n_res)]]
                both = jnp.concatenate(mine, axis=1) if len(mine) == 2 else mine[0]
                both = jnp.dot(pick, both, preferred_element_type=f32)
                got += [both[:, i * ny : (i + 1) * ny] for i in range(len(mine))]
            if len(got) == 3:
                got.append(jnp.zeros((2 * HALO_X, ny), f32))
            for i in range(3):
                for ref, at in ((lo_ref, 0), (hi_ref, HALO_X)):
                    extra = got[3][at + spare * i : at + spare * (i + 1)]
                    ref[3 * group + i] = jnp.concatenate([got[i][at : at + used], extra], axis=0).astype(bf16)

        for l in range(per):
            loads[l].wait()
            mine = pl.ds(8 * l, 8)
            send(pert_ref.at[mine, z], first_any.at[mine])
        for s, nb_any in enumerate(nb_anys):
            for i in range(modes * 2):
                send(pert_ref.at[pl.ds(sent(s, scal) * 8 + 4 * i, 3)], nb_any.at[pl.ds(3 * i, 3)])
        for group in range(n_pert // 4):
            edges(group)
        loads[per].wait()
        loads[per + 1].wait()
        send(mean_ref.at[:, z], second_any.at[pl.ds(0, n_mean)])
        send(mode_ref.at[:, z], second_any.at[pl.ds(n_mean, n_modes)])
        for group in range(n_pert // 4, tiles // 3):
            edges(group)
        send(lo_ref, lo_any)
        send(hi_ref, hi_any)
        for copy in out:
            copy.wait()

    edge = jax.ShapeDtypeStruct((tiles, HALO_X, ny), bf16)
    with jax.named_scope("pack"):
        first, second, edge_lo, edge_hi, *nb_send = pl.pallas_call(
            pack,
            out_shape=(face(n_pert), face(n_base), edge, edge) + tuple(jax.ShapeDtypeStruct((n_nb, nz, nx, ny), bf16) for _ in range(sides)),
            in_specs=[HBM] * 3,
            out_specs=(ANY,) * (4 + sides),
            scratch_shapes=[
                pltpu.VMEM((n_pert, nz, nx, ny), bf16),
                pltpu.VMEM((n_mean, nz, nx, ny), bf16),
                pltpu.VMEM((n_modes, nz, nx, ny), bf16),
                pltpu.VMEM((tiles, HALO_X, ny), bf16),
                pltpu.VMEM((tiles, HALO_X, ny), bf16),
                pltpu.SemaphoreType.DMA((per + 2,)),
                pltpu.SemaphoreType.DMA((per + sides * modes * 2 + 4,)),
            ],
            compiler_params=pltpu.CompilerParams(vmem_limit_bytes=VMEM_BYTES),
        )(pert, mean, mode)
    first_got = lax.ppermute(first, "gz", cross_pairs)
    nb_got = [lax.ppermute(b, "harm", p) for b, p in zip(nb_send, harm_perms)]
    xb_got = lax.ppermute(edge_hi, "gx", up_x)
    xa_got = lax.ppermute(edge_lo, "gx", down_x)
    second_got = lax.ppermute(second, "gz", cross_pairs)

    PAIRS = ((0, 3), (1, 2))
    DRIFT = (-1.5 * FREQUENCY_STEP, -0.5 * FREQUENCY_STEP)

    def entries(t, p, q, r, s):
        return t, q, p + r, p - r, q + s, s - q, t + p, t - p

    def couple(acc, ent, vec):
        t, q, pr, pmr, qs, sq, tp, tmp = ent
        out = []
        for i in range(2):
            a, e, b, g = (vec[j][i] for j in range(4))
            out.append(
                (
                    acc[0][i] + t * a + pr * b + sq * g,
                    acc[1][i] + t * e + qs * b + pmr * g,
                    acc[2][i] + pr * a + qs * e + tp * b + q * g,
                    acc[3][i] + sq * a + pmr * e + q * b + tmp * g,
                )
            )
        return [(out[0][j], out[1][j]) for j in range(4)]

    def harmonics_of(acc, scale):
        out = [None] * 4
        for at, (lo, hi) in enumerate(PAIRS):
            (ar, ai), (er, ei) = acc[2 * at], acc[2 * at + 1]
            out[lo] = ((ar + ei) * scale, (ai - er) * scale)
            out[hi] = ((ar - ei) * scale, (ai + er) * scale)
        return out

    def basis_of(values):
        out = []
        for lo, hi in PAIRS:
            (lr, li), (hr, hi_) = values[lo], values[hi]
            out += [(lr + hr, li + hi_), (hi_ - li, lr - hr)]
        return out

    def resident(pert_ref, mean_ref, mode_ref, out_ref, grads, plain, ents, lin, rows_ref, walls_ref):
        me_h = place()[0]
        row, column = iotas(own, own)
        to_z, to_x = column_cells(column, nz, nx)
        for i in range(3):
            rows_ref[i * own : (i + 1) * own] = slope_matrix(i, row >> nx.bit_length() - 1, row & (nx - 1), to_z, to_x).astype(bf16)
        store_walls(walls_ref, ny)
        mean_freq = 12.0 * FREQUENCY_STEP * (me_h * per + 1.5 - per * harms / 2).astype(f32)

        def rhs(ref, fields):
            cols = [ref[f] for f in fields]
            return cols[0] if len(cols) == 1 else jnp.concatenate(cols, axis=1)

        def dot(a, b):
            return jnp.dot(a, b, preferred_element_type=f32)

        for at, (lo, hi) in enumerate(PAIRS):
            for i in range(2):
                fl, fr = lo * 8 + i * 4 + 3, hi * 8 + i * 4 + 3
                got = dot(rows_ref[: 2 * own], rhs(pert_ref, (fl, fr)))
                wall = dot(rhs(pert_ref, (fl, fr)), walls_ref[:, : 2 * ny])
                for d in range(3):
                    if d == 1:
                        total, diff = wall[:, :ny], wall[:, ny:]
                    else:
                        span = slice(0, own) if d == 0 else slice(own, 2 * own)
                        total, diff = got[span, :ny] + got[span, ny:], got[span, :ny] - got[span, ny:]
                    lin[2 * at, i, d] = total
                    lin[2 * at + 1, 1 - i, d] = diff if i == 0 else -diff
        for at, (lo, hi) in enumerate(PAIRS):
            for c in range(3):
                for i in range(2):
                    sign = 1.0 if i == 0 else -1.0
                    fl, fr = lo * 8 + i * 4 + c, hi * 8 + i * 4 + c
                    got = dot(rows_ref[...], rhs(pert_ref, (fl, fr)))
                    xl, xr = pert_ref[fl].astype(f32), pert_ref[fr].astype(f32)
                    wall = dot(rhs(pert_ref, (fl, fr)), walls_ref[...])
                    total, diff = xl + xr, xl - xr
                    plain[2 * at, i, c] = total
                    plain[2 * at + 1, 1 - i, c] = sign * diff
                    for d in range(3):
                        if d == 1:
                            gt, gd = wall[:, :ny], wall[:, ny : 2 * ny]
                        else:
                            span = slice(0, own) if d == 0 else slice(own, 2 * own)
                            gt, gd = got[span, :ny] + got[span, ny:], got[span, :ny] - got[span, ny:]
                        gd = sign * gd
                        grads[2 * at, i, c, d] = gt
                        grads[2 * at + 1, 1 - i, c, d] = gd
                        if d == c:
                            if c == 0:
                                lin[2 * at, i, 3] = gt
                                lin[2 * at + 1, 1 - i, 3] = gd
                            else:
                                lin[2 * at, i, 3] = lin[2 * at, i, 3] + gt
                                lin[2 * at + 1, 1 - i, 3] = lin[2 * at + 1, 1 - i, 3] + gd
                    lt = got[2 * own :, :ny] + got[2 * own :, ny:] + wall[:, 2 * ny : 3 * ny]
                    ld = got[2 * own :, :ny] - got[2 * own :, ny:] + wall[:, 3 * ny :]
                    drift = 12.0 * DRIFT[at]
                    lin[2 * at, i, c] = lin[2 * at, i, c] - VISCOSITY * lt
                    lin[2 * at + 1, 1 - i, c] = lin[2 * at + 1, 1 - i, c] - sign * VISCOSITY * ld
                    lin[2 * at, 1 - i, c] = lin[2 * at, 1 - i, c] + sign * (mean_freq * total + drift * diff)
                    lin[2 * at + 1, i, c] = lin[2 * at + 1, i, c] - (mean_freq * diff + drift * total)
        for c in range(3):
            picked = [mean_ref[c].astype(f32)] + [mode_ref[3 * i + c].astype(f32) for i in range(4)]
            for n, ent in enumerate(entries(*picked)):
                ents[c, n] = ent
            mean_at = dot(rows_ref[: 2 * own], rhs(mean_ref, (c,)))
            mean_wall = dot(mean_ref[c], walls_ref[:ny, :ny])
            real = dot(rows_ref[: 2 * own], rhs(mode_ref, (c, 6 + c)))
            imag = dot(rows_ref[: 2 * own], rhs(mode_ref, (3 + c, 9 + c)))
            wall_real = dot(rhs(mode_ref, (c, 6 + c)), walls_ref[:, : 2 * ny])
            wall_imag = dot(rhs(mode_ref, (3 + c, 9 + c)), walls_ref[:, : 2 * ny])
            for d in range(3):
                if d == 1:
                    pr, pmr = wall_real[:, :ny], wall_real[:, ny:]
                    qs, qms = wall_imag[:, :ny], wall_imag[:, ny:]
                    t, p, q = mean_wall, 0.5 * (pr + pmr), 0.5 * (qs + qms)
                    values = (t, q, pr, pmr, qs, -qms, t + p, t - p)
                else:
                    span = slice(0, own) if d == 0 else slice(own, 2 * own)
                    values = entries(mean_at[span], real[span, :ny], imag[span, :ny], real[span, ny:], imag[span, ny:])
                for n, ent in enumerate(values):
                    ents[3 + 3 * d + c, n] = ent

        def block(b, carry):
            rows = pl.ds(pl.multiple_of(b * 8, 8), 8)
            accs = [[(lin[j, 0, c, rows], lin[j, 1, c, rows]) for j in range(4)] for c in range(4)]
            for d in range(3):
                flow = [ents[d, n, rows] for n in range(8)]
                for c in range(3):
                    accs[c] = couple(accs[c], flow, [(grads[j, 0, c, d, rows], grads[j, 1, c, d, rows]) for j in range(4)])
                along = [(plain[j, 0, d, rows], plain[j, 1, d, rows]) for j in range(4)]
                for c in range(3):
                    slope = [ents[3 + 3 * d + c, n, rows] for n in range(8)]
                    accs[c] = couple(accs[c], slope, along)
            for c in range(4):
                for k, (re, im) in enumerate(harmonics_of(accs[c], 1.0 / 24.0)):
                    out_ref[k * 8 + c, rows] = re
                    out_ref[k * 8 + 4 + c, rows] = im
            return carry

        lax.fori_loop(0, own // 8, block, 0, unroll=2)

    flat = lambda a: a.reshape(a.shape[0], -1, ny)
    with jax.named_scope("resident"):
        whole = pl.pallas_call(
            resident,
            out_shape=jax.ShapeDtypeStruct((n_pert, own, ny), f32),
            scratch_shapes=[
                pltpu.VMEM((4, 2, 3, 3, own, ny), f32),
                pltpu.VMEM((4, 2, 3, own, ny), f32),
                pltpu.VMEM((12, 8, own, ny), f32),
                pltpu.VMEM((4, 2, 4, own, ny), f32),
                pltpu.VMEM((3 * own, own), bf16),
                pltpu.VMEM((2 * ny, 4 * ny), bf16),
            ],
            compiler_params=roomy,
        )(flat(pert), flat(mean), flat(mode))

    deep = 2 * nx + 2 * HALO_X

    def pack_relay(first_ref, xb_ref, xa_ref, _, *outs):
        scal = place()
        for s, out in enumerate(outs):
            for i in range(modes * 2):
                group = sent(s, scal) * 2 + i
                for c in range(3):
                    out[3 * i + c, : 2 * nx] = first_ref[group * 4 + c].reshape(2 * nx, ny)
                    out[3 * i + c, 2 * nx : 2 * nx + HALO_X] = xb_ref[group * 3 + c]
                    out[3 * i + c, 2 * nx + HALO_X :] = xa_ref[group * 3 + c]

    with jax.named_scope("pack_relay"):
        relay = pl.pallas_call(
            pack_relay,
            out_shape=tuple(jax.ShapeDtypeStruct((n_nb, deep, ny), bf16) for _ in range(sides)),
            in_specs=[VMEM] * 3 + [ANY],
            compiler_params=roomy,
        )(first_got, xb_got, xa_got, whole)
    relay_got = [lax.ppermute(b, "harm", p) for b, p in zip(relay, harm_perms)]

    def pack_near(pert_ref, mean_ref, mode_ref, *rest):
        out = rest[-1]
        z = pl.ds(place()[3], 2)
        out[:n_pert] = pert_ref[:, z]
        out[n_pert : n_pert + n_mean] = mean_ref[:, z]
        out[n_pert + n_mean : n_res] = mode_ref[:, z]
        for s in range(sides):
            out[n_res + s * n_nb : n_res + (s + 1) * n_nb] = rest[s][:, z]

    with jax.named_scope("pack_near"):
        near = pl.pallas_call(
            pack_near,
            out_shape=face(n_all),
            in_specs=[VMEM] * (3 + sides) + [ANY],
            compiler_params=roomy,
        )(pert, mean, mode, *nb_got, relay[0])
    near_got = lax.ppermute(near, "gz", near_pairs)

    below, above = [], []
    for k in range(per):
        for m in range(-modes, modes + 1):
            l = k - m
            if l < 0:
                below.append((k, m, 0, (l + modes) * 6))
            elif l >= per:
                above.append((k, m, sides - 1, (l - per) * 6))

    ends = 16 * nz

    def edge_taps(tables):
        row, column = iotas(ends, own + 2 * HALO_X)
        last = row >= 8 * nz
        row = jnp.where(last, row - 8 * nz, row)
        to_z, to_x = column_cells(column, nz, nx)
        dz, dx = to_z - (row >> 3), to_x - (row & 7) - jnp.where(last, nx - 8, 0)
        return jnp.concatenate([jnp.where(dz == 0, taps(dx, table), 0.0)[:, own:] for table in tables], axis=0).astype(bf16)

    def on_sides(work):
        me_h = lax.axis_index("harm")
        pl.when(me_h > 0)(lambda: work(below))
        pl.when(me_h < harms - 1)(lambda: work(above))

    def product(acc, flow, value, m):
        (fr, fi), (vr, vi) = flow, value
        if m > 0:
            return acc[0] + fr * vr - fi * vi, acc[1] + fr * vi + fi * vr
        return acc[0] + fr * vr + fi * vi, acc[1] + fr * vi - fi * vr

    base_modes_at = n_pert + n_mean

    def neighbours(mask_ref, pert_ref, mean_ref, mode_ref, xb_ref, xa_ref, whole_ref, *rest):
        nb_refs = rest[:sides]
        out_ref, grads, plain, stencil_ref, walls_ref, vecs, lins, bends = rest[-8:]
        row, column = iotas(own, own + 2 * HALO_X)
        to_z, to_x = column_cells(column, nz, nx)
        for i in range(2):
            stencil_ref[i * own : (i + 1) * own] = slope_matrix(i, row >> nx.bit_length() - 1, row & (nx - 1), to_z, to_x).astype(bf16)
        store_walls(walls_ref, ny)

        def slopes(at, mine, halo):
            both = jnp.concatenate(mine, axis=1)
            rows = both if halo is None else jnp.concatenate([both, halo], axis=0)
            got = jnp.dot(stencil_ref[:, : rows.shape[0]], rows, preferred_element_type=f32)
            wall = [jnp.dot(x, walls_ref[:ny, :ny], preferred_element_type=f32) for x in mine]
            for i in range(2):
                lanes = slice(i * ny, (i + 1) * ny)
                grads[at + i, 0] = got[:own, lanes]
                grads[at + i, 2] = got[own:, lanes]
                grads[at + i, 1] = wall[i]
                plain[at + i] = mine[i].astype(f32)

        for f in range(0, n_modes, 2):
            at = base_modes_at + f
            halo = [jnp.concatenate([edge_tile(ref, at), edge_tile(ref, at + 1)], axis=1) for ref in (xb_ref, xa_ref)]
            slopes(f, [mode_ref[f], mode_ref[f + 1]], jnp.concatenate(halo, axis=0))
        for s in range(sides):
            for f in range(0, n_nb, 2):
                slopes(n_modes + s * n_nb + f, [nb_refs[s][f], nb_refs[s][f + 1]], None)

        taps_of = edge_taps((FIRST, SECOND))

        def bent(fields, lap):
            cols = [jnp.concatenate([edge_tile(xb_ref, f), edge_tile(xa_ref, f)], axis=0) for f in fields]
            both = cols[0] if len(cols) == 1 else jnp.concatenate(cols, axis=1)
            got = jnp.dot(taps_of if lap else taps_of[:ends], both, preferred_element_type=f32)
            return [(got[:ends, i * ny : (i + 1) * ny], got[ends:, i * ny : (i + 1) * ny]) for i in range(len(fields))]

        for at, (lo, hi) in enumerate(PAIRS):
            for i in range(2):
                sign = 1.0 if i == 0 else -1.0
                for c in range(4):
                    (gl, ll), (gr, lr) = bent((lo * 8 + 4 * i + c, hi * 8 + 4 * i + c), c < 3)
                    if c < 3:
                        vecs[2 * at, i, c] = gl + gr
                        vecs[2 * at + 1, 1 - i, c] = sign * (gl - gr)
                        lins[2 * at, i, c] = -VISCOSITY * (ll + lr)
                        lins[2 * at + 1, 1 - i, c] = (-VISCOSITY * sign) * (ll - lr)
                    else:
                        lins[2 * at, i, 0] = lins[2 * at, i, 0] + (gl + gr)
                        lins[2 * at + 1, 1 - i, 0] = lins[2 * at + 1, 1 - i, 0] + sign * (gl - gr)
        for c in range(3):
            at = base_modes_at + c
            (t, _), = bent((n_pert + c,), False)
            (p, _), (r, _) = bent((at, at + 6), False)
            (q, _), (s_, _) = bent((at + 3, at + 9), False)
            for n, ent in enumerate(entries(t, p, q, r, s_)):
                bends[c, n] = ent

        for z in range(nz):
            rows = slice(z * nx, (z + 1) * nx)
            solid = PENALTY * mask_ref[rows].astype(f32)
            for f in range(n_pert):
                if f % 4 < 3:
                    out_ref[f, rows] = whole_ref[f, rows] + solid * pert_ref[f, rows].astype(f32)
                else:
                    out_ref[f, rows] = whole_ref[f, rows]

        def layer_ends(z, carry):
            for end in range(2):
                strip = pl.ds(pl.multiple_of(z * nx + end * (nx // 2), 16), 16)
                keep = slice(8 * end, 8 * end + 8)
                rows = pl.ds(pl.multiple_of(z * nx + end * (nx - 8), 8), 8)
                mine = pl.ds(pl.multiple_of((end * nz + z) * 8, 8), 8)

                def read(ref, f):
                    return ref[f, strip].astype(f32)[keep]

                flow = entries(read(mean_ref, 0), *[read(mode_ref, 3 * i) for i in range(4)])
                along = basis_of([(read(pert_ref, l * 8), read(pert_ref, l * 8 + 4)) for l in range(per)])
                for c in range(4):
                    if c < 3:
                        acc = [(lins[j, 0, c, mine], lins[j, 1, c, mine]) for j in range(4)]
                        acc = couple(acc, flow, [(vecs[j, 0, c, mine], vecs[j, 1, c, mine]) for j in range(4)])
                        acc = couple(acc, [bends[c, n, mine] for n in range(8)], along)
                    else:
                        acc = [(vecs[j, 0, 0, mine], vecs[j, 1, 0, mine]) for j in range(4)]
                    for k, parts in enumerate(harmonics_of(acc, 1.0 / 24.0)):
                        for i in range(2):
                            at = k * 8 + 4 * i + c
                            out_ref[at, rows] = out_ref[at, rows] + parts[i]
            return carry

        lax.fori_loop(0, nz, layer_ends, 0)

        def work(pairs):
            def block(b, carry):
                rows = pl.ds(pl.multiple_of(b * 8, 8), 8)
                for k in sorted({p[0] for p in pairs}):
                    zero = jnp.zeros((8, ny), f32)
                    acc = [(zero, zero)] * 3
                    for _, m, s, f in [p for p in pairs if p[0] == k]:
                        at, base = n_modes + s * n_nb + f, (abs(m) - 1) * 6
                        for d in range(3):
                            flow = plain[base + d, rows], plain[base + 3 + d, rows]
                            along = plain[at + d, rows], plain[at + 3 + d, rows]
                            for c in range(3):
                                slope = grads[base + c, d, rows], grads[base + 3 + c, d, rows]
                                grad = grads[at + c, d, rows], grads[at + 3 + c, d, rows]
                                acc[c] = product(acc[c], flow, grad, m)
                                acc[c] = product(acc[c], slope, along, m)
                    for c in range(3):
                        for i in range(2):
                            at = k * 8 + 4 * i + c
                            out_ref[at, rows] = out_ref[at, rows] + acc[c][i] * (1.0 / 12.0)
                return carry

            lax.fori_loop(0, own // 8, block, 0)

        on_sides(work)

    n_ext = n_modes + sides * n_nb
    with jax.named_scope("neighbours"):
        inner = pl.pallas_call(
            neighbours,
            out_shape=jax.ShapeDtypeStruct((n_pert, own, ny), f32),
            scratch_shapes=[
                pltpu.VMEM((n_ext, 3, own, ny), f32),
                pltpu.VMEM((n_ext, own, ny), f32),
                pltpu.VMEM((2 * own, own + 2 * HALO_X), bf16),
                pltpu.VMEM((ny, ny), bf16),
                pltpu.VMEM((4, 2, 3, ends, ny), f32),
                pltpu.VMEM((4, 2, 3, ends, ny), f32),
                pltpu.VMEM((3, 8, ends, ny), f32),
            ],
            compiler_params=roomy,
        )(mask, flat(pert), flat(mean), flat(mode), xb_got, xa_got, whole, *[flat(b) for b in nb_got])

    def finish(pert_ref, mean_ref, mode_ref, inner_ref, first_ref, second_ref, near_ref, *rest):
        relay_refs, nb_refs = rest[:sides], rest[sides : 2 * sides]
        out_any, done, bends, sems = rest[2 * sides :]
        odd = place()[1]
        half = nx // 2
        done[...] = inner_ref[...]
        taps_of = edge_taps((FIRST,))

        def send(layer):
            rows = pl.ds(pl.multiple_of(layer * nx, nx), nx)
            return pltpu.make_async_copy(done.at[:, rows], out_any.at[:, rows], sems.at[layer])

        for s in range(sides):
            for f in range(0, n_nb, 2):
                both = jnp.concatenate([relay_refs[s][f + i, 2 * nx :] for i in range(2)], axis=1)
                got = jnp.dot(taps_of, both, preferred_element_type=f32)
                for i in range(2):
                    bends[s * n_nb + f + i] = got[:, i * ny : (i + 1) * ny]

        def edge_work(pairs):
            def layer_edges(z, carry):
                for end in range(2):
                    strip = pl.ds(pl.multiple_of(z * nx + end * half, 16), 16)
                    keep = slice(8 * end, 8 * end + 8)
                    rows = pl.ds(pl.multiple_of(z * nx + end * (nx - 8), 8), 8)
                    bent = pl.ds(pl.multiple_of((end * nz + z) * 8, 8), 8)
                    for k in sorted({p[0] for p in pairs}):
                        zero = jnp.zeros((8, ny), f32)
                        acc = [(zero, zero)] * 3
                        for _, m, s, f in [p for p in pairs if p[0] == k]:
                            base = (abs(m) - 1) * 6
                            flow = tuple(mode_ref[base + 3 * i, strip].astype(f32)[keep] for i in range(2))
                            for c in range(3):
                                at = s * n_nb + f + c
                                acc[c] = product(acc[c], flow, (bends[at, bent], bends[at + 3, bent]), m)
                        for c in range(3):
                            for i in range(2):
                                at = k * 8 + 4 * i + c
                                done[at, rows] = done[at, rows] + acc[c][i] * (1.0 / 12.0)
                return carry

            lax.fori_loop(0, nz, layer_edges, 0)

        on_sides(edge_work)
        for layer in range(2, nz - 2):
            send(layer).start()

        def face_layer(cross, step):
            before = (odd == 0) if cross else (odd == 1)
            near_at = jnp.where(before, 1, 0)
            layer = jnp.where(before, step, nz - 1 - step)
            turn = jnp.where(before, 1.0, -1.0)

            def mix(pair):
                return pair[1] - 8.0 * pair[0] if step == 0 else pair[0]

            def mix_lap(pair):
                return pair[1] - 16.0 * pair[0] if step == 0 else pair[0]

            def chunk_work(chunk):
                rows = pl.ds(pl.multiple_of(layer * nx + chunk * 16, 16), 16)
                strip = pl.ds(pl.multiple_of(chunk * 16, 16), 16)

                def halos(f):
                    if not cross:
                        ref, at = near_ref, f
                    elif f < n_pert:
                        ref, at = first_ref, f
                    else:
                        ref, at = second_ref, f - n_pert
                    return ref[at, near_at, strip].astype(f32), (ref[at, 1 - near_at, strip].astype(f32) if step == 0 else None)

                def nb_halos(s, f):
                    if not cross:
                        return halos(n_res + s * n_nb + f)
                    at = [pl.ds(pl.multiple_of(j * nx + chunk * 16, 16), 16) for j in (near_at, 1 - near_at)]
                    return tuple(relay_refs[s][f, r].astype(f32) for r in at)

                flows = [mean_ref[2, rows].astype(f32)] + [mode_ref[3 * i + 2, rows].astype(f32) for i in range(4)]
                flow = entries(*flows)
                along = basis_of([(pert_ref[l * 8 + 2, rows].astype(f32), pert_ref[l * 8 + 6, rows].astype(f32)) for l in range(per)])
                for c in range(4):
                    if c < 3:
                        got = [[halos(l * 8 + 4 * i + c) for i in range(2)] for l in range(per)]
                        vec = basis_of([(mix(g[0]), mix(g[1])) for g in got])
                        lap = basis_of([(mix_lap(g[0]), mix_lap(g[1])) for g in got])
                        if c == 2:
                            acc = basis_of([(mix(halos(l * 8 + 3)), mix(halos(l * 8 + 7))) for l in range(per)])
                        else:
                            acc = [(0.0, 0.0)] * 4
                        acc = couple(acc, flow, vec)
                        bend = entries(mix(halos(n_pert + c)), *[mix(halos(base_modes_at + 3 * i + c)) for i in range(4)])
                        acc = couple(acc, bend, along)
                        acc = [tuple(turn * a + VISCOSITY * v for a, v in zip(*pair)) for pair in zip(acc, lap)]
                    else:
                        acc = [tuple(turn * v for v in pair) for pair in vec]
                    for k, parts in enumerate(harmonics_of(acc, 1.0 / 24.0)):
                        for i in range(2):
                            at = k * 8 + 4 * i + c
                            done[at, rows] = done[at, rows] + parts[i]

                def nb_work(pairs):
                    for k in sorted({p[0] for p in pairs}):
                        zero = jnp.zeros((16, ny), f32)
                        for c in range(3):
                            acc = (zero, zero)
                            for _, m, s, f in [p for p in pairs if p[0] == k]:
                                base = (abs(m) - 1) * 6
                                mine = tuple(mode_ref[base + 3 * i + 2, rows].astype(f32) for i in range(2))
                                acc = product(acc, mine, tuple(mix(nb_halos(s, f + 3 * i + c)) for i in range(2)), m)
                                bent = tuple(mix(halos(base_modes_at + base + 3 * i + c)) for i in range(2))
                                carried = tuple(nb_refs[s][f + 3 * i + 2, rows].astype(f32) for i in range(2))
                                acc = product(acc, bent, carried, m)
                            for i in range(2):
                                at = k * 8 + 4 * i + c
                                done[at, rows] = done[at, rows] + (turn * (1.0 / 12.0)) * acc[i]

                on_sides(nb_work)

            lax.fori_loop(0, nx // 16, lambda chunk, carry: (chunk_work(chunk), carry)[1], 0)
            send(layer).start()

        for cross in (False, True):
            for step in range(2):
                face_layer(cross, step)
        for layer in range(nz):
            send(layer).wait()

    with jax.named_scope("finish"):
        out = pl.pallas_call(
            finish,
            out_shape=jax.ShapeDtypeStruct((n_pert, own, ny), f32),
            out_specs=HBM,
            scratch_shapes=[
                pltpu.VMEM((n_pert, own, ny), f32),
                pltpu.VMEM((sides * n_nb, ends, ny), f32),
                pltpu.SemaphoreType.DMA((nz,)),
            ],
            compiler_params=roomy,
        )(
            flat(pert), flat(mean), flat(mode), inner, first_got, second_got, near_got,
            *relay_got, *[flat(b) for b in nb_got],
        )
    return jnp.swapaxes(out.reshape(per, 2, 4, nz, nx, ny), 3, 4)


def solution(mesh):
    return jax.shard_map(
        shards,
        mesh=mesh,
        in_specs=(
            P("harm", None, None, "gx", "gz", None),
            P(None, "gx", "gz", None),
            P(None, None, None, "gx", "gz", None),
            P("gx", "gz", None),
        ),
        out_specs=P("harm", None, None, "gx", "gz", None),
        check_vma=False,
    )
```

```python
import jax
import jax.numpy as jnp
from jax import lax
from jax.experimental import pallas as pl
from jax.experimental.pallas import tpu as pltpu
from jax.sharding import PartitionSpec as P

FREQUENCY_STEP = 0.2
VISCOSITY = 0.05
PENALTY = 4.0
FIRST = {-2: 1.0, -1: -8.0, 1: 8.0, 2: -1.0}
SECOND = {-2: -1.0, -1: 16.0, 0: -30.0, 1: 16.0, 2: -1.0}
HALO_X = 16
VMEM_BYTES = 58 * 1024 * 1024
ANY = pl.BlockSpec(memory_space=pl.ANY)
VMEM = pl.BlockSpec(memory_space=pltpu.VMEM)
HBM = pl.BlockSpec(memory_space=pltpu.HBM)


def taps(delta, table):
    out = jnp.zeros(delta.shape, jnp.float32)
    for step, weight in table.items():
        out = jnp.where(delta == step, weight, out)
    return out


def iotas(rows, columns):
    return lax.broadcasted_iota(jnp.int32, (rows, 1), 0), lax.broadcasted_iota(jnp.int32, (1, columns), 1)


def column_cells(column, nz, nx):
    shift, own = nx.bit_length() - 1, nz * nx
    halo = column - own
    after = halo >= HALO_X
    edge = jnp.where(after, halo - HALO_X, halo)
    inside = column < own
    z = jnp.where(inside, column >> shift, edge >> 1)
    x = jnp.where(inside, column & (nx - 1), (edge & 1) + jnp.where(after, nx, -2))
    return z, x


def slope_matrix(part, z, x, to_z, to_x):
    dz, dx = to_z - z, to_x - x
    if part == 0:
        return jnp.where(dz == 0, taps(dx, FIRST), 0.0)
    if part == 1:
        return jnp.where(dx == 0, taps(dz, FIRST), 0.0)
    return jnp.where(dz == 0, taps(dx, SECOND), 0.0) + jnp.where(dx == 0, taps(dz, SECOND), 0.0)


def store_walls(walls_ref, ny):
    row, column = iotas(ny, ny)
    first, second = (taps(row - column, table).astype(jnp.bfloat16) for table in (FIRST, SECOND))
    for i, (block, sign) in enumerate(((first, 1), (first, -1), (second, 1), (second, -1))):
        if i * ny < walls_ref.shape[1]:
            walls_ref[:ny, i * ny : (i + 1) * ny] = block
            if walls_ref.shape[0] > ny:
                walls_ref[ny:, i * ny : (i + 1) * ny] = block if sign > 0 else -block


def run_copies(copies, sems):
    started = [pltpu.make_async_copy(src, dst, sems.at[i]) for i, (src, dst) in enumerate(copies)]
    for copy in started:
        copy.start()
    for copy in started:
        copy.wait()


def shards(perturbation, base_mean, base_modes, solid_mask):
    per, modes = perturbation.shape[0], base_modes.shape[0]
    nx, nz, ny = perturbation.shape[3], perturbation.shape[4], perturbation.shape[5]
    own = nz * nx
    bf16, f32 = jnp.bfloat16, jnp.float32
    harms, size_x, size_z = (lax.axis_size(a) for a in ("harm", "gx", "gz"))
    swap = harms == 2
    sides = 1 if swap else 2
    n_pert, n_mean, n_modes = per * 8, 3, modes * 6
    n_base = n_mean + n_modes
    n_res = n_pert + n_base
    n_nb = modes * 6
    n_all = n_res + sides * n_nb

    pert = jnp.swapaxes(perturbation, 3, 4).reshape(n_pert, nz, nx, ny)
    mean = jnp.swapaxes(base_mean, 1, 2)
    mode = jnp.swapaxes(base_modes, 3, 4).reshape(n_modes, nz, nx, ny)
    mask = jnp.swapaxes(solid_mask, 0, 1).reshape(own, ny)

    def place():
        me_h, odd = lax.axis_index("harm"), lax.rem(lax.axis_index("gz"), 2)
        shared = jnp.where(me_h == 0, per - modes, 0) if swap else 0
        return me_h, odd, odd * (nz - 2), (1 - odd) * (nz - 2), shared

    cross_pairs = [(i, (i + 1) % size_z if i % 2 else (i - 1) % size_z) for i in range(size_z)]
    near_pairs = [(i, i + 1 if i % 2 == 0 else i - 1) for i in range(size_z)]
    up_x = [(i, (i + 1) % size_x) for i in range(size_x)]
    down_x = [(j, i) for i, j in up_x]
    if swap:
        harm_perms = [[(0, 1), (1, 0)]]
    else:
        up_h = [(i, i + 1) for i in range(harms - 1)]
        harm_perms = [up_h, [(j, i) for i, j in up_h]]
    def sent(s, scal):
        return scal[4] if swap else (per - modes if s == 0 else 0)

    face = lambda n: jax.ShapeDtypeStruct((n, 2, nx, ny), bf16)
    roomy = pltpu.CompilerParams(vmem_limit_bytes=32 * 1024 * 1024)

    used = 2 * nz
    spare = HALO_X - used
    tiles = 3 * (-(-n_res // 4))

    def edge_tile(ref, f):
        group, i = divmod(f, 4)
        if i < 3:
            return ref[3 * group + i]
        parts = [ref[3 * group + j].astype(f32)[used:] for j in range(3)]
        return jnp.concatenate(parts + [jnp.zeros((spare, ny), f32)], axis=0).astype(bf16)

    def pack(pert_any, mean_any, mode_any, first_any, second_any, lo_any, hi_any, *rest):
        nb_anys = rest[:sides]
        pert_ref, mean_ref, mode_ref, lo_ref, hi_ref, in_sems, out_sems = rest[sides:]
        scal = place()
        z = pl.ds(scal[2], 2)
        loads = [(pert_any.at[pl.ds(8 * l, 8)], pert_ref.at[pl.ds(8 * l, 8)]) for l in range(per)]
        loads += [(mean_any, mean_ref), (mode_any, mode_ref)]
        loads = [pltpu.make_async_copy(src, dst, in_sems.at[i]) for i, (src, dst) in enumerate(loads)]
        for copy in loads:
            copy.start()
        out = []

        def send(src, dst):
            out.append(pltpu.make_async_copy(src, dst, out_sems.at[len(out)]))
            out[-1].start()

        row, column = iotas(2 * HALO_X, own)
        low = row < HALO_X
        row = jnp.where(low, row, row - HALO_X)
        target = (row >> 1) * nx + (row & 1) + jnp.where(low, 0, nx - 2)
        pick = jnp.where(column == target, 1.0, 0.0).astype(bf16)
        where = [(pert_ref, f) for f in range(n_pert)] + [(mean_ref, f) for f in range(n_mean)] + [(mode_ref, f) for f in range(n_modes)]

        def edges(group):
            got = []
            for f in range(4 * group, min(4 * group + 4, n_res), 2):
                mine = [ref[i].reshape(own, ny) for ref, i in where[f : min(f + 2, n_res)]]
                both = jnp.concatenate(mine, axis=1) if len(mine) == 2 else mine[0]
                both = jnp.dot(pick, both, preferred_element_type=f32)
                got += [both[:, i * ny : (i + 1) * ny] for i in range(len(mine))]
            if len(got) == 3:
                got.append(jnp.zeros((2 * HALO_X, ny), f32))
            for i in range(3):
                for ref, at in ((lo_ref, 0), (hi_ref, HALO_X)):
                    extra = got[3][at + spare * i : at + spare * (i + 1)]
                    ref[3 * group + i] = jnp.concatenate([got[i][at : at + used], extra], axis=0).astype(bf16)

        for l in range(per):
            loads[l].wait()
            mine = pl.ds(8 * l, 8)
            send(pert_ref.at[mine, z], first_any.at[mine])
        for s, nb_any in enumerate(nb_anys):
            for i in range(modes * 2):
                send(pert_ref.at[pl.ds(sent(s, scal) * 8 + 4 * i, 3)], nb_any.at[pl.ds(3 * i, 3)])
        for group in range(n_pert // 4):
            edges(group)
        loads[per].wait()
        loads[per + 1].wait()
        send(mean_ref.at[:, z], second_any.at[pl.ds(0, n_mean)])
        send(mode_ref.at[:, z], second_any.at[pl.ds(n_mean, n_modes)])
        for group in range(n_pert // 4, tiles // 3):
            edges(group)
        send(lo_ref, lo_any)
        send(hi_ref, hi_any)
        for copy in out:
            copy.wait()

    edge = jax.ShapeDtypeStruct((tiles, HALO_X, ny), bf16)
    with jax.named_scope("pack"):
        first, second, edge_lo, edge_hi, *nb_send = pl.pallas_call(
            pack,
            out_shape=(face(n_pert), face(n_base), edge, edge) + tuple(jax.ShapeDtypeStruct((n_nb, nz, nx, ny), bf16) for _ in range(sides)),
            in_specs=[HBM] * 3,
            out_specs=(ANY,) * (4 + sides),
            scratch_shapes=[
                pltpu.VMEM((n_pert, nz, nx, ny), bf16),
                pltpu.VMEM((n_mean, nz, nx, ny), bf16),
                pltpu.VMEM((n_modes, nz, nx, ny), bf16),
                pltpu.VMEM((tiles, HALO_X, ny), bf16),
                pltpu.VMEM((tiles, HALO_X, ny), bf16),
                pltpu.SemaphoreType.DMA((per + 2,)),
                pltpu.SemaphoreType.DMA((per + sides * modes * 2 + 4,)),
            ],
            compiler_params=pltpu.CompilerParams(vmem_limit_bytes=VMEM_BYTES),
        )(pert, mean, mode)
    first_got = lax.ppermute(first, "gz", cross_pairs)
    nb_got = [lax.ppermute(b, "harm", p) for b, p in zip(nb_send, harm_perms)]
    xb_got = lax.ppermute(edge_hi, "gx", up_x)
    xa_got = lax.ppermute(edge_lo, "gx", down_x)
    second_got = lax.ppermute(second, "gz", cross_pairs)

    PAIRS = ((0, 3), (1, 2))
    DRIFT = (-1.5 * FREQUENCY_STEP, -0.5 * FREQUENCY_STEP)

    def entries(t, p, q, r, s):
        return t, q, p + r, p - r, q + s, s - q, t + p, t - p

    def couple(acc, ent, vec):
        t, q, pr, pmr, qs, sq, tp, tmp = ent
        out = []
        for i in range(2):
            a, e, b, g = (vec[j][i] for j in range(4))
            out.append(
                (
                    acc[0][i] + t * a + pr * b + sq * g,
                    acc[1][i] + t * e + qs * b + pmr * g,
                    acc[2][i] + pr * a + qs * e + tp * b + q * g,
                    acc[3][i] + sq * a + pmr * e + q * b + tmp * g,
                )
            )
        return [(out[0][j], out[1][j]) for j in range(4)]

    def harmonics_of(acc, scale):
        out = [None] * 4
        for at, (lo, hi) in enumerate(PAIRS):
            (ar, ai), (er, ei) = acc[2 * at], acc[2 * at + 1]
            out[lo] = ((ar + ei) * scale, (ai - er) * scale)
            out[hi] = ((ar - ei) * scale, (ai + er) * scale)
        return out

    def basis_of(values):
        out = []
        for lo, hi in PAIRS:
            (lr, li), (hr, hi_) = values[lo], values[hi]
            out += [(lr + hr, li + hi_), (hi_ - li, lr - hr)]
        return out

    def resident(pert_ref, mean_ref, mode_ref, out_ref, grads, plain, ents, lin, rows_ref, walls_ref):
        me_h = place()[0]
        row, column = iotas(own, own)
        to_z, to_x = column_cells(column, nz, nx)
        for i in range(3):
            rows_ref[i * own : (i + 1) * own] = slope_matrix(i, row >> nx.bit_length() - 1, row & (nx - 1), to_z, to_x).astype(bf16)
        store_walls(walls_ref, ny)
        mean_freq = 12.0 * FREQUENCY_STEP * (me_h * per + 1.5 - per * harms / 2).astype(f32)

        def rhs(ref, fields):
            cols = [ref[f] for f in fields]
            return cols[0] if len(cols) == 1 else jnp.concatenate(cols, axis=1)

        def dot(a, b):
            return jnp.dot(a, b, preferred_element_type=f32)

        for at, (lo, hi) in enumerate(PAIRS):
            for i in range(2):
                fl, fr = lo * 8 + i * 4 + 3, hi * 8 + i * 4 + 3
                got = dot(rows_ref[: 2 * own], rhs(pert_ref, (fl, fr)))
                wall = dot(rhs(pert_ref, (fl, fr)), walls_ref[:, : 2 * ny])
                for d in range(3):
                    if d == 1:
                        total, diff = wall[:, :ny], wall[:, ny:]
                    else:
                        span = slice(0, own) if d == 0 else slice(own, 2 * own)
                        total, diff = got[span, :ny] + got[span, ny:], got[span, :ny] - got[span, ny:]
                    lin[2 * at, i, d] = total
                    lin[2 * at + 1, 1 - i, d] = diff if i == 0 else -diff
        for at, (lo, hi) in enumerate(PAIRS):
            for c in range(3):
                for i in range(2):
                    sign = 1.0 if i == 0 else -1.0
                    fl, fr = lo * 8 + i * 4 + c, hi * 8 + i * 4 + c
                    got = dot(rows_ref[...], rhs(pert_ref, (fl, fr)))
                    xl, xr = pert_ref[fl].astype(f32), pert_ref[fr].astype(f32)
                    wall = dot(rhs(pert_ref, (fl, fr)), walls_ref[...])
                    total, diff = xl + xr, xl - xr
                    plain[2 * at, i, c] = total
                    plain[2 * at + 1, 1 - i, c] = sign * diff
                    for d in range(3):
                        if d == 1:
                            gt, gd = wall[:, :ny], wall[:, ny : 2 * ny]
                        else:
                            span = slice(0, own) if d == 0 else slice(own, 2 * own)
                            gt, gd = got[span, :ny] + got[span, ny:], got[span, :ny] - got[span, ny:]
                        gd = sign * gd
                        grads[2 * at, i, c, d] = gt
                        grads[2 * at + 1, 1 - i, c, d] = gd
                        if d == c:
                            if c == 0:
                                lin[2 * at, i, 3] = gt
                                lin[2 * at + 1, 1 - i, 3] = gd
                            else:
                                lin[2 * at, i, 3] = lin[2 * at, i, 3] + gt
                                lin[2 * at + 1, 1 - i, 3] = lin[2 * at + 1, 1 - i, 3] + gd
                    lt = got[2 * own :, :ny] + got[2 * own :, ny:] + wall[:, 2 * ny : 3 * ny]
                    ld = got[2 * own :, :ny] - got[2 * own :, ny:] + wall[:, 3 * ny :]
                    drift = 12.0 * DRIFT[at]
                    lin[2 * at, i, c] = lin[2 * at, i, c] - VISCOSITY * lt
                    lin[2 * at + 1, 1 - i, c] = lin[2 * at + 1, 1 - i, c] - sign * VISCOSITY * ld
                    lin[2 * at, 1 - i, c] = lin[2 * at, 1 - i, c] + sign * (mean_freq * total + drift * diff)
                    lin[2 * at + 1, i, c] = lin[2 * at + 1, i, c] - (mean_freq * diff + drift * total)
        for c in range(3):
            picked = [mean_ref[c].astype(f32)] + [mode_ref[3 * i + c].astype(f32) for i in range(4)]
            for n, ent in enumerate(entries(*picked)):
                ents[c, n] = ent
            mean_at = dot(rows_ref[: 2 * own], rhs(mean_ref, (c,)))
            mean_wall = dot(mean_ref[c], walls_ref[:ny, :ny])
            real = dot(rows_ref[: 2 * own], rhs(mode_ref, (c, 6 + c)))
            imag = dot(rows_ref[: 2 * own], rhs(mode_ref, (3 + c, 9 + c)))
            wall_real = dot(rhs(mode_ref, (c, 6 + c)), walls_ref[:, : 2 * ny])
            wall_imag = dot(rhs(mode_ref, (3 + c, 9 + c)), walls_ref[:, : 2 * ny])
            for d in range(3):
                if d == 1:
                    pr, pmr = wall_real[:, :ny], wall_real[:, ny:]
                    qs, qms = wall_imag[:, :ny], wall_imag[:, ny:]
                    t, p, q = mean_wall, 0.5 * (pr + pmr), 0.5 * (qs + qms)
                    values = (t, q, pr, pmr, qs, -qms, t + p, t - p)
                else:
                    span = slice(0, own) if d == 0 else slice(own, 2 * own)
                    values = entries(mean_at[span], real[span, :ny], imag[span, :ny], real[span, ny:], imag[span, ny:])
                for n, ent in enumerate(values):
                    ents[3 + 3 * d + c, n] = ent

        def block(b, carry):
            rows = pl.ds(pl.multiple_of(b * 8, 8), 8)
            accs = [[(lin[j, 0, c, rows], lin[j, 1, c, rows]) for j in range(4)] for c in range(4)]
            for d in range(3):
                flow = [ents[d, n, rows] for n in range(8)]
                for c in range(3):
                    accs[c] = couple(accs[c], flow, [(grads[j, 0, c, d, rows], grads[j, 1, c, d, rows]) for j in range(4)])
                along = [(plain[j, 0, d, rows], plain[j, 1, d, rows]) for j in range(4)]
                for c in range(3):
                    slope = [ents[3 + 3 * d + c, n, rows] for n in range(8)]
                    accs[c] = couple(accs[c], slope, along)
            for c in range(4):
                for k, (re, im) in enumerate(harmonics_of(accs[c], 1.0 / 24.0)):
                    out_ref[k * 8 + c, rows] = re
                    out_ref[k * 8 + 4 + c, rows] = im
            return carry

        lax.fori_loop(0, own // 8, block, 0, unroll=2)

    flat = lambda a: a.reshape(a.shape[0], -1, ny)
    with jax.named_scope("resident"):
        whole = pl.pallas_call(
            resident,
            out_shape=jax.ShapeDtypeStruct((n_pert, own, ny), f32),
            scratch_shapes=[
                pltpu.VMEM((4, 2, 3, 3, own, ny), f32),
                pltpu.VMEM((4, 2, 3, own, ny), f32),
                pltpu.VMEM((12, 8, own, ny), f32),
                pltpu.VMEM((4, 2, 4, own, ny), f32),
                pltpu.VMEM((3 * own, own), bf16),
                pltpu.VMEM((2 * ny, 4 * ny), bf16),
            ],
            compiler_params=roomy,
        )(flat(pert), flat(mean), flat(mode))

    deep = 2 * nx + 2 * HALO_X

    def pack_relay(first_ref, xb_ref, xa_ref, _, *outs):
        scal = place()
        for s, out in enumerate(outs):
            for i in range(modes * 2):
                group = sent(s, scal) * 2 + i
                for c in range(3):
                    out[3 * i + c, : 2 * nx] = first_ref[group * 4 + c].reshape(2 * nx, ny)
                    out[3 * i + c, 2 * nx : 2 * nx + HALO_X] = xb_ref[group * 3 + c]
                    out[3 * i + c, 2 * nx + HALO_X :] = xa_ref[group * 3 + c]

    with jax.named_scope("pack_relay"):
        relay = pl.pallas_call(
            pack_relay,
            out_shape=tuple(jax.ShapeDtypeStruct((n_nb, deep, ny), bf16) for _ in range(sides)),
            in_specs=[VMEM] * 3 + [ANY],
            compiler_params=roomy,
        )(first_got, xb_got, xa_got, whole)
    relay_got = [lax.ppermute(b, "harm", p) for b, p in zip(relay, harm_perms)]

    def pack_near(pert_ref, mean_ref, mode_ref, *rest):
        out = rest[-1]
        z = pl.ds(place()[3], 2)
        out[:n_pert] = pert_ref[:, z]
        out[n_pert : n_pert + n_mean] = mean_ref[:, z]
        out[n_pert + n_mean : n_res] = mode_ref[:, z]
        for s in range(sides):
            out[n_res + s * n_nb : n_res + (s + 1) * n_nb] = rest[s][:, z]

    with jax.named_scope("pack_near"):
        near = pl.pallas_call(
            pack_near,
            out_shape=face(n_all),
            in_specs=[VMEM] * (3 + sides) + [ANY],
            compiler_params=roomy,
        )(pert, mean, mode, *nb_got, relay[0])
    near_got = lax.ppermute(near, "gz", near_pairs)

    below, above = [], []
    for k in range(per):
        for m in range(-modes, modes + 1):
            l = k - m
            if l < 0:
                below.append((k, m, 0, (l + modes) * 6))
            elif l >= per:
                above.append((k, m, sides - 1, (l - per) * 6))

    ends = 16 * nz

    def edge_taps(tables):
        row, column = iotas(ends, own + 2 * HALO_X)
        last = row >= 8 * nz
        row = jnp.where(last, row - 8 * nz, row)
        to_z, to_x = column_cells(column, nz, nx)
        dz, dx = to_z - (row >> 3), to_x - (row & 7) - jnp.where(last, nx - 8, 0)
        return jnp.concatenate([jnp.where(dz == 0, taps(dx, table), 0.0)[:, own:] for table in tables], axis=0).astype(bf16)

    def on_sides(work):
        me_h = lax.axis_index("harm")
        pl.when(me_h > 0)(lambda: work(below))
        pl.when(me_h < harms - 1)(lambda: work(above))

    def product(acc, flow, value, m):
        (fr, fi), (vr, vi) = flow, value
        if m > 0:
            return acc[0] + fr * vr - fi * vi, acc[1] + fr * vi + fi * vr
        return acc[0] + fr * vr + fi * vi, acc[1] + fr * vi - fi * vr

    base_modes_at = n_pert + n_mean

    def face_place(cross, step):
        odd = place()[1]
        before = (odd == 0) if cross else (odd == 1)
        return before, jnp.where(before, step, nz - 1 - step), jnp.where(before, 1, 0)

    def faces(out_ref, mean_ref, mode_ref, pert_ref, nb_refs, first_ref, second_ref, near_ref, relay_refs, step):
        cross = near_ref is None
        before, layer, near_at = face_place(cross, step)
        turn = jnp.where(before, 1.0, -1.0)

        def mix(pair):
            return pair[1] - 8.0 * pair[0] if step == 0 else pair[0]

        def mix_lap(pair):
            return pair[1] - 16.0 * pair[0] if step == 0 else pair[0]

        def chunk_work(chunk, carry):
            rows = pl.ds(pl.multiple_of(layer * nx + chunk * 16, 16), 16)
            strip = pl.ds(pl.multiple_of(chunk * 16, 16), 16)

            def halos(f):
                if not cross:
                    ref, at = near_ref, f
                elif f < n_pert:
                    ref, at = first_ref, f
                else:
                    ref, at = second_ref, f - n_pert
                return ref[at, near_at, strip].astype(f32), (ref[at, 1 - near_at, strip].astype(f32) if step == 0 else None)

            def nb_halos(s, f):
                if not cross:
                    return halos(n_res + s * n_nb + f)
                at = [pl.ds(pl.multiple_of(j * nx + chunk * 16, 16), 16) for j in (near_at, 1 - near_at)]
                return tuple(relay_refs[s][f, r].astype(f32) for r in at)

            velocity, base = first_ref is not None or not cross, second_ref is not None or not cross
            if velocity:
                flow = entries(mean_ref[2, rows].astype(f32), *[mode_ref[3 * i + 2, rows].astype(f32) for i in range(4)])
            if base:
                along = basis_of([(pert_ref[l * 8 + 2, rows].astype(f32), pert_ref[l * 8 + 6, rows].astype(f32)) for l in range(per)])
            for c in range(4 if velocity else 3):
                acc = [(0.0, 0.0)] * 4
                if velocity and c < 3:
                    got = [[halos(l * 8 + 4 * i + c) for i in range(2)] for l in range(per)]
                    vec = basis_of([(mix(g[0]), mix(g[1])) for g in got])
                    lap = basis_of([(mix_lap(g[0]), mix_lap(g[1])) for g in got])
                    if c == 2:
                        acc = basis_of([(mix(halos(l * 8 + 3)), mix(halos(l * 8 + 7))) for l in range(per)])
                    acc = couple(acc, flow, vec)
                if base and c < 3:
                    bend = entries(mix(halos(n_pert + c)), *[mix(halos(base_modes_at + 3 * i + c)) for i in range(4)])
                    acc = couple(acc, bend, along)
                if c == 3:
                    acc = vec
                if velocity and c < 3:
                    acc = [tuple(turn * a + VISCOSITY * v for a, v in zip(*pair)) for pair in zip(acc, lap)]
                else:
                    acc = [tuple(turn * a for a in pair) for pair in acc]
                for k, parts in enumerate(harmonics_of(acc, 1.0 / 24.0)):
                    for i in range(2):
                        at = k * 8 + 4 * i + c
                        out_ref[at, rows] = out_ref[at, rows] + parts[i]

            def nb_work(pairs):
                for k in sorted({p[0] for p in pairs}):
                    zero = jnp.zeros((16, ny), f32)
                    for c in range(3):
                        acc = (zero, zero)
                        for _, m, s, f in [p for p in pairs if p[0] == k]:
                            at = (abs(m) - 1) * 6
                            mine = tuple(mode_ref[at + 3 * i + 2, rows].astype(f32) for i in range(2))
                            acc = product(acc, mine, tuple(mix(nb_halos(s, f + 3 * i + c)) for i in range(2)), m)
                            bent = tuple(mix(halos(base_modes_at + at + 3 * i + c)) for i in range(2))
                            carried = tuple(nb_refs[s][f + 3 * i + 2, rows].astype(f32) for i in range(2))
                            acc = product(acc, bent, carried, m)
                        for i in range(2):
                            at = k * 8 + 4 * i + c
                            out_ref[at, rows] = out_ref[at, rows] + (turn * (1.0 / 12.0)) * acc[i]

            if base:
                on_sides(nb_work)
            return carry

        lax.fori_loop(0, nx // 16, chunk_work, 0)

    def neighbours(mask_ref, pert_ref, mean_ref, mode_ref, xb_ref, xa_ref, whole_ref, first_ref, near_ref, *rest):
        nb_refs = rest[:sides]
        out_ref, grads, plain, stencil_ref, walls_ref, vecs, lins, bends = rest[-8:]
        row, column = iotas(own, own + 2 * HALO_X)
        to_z, to_x = column_cells(column, nz, nx)
        for i in range(2):
            stencil_ref[i * own : (i + 1) * own] = slope_matrix(i, row >> nx.bit_length() - 1, row & (nx - 1), to_z, to_x).astype(bf16)
        store_walls(walls_ref, ny)

        def slopes(at, mine, halo):
            both = jnp.concatenate(mine, axis=1)
            rows = both if halo is None else jnp.concatenate([both, halo], axis=0)
            got = jnp.dot(stencil_ref[:, : rows.shape[0]], rows, preferred_element_type=f32)
            wall = [jnp.dot(x, walls_ref[:ny, :ny], preferred_element_type=f32) for x in mine]
            for i in range(2):
                lanes = slice(i * ny, (i + 1) * ny)
                grads[at + i, 0] = got[:own, lanes]
                grads[at + i, 2] = got[own:, lanes]
                grads[at + i, 1] = wall[i]
                plain[at + i] = mine[i].astype(f32)

        for f in range(0, n_modes, 2):
            at = base_modes_at + f
            halo = [jnp.concatenate([edge_tile(ref, at), edge_tile(ref, at + 1)], axis=1) for ref in (xb_ref, xa_ref)]
            slopes(f, [mode_ref[f], mode_ref[f + 1]], jnp.concatenate(halo, axis=0))
        for s in range(sides):
            for f in range(0, n_nb, 2):
                slopes(n_modes + s * n_nb + f, [nb_refs[s][f], nb_refs[s][f + 1]], None)

        taps_of = edge_taps((FIRST, SECOND))

        def bent(fields, lap):
            cols = [jnp.concatenate([edge_tile(xb_ref, f), edge_tile(xa_ref, f)], axis=0) for f in fields]
            both = cols[0] if len(cols) == 1 else jnp.concatenate(cols, axis=1)
            got = jnp.dot(taps_of if lap else taps_of[:ends], both, preferred_element_type=f32)
            return [(got[:ends, i * ny : (i + 1) * ny], got[ends:, i * ny : (i + 1) * ny]) for i in range(len(fields))]

        for at, (lo, hi) in enumerate(PAIRS):
            for i in range(2):
                sign = 1.0 if i == 0 else -1.0
                for c in range(4):
                    (gl, ll), (gr, lr) = bent((lo * 8 + 4 * i + c, hi * 8 + 4 * i + c), c < 3)
                    if c < 3:
                        vecs[2 * at, i, c] = gl + gr
                        vecs[2 * at + 1, 1 - i, c] = sign * (gl - gr)
                        lins[2 * at, i, c] = -VISCOSITY * (ll + lr)
                        lins[2 * at + 1, 1 - i, c] = (-VISCOSITY * sign) * (ll - lr)
                    else:
                        lins[2 * at, i, 0] = lins[2 * at, i, 0] + (gl + gr)
                        lins[2 * at + 1, 1 - i, 0] = lins[2 * at + 1, 1 - i, 0] + sign * (gl - gr)
        for c in range(3):
            at = base_modes_at + c
            (t, _), = bent((n_pert + c,), False)
            (p, _), (r, _) = bent((at, at + 6), False)
            (q, _), (s_, _) = bent((at + 3, at + 9), False)
            for n, ent in enumerate(entries(t, p, q, r, s_)):
                bends[c, n] = ent

        for z in range(nz):
            rows = slice(z * nx, (z + 1) * nx)
            solid = PENALTY * mask_ref[rows].astype(f32)
            for f in range(n_pert):
                if f % 4 < 3:
                    out_ref[f, rows] = whole_ref[f, rows] + solid * pert_ref[f, rows].astype(f32)
                else:
                    out_ref[f, rows] = whole_ref[f, rows]

        def layer_ends(z, carry):
            for end in range(2):
                strip = pl.ds(pl.multiple_of(z * nx + end * (nx // 2), 16), 16)
                keep = slice(8 * end, 8 * end + 8)
                rows = pl.ds(pl.multiple_of(z * nx + end * (nx - 8), 8), 8)
                mine = pl.ds(pl.multiple_of((end * nz + z) * 8, 8), 8)

                def read(ref, f):
                    return ref[f, strip].astype(f32)[keep]

                flow = entries(read(mean_ref, 0), *[read(mode_ref, 3 * i) for i in range(4)])
                along = basis_of([(read(pert_ref, l * 8), read(pert_ref, l * 8 + 4)) for l in range(per)])
                for c in range(4):
                    if c < 3:
                        acc = [(lins[j, 0, c, mine], lins[j, 1, c, mine]) for j in range(4)]
                        acc = couple(acc, flow, [(vecs[j, 0, c, mine], vecs[j, 1, c, mine]) for j in range(4)])
                        acc = couple(acc, [bends[c, n, mine] for n in range(8)], along)
                    else:
                        acc = [(vecs[j, 0, 0, mine], vecs[j, 1, 0, mine]) for j in range(4)]
                    for k, parts in enumerate(harmonics_of(acc, 1.0 / 24.0)):
                        for i in range(2):
                            at = k * 8 + 4 * i + c
                            out_ref[at, rows] = out_ref[at, rows] + parts[i]
            return carry

        lax.fori_loop(0, nz, layer_ends, 0)

        def work(pairs):
            def block(b, carry):
                rows = pl.ds(pl.multiple_of(b * 8, 8), 8)
                for k in sorted({p[0] for p in pairs}):
                    zero = jnp.zeros((8, ny), f32)
                    acc = [(zero, zero)] * 3
                    for _, m, s, f in [p for p in pairs if p[0] == k]:
                        at, base = n_modes + s * n_nb + f, (abs(m) - 1) * 6
                        for d in range(3):
                            flow = plain[base + d, rows], plain[base + 3 + d, rows]
                            along = plain[at + d, rows], plain[at + 3 + d, rows]
                            for c in range(3):
                                slope = grads[base + c, d, rows], grads[base + 3 + c, d, rows]
                                grad = grads[at + c, d, rows], grads[at + 3 + c, d, rows]
                                acc[c] = product(acc[c], flow, grad, m)
                                acc[c] = product(acc[c], slope, along, m)
                    for c in range(3):
                        for i in range(2):
                            at = k * 8 + 4 * i + c
                            out_ref[at, rows] = out_ref[at, rows] + acc[c][i] * (1.0 / 12.0)
                return carry

            lax.fori_loop(0, own // 8, block, 0)

        on_sides(work)
        for step in range(2):
            faces(out_ref, mean_ref, mode_ref, pert_ref, nb_refs, first_ref, None, None, None, step)
            faces(out_ref, mean_ref, mode_ref, pert_ref, nb_refs, None, None, near_ref, None, step)

    n_ext = n_modes + sides * n_nb
    with jax.named_scope("neighbours"):
        inner = pl.pallas_call(
            neighbours,
            out_shape=jax.ShapeDtypeStruct((n_pert, own, ny), f32),
            scratch_shapes=[
                pltpu.VMEM((n_ext, 3, own, ny), f32),
                pltpu.VMEM((n_ext, own, ny), f32),
                pltpu.VMEM((2 * own, own + 2 * HALO_X), bf16),
                pltpu.VMEM((ny, ny), bf16),
                pltpu.VMEM((4, 2, 3, ends, ny), f32),
                pltpu.VMEM((4, 2, 3, ends, ny), f32),
                pltpu.VMEM((3, 8, ends, ny), f32),
            ],
            compiler_params=roomy,
        )(mask, flat(pert), flat(mean), flat(mode), xb_got, xa_got, whole, first_got, near_got, *[flat(b) for b in nb_got])

    def finish(pert_ref, mean_ref, mode_ref, inner_ref, second_ref, *rest):
        relay_refs, nb_refs = rest[:sides], rest[sides : 2 * sides]
        out_any, done, bends, sems = rest[2 * sides :]
        half = nx // 2
        done[...] = inner_ref[...]
        taps_of = edge_taps((FIRST,))

        def send(layer):
            rows = pl.ds(pl.multiple_of(layer * nx, nx), nx)
            return pltpu.make_async_copy(done.at[:, rows], out_any.at[:, rows], sems.at[layer])

        for s in range(sides):
            for f in range(0, n_nb, 2):
                both = jnp.concatenate([relay_refs[s][f + i, 2 * nx :] for i in range(2)], axis=1)
                got = jnp.dot(taps_of, both, preferred_element_type=f32)
                for i in range(2):
                    bends[s * n_nb + f + i] = got[:, i * ny : (i + 1) * ny]

        def edge_work(pairs):
            def layer_edges(z, carry):
                for end in range(2):
                    strip = pl.ds(pl.multiple_of(z * nx + end * half, 16), 16)
                    keep = slice(8 * end, 8 * end + 8)
                    rows = pl.ds(pl.multiple_of(z * nx + end * (nx - 8), 8), 8)
                    bent = pl.ds(pl.multiple_of((end * nz + z) * 8, 8), 8)
                    for k in sorted({p[0] for p in pairs}):
                        zero = jnp.zeros((8, ny), f32)
                        acc = [(zero, zero)] * 3
                        for _, m, s, f in [p for p in pairs if p[0] == k]:
                            base = (abs(m) - 1) * 6
                            flow = tuple(mode_ref[base + 3 * i, strip].astype(f32)[keep] for i in range(2))
                            for c in range(3):
                                at = s * n_nb + f + c
                                acc[c] = product(acc[c], flow, (bends[at, bent], bends[at + 3, bent]), m)
                        for c in range(3):
                            for i in range(2):
                                at = k * 8 + 4 * i + c
                                done[at, rows] = done[at, rows] + acc[c][i] * (1.0 / 12.0)
                return carry

            lax.fori_loop(0, nz, layer_edges, 0)

        on_sides(edge_work)
        for layer in range(2, nz - 2):
            send(layer).start()
        for step in range(2):
            send(face_place(False, step)[1]).start()

        for step in range(2):
            faces(done, mean_ref, mode_ref, pert_ref, nb_refs, None, second_ref, None, relay_refs, step)
            send(face_place(True, step)[1]).start()
        for layer in range(nz):
            send(layer).wait()

    with jax.named_scope("finish"):
        out = pl.pallas_call(
            finish,
            out_shape=jax.ShapeDtypeStruct((n_pert, own, ny), f32),
            out_specs=HBM,
            scratch_shapes=[
                pltpu.VMEM((n_pert, own, ny), f32),
                pltpu.VMEM((sides * n_nb, ends, ny), f32),
                pltpu.SemaphoreType.DMA((nz,)),
            ],
            compiler_params=roomy,
        )(
            flat(pert), flat(mean), flat(mode), inner, second_got,
            *relay_got, *[flat(b) for b in nb_got],
        )
    return jnp.swapaxes(out.reshape(per, 2, 4, nz, nx, ny), 3, 4)


def solution(mesh):
    return jax.shard_map(
        shards,
        mesh=mesh,
        in_specs=(
            P("harm", None, None, "gx", "gz", None),
            P(None, "gx", "gz", None),
            P(None, None, None, "gx", "gz", None),
            P("gx", "gz", None),
        ),
        out_specs=P("harm", None, None, "gx", "gz", None),
        check_vma=False,
    )
```

```python
import jax
import jax.numpy as jnp
from jax import lax
from jax.experimental import pallas as pl
from jax.experimental.pallas import tpu as pltpu
from jax.sharding import PartitionSpec as P

FREQUENCY_STEP = 0.2
VISCOSITY = 0.05
PENALTY = 4.0
FIRST = {-2: 1.0, -1: -8.0, 1: 8.0, 2: -1.0}
SECOND = {-2: -1.0, -1: 16.0, 0: -30.0, 1: 16.0, 2: -1.0}
HALO_X = 16
VMEM_BYTES = 58 * 1024 * 1024
ANY = pl.BlockSpec(memory_space=pl.ANY)
VMEM = pl.BlockSpec(memory_space=pltpu.VMEM)
HBM = pl.BlockSpec(memory_space=pltpu.HBM)


def taps(delta, table):
    out = jnp.zeros(delta.shape, jnp.float32)
    for step, weight in table.items():
        out = jnp.where(delta == step, weight, out)
    return out


def iotas(rows, columns):
    return lax.broadcasted_iota(jnp.int32, (rows, 1), 0), lax.broadcasted_iota(jnp.int32, (1, columns), 1)


def column_cells(column, nz, nx):
    shift, own = nx.bit_length() - 1, nz * nx
    halo = column - own
    after = halo >= HALO_X
    edge = jnp.where(after, halo - HALO_X, halo)
    inside = column < own
    z = jnp.where(inside, column >> shift, edge >> 1)
    x = jnp.where(inside, column & (nx - 1), (edge & 1) + jnp.where(after, nx, -2))
    return z, x


def slope_matrix(part, z, x, to_z, to_x):
    dz, dx = to_z - z, to_x - x
    if part == 0:
        return jnp.where(dz == 0, taps(dx, FIRST), 0.0)
    if part == 1:
        return jnp.where(dx == 0, taps(dz, FIRST), 0.0)
    return jnp.where(dz == 0, taps(dx, SECOND), 0.0) + jnp.where(dx == 0, taps(dz, SECOND), 0.0)


def store_walls(walls_ref, ny):
    row, column = iotas(ny, ny)
    first, second = (taps(row - column, table).astype(jnp.bfloat16) for table in (FIRST, SECOND))
    for i, (block, sign) in enumerate(((first, 1), (first, -1), (second, 1), (second, -1))):
        if i * ny < walls_ref.shape[1]:
            walls_ref[:ny, i * ny : (i + 1) * ny] = block
            if walls_ref.shape[0] > ny:
                walls_ref[ny:, i * ny : (i + 1) * ny] = block if sign > 0 else -block


def run_copies(copies, sems):
    started = [pltpu.make_async_copy(src, dst, sems.at[i]) for i, (src, dst) in enumerate(copies)]
    for copy in started:
        copy.start()
    for copy in started:
        copy.wait()


def shards(perturbation, base_mean, base_modes, solid_mask):
    per, modes = perturbation.shape[0], base_modes.shape[0]
    nx, nz, ny = perturbation.shape[3], perturbation.shape[4], perturbation.shape[5]
    own = nz * nx
    bf16, f32 = jnp.bfloat16, jnp.float32
    harms, size_x, size_z = (lax.axis_size(a) for a in ("harm", "gx", "gz"))
    swap = harms == 2
    sides = 1 if swap else 2
    n_pert, n_mean, n_modes = per * 8, 3, modes * 6
    n_base = n_mean + n_modes
    n_res = n_pert + n_base
    n_nb = modes * 6
    n_all = n_res + sides * n_nb

    pert = jnp.swapaxes(perturbation, 3, 4).reshape(n_pert, nz, nx, ny)
    mean = jnp.swapaxes(base_mean, 1, 2)
    mode = jnp.swapaxes(base_modes, 3, 4).reshape(n_modes, nz, nx, ny)
    mask = jnp.swapaxes(solid_mask, 0, 1).reshape(own, ny)

    def place():
        me_h, odd = lax.axis_index("harm"), lax.rem(lax.axis_index("gz"), 2)
        shared = jnp.where(me_h == 0, per - modes, 0) if swap else 0
        return me_h, odd, odd * (nz - 2), (1 - odd) * (nz - 2), shared

    cross_pairs = [(i, (i + 1) % size_z if i % 2 else (i - 1) % size_z) for i in range(size_z)]
    near_pairs = [(i, i + 1 if i % 2 == 0 else i - 1) for i in range(size_z)]
    up_x = [(i, (i + 1) % size_x) for i in range(size_x)]
    down_x = [(j, i) for i, j in up_x]
    if swap:
        harm_perms = [[(0, 1), (1, 0)]]
    else:
        up_h = [(i, i + 1) for i in range(harms - 1)]
        harm_perms = [up_h, [(j, i) for i, j in up_h]]
    def sent(s, scal):
        return scal[4] if swap else (per - modes if s == 0 else 0)

    face = lambda n: jax.ShapeDtypeStruct((n, 2, nx, ny), bf16)
    roomy = pltpu.CompilerParams(vmem_limit_bytes=32 * 1024 * 1024)

    used = 2 * nz
    spare = HALO_X - used
    tiles = 3 * (-(-n_res // 4))

    def edge_tile(ref, f):
        group, i = divmod(f, 4)
        if i < 3:
            return ref[3 * group + i]
        parts = [ref[3 * group + j].astype(f32)[used:] for j in range(3)]
        return jnp.concatenate(parts + [jnp.zeros((spare, ny), f32)], axis=0).astype(bf16)

    def pack(pert_any, mean_any, mode_any, first_any, second_any, lo_any, hi_any, *rest):
        nb_anys = rest[:sides]
        pert_ref, mean_ref, mode_ref, lo_ref, hi_ref, in_sems, out_sems = rest[sides:]
        scal = place()
        z = pl.ds(scal[2], 2)
        loads = [(pert_any.at[pl.ds(8 * l, 8)], pert_ref.at[pl.ds(8 * l, 8)]) for l in range(per)]
        loads += [(mean_any, mean_ref), (mode_any, mode_ref)]
        loads = [pltpu.make_async_copy(src, dst, in_sems.at[i]) for i, (src, dst) in enumerate(loads)]
        for copy in loads:
            copy.start()
        out = []

        def send(src, dst):
            out.append(pltpu.make_async_copy(src, dst, out_sems.at[len(out)]))
            out[-1].start()

        row, column = iotas(2 * HALO_X, own)
        low = row < HALO_X
        row = jnp.where(low, row, row - HALO_X)
        target = (row >> 1) * nx + (row & 1) + jnp.where(low, 0, nx - 2)
        pick = jnp.where(column == target, 1.0, 0.0).astype(bf16)
        where = [(pert_ref, f) for f in range(n_pert)] + [(mean_ref, f) for f in range(n_mean)] + [(mode_ref, f) for f in range(n_modes)]

        def edges(group):
            got = []
            for f in range(4 * group, min(4 * group + 4, n_res), 2):
                mine = [ref[i].reshape(own, ny) for ref, i in where[f : min(f + 2, n_res)]]
                both = jnp.concatenate(mine, axis=1) if len(mine) == 2 else mine[0]
                both = jnp.dot(pick, both, preferred_element_type=f32)
                got += [both[:, i * ny : (i + 1) * ny] for i in range(len(mine))]
            if len(got) == 3:
                got.append(jnp.zeros((2 * HALO_X, ny), f32))
            for i in range(3):
                for ref, at in ((lo_ref, 0), (hi_ref, HALO_X)):
                    extra = got[3][at + spare * i : at + spare * (i + 1)]
                    ref[3 * group + i] = jnp.concatenate([got[i][at : at + used], extra], axis=0).astype(bf16)

        for l in range(per):
            loads[l].wait()
            mine = pl.ds(8 * l, 8)
            send(pert_ref.at[mine, z], first_any.at[mine])
        for s, nb_any in enumerate(nb_anys):
            for i in range(modes * 2):
                send(pert_ref.at[pl.ds(sent(s, scal) * 8 + 4 * i, 3)], nb_any.at[pl.ds(3 * i, 3)])
        for group in range(n_pert // 4):
            edges(group)
        loads[per].wait()
        loads[per + 1].wait()
        send(mean_ref.at[:, z], second_any.at[pl.ds(0, n_mean)])
        send(mode_ref.at[:, z], second_any.at[pl.ds(n_mean, n_modes)])
        for group in range(n_pert // 4, tiles // 3):
            edges(group)
        send(lo_ref, lo_any)
        send(hi_ref, hi_any)
        for copy in out:
            copy.wait()

    edge = jax.ShapeDtypeStruct((tiles, HALO_X, ny), bf16)
    with jax.named_scope("pack"):
        first, second, edge_lo, edge_hi, *nb_send = pl.pallas_call(
            pack,
            out_shape=(face(n_pert), face(n_base), edge, edge) + tuple(jax.ShapeDtypeStruct((n_nb, nz, nx, ny), bf16) for _ in range(sides)),
            in_specs=[HBM] * 3,
            out_specs=(ANY,) * (4 + sides),
            scratch_shapes=[
                pltpu.VMEM((n_pert, nz, nx, ny), bf16),
                pltpu.VMEM((n_mean, nz, nx, ny), bf16),
                pltpu.VMEM((n_modes, nz, nx, ny), bf16),
                pltpu.VMEM((tiles, HALO_X, ny), bf16),
                pltpu.VMEM((tiles, HALO_X, ny), bf16),
                pltpu.SemaphoreType.DMA((per + 2,)),
                pltpu.SemaphoreType.DMA((per + sides * modes * 2 + 4,)),
            ],
            compiler_params=pltpu.CompilerParams(vmem_limit_bytes=VMEM_BYTES),
        )(pert, mean, mode)
    first_got = lax.ppermute(first, "gz", cross_pairs)
    nb_got = [lax.ppermute(b, "harm", p) for b, p in zip(nb_send, harm_perms)]
    xb_got = lax.ppermute(edge_hi, "gx", up_x)
    xa_got = lax.ppermute(edge_lo, "gx", down_x)
    second_got = lax.ppermute(second, "gz", cross_pairs)

    PAIRS = ((0, 3), (1, 2))
    DRIFT = (-1.5 * FREQUENCY_STEP, -0.5 * FREQUENCY_STEP)

    def entries(t, p, q, r, s):
        return t, q, p + r, p - r, q + s, s - q, t + p, t - p

    def couple(acc, ent, vec):
        t, q, pr, pmr, qs, sq, tp, tmp = ent
        out = []
        for i in range(2):
            a, e, b, g = (vec[j][i] for j in range(4))
            out.append(
                (
                    acc[0][i] + t * a + pr * b + sq * g,
                    acc[1][i] + t * e + qs * b + pmr * g,
                    acc[2][i] + pr * a + qs * e + tp * b + q * g,
                    acc[3][i] + sq * a + pmr * e + q * b + tmp * g,
                )
            )
        return [(out[0][j], out[1][j]) for j in range(4)]

    def harmonics_of(acc, scale):
        out = [None] * 4
        for at, (lo, hi) in enumerate(PAIRS):
            (ar, ai), (er, ei) = acc[2 * at], acc[2 * at + 1]
            out[lo] = ((ar + ei) * scale, (ai - er) * scale)
            out[hi] = ((ar - ei) * scale, (ai + er) * scale)
        return out

    def basis_of(values):
        out = []
        for lo, hi in PAIRS:
            (lr, li), (hr, hi_) = values[lo], values[hi]
            out += [(lr + hr, li + hi_), (hi_ - li, lr - hr)]
        return out

    def rhs(ref, fields):
        cols = [ref[f] for f in fields]
        return cols[0] if len(cols) == 1 else jnp.concatenate(cols, axis=1)

    def dot(a, b):
        return jnp.dot(a, b, preferred_element_type=f32)

    def resident_slopes(pert_ref, grads, plain, lin, rows_ref, walls_ref):
        me_h = place()[0]
        row, column = iotas(own, own)
        to_z, to_x = column_cells(column, nz, nx)
        for i in range(3):
            rows_ref[i * own : (i + 1) * own] = slope_matrix(i, row >> nx.bit_length() - 1, row & (nx - 1), to_z, to_x).astype(bf16)
        store_walls(walls_ref, ny)
        mean_freq = 12.0 * FREQUENCY_STEP * (me_h * per + 1.5 - per * harms / 2).astype(f32)

        for at, (lo, hi) in enumerate(PAIRS):
            for i in range(2):
                fl, fr = lo * 8 + i * 4 + 3, hi * 8 + i * 4 + 3
                got = dot(rows_ref[: 2 * own], rhs(pert_ref, (fl, fr)))
                wall = dot(rhs(pert_ref, (fl, fr)), walls_ref[:, : 2 * ny])
                for d in range(3):
                    if d == 1:
                        total, diff = wall[:, :ny], wall[:, ny:]
                    else:
                        span = slice(0, own) if d == 0 else slice(own, 2 * own)
                        total, diff = got[span, :ny] + got[span, ny:], got[span, :ny] - got[span, ny:]
                    lin[2 * at, i, d] = total
                    lin[2 * at + 1, 1 - i, d] = diff if i == 0 else -diff
        for at, (lo, hi) in enumerate(PAIRS):
            for c in range(3):
                for i in range(2):
                    sign = 1.0 if i == 0 else -1.0
                    fl, fr = lo * 8 + i * 4 + c, hi * 8 + i * 4 + c
                    got = dot(rows_ref[...], rhs(pert_ref, (fl, fr)))
                    xl, xr = pert_ref[fl].astype(f32), pert_ref[fr].astype(f32)
                    wall = dot(rhs(pert_ref, (fl, fr)), walls_ref[...])
                    total, diff = xl + xr, xl - xr
                    plain[2 * at, i, c] = total
                    plain[2 * at + 1, 1 - i, c] = sign * diff
                    for d in range(3):
                        if d == 1:
                            gt, gd = wall[:, :ny], wall[:, ny : 2 * ny]
                        else:
                            span = slice(0, own) if d == 0 else slice(own, 2 * own)
                            gt, gd = got[span, :ny] + got[span, ny:], got[span, :ny] - got[span, ny:]
                        gd = sign * gd
                        grads[2 * at, i, c, d] = gt
                        grads[2 * at + 1, 1 - i, c, d] = gd
                        if d == c:
                            if c == 0:
                                lin[2 * at, i, 3] = gt
                                lin[2 * at + 1, 1 - i, 3] = gd
                            else:
                                lin[2 * at, i, 3] = lin[2 * at, i, 3] + gt
                                lin[2 * at + 1, 1 - i, 3] = lin[2 * at + 1, 1 - i, 3] + gd
                    lt = got[2 * own :, :ny] + got[2 * own :, ny:] + wall[:, 2 * ny : 3 * ny]
                    ld = got[2 * own :, :ny] - got[2 * own :, ny:] + wall[:, 3 * ny :]
                    drift = 12.0 * DRIFT[at]
                    lin[2 * at, i, c] = lin[2 * at, i, c] - VISCOSITY * lt
                    lin[2 * at + 1, 1 - i, c] = lin[2 * at + 1, 1 - i, c] - sign * VISCOSITY * ld
                    lin[2 * at, 1 - i, c] = lin[2 * at, 1 - i, c] + sign * (mean_freq * total + drift * diff)
                    lin[2 * at + 1, i, c] = lin[2 * at + 1, i, c] - (mean_freq * diff + drift * total)

    def resident(mean_ref, mode_ref, grads, plain, lin, out_ref, ents, rows_ref, walls_ref):
        row, column = iotas(own, own)
        to_z, to_x = column_cells(column, nz, nx)
        for i in range(2):
            rows_ref[i * own : (i + 1) * own] = slope_matrix(i, row >> nx.bit_length() - 1, row & (nx - 1), to_z, to_x).astype(bf16)
        store_walls(walls_ref, ny)
        for c in range(3):
            picked = [mean_ref[c].astype(f32)] + [mode_ref[3 * i + c].astype(f32) for i in range(4)]
            for n, ent in enumerate(entries(*picked)):
                ents[c, n] = ent
            mean_at = dot(rows_ref[...], rhs(mean_ref, (c,)))
            mean_wall = dot(mean_ref[c], walls_ref[:ny, :ny])
            real = dot(rows_ref[...], rhs(mode_ref, (c, 6 + c)))
            imag = dot(rows_ref[...], rhs(mode_ref, (3 + c, 9 + c)))
            wall_real = dot(rhs(mode_ref, (c, 6 + c)), walls_ref[:, : 2 * ny])
            wall_imag = dot(rhs(mode_ref, (3 + c, 9 + c)), walls_ref[:, : 2 * ny])
            for d in range(3):
                if d == 1:
                    pr, pmr = wall_real[:, :ny], wall_real[:, ny:]
                    qs, qms = wall_imag[:, :ny], wall_imag[:, ny:]
                    t, p, q = mean_wall, 0.5 * (pr + pmr), 0.5 * (qs + qms)
                    values = (t, q, pr, pmr, qs, -qms, t + p, t - p)
                else:
                    span = slice(0, own) if d == 0 else slice(own, 2 * own)
                    values = entries(mean_at[span], real[span, :ny], imag[span, :ny], real[span, ny:], imag[span, ny:])
                for n, ent in enumerate(values):
                    ents[3 + 3 * d + c, n] = ent

        def block(b, carry):
            rows = pl.ds(pl.multiple_of(b * 8, 8), 8)
            accs = [[(lin[j, 0, c, rows], lin[j, 1, c, rows]) for j in range(4)] for c in range(4)]
            for d in range(3):
                flow = [ents[d, n, rows] for n in range(8)]
                for c in range(3):
                    accs[c] = couple(accs[c], flow, [(grads[j, 0, c, d, rows], grads[j, 1, c, d, rows]) for j in range(4)])
                along = [(plain[j, 0, d, rows], plain[j, 1, d, rows]) for j in range(4)]
                for c in range(3):
                    slope = [ents[3 + 3 * d + c, n, rows] for n in range(8)]
                    accs[c] = couple(accs[c], slope, along)
            for c in range(4):
                for k, (re, im) in enumerate(harmonics_of(accs[c], 1.0 / 24.0)):
                    out_ref[k * 8 + c, rows] = re
                    out_ref[k * 8 + 4 + c, rows] = im
            return carry

        lax.fori_loop(0, own // 8, block, 0, unroll=2)

    flat = lambda a: a.reshape(a.shape[0], -1, ny)
    with jax.named_scope("resident_slopes"):
        slopes = pl.pallas_call(
            resident_slopes,
            out_shape=tuple(jax.ShapeDtypeStruct(n + (own, ny), f32) for n in ((4, 2, 3, 3), (4, 2, 3), (4, 2, 4))),
            scratch_shapes=[pltpu.VMEM((3 * own, own), bf16), pltpu.VMEM((2 * ny, 4 * ny), bf16)],
            compiler_params=pltpu.CompilerParams(vmem_limit_bytes=20 * 1024 * 1024),
        )(flat(pert))
    with jax.named_scope("resident"):
        whole = pl.pallas_call(
            resident,
            out_shape=jax.ShapeDtypeStruct((n_pert, own, ny), f32),
            scratch_shapes=[
                pltpu.VMEM((12, 8, own, ny), f32),
                pltpu.VMEM((2 * own, own), bf16),
                pltpu.VMEM((2 * ny, 2 * ny), bf16),
            ],
            compiler_params=roomy,
        )(flat(mean), flat(mode), *slopes)

    deep = 2 * nx + 2 * HALO_X

    def pack_relay(first_ref, xb_ref, xa_ref, _, *outs):
        scal = place()
        for s, out in enumerate(outs):
            for i in range(modes * 2):
                group = sent(s, scal) * 2 + i
                for c in range(3):
                    out[3 * i + c, : 2 * nx] = first_ref[group * 4 + c].reshape(2 * nx, ny)
                    out[3 * i + c, 2 * nx : 2 * nx + HALO_X] = xb_ref[group * 3 + c]
                    out[3 * i + c, 2 * nx + HALO_X :] = xa_ref[group * 3 + c]

    with jax.named_scope("pack_relay"):
        relay = pl.pallas_call(
            pack_relay,
            out_shape=tuple(jax.ShapeDtypeStruct((n_nb, deep, ny), bf16) for _ in range(sides)),
            in_specs=[VMEM] * 3 + [ANY],
            compiler_params=roomy,
        )(first_got, xb_got, xa_got, whole)
    relay_got = [lax.ppermute(b, "harm", p) for b, p in zip(relay, harm_perms)]

    def pack_near(pert_ref, mean_ref, mode_ref, *rest):
        out = rest[-1]
        z = pl.ds(place()[3], 2)
        out[:n_pert] = pert_ref[:, z]
        out[n_pert : n_pert + n_mean] = mean_ref[:, z]
        out[n_pert + n_mean : n_res] = mode_ref[:, z]
        for s in range(sides):
            out[n_res + s * n_nb : n_res + (s + 1) * n_nb] = rest[s][:, z]

    with jax.named_scope("pack_near"):
        near = pl.pallas_call(
            pack_near,
            out_shape=face(n_all),
            in_specs=[VMEM] * (3 + sides) + [ANY],
            compiler_params=roomy,
        )(pert, mean, mode, *nb_got, relay[0])
    near_got = lax.ppermute(near, "gz", near_pairs)

    below, above = [], []
    for k in range(per):
        for m in range(-modes, modes + 1):
            l = k - m
            if l < 0:
                below.append((k, m, 0, (l + modes) * 6))
            elif l >= per:
                above.append((k, m, sides - 1, (l - per) * 6))

    ends = 16 * nz

    def edge_taps(tables):
        row, column = iotas(ends, own + 2 * HALO_X)
        last = row >= 8 * nz
        row = jnp.where(last, row - 8 * nz, row)
        to_z, to_x = column_cells(column, nz, nx)
        dz, dx = to_z - (row >> 3), to_x - (row & 7) - jnp.where(last, nx - 8, 0)
        return jnp.concatenate([jnp.where(dz == 0, taps(dx, table), 0.0)[:, own:] for table in tables], axis=0).astype(bf16)

    def on_sides(work):
        me_h = lax.axis_index("harm")
        pl.when(me_h > 0)(lambda: work(below))
        pl.when(me_h < harms - 1)(lambda: work(above))

    def product(acc, flow, value, m):
        (fr, fi), (vr, vi) = flow, value
        if m > 0:
            return acc[0] + fr * vr - fi * vi, acc[1] + fr * vi + fi * vr
        return acc[0] + fr * vr + fi * vi, acc[1] + fr * vi - fi * vr

    base_modes_at = n_pert + n_mean

    def face_place(cross, step):
        odd = place()[1]
        before = (odd == 0) if cross else (odd == 1)
        return before, jnp.where(before, step, nz - 1 - step), jnp.where(before, 1, 0)

    def faces(out_ref, mean_ref, mode_ref, pert_ref, nb_refs, first_ref, second_ref, near_ref, relay_refs, step, lowest=0):
        cross = near_ref is None
        before, layer, near_at = face_place(cross, step)
        turn = jnp.where(before, 1.0, -1.0)

        def mix(pair):
            return pair[1] - 8.0 * pair[0] if step == 0 else pair[0]

        def mix_lap(pair):
            return pair[1] - 16.0 * pair[0] if step == 0 else pair[0]

        def chunk_work(chunk, carry):
            rows = pl.ds(pl.multiple_of(layer * nx + chunk * 16, 16), 16)
            out_rows = pl.ds(pl.multiple_of((layer - lowest) * nx + chunk * 16, 16), 16)
            strip = pl.ds(pl.multiple_of(chunk * 16, 16), 16)

            def halos(f):
                if not cross:
                    ref, at = near_ref, f
                elif f < n_pert:
                    ref, at = first_ref, f
                else:
                    ref, at = second_ref, f - n_pert
                return ref[at, near_at, strip].astype(f32), (ref[at, 1 - near_at, strip].astype(f32) if step == 0 else None)

            def nb_halos(s, f):
                if not cross:
                    return halos(n_res + s * n_nb + f)
                at = [pl.ds(pl.multiple_of(j * nx + chunk * 16, 16), 16) for j in (near_at, 1 - near_at)]
                return tuple(relay_refs[s][f, r].astype(f32) for r in at)

            velocity, base = first_ref is not None or not cross, second_ref is not None or not cross
            if velocity:
                flow = entries(mean_ref[2, rows].astype(f32), *[mode_ref[3 * i + 2, rows].astype(f32) for i in range(4)])
            if base:
                along = basis_of([(pert_ref[l * 8 + 2, rows].astype(f32), pert_ref[l * 8 + 6, rows].astype(f32)) for l in range(per)])
            for c in range(4 if velocity else 3):
                acc = [(0.0, 0.0)] * 4
                if velocity and c < 3:
                    got = [[halos(l * 8 + 4 * i + c) for i in range(2)] for l in range(per)]
                    vec = basis_of([(mix(g[0]), mix(g[1])) for g in got])
                    lap = basis_of([(mix_lap(g[0]), mix_lap(g[1])) for g in got])
                    if c == 2:
                        acc = basis_of([(mix(halos(l * 8 + 3)), mix(halos(l * 8 + 7))) for l in range(per)])
                    acc = couple(acc, flow, vec)
                if base and c < 3:
                    bend = entries(mix(halos(n_pert + c)), *[mix(halos(base_modes_at + 3 * i + c)) for i in range(4)])
                    acc = couple(acc, bend, along)
                if c == 3:
                    acc = vec
                if velocity and c < 3:
                    acc = [tuple(turn * a + VISCOSITY * v for a, v in zip(*pair)) for pair in zip(acc, lap)]
                else:
                    acc = [tuple(turn * a for a in pair) for pair in acc]
                for k, parts in enumerate(harmonics_of(acc, 1.0 / 24.0)):
                    for i in range(2):
                        at = k * 8 + 4 * i + c
                        out_ref[at, out_rows] = out_ref[at, out_rows] + parts[i]

            def nb_work(pairs):
                for k in sorted({p[0] for p in pairs}):
                    zero = jnp.zeros((16, ny), f32)
                    for c in range(3):
                        acc = (zero, zero)
                        for _, m, s, f in [p for p in pairs if p[0] == k]:
                            at = (abs(m) - 1) * 6
                            mine = tuple(mode_ref[at + 3 * i + 2, rows].astype(f32) for i in range(2))
                            acc = product(acc, mine, tuple(mix(nb_halos(s, f + 3 * i + c)) for i in range(2)), m)
                            bent = tuple(mix(halos(base_modes_at + at + 3 * i + c)) for i in range(2))
                            carried = tuple(nb_refs[s][f + 3 * i + 2, rows].astype(f32) for i in range(2))
                            acc = product(acc, bent, carried, m)
                        for i in range(2):
                            at = k * 8 + 4 * i + c
                            out_ref[at, out_rows] = out_ref[at, out_rows] + (turn * (1.0 / 12.0)) * acc[i]

            if base:
                on_sides(nb_work)
            return carry

        lax.fori_loop(0, nx // 16, chunk_work, 0)

    def neighbours(mask_ref, pert_ref, mean_ref, mode_ref, xb_ref, xa_ref, whole_ref, first_ref, near_ref, *rest):
        nb_refs = rest[:sides]
        out_any, out_ref, grads, plain, stencil_ref, walls_ref, vecs, lins, bends, sems = rest[-10:]
        row, column = iotas(own, own + 2 * HALO_X)
        to_z, to_x = column_cells(column, nz, nx)
        for i in range(2):
            stencil_ref[i * own : (i + 1) * own] = slope_matrix(i, row >> nx.bit_length() - 1, row & (nx - 1), to_z, to_x).astype(bf16)
        store_walls(walls_ref, ny)

        def slopes(at, mine, halo):
            both = jnp.concatenate(mine, axis=1)
            rows = both if halo is None else jnp.concatenate([both, halo], axis=0)
            got = jnp.dot(stencil_ref[:, : rows.shape[0]], rows, preferred_element_type=f32)
            wall = [jnp.dot(x, walls_ref[:ny, :ny], preferred_element_type=f32) for x in mine]
            for i in range(2):
                lanes = slice(i * ny, (i + 1) * ny)
                grads[at + i, 0] = got[:own, lanes]
                grads[at + i, 2] = got[own:, lanes]
                grads[at + i, 1] = wall[i]
                plain[at + i] = mine[i].astype(f32)

        for f in range(0, n_modes, 2):
            at = base_modes_at + f
            halo = [jnp.concatenate([edge_tile(ref, at), edge_tile(ref, at + 1)], axis=1) for ref in (xb_ref, xa_ref)]
            slopes(f, [mode_ref[f], mode_ref[f + 1]], jnp.concatenate(halo, axis=0))
        for s in range(sides):
            for f in range(0, n_nb, 2):
                slopes(n_modes + s * n_nb + f, [nb_refs[s][f], nb_refs[s][f + 1]], None)

        taps_of = edge_taps((FIRST, SECOND))

        def bent(fields, lap):
            cols = [jnp.concatenate([edge_tile(xb_ref, f), edge_tile(xa_ref, f)], axis=0) for f in fields]
            both = cols[0] if len(cols) == 1 else jnp.concatenate(cols, axis=1)
            got = jnp.dot(taps_of if lap else taps_of[:ends], both, preferred_element_type=f32)
            return [(got[:ends, i * ny : (i + 1) * ny], got[ends:, i * ny : (i + 1) * ny]) for i in range(len(fields))]

        for at, (lo, hi) in enumerate(PAIRS):
            for i in range(2):
                sign = 1.0 if i == 0 else -1.0
                for c in range(4):
                    (gl, ll), (gr, lr) = bent((lo * 8 + 4 * i + c, hi * 8 + 4 * i + c), c < 3)
                    if c < 3:
                        vecs[2 * at, i, c] = gl + gr
                        vecs[2 * at + 1, 1 - i, c] = sign * (gl - gr)
                        lins[2 * at, i, c] = -VISCOSITY * (ll + lr)
                        lins[2 * at + 1, 1 - i, c] = (-VISCOSITY * sign) * (ll - lr)
                    else:
                        lins[2 * at, i, 0] = lins[2 * at, i, 0] + (gl + gr)
                        lins[2 * at + 1, 1 - i, 0] = lins[2 * at + 1, 1 - i, 0] + sign * (gl - gr)
        for c in range(3):
            at = base_modes_at + c
            (t, _), = bent((n_pert + c,), False)
            (p, _), (r, _) = bent((at, at + 6), False)
            (q, _), (s_, _) = bent((at + 3, at + 9), False)
            for n, ent in enumerate(entries(t, p, q, r, s_)):
                bends[c, n] = ent

        for z in range(nz):
            rows = slice(z * nx, (z + 1) * nx)
            solid = PENALTY * mask_ref[rows].astype(f32)
            for f in range(n_pert):
                if f % 4 < 3:
                    out_ref[f, rows] = whole_ref[f, rows] + solid * pert_ref[f, rows].astype(f32)
                else:
                    out_ref[f, rows] = whole_ref[f, rows]

        def layer_ends(z, carry):
            for end in range(2):
                strip = pl.ds(pl.multiple_of(z * nx + end * (nx // 2), 16), 16)
                keep = slice(8 * end, 8 * end + 8)
                rows = pl.ds(pl.multiple_of(z * nx + end * (nx - 8), 8), 8)
                mine = pl.ds(pl.multiple_of((end * nz + z) * 8, 8), 8)

                def read(ref, f):
                    return ref[f, strip].astype(f32)[keep]

                flow = entries(read(mean_ref, 0), *[read(mode_ref, 3 * i) for i in range(4)])
                along = basis_of([(read(pert_ref, l * 8), read(pert_ref, l * 8 + 4)) for l in range(per)])
                for c in range(4):
                    if c < 3:
                        acc = [(lins[j, 0, c, mine], lins[j, 1, c, mine]) for j in range(4)]
                        acc = couple(acc, flow, [(vecs[j, 0, c, mine], vecs[j, 1, c, mine]) for j in range(4)])
                        acc = couple(acc, [bends[c, n, mine] for n in range(8)], along)
                    else:
                        acc = [(vecs[j, 0, 0, mine], vecs[j, 1, 0, mine]) for j in range(4)]
                    for k, parts in enumerate(harmonics_of(acc, 1.0 / 24.0)):
                        for i in range(2):
                            at = k * 8 + 4 * i + c
                            out_ref[at, rows] = out_ref[at, rows] + parts[i]
            return carry

        lax.fori_loop(0, nz, layer_ends, 0)

        def work(pairs):
            def block(b, carry):
                rows = pl.ds(pl.multiple_of(b * 8, 8), 8)
                for k in sorted({p[0] for p in pairs}):
                    zero = jnp.zeros((8, ny), f32)
                    acc = [(zero, zero)] * 3
                    for _, m, s, f in [p for p in pairs if p[0] == k]:
                        at, base = n_modes + s * n_nb + f, (abs(m) - 1) * 6
                        for d in range(3):
                            flow = plain[base + d, rows], plain[base + 3 + d, rows]
                            along = plain[at + d, rows], plain[at + 3 + d, rows]
                            for c in range(3):
                                slope = grads[base + c, d, rows], grads[base + 3 + c, d, rows]
                                grad = grads[at + c, d, rows], grads[at + 3 + c, d, rows]
                                acc[c] = product(acc[c], flow, grad, m)
                                acc[c] = product(acc[c], slope, along, m)
                    for c in range(3):
                        for i in range(2):
                            at = k * 8 + 4 * i + c
                            out_ref[at, rows] = out_ref[at, rows] + acc[c][i] * (1.0 / 12.0)
                return carry

            lax.fori_loop(0, own // 8, block, 0)

        on_sides(work)
        sends = []

        def send(layer):
            rows = pl.ds(pl.multiple_of(layer * nx, nx), nx)
            sends.append(pltpu.make_async_copy(out_ref.at[:, rows], out_any.at[:, rows], sems.at[len(sends)]))
            sends[-1].start()

        for layer in range(2, nz - 2):
            send(layer)
        for step in range(2):
            faces(out_ref, mean_ref, mode_ref, pert_ref, nb_refs, None, None, near_ref, None, step)
            send(face_place(False, step)[1])
        for step in range(2):
            faces(out_ref, mean_ref, mode_ref, pert_ref, nb_refs, first_ref, None, None, None, step)
        for copy in sends:
            copy.wait()

    n_ext = n_modes + sides * n_nb
    with jax.named_scope("neighbours"):
        result, inner = pl.pallas_call(
            neighbours,
            out_shape=(jax.ShapeDtypeStruct((n_pert, own, ny), f32),) * 2,
            out_specs=(HBM, VMEM),
            scratch_shapes=[
                pltpu.VMEM((n_ext, 3, own, ny), f32),
                pltpu.VMEM((n_ext, own, ny), f32),
                pltpu.VMEM((2 * own, own + 2 * HALO_X), bf16),
                pltpu.VMEM((ny, ny), bf16),
                pltpu.VMEM((4, 2, 3, ends, ny), f32),
                pltpu.VMEM((4, 2, 3, ends, ny), f32),
                pltpu.VMEM((3, 8, ends, ny), f32),
                pltpu.SemaphoreType.DMA((nz - 2,)),
            ],
            compiler_params=roomy,
        )(mask, flat(pert), flat(mean), flat(mode), xb_got, xa_got, whole, first_got, near_got, *[flat(b) for b in nb_got])

    n_keys = n_pert // 2 if swap else n_pert

    def finish(pert_ref, mean_ref, mode_ref, inner_ref, second_ref, _, *rest):
        relay_refs, nb_refs = rest[:sides], rest[sides : 2 * sides]
        out_any, done, fringe, bends, sems = rest[2 * sides :]
        half = nx // 2
        keys = jnp.where(lax.axis_index("harm") == 0, n_pert - n_keys, 0) if swap else 0
        inner_layer = jnp.where(face_place(True, 0)[0], 2, 0)
        taps_of = edge_taps((FIRST,))
        sends = []

        def send(src, dst):
            sends.append(pltpu.make_async_copy(src, dst, sems.at[len(sends)]))
            sends[-1].start()

        for s in range(sides):
            for f in range(0, n_nb, 2):
                both = jnp.concatenate([relay_refs[s][f + i, 2 * nx :] for i in range(2)], axis=1)
                got = jnp.dot(taps_of, both, preferred_element_type=f32)
                for i in range(2):
                    bends[s * n_nb + f + i] = got[:, i * ny : (i + 1) * ny]

        def edge_terms(pairs, z, end, add):
            strip = pl.ds(pl.multiple_of(z * nx + end * half, 16), 16)
            keep = slice(8 * end, 8 * end + 8)
            bent = pl.ds(pl.multiple_of((end * nz + z) * 8, 8), 8)
            for k in sorted({p[0] for p in pairs}):
                zero = jnp.zeros((8, ny), f32)
                acc = [(zero, zero)] * 3
                for _, m, s, f in [p for p in pairs if p[0] == k]:
                    base = (abs(m) - 1) * 6
                    flow = tuple(mode_ref[base + 3 * i, strip].astype(f32)[keep] for i in range(2))
                    for c in range(3):
                        at = s * n_nb + f + c
                        acc[c] = product(acc[c], flow, (bends[at, bent], bends[at + 3, bent]), m)
                for c in range(3):
                    for i in range(2):
                        add(k, 4 * i + c, acc[c][i] * (1.0 / 12.0))

        def end_rows(z, end):
            return pl.ds(pl.multiple_of(z * nx + end * (nx - 8), 8), 8)

        first_row = pl.multiple_of(jnp.where(face_place(True, 0)[0], 0, (nz - 2) * nx), nx)
        done[...] = inner_ref[:, pl.ds(first_row, 2 * nx)]
        cross_layer = first_row // nx

        def cross_edges(pairs):
            def at_layer(j, carry):
                for end in range(2):
                    rows = end_rows(j, end)

                    def add(k, part, value):
                        done[k * 8 + part, rows] = done[k * 8 + part, rows] + value

                    edge_terms(pairs, cross_layer + j, end, add)
                return carry

            lax.fori_loop(0, 2, at_layer, 0)

        on_sides(cross_edges)
        for step in range(2):
            faces(done, mean_ref, mode_ref, pert_ref, nb_refs, None, second_ref, None, relay_refs, step, cross_layer)
        send(done, out_any.at[:, pl.ds(first_row, 2 * nx)])

        def other_edges(pairs):
            lowest = min(p[0] for p in pairs) * 8 if swap else 0

            def at_layer(j, carry):
                for end in range(2):

                    def add(k, part, value):
                        at = k * 8 + part - lowest
                        fringe[end, at, j] = fringe[end, at, j] + value

                    edge_terms(pairs, inner_layer + j, end, add)
                return carry

            lax.fori_loop(0, nz - 2, at_layer, 0)

        for j in range(nz - 2):
            for end in range(2):
                fringe[end, :, j] = inner_ref[pl.ds(keys, n_keys), end_rows(inner_layer + j, end)]
        on_sides(other_edges)
        for j in range(nz - 2):
            for end in range(2):
                send(fringe.at[end, :, j], out_any.at[pl.ds(keys, n_keys), end_rows(inner_layer + j, end)])
        for copy in sends:
            copy.wait()

    with jax.named_scope("finish"):
        out = pl.pallas_call(
            finish,
            out_shape=jax.ShapeDtypeStruct((n_pert, own, ny), f32),
            in_specs=[VMEM] * 5 + [HBM] + [VMEM] * (2 * sides),
            out_specs=HBM,
            input_output_aliases={5: 0},
            scratch_shapes=[
                pltpu.VMEM((n_pert, 2 * nx, ny), f32),
                pltpu.VMEM((2, n_keys, nz - 2, 8, ny), f32),
                pltpu.VMEM((sides * n_nb, ends, ny), f32),
                pltpu.SemaphoreType.DMA((1 + 2 * (nz - 2),)),
            ],
            compiler_params=roomy,
        )(
            flat(pert), flat(mean), flat(mode), inner, second_got, result,
            *relay_got, *[flat(b) for b in nb_got],
        )
    return jnp.swapaxes(out.reshape(per, 2, 4, nz, nx, ny), 3, 4)


def solution(mesh):
    return jax.shard_map(
        shards,
        mesh=mesh,
        in_specs=(
            P("harm", None, None, "gx", "gz", None),
            P(None, "gx", "gz", None),
            P(None, None, None, "gx", "gz", None),
            P("gx", "gz", None),
        ),
        out_specs=P("harm", None, None, "gx", "gz", None),
        check_vma=False,
    )
```

```python
import jax
import jax.numpy as jnp
from jax import lax
from jax.experimental import pallas as pl
from jax.experimental.pallas import tpu as pltpu
from jax.sharding import PartitionSpec as P

FREQUENCY_STEP = 0.2
VISCOSITY = 0.05
PENALTY = 4.0
FIRST = {-2: 1.0, -1: -8.0, 1: 8.0, 2: -1.0}
SECOND = {-2: -1.0, -1: 16.0, 0: -30.0, 1: 16.0, 2: -1.0}
HALO_X = 16
VMEM_BYTES = 58 * 1024 * 1024
ANY = pl.BlockSpec(memory_space=pl.ANY)
VMEM = pl.BlockSpec(memory_space=pltpu.VMEM)
HBM = pl.BlockSpec(memory_space=pltpu.HBM)


def taps(delta, table):
    out = jnp.zeros(delta.shape, jnp.float32)
    for step, weight in table.items():
        out = jnp.where(delta == step, weight, out)
    return out


def iotas(rows, columns):
    return lax.broadcasted_iota(jnp.int32, (rows, 1), 0), lax.broadcasted_iota(jnp.int32, (1, columns), 1)


def column_cells(column, nz, nx):
    shift, own = nx.bit_length() - 1, nz * nx
    halo = column - own
    after = halo >= HALO_X
    edge = jnp.where(after, halo - HALO_X, halo)
    inside = column < own
    z = jnp.where(inside, column >> shift, edge >> 1)
    x = jnp.where(inside, column & (nx - 1), (edge & 1) + jnp.where(after, nx, -2))
    return z, x


def slope_matrix(part, z, x, to_z, to_x):
    dz, dx = to_z - z, to_x - x
    if part == 0:
        return jnp.where(dz == 0, taps(dx, FIRST), 0.0)
    if part == 1:
        return jnp.where(dx == 0, taps(dz, FIRST), 0.0)
    return jnp.where(dz == 0, taps(dx, SECOND), 0.0) + jnp.where(dx == 0, taps(dz, SECOND), 0.0)


def store_walls(walls_ref, ny):
    row, column = iotas(ny, ny)
    first, second = (taps(row - column, table).astype(jnp.bfloat16) for table in (FIRST, SECOND))
    for i, (block, sign) in enumerate(((first, 1), (first, -1), (second, 1), (second, -1))):
        if i * ny < walls_ref.shape[1]:
            walls_ref[:ny, i * ny : (i + 1) * ny] = block
            if walls_ref.shape[0] > ny:
                walls_ref[ny:, i * ny : (i + 1) * ny] = block if sign > 0 else -block


def run_copies(copies, sems):
    started = [pltpu.make_async_copy(src, dst, sems.at[i]) for i, (src, dst) in enumerate(copies)]
    for copy in started:
        copy.start()
    for copy in started:
        copy.wait()


def shards(perturbation, base_mean, base_modes, solid_mask):
    per, modes = perturbation.shape[0], base_modes.shape[0]
    nx, nz, ny = perturbation.shape[3], perturbation.shape[4], perturbation.shape[5]
    own = nz * nx
    bf16, f32 = jnp.bfloat16, jnp.float32
    harms, size_x, size_z = (lax.axis_size(a) for a in ("harm", "gx", "gz"))
    swap = harms == 2
    sides = 1 if swap else 2
    n_pert, n_mean, n_modes = per * 8, 3, modes * 6
    n_base = n_mean + n_modes
    n_res = n_pert + n_base
    n_nb = modes * 6
    n_all = n_res + sides * n_nb

    pert = jnp.swapaxes(perturbation, 3, 4).reshape(n_pert, nz, nx, ny)
    mean = jnp.swapaxes(base_mean, 1, 2)
    mode = jnp.swapaxes(base_modes, 3, 4).reshape(n_modes, nz, nx, ny)
    mask = jnp.swapaxes(solid_mask, 0, 1).reshape(own, ny)

    def place():
        me_h, odd = lax.axis_index("harm"), lax.rem(lax.axis_index("gz"), 2)
        shared = jnp.where(me_h == 0, per - modes, 0) if swap else 0
        return me_h, odd, odd * (nz - 2), (1 - odd) * (nz - 2), shared

    cross_pairs = [(i, (i + 1) % size_z if i % 2 else (i - 1) % size_z) for i in range(size_z)]
    near_pairs = [(i, i + 1 if i % 2 == 0 else i - 1) for i in range(size_z)]
    up_x = [(i, (i + 1) % size_x) for i in range(size_x)]
    down_x = [(j, i) for i, j in up_x]
    if swap:
        harm_perms = [[(0, 1), (1, 0)]]
    else:
        up_h = [(i, i + 1) for i in range(harms - 1)]
        harm_perms = [up_h, [(j, i) for i, j in up_h]]
    def sent(s, scal):
        return scal[4] if swap else (per - modes if s == 0 else 0)

    face = lambda n: jax.ShapeDtypeStruct((n, 2, nx, ny), bf16)
    roomy = pltpu.CompilerParams(vmem_limit_bytes=32 * 1024 * 1024)

    used = 2 * nz
    spare = HALO_X - used
    tiles = 3 * (-(-n_res // 4))

    def edge_tile(ref, f):
        group, i = divmod(f, 4)
        if i < 3:
            return ref[3 * group + i]
        parts = [ref[3 * group + j].astype(f32)[used:] for j in range(3)]
        return jnp.concatenate(parts + [jnp.zeros((spare, ny), f32)], axis=0).astype(bf16)

    def pack(pert_any, mean_any, mode_any, first_any, second_any, lo_any, hi_any, *rest):
        nb_anys = rest[:sides]
        pert_ref, mean_ref, mode_ref, lo_ref, hi_ref, in_sems, out_sems = rest[sides:]
        scal = place()
        z = pl.ds(scal[2], 2)
        loads = [(pert_any.at[pl.ds(8 * l, 8)], pert_ref.at[pl.ds(8 * l, 8)]) for l in range(per)]
        loads += [(mean_any, mean_ref), (mode_any, mode_ref)]
        loads = [pltpu.make_async_copy(src, dst, in_sems.at[i]) for i, (src, dst) in enumerate(loads)]
        for copy in loads:
            copy.start()
        out = []

        def send(src, dst):
            out.append(pltpu.make_async_copy(src, dst, out_sems.at[len(out)]))
            out[-1].start()

        row, column = iotas(2 * HALO_X, own)
        low = row < HALO_X
        row = jnp.where(low, row, row - HALO_X)
        target = (row >> 1) * nx + (row & 1) + jnp.where(low, 0, nx - 2)
        pick = jnp.where(column == target, 1.0, 0.0).astype(bf16)
        where = [(pert_ref, f) for f in range(n_pert)] + [(mean_ref, f) for f in range(n_mean)] + [(mode_ref, f) for f in range(n_modes)]

        def edges(group):
            got = []
            for f in range(4 * group, min(4 * group + 4, n_res), 2):
                mine = [ref[i].reshape(own, ny) for ref, i in where[f : min(f + 2, n_res)]]
                both = jnp.concatenate(mine, axis=1) if len(mine) == 2 else mine[0]
                both = jnp.dot(pick, both, preferred_element_type=f32)
                got += [both[:, i * ny : (i + 1) * ny] for i in range(len(mine))]
            if len(got) == 3:
                got.append(jnp.zeros((2 * HALO_X, ny), f32))
            for i in range(3):
                for ref, at in ((lo_ref, 0), (hi_ref, HALO_X)):
                    extra = got[3][at + spare * i : at + spare * (i + 1)]
                    ref[3 * group + i] = jnp.concatenate([got[i][at : at + used], extra], axis=0).astype(bf16)

        for l in range(per):
            loads[l].wait()
            mine = pl.ds(8 * l, 8)
            send(pert_ref.at[mine, z], first_any.at[mine])
        for s, nb_any in enumerate(nb_anys):
            for i in range(modes * 2):
                send(pert_ref.at[pl.ds(sent(s, scal) * 8 + 4 * i, 3)], nb_any.at[pl.ds(3 * i, 3)])
        for group in range(n_pert // 4):
            edges(group)
        loads[per].wait()
        loads[per + 1].wait()
        send(mean_ref.at[:, z], second_any.at[pl.ds(0, n_mean)])
        send(mode_ref.at[:, z], second_any.at[pl.ds(n_mean, n_modes)])
        for group in range(n_pert // 4, tiles // 3):
            edges(group)
        send(lo_ref, lo_any)
        send(hi_ref, hi_any)
        for copy in out:
            copy.wait()

    edge = jax.ShapeDtypeStruct((tiles, HALO_X, ny), bf16)
    with jax.named_scope("pack"):
        first, second, edge_lo, edge_hi, *nb_send = pl.pallas_call(
            pack,
            out_shape=(face(n_pert), face(n_base), edge, edge) + tuple(jax.ShapeDtypeStruct((n_nb, nz, nx, ny), bf16) for _ in range(sides)),
            in_specs=[HBM] * 3,
            out_specs=(ANY,) * (4 + sides),
            scratch_shapes=[
                pltpu.VMEM((n_pert, nz, nx, ny), bf16),
                pltpu.VMEM((n_mean, nz, nx, ny), bf16),
                pltpu.VMEM((n_modes, nz, nx, ny), bf16),
                pltpu.VMEM((tiles, HALO_X, ny), bf16),
                pltpu.VMEM((tiles, HALO_X, ny), bf16),
                pltpu.SemaphoreType.DMA((per + 2,)),
                pltpu.SemaphoreType.DMA((per + sides * modes * 2 + 4,)),
            ],
            compiler_params=pltpu.CompilerParams(vmem_limit_bytes=VMEM_BYTES),
        )(pert, mean, mode)
    first_got = lax.ppermute(first, "gz", cross_pairs)
    nb_got = [lax.ppermute(b, "harm", p) for b, p in zip(nb_send, harm_perms)]
    xb_got = lax.ppermute(edge_hi, "gx", up_x)
    xa_got = lax.ppermute(edge_lo, "gx", down_x)
    second_got = lax.ppermute(second, "gz", cross_pairs)

    PAIRS = ((0, 3), (1, 2))
    DRIFT = (-1.5 * FREQUENCY_STEP, -0.5 * FREQUENCY_STEP)

    def entries(t, p, q, r, s):
        return t, q, p + r, p - r, q + s, s - q, t + p, t - p

    def couple(acc, ent, vec):
        t, q, pr, pmr, qs, sq, tp, tmp = ent
        out = []
        for i in range(2):
            a, e, b, g = (vec[j][i] for j in range(4))
            out.append(
                (
                    acc[0][i] + t * a + pr * b + sq * g,
                    acc[1][i] + t * e + qs * b + pmr * g,
                    acc[2][i] + pr * a + qs * e + tp * b + q * g,
                    acc[3][i] + sq * a + pmr * e + q * b + tmp * g,
                )
            )
        return [(out[0][j], out[1][j]) for j in range(4)]

    def harmonics_of(acc, scale):
        out = [None] * 4
        for at, (lo, hi) in enumerate(PAIRS):
            (ar, ai), (er, ei) = acc[2 * at], acc[2 * at + 1]
            out[lo] = ((ar + ei) * scale, (ai - er) * scale)
            out[hi] = ((ar - ei) * scale, (ai + er) * scale)
        return out

    def basis_of(values):
        out = []
        for lo, hi in PAIRS:
            (lr, li), (hr, hi_) = values[lo], values[hi]
            out += [(lr + hr, li + hi_), (hi_ - li, lr - hr)]
        return out

    def rhs(ref, fields):
        cols = [ref[f] for f in fields]
        return cols[0] if len(cols) == 1 else jnp.concatenate(cols, axis=1)

    def dot(a, b):
        return jnp.dot(a, b, preferred_element_type=f32)

    def resident_slopes(pert_ref, grads, plain, lin, rows_ref, walls_ref):
        me_h = place()[0]
        row, column = iotas(own, own)
        to_z, to_x = column_cells(column, nz, nx)
        for i in range(3):
            rows_ref[i * own : (i + 1) * own] = slope_matrix(i, row >> nx.bit_length() - 1, row & (nx - 1), to_z, to_x).astype(bf16)
        store_walls(walls_ref, ny)
        mean_freq = 12.0 * FREQUENCY_STEP * (me_h * per + 1.5 - per * harms / 2).astype(f32)

        for at, (lo, hi) in enumerate(PAIRS):
            for i in range(2):
                fl, fr = lo * 8 + i * 4 + 3, hi * 8 + i * 4 + 3
                got = dot(rows_ref[: 2 * own], rhs(pert_ref, (fl, fr)))
                wall = dot(rhs(pert_ref, (fl, fr)), walls_ref[:, : 2 * ny])
                for d in range(3):
                    if d == 1:
                        total, diff = wall[:, :ny], wall[:, ny:]
                    else:
                        span = slice(0, own) if d == 0 else slice(own, 2 * own)
                        total, diff = got[span, :ny] + got[span, ny:], got[span, :ny] - got[span, ny:]
                    lin[2 * at, i, d] = total
                    lin[2 * at + 1, 1 - i, d] = diff if i == 0 else -diff
        for at, (lo, hi) in enumerate(PAIRS):
            for c in range(3):
                for i in range(2):
                    sign = 1.0 if i == 0 else -1.0
                    fl, fr = lo * 8 + i * 4 + c, hi * 8 + i * 4 + c
                    got = dot(rows_ref[...], rhs(pert_ref, (fl, fr)))
                    xl, xr = pert_ref[fl].astype(f32), pert_ref[fr].astype(f32)
                    wall = dot(rhs(pert_ref, (fl, fr)), walls_ref[...])
                    total, diff = xl + xr, xl - xr
                    plain[2 * at, i, c] = total
                    plain[2 * at + 1, 1 - i, c] = sign * diff
                    for d in range(3):
                        if d == 1:
                            gt, gd = wall[:, :ny], wall[:, ny : 2 * ny]
                        else:
                            span = slice(0, own) if d == 0 else slice(own, 2 * own)
                            gt, gd = got[span, :ny] + got[span, ny:], got[span, :ny] - got[span, ny:]
                        gd = sign * gd
                        grads[2 * at, i, c, d] = gt
                        grads[2 * at + 1, 1 - i, c, d] = gd
                        if d == c:
                            if c == 0:
                                lin[2 * at, i, 3] = gt
                                lin[2 * at + 1, 1 - i, 3] = gd
                            else:
                                lin[2 * at, i, 3] = lin[2 * at, i, 3] + gt
                                lin[2 * at + 1, 1 - i, 3] = lin[2 * at + 1, 1 - i, 3] + gd
                    lt = got[2 * own :, :ny] + got[2 * own :, ny:] + wall[:, 2 * ny : 3 * ny]
                    ld = got[2 * own :, :ny] - got[2 * own :, ny:] + wall[:, 3 * ny :]
                    drift = 12.0 * DRIFT[at]
                    lin[2 * at, i, c] = lin[2 * at, i, c] - VISCOSITY * lt
                    lin[2 * at + 1, 1 - i, c] = lin[2 * at + 1, 1 - i, c] - sign * VISCOSITY * ld
                    lin[2 * at, 1 - i, c] = lin[2 * at, 1 - i, c] + sign * (mean_freq * total + drift * diff)
                    lin[2 * at + 1, i, c] = lin[2 * at + 1, i, c] - (mean_freq * diff + drift * total)

    def resident(mean_ref, mode_ref, grads, plain, lin, out_ref, ents, rows_ref, walls_ref):
        row, column = iotas(own, own)
        to_z, to_x = column_cells(column, nz, nx)
        for i in range(2):
            rows_ref[i * own : (i + 1) * own] = slope_matrix(i, row >> nx.bit_length() - 1, row & (nx - 1), to_z, to_x).astype(bf16)
        store_walls(walls_ref, ny)
        for c in range(3):
            picked = [mean_ref[c].astype(f32)] + [mode_ref[3 * i + c].astype(f32) for i in range(4)]
            for n, ent in enumerate(entries(*picked)):
                ents[c, n] = ent
            mean_at = dot(rows_ref[...], rhs(mean_ref, (c,)))
            mean_wall = dot(mean_ref[c], walls_ref[:ny, :ny])
            real = dot(rows_ref[...], rhs(mode_ref, (c, 6 + c)))
            imag = dot(rows_ref[...], rhs(mode_ref, (3 + c, 9 + c)))
            wall_real = dot(rhs(mode_ref, (c, 6 + c)), walls_ref[:, : 2 * ny])
            wall_imag = dot(rhs(mode_ref, (3 + c, 9 + c)), walls_ref[:, : 2 * ny])
            for d in range(3):
                if d == 1:
                    pr, pmr = wall_real[:, :ny], wall_real[:, ny:]
                    qs, qms = wall_imag[:, :ny], wall_imag[:, ny:]
                    t, p, q = mean_wall, 0.5 * (pr + pmr), 0.5 * (qs + qms)
                    values = (t, q, pr, pmr, qs, -qms, t + p, t - p)
                else:
                    span = slice(0, own) if d == 0 else slice(own, 2 * own)
                    values = entries(mean_at[span], real[span, :ny], imag[span, :ny], real[span, ny:], imag[span, ny:])
                for n, ent in enumerate(values):
                    ents[3 + 3 * d + c, n] = ent

        def block(b, carry):
            rows = pl.ds(pl.multiple_of(b * 8, 8), 8)
            accs = [[(lin[j, 0, c, rows], lin[j, 1, c, rows]) for j in range(4)] for c in range(4)]
            for d in range(3):
                flow = [ents[d, n, rows] for n in range(8)]
                for c in range(3):
                    accs[c] = couple(accs[c], flow, [(grads[j, 0, c, d, rows], grads[j, 1, c, d, rows]) for j in range(4)])
                along = [(plain[j, 0, d, rows], plain[j, 1, d, rows]) for j in range(4)]
                for c in range(3):
                    slope = [ents[3 + 3 * d + c, n, rows] for n in range(8)]
                    accs[c] = couple(accs[c], slope, along)
            for c in range(4):
                for k, (re, im) in enumerate(harmonics_of(accs[c], 1.0 / 24.0)):
                    out_ref[k * 8 + c, rows] = re
                    out_ref[k * 8 + 4 + c, rows] = im
            return carry

        lax.fori_loop(0, own // 8, block, 0, unroll=2)

    flat = lambda a: a.reshape(a.shape[0], -1, ny)
    with jax.named_scope("resident_slopes"):
        slopes = pl.pallas_call(
            resident_slopes,
            out_shape=tuple(jax.ShapeDtypeStruct(n + (own, ny), f32) for n in ((4, 2, 3, 3), (4, 2, 3), (4, 2, 4))),
            scratch_shapes=[pltpu.VMEM((3 * own, own), bf16), pltpu.VMEM((2 * ny, 4 * ny), bf16)],
            compiler_params=pltpu.CompilerParams(vmem_limit_bytes=20 * 1024 * 1024),
        )(flat(pert))
    with jax.named_scope("resident"):
        whole = pl.pallas_call(
            resident,
            out_shape=jax.ShapeDtypeStruct((n_pert, own, ny), f32),
            scratch_shapes=[
                pltpu.VMEM((12, 8, own, ny), f32),
                pltpu.VMEM((2 * own, own), bf16),
                pltpu.VMEM((2 * ny, 2 * ny), bf16),
            ],
            compiler_params=roomy,
        )(flat(mean), flat(mode), *slopes)

    base_modes_at = n_pert + n_mean
    ends = 16 * nz

    def edge_taps(tables):
        row, column = iotas(ends, own + 2 * HALO_X)
        last = row >= 8 * nz
        row = jnp.where(last, row - 8 * nz, row)
        to_z, to_x = column_cells(column, nz, nx)
        dz, dx = to_z - (row >> 3), to_x - (row & 7) - jnp.where(last, nx - 8, 0)
        return jnp.concatenate([jnp.where(dz == 0, taps(dx, table), 0.0)[:, own:] for table in tables], axis=0).astype(bf16)

    def add_edges(mask_ref, pert_ref, mean_ref, mode_ref, xb_ref, xa_ref, whole_ref, out_ref, vecs, lins, bends):
        taps_of = edge_taps((FIRST, SECOND))

        def bent(fields, lap):
            cols = [jnp.concatenate([edge_tile(xb_ref, f), edge_tile(xa_ref, f)], axis=0) for f in fields]
            both = cols[0] if len(cols) == 1 else jnp.concatenate(cols, axis=1)
            got = jnp.dot(taps_of if lap else taps_of[:ends], both, preferred_element_type=f32)
            return [(got[:ends, i * ny : (i + 1) * ny], got[ends:, i * ny : (i + 1) * ny]) for i in range(len(fields))]

        for at, (lo, hi) in enumerate(PAIRS):
            for i in range(2):
                sign = 1.0 if i == 0 else -1.0
                for c in range(4):
                    (gl, ll), (gr, lr) = bent((lo * 8 + 4 * i + c, hi * 8 + 4 * i + c), c < 3)
                    if c < 3:
                        vecs[2 * at, i, c] = gl + gr
                        vecs[2 * at + 1, 1 - i, c] = sign * (gl - gr)
                        lins[2 * at, i, c] = -VISCOSITY * (ll + lr)
                        lins[2 * at + 1, 1 - i, c] = (-VISCOSITY * sign) * (ll - lr)
                    else:
                        lins[2 * at, i, 0] = lins[2 * at, i, 0] + (gl + gr)
                        lins[2 * at + 1, 1 - i, 0] = lins[2 * at + 1, 1 - i, 0] + sign * (gl - gr)
        for c in range(3):
            at = base_modes_at + c
            (t, _), = bent((n_pert + c,), False)
            (p, _), (r, _) = bent((at, at + 6), False)
            (q, _), (s_, _) = bent((at + 3, at + 9), False)
            for n, ent in enumerate(entries(t, p, q, r, s_)):
                bends[c, n] = ent

        for z in range(nz):
            rows = slice(z * nx, (z + 1) * nx)
            solid = PENALTY * mask_ref[rows].astype(f32)
            for f in range(n_pert):
                if f % 4 < 3:
                    out_ref[f, rows] = whole_ref[f, rows] + solid * pert_ref[f, rows].astype(f32)
                else:
                    out_ref[f, rows] = whole_ref[f, rows]

        def layer_ends(z, carry):
            for end in range(2):
                strip = pl.ds(pl.multiple_of(z * nx + end * (nx // 2), 16), 16)
                keep = slice(8 * end, 8 * end + 8)
                rows = pl.ds(pl.multiple_of(z * nx + end * (nx - 8), 8), 8)
                mine = pl.ds(pl.multiple_of((end * nz + z) * 8, 8), 8)

                def read(ref, f):
                    return ref[f, strip].astype(f32)[keep]

                flow = entries(read(mean_ref, 0), *[read(mode_ref, 3 * i) for i in range(4)])
                along = basis_of([(read(pert_ref, l * 8), read(pert_ref, l * 8 + 4)) for l in range(per)])
                for c in range(4):
                    if c < 3:
                        acc = [(lins[j, 0, c, mine], lins[j, 1, c, mine]) for j in range(4)]
                        acc = couple(acc, flow, [(vecs[j, 0, c, mine], vecs[j, 1, c, mine]) for j in range(4)])
                        acc = couple(acc, [bends[c, n, mine] for n in range(8)], along)
                    else:
                        acc = [(vecs[j, 0, 0, mine], vecs[j, 1, 0, mine]) for j in range(4)]
                    for k, parts in enumerate(harmonics_of(acc, 1.0 / 24.0)):
                        for i in range(2):
                            at = k * 8 + 4 * i + c
                            out_ref[at, rows] = out_ref[at, rows] + parts[i]
            return carry

        lax.fori_loop(0, nz, layer_ends, 0)

    with jax.named_scope("edges"):
        edged = pl.pallas_call(
            add_edges,
            out_shape=jax.ShapeDtypeStruct((n_pert, own, ny), f32),
            scratch_shapes=[
                pltpu.VMEM((4, 2, 3, ends, ny), f32),
                pltpu.VMEM((4, 2, 3, ends, ny), f32),
                pltpu.VMEM((3, 8, ends, ny), f32),
            ],
            compiler_params=roomy,
        )(mask, flat(pert), flat(mean), flat(mode), xb_got, xa_got, whole)

    faces_deep = n_nb * 2 * nx
    nb_tiles = 3 * n_nb // 4
    deep = faces_deep + 2 * nb_tiles * HALO_X

    def nb_tile(ref, after, f):
        group, i = divmod(f, 4)
        at = [faces_deep + (after * nb_tiles + 3 * group + j) * HALO_X for j in range(3)]
        if i < 3:
            return ref[at[i] : at[i] + HALO_X]
        parts = [ref[row : row + HALO_X].astype(f32)[used:] for row in at]
        return jnp.concatenate(parts + [jnp.zeros((spare, ny), f32)], axis=0).astype(bf16)

    def pack_relay(first_ref, xb_ref, xa_ref, _, *outs):
        scal = place()
        for s, out in enumerate(outs):
            for i in range(modes * 2):
                group = sent(s, scal) * 2 + i
                for c in range(3):
                    at = (3 * i + c) * 2 * nx
                    out[at : at + 2 * nx] = first_ref[group * 4 + c].reshape(2 * nx, ny)
            for after, ref in enumerate((xb_ref, xa_ref)):
                for group in range(n_nb // 4):
                    rows = []
                    for f in range(4 * group, 4 * group + 4):
                        rows.append(ref[(sent(s, scal) * 2 + f // 3) * 3 + f % 3].astype(f32))
                    for i in range(3):
                        at = faces_deep + (after * nb_tiles + 3 * group + i) * HALO_X
                        tile = jnp.concatenate([rows[i][:used], rows[3][spare * i : spare * (i + 1)]], axis=0)
                        out[at : at + HALO_X] = tile.astype(bf16)

    with jax.named_scope("pack_relay"):
        relay = pl.pallas_call(
            pack_relay,
            out_shape=tuple(jax.ShapeDtypeStruct((deep, ny), bf16) for _ in range(sides)),
            in_specs=[VMEM] * 3 + [ANY],
            compiler_params=roomy,
        )(first_got, xb_got, xa_got, edged)
    relay_got = [lax.ppermute(b, "harm", p) for b, p in zip(relay, harm_perms)]

    def pack_near(pert_ref, mean_ref, mode_ref, *rest):
        out = rest[-1]
        z = pl.ds(place()[3], 2)
        out[:n_pert] = pert_ref[:, z]
        out[n_pert : n_pert + n_mean] = mean_ref[:, z]
        out[n_pert + n_mean : n_res] = mode_ref[:, z]
        for s in range(sides):
            out[n_res + s * n_nb : n_res + (s + 1) * n_nb] = rest[s][:, z]

    with jax.named_scope("pack_near"):
        near = pl.pallas_call(
            pack_near,
            out_shape=face(n_all),
            in_specs=[VMEM] * (3 + sides) + [ANY],
            compiler_params=roomy,
        )(pert, mean, mode, *nb_got, relay[0])
    near_got = lax.ppermute(near, "gz", near_pairs)

    below, above = [], []
    for k in range(per):
        for m in range(-modes, modes + 1):
            l = k - m
            if l < 0:
                below.append((k, m, 0, (l + modes) * 6))
            elif l >= per:
                above.append((k, m, sides - 1, (l - per) * 6))

    def on_sides(work):
        me_h = lax.axis_index("harm")
        pl.when(me_h > 0)(lambda: work(below))
        pl.when(me_h < harms - 1)(lambda: work(above))

    def product(acc, flow, value, m):
        (fr, fi), (vr, vi) = flow, value
        if m > 0:
            return acc[0] + fr * vr - fi * vi, acc[1] + fr * vi + fi * vr
        return acc[0] + fr * vr + fi * vi, acc[1] + fr * vi - fi * vr


    def face_place(cross, step):
        odd = place()[1]
        before = (odd == 0) if cross else (odd == 1)
        return before, jnp.where(before, step, nz - 1 - step), jnp.where(before, 1, 0)

    def faces(out_ref, mean_ref, mode_ref, pert_ref, nb_refs, first_ref, second_ref, near_ref, relay_refs, step, lowest=0):
        cross = near_ref is None
        before, layer, near_at = face_place(cross, step)
        turn = jnp.where(before, 1.0, -1.0)

        def mix(pair):
            return pair[1] - 8.0 * pair[0] if step == 0 else pair[0]

        def mix_lap(pair):
            return pair[1] - 16.0 * pair[0] if step == 0 else pair[0]

        def chunk_work(chunk, carry):
            rows = pl.ds(pl.multiple_of(layer * nx + chunk * 16, 16), 16)
            out_rows = pl.ds(pl.multiple_of((layer - lowest) * nx + chunk * 16, 16), 16)
            strip = pl.ds(pl.multiple_of(chunk * 16, 16), 16)

            def halos(f):
                if not cross:
                    ref, at = near_ref, f
                elif f < n_pert:
                    ref, at = first_ref, f
                else:
                    ref, at = second_ref, f - n_pert
                return ref[at, near_at, strip].astype(f32), (ref[at, 1 - near_at, strip].astype(f32) if step == 0 else None)

            def nb_halos(s, f):
                if not cross:
                    return halos(n_res + s * n_nb + f)
                at = [pl.ds(pl.multiple_of((2 * f + j) * nx + chunk * 16, 16), 16) for j in (near_at, 1 - near_at)]
                return tuple(relay_refs[s][r].astype(f32) for r in at)

            velocity, base = first_ref is not None or not cross, second_ref is not None or not cross
            if velocity:
                flow = entries(mean_ref[2, rows].astype(f32), *[mode_ref[3 * i + 2, rows].astype(f32) for i in range(4)])
            if base:
                along = basis_of([(pert_ref[l * 8 + 2, rows].astype(f32), pert_ref[l * 8 + 6, rows].astype(f32)) for l in range(per)])
            for c in range(4 if velocity else 3):
                acc = [(0.0, 0.0)] * 4
                if velocity and c < 3:
                    got = [[halos(l * 8 + 4 * i + c) for i in range(2)] for l in range(per)]
                    vec = basis_of([(mix(g[0]), mix(g[1])) for g in got])
                    lap = basis_of([(mix_lap(g[0]), mix_lap(g[1])) for g in got])
                    if c == 2:
                        acc = basis_of([(mix(halos(l * 8 + 3)), mix(halos(l * 8 + 7))) for l in range(per)])
                    acc = couple(acc, flow, vec)
                if base and c < 3:
                    bend = entries(mix(halos(n_pert + c)), *[mix(halos(base_modes_at + 3 * i + c)) for i in range(4)])
                    acc = couple(acc, bend, along)
                if c == 3:
                    acc = vec
                if velocity and c < 3:
                    acc = [tuple(turn * a + VISCOSITY * v for a, v in zip(*pair)) for pair in zip(acc, lap)]
                else:
                    acc = [tuple(turn * a for a in pair) for pair in acc]
                for k, parts in enumerate(harmonics_of(acc, 1.0 / 24.0)):
                    for i in range(2):
                        at = k * 8 + 4 * i + c
                        out_ref[at, out_rows] = out_ref[at, out_rows] + parts[i]

            def nb_work(pairs):
                for k in sorted({p[0] for p in pairs}):
                    zero = jnp.zeros((16, ny), f32)
                    for c in range(3):
                        acc = (zero, zero)
                        for _, m, s, f in [p for p in pairs if p[0] == k]:
                            at = (abs(m) - 1) * 6
                            mine = tuple(mode_ref[at + 3 * i + 2, rows].astype(f32) for i in range(2))
                            acc = product(acc, mine, tuple(mix(nb_halos(s, f + 3 * i + c)) for i in range(2)), m)
                            bent = tuple(mix(halos(base_modes_at + at + 3 * i + c)) for i in range(2))
                            carried = tuple(nb_refs[s][f + 3 * i + 2, rows].astype(f32) for i in range(2))
                            acc = product(acc, bent, carried, m)
                        for i in range(2):
                            at = k * 8 + 4 * i + c
                            out_ref[at, out_rows] = out_ref[at, out_rows] + (turn * (1.0 / 12.0)) * acc[i]

            if base:
                on_sides(nb_work)
            return carry

        lax.fori_loop(0, nx // 16, chunk_work, 0)

    def neighbours(pert_ref, mean_ref, mode_ref, xb_ref, xa_ref, edged_ref, first_ref, near_ref, *rest):
        nb_refs = rest[:sides]
        out_any, out_ref, grads, plain, stencil_ref, walls_ref, sems = rest[-7:]
        row, column = iotas(own, own + 2 * HALO_X)
        to_z, to_x = column_cells(column, nz, nx)
        for i in range(2):
            stencil_ref[i * own : (i + 1) * own] = slope_matrix(i, row >> nx.bit_length() - 1, row & (nx - 1), to_z, to_x).astype(bf16)
        store_walls(walls_ref, ny)

        def slopes(at, mine, halo):
            both = jnp.concatenate(mine, axis=1)
            rows = both if halo is None else jnp.concatenate([both, halo], axis=0)
            got = jnp.dot(stencil_ref[:, : rows.shape[0]], rows, preferred_element_type=f32)
            wall = [jnp.dot(x, walls_ref[:ny, :ny], preferred_element_type=f32) for x in mine]
            for i in range(2):
                lanes = slice(i * ny, (i + 1) * ny)
                grads[at + i, 0] = got[:own, lanes]
                grads[at + i, 2] = got[own:, lanes]
                grads[at + i, 1] = wall[i]
                plain[at + i] = mine[i].astype(f32)

        for f in range(0, n_modes, 2):
            at = base_modes_at + f
            halo = [jnp.concatenate([edge_tile(ref, at), edge_tile(ref, at + 1)], axis=1) for ref in (xb_ref, xa_ref)]
            slopes(f, [mode_ref[f], mode_ref[f + 1]], jnp.concatenate(halo, axis=0))
        for s in range(sides):
            for f in range(0, n_nb, 2):
                slopes(n_modes + s * n_nb + f, [nb_refs[s][f], nb_refs[s][f + 1]], None)

        out_ref[...] = edged_ref[...]

        def work(pairs):
            def block(b, carry):
                rows = pl.ds(pl.multiple_of(b * 8, 8), 8)
                for k in sorted({p[0] for p in pairs}):
                    zero = jnp.zeros((8, ny), f32)
                    acc = [(zero, zero)] * 3
                    for _, m, s, f in [p for p in pairs if p[0] == k]:
                        at, base = n_modes + s * n_nb + f, (abs(m) - 1) * 6
                        for d in range(3):
                            flow = plain[base + d, rows], plain[base + 3 + d, rows]
                            along = plain[at + d, rows], plain[at + 3 + d, rows]
                            for c in range(3):
                                slope = grads[base + c, d, rows], grads[base + 3 + c, d, rows]
                                grad = grads[at + c, d, rows], grads[at + 3 + c, d, rows]
                                acc[c] = product(acc[c], flow, grad, m)
                                acc[c] = product(acc[c], slope, along, m)
                    for c in range(3):
                        for i in range(2):
                            at = k * 8 + 4 * i + c
                            out_ref[at, rows] = out_ref[at, rows] + acc[c][i] * (1.0 / 12.0)
                return carry

            lax.fori_loop(0, own // 8, block, 0)

        on_sides(work)
        sends = []

        def send(layer):
            rows = pl.ds(pl.multiple_of(layer * nx, nx), nx)
            sends.append(pltpu.make_async_copy(out_ref.at[:, rows], out_any.at[:, rows], sems.at[len(sends)]))
            sends[-1].start()

        for layer in range(2, nz - 2):
            send(layer)
        for step in range(2):
            faces(out_ref, mean_ref, mode_ref, pert_ref, nb_refs, None, None, near_ref, None, step)
            send(face_place(False, step)[1])
        for step in range(2):
            faces(out_ref, mean_ref, mode_ref, pert_ref, nb_refs, first_ref, None, None, None, step)
        for copy in sends:
            copy.wait()

    n_ext = n_modes + sides * n_nb
    with jax.named_scope("neighbours"):
        result, inner = pl.pallas_call(
            neighbours,
            out_shape=(jax.ShapeDtypeStruct((n_pert, own, ny), f32),) * 2,
            out_specs=(HBM, VMEM),
            scratch_shapes=[
                pltpu.VMEM((n_ext, 3, own, ny), f32),
                pltpu.VMEM((n_ext, own, ny), f32),
                pltpu.VMEM((2 * own, own + 2 * HALO_X), bf16),
                pltpu.VMEM((ny, ny), bf16),
                pltpu.SemaphoreType.DMA((nz - 2,)),
            ],
            compiler_params=roomy,
        )(flat(pert), flat(mean), flat(mode), xb_got, xa_got, edged, first_got, near_got, *[flat(b) for b in nb_got])

    n_keys = n_pert // 2 if swap else n_pert

    def finish(pert_ref, mean_ref, mode_ref, inner_ref, second_ref, _, *rest):
        relay_refs, nb_refs = rest[:sides], rest[sides : 2 * sides]
        out_any, done, fringe, bends, sems = rest[2 * sides :]
        half = nx // 2
        keys = jnp.where(lax.axis_index("harm") == 0, n_pert - n_keys, 0) if swap else 0
        inner_layer = jnp.where(face_place(True, 0)[0], 2, 0)
        taps_of = edge_taps((FIRST,))
        sends = []

        def send(src, dst):
            sends.append(pltpu.make_async_copy(src, dst, sems.at[len(sends)]))
            sends[-1].start()

        for s in range(sides):
            for f in range(0, n_nb, 2):
                both = [jnp.concatenate([nb_tile(relay_refs[s], after, f + i) for after in range(2)], axis=0) for i in range(2)]
                both = jnp.concatenate(both, axis=1)
                got = jnp.dot(taps_of, both, preferred_element_type=f32)
                for i in range(2):
                    bends[s * n_nb + f + i] = got[:, i * ny : (i + 1) * ny]

        def edge_terms(pairs, z, end, add):
            strip = pl.ds(pl.multiple_of(z * nx + end * half, 16), 16)
            keep = slice(8 * end, 8 * end + 8)
            bent = pl.ds(pl.multiple_of((end * nz + z) * 8, 8), 8)
            for k in sorted({p[0] for p in pairs}):
                zero = jnp.zeros((8, ny), f32)
                acc = [(zero, zero)] * 3
                for _, m, s, f in [p for p in pairs if p[0] == k]:
                    base = (abs(m) - 1) * 6
                    flow = tuple(mode_ref[base + 3 * i, strip].astype(f32)[keep] for i in range(2))
                    for c in range(3):
                        at = s * n_nb + f + c
                        acc[c] = product(acc[c], flow, (bends[at, bent], bends[at + 3, bent]), m)
                for c in range(3):
                    for i in range(2):
                        add(k, 4 * i + c, acc[c][i] * (1.0 / 12.0))

        def end_rows(z, end):
            return pl.ds(pl.multiple_of(z * nx + end * (nx - 8), 8), 8)

        first_row = pl.multiple_of(jnp.where(face_place(True, 0)[0], 0, (nz - 2) * nx), nx)
        done[...] = inner_ref[:, pl.ds(first_row, 2 * nx)]
        cross_layer = first_row // nx

        def cross_edges(pairs):
            def at_layer(j, carry):
                for end in range(2):
                    rows = end_rows(j, end)

                    def add(k, part, value):
                        done[k * 8 + part, rows] = done[k * 8 + part, rows] + value

                    edge_terms(pairs, cross_layer + j, end, add)
                return carry

            lax.fori_loop(0, 2, at_layer, 0)

        on_sides(cross_edges)
        for step in range(2):
            faces(done, mean_ref, mode_ref, pert_ref, nb_refs, None, second_ref, None, relay_refs, step, cross_layer)
            layer = face_place(True, step)[1]
            here = pl.ds(pl.multiple_of((layer - cross_layer) * nx, nx), nx)
            send(done.at[:, here], out_any.at[:, pl.ds(pl.multiple_of(layer * nx, nx), nx)])

        def other_edges(pairs):
            lowest = min(p[0] for p in pairs) * 8 if swap else 0

            def at_layer(j, carry):
                for end in range(2):

                    def add(k, part, value):
                        at = k * 8 + part - lowest
                        fringe[end, at, j] = fringe[end, at, j] + value

                    edge_terms(pairs, inner_layer + j, end, add)
                return carry

            lax.fori_loop(0, nz - 2, at_layer, 0)

        for j in range(nz - 2):
            for end in range(2):
                fringe[end, :, j] = inner_ref[pl.ds(keys, n_keys), end_rows(inner_layer + j, end)]
        on_sides(other_edges)
        for j in range(nz - 2):
            for end in range(2):
                send(fringe.at[end, :, j], out_any.at[pl.ds(keys, n_keys), end_rows(inner_layer + j, end)])
        for copy in sends:
            copy.wait()

    with jax.named_scope("finish"):
        out = pl.pallas_call(
            finish,
            out_shape=jax.ShapeDtypeStruct((n_pert, own, ny), f32),
            in_specs=[VMEM] * 5 + [HBM] + [VMEM] * (2 * sides),
            out_specs=HBM,
            input_output_aliases={5: 0},
            scratch_shapes=[
                pltpu.VMEM((n_pert, 2 * nx, ny), f32),
                pltpu.VMEM((2, n_keys, nz - 2, 8, ny), f32),
                pltpu.VMEM((sides * n_nb, ends, ny), f32),
                pltpu.SemaphoreType.DMA((2 + 2 * (nz - 2),)),
            ],
            compiler_params=roomy,
        )(
            flat(pert), flat(mean), flat(mode), inner, second_got, result,
            *relay_got, *[flat(b) for b in nb_got],
        )
    return jnp.swapaxes(out.reshape(per, 2, 4, nz, nx, ny), 3, 4)


def solution(mesh):
    return jax.shard_map(
        shards,
        mesh=mesh,
        in_specs=(
            P("harm", None, None, "gx", "gz", None),
            P(None, "gx", "gz", None),
            P(None, None, None, "gx", "gz", None),
            P("gx", "gz", None),
        ),
        out_specs=P("harm", None, None, "gx", "gz", None),
        check_vma=False,
    )
```

```python
import jax
import jax.numpy as jnp
from jax import lax
from jax.experimental import pallas as pl
from jax.experimental.pallas import tpu as pltpu
from jax.sharding import PartitionSpec as P

FREQUENCY_STEP = 0.2
VISCOSITY = 0.05
PENALTY = 4.0
FIRST = {-2: 1.0, -1: -8.0, 1: 8.0, 2: -1.0}
SECOND = {-2: -1.0, -1: 16.0, 0: -30.0, 1: 16.0, 2: -1.0}
HALO_X = 16
VMEM_BYTES = 58 * 1024 * 1024
ANY = pl.BlockSpec(memory_space=pl.ANY)
VMEM = pl.BlockSpec(memory_space=pltpu.VMEM)
HBM = pl.BlockSpec(memory_space=pltpu.HBM)


def taps(delta, table):
    out = jnp.zeros(delta.shape, jnp.float32)
    for step, weight in table.items():
        out = jnp.where(delta == step, weight, out)
    return out


def iotas(rows, columns):
    return lax.broadcasted_iota(jnp.int32, (rows, 1), 0), lax.broadcasted_iota(jnp.int32, (1, columns), 1)


def column_cells(column, nz, nx):
    shift, own = nx.bit_length() - 1, nz * nx
    halo = column - own
    after = halo >= HALO_X
    edge = jnp.where(after, halo - HALO_X, halo)
    inside = column < own
    z = jnp.where(inside, column >> shift, edge >> 1)
    x = jnp.where(inside, column & (nx - 1), (edge & 1) + jnp.where(after, nx, -2))
    return z, x


def slope_matrix(part, z, x, to_z, to_x):
    dz, dx = to_z - z, to_x - x
    if part == 0:
        return jnp.where(dz == 0, taps(dx, FIRST), 0.0)
    if part == 1:
        return jnp.where(dx == 0, taps(dz, FIRST), 0.0)
    return jnp.where(dz == 0, taps(dx, SECOND), 0.0) + jnp.where(dx == 0, taps(dz, SECOND), 0.0)


def store_walls(walls_ref, ny):
    row, column = iotas(ny, ny)
    first, second = (taps(row - column, table).astype(jnp.bfloat16) for table in (FIRST, SECOND))
    for i, (block, sign) in enumerate(((first, 1), (first, -1), (second, 1), (second, -1))):
        if i * ny < walls_ref.shape[1]:
            walls_ref[:ny, i * ny : (i + 1) * ny] = block
            if walls_ref.shape[0] > ny:
                walls_ref[ny:, i * ny : (i + 1) * ny] = block if sign > 0 else -block


def run_copies(copies, sems):
    started = [pltpu.make_async_copy(src, dst, sems.at[i]) for i, (src, dst) in enumerate(copies)]
    for copy in started:
        copy.start()
    for copy in started:
        copy.wait()


def shards(perturbation, base_mean, base_modes, solid_mask):
    per, modes = perturbation.shape[0], base_modes.shape[0]
    nx, nz, ny = perturbation.shape[3], perturbation.shape[4], perturbation.shape[5]
    own = nz * nx
    bf16, f32 = jnp.bfloat16, jnp.float32
    harms, size_x, size_z = (lax.axis_size(a) for a in ("harm", "gx", "gz"))
    swap = harms == 2
    sides = 1 if swap else 2
    n_pert, n_mean, n_modes = per * 8, 3, modes * 6
    n_base = n_mean + n_modes
    n_res = n_pert + n_base
    n_nb = modes * 6
    n_all = n_res + sides * n_nb

    pert = jnp.swapaxes(perturbation, 3, 4).reshape(n_pert, nz, nx, ny)
    mean = jnp.swapaxes(base_mean, 1, 2)
    mode = jnp.swapaxes(base_modes, 3, 4).reshape(n_modes, nz, nx, ny)
    mask = jnp.swapaxes(solid_mask, 0, 1).reshape(own, ny)

    def place():
        me_h, odd = lax.axis_index("harm"), lax.rem(lax.axis_index("gz"), 2)
        shared = jnp.where(me_h == 0, per - modes, 0) if swap else 0
        return me_h, odd, odd * (nz - 2), (1 - odd) * (nz - 2), shared

    cross_pairs = [(i, (i + 1) % size_z if i % 2 else (i - 1) % size_z) for i in range(size_z)]
    near_pairs = [(i, i + 1 if i % 2 == 0 else i - 1) for i in range(size_z)]
    up_x = [(i, (i + 1) % size_x) for i in range(size_x)]
    down_x = [(j, i) for i, j in up_x]
    if swap:
        harm_perms = [[(0, 1), (1, 0)]]
    else:
        up_h = [(i, i + 1) for i in range(harms - 1)]
        harm_perms = [up_h, [(j, i) for i, j in up_h]]
    def sent(s, scal):
        return scal[4] if swap else (per - modes if s == 0 else 0)

    face = lambda n: jax.ShapeDtypeStruct((n, 2, nx, ny), bf16)
    roomy = pltpu.CompilerParams(vmem_limit_bytes=32 * 1024 * 1024)

    used = 2 * nz
    spare = HALO_X - used
    tiles = 3 * (-(-n_res // 4))

    def edge_tile(ref, f):
        group, i = divmod(f, 4)
        if i < 3:
            return ref[3 * group + i]
        parts = [ref[3 * group + j].astype(f32)[used:] for j in range(3)]
        return jnp.concatenate(parts + [jnp.zeros((spare, ny), f32)], axis=0).astype(bf16)

    def pack(pert_any, mean_any, mode_any, first_any, second_any, lo_any, hi_any, *rest):
        nb_anys = rest[:sides]
        pert_ref, mean_ref, mode_ref, lo_ref, hi_ref, in_sems, out_sems = rest[sides:]
        scal = place()
        z = pl.ds(scal[2], 2)
        loads = [(pert_any.at[pl.ds(8 * l, 8)], pert_ref.at[pl.ds(8 * l, 8)]) for l in range(per)]
        loads += [(mean_any, mean_ref), (mode_any, mode_ref)]
        loads = [pltpu.make_async_copy(src, dst, in_sems.at[i]) for i, (src, dst) in enumerate(loads)]
        for copy in loads:
            copy.start()
        out = []

        def send(src, dst):
            out.append(pltpu.make_async_copy(src, dst, out_sems.at[len(out)]))
            out[-1].start()

        row, column = iotas(2 * HALO_X, own)
        low = row < HALO_X
        row = jnp.where(low, row, row - HALO_X)
        target = (row >> 1) * nx + (row & 1) + jnp.where(low, 0, nx - 2)
        pick = jnp.where(column == target, 1.0, 0.0).astype(bf16)
        where = [(pert_ref, f) for f in range(n_pert)] + [(mean_ref, f) for f in range(n_mean)] + [(mode_ref, f) for f in range(n_modes)]

        def edges(group):
            got = []
            for f in range(4 * group, min(4 * group + 4, n_res), 2):
                mine = [ref[i].reshape(own, ny) for ref, i in where[f : min(f + 2, n_res)]]
                both = jnp.concatenate(mine, axis=1) if len(mine) == 2 else mine[0]
                both = jnp.dot(pick, both, preferred_element_type=f32)
                got += [both[:, i * ny : (i + 1) * ny] for i in range(len(mine))]
            if len(got) == 3:
                got.append(jnp.zeros((2 * HALO_X, ny), f32))
            for i in range(3):
                for ref, at in ((lo_ref, 0), (hi_ref, HALO_X)):
                    extra = got[3][at + spare * i : at + spare * (i + 1)]
                    ref[3 * group + i] = jnp.concatenate([got[i][at : at + used], extra], axis=0).astype(bf16)

        for l in range(per):
            loads[l].wait()
            mine = pl.ds(8 * l, 8)
            send(pert_ref.at[mine, z], first_any.at[mine])
        for s, nb_any in enumerate(nb_anys):
            for i in range(modes * 2):
                send(pert_ref.at[pl.ds(sent(s, scal) * 8 + 4 * i, 3)], nb_any.at[pl.ds(3 * i, 3)])
        for group in range(n_pert // 4):
            edges(group)
        loads[per].wait()
        loads[per + 1].wait()
        send(mean_ref.at[:, z], second_any.at[pl.ds(0, n_mean)])
        send(mode_ref.at[:, z], second_any.at[pl.ds(n_mean, n_modes)])
        for group in range(n_pert // 4, tiles // 3):
            edges(group)
        send(lo_ref, lo_any)
        send(hi_ref, hi_any)
        for copy in out:
            copy.wait()

    edge = jax.ShapeDtypeStruct((tiles, HALO_X, ny), bf16)
    with jax.named_scope("pack"):
        first, second, edge_lo, edge_hi, *nb_send = pl.pallas_call(
            pack,
            out_shape=(face(n_pert), face(n_base), edge, edge) + tuple(jax.ShapeDtypeStruct((n_nb, nz, nx, ny), bf16) for _ in range(sides)),
            in_specs=[HBM] * 3,
            out_specs=(ANY,) * (4 + sides),
            scratch_shapes=[
                pltpu.VMEM((n_pert, nz, nx, ny), bf16),
                pltpu.VMEM((n_mean, nz, nx, ny), bf16),
                pltpu.VMEM((n_modes, nz, nx, ny), bf16),
                pltpu.VMEM((tiles, HALO_X, ny), bf16),
                pltpu.VMEM((tiles, HALO_X, ny), bf16),
                pltpu.SemaphoreType.DMA((per + 2,)),
                pltpu.SemaphoreType.DMA((per + sides * modes * 2 + 4,)),
            ],
            compiler_params=pltpu.CompilerParams(vmem_limit_bytes=VMEM_BYTES),
        )(pert, mean, mode)
    first_got = lax.ppermute(first, "gz", cross_pairs)
    nb_got = [lax.ppermute(b, "harm", p) for b, p in zip(nb_send, harm_perms)]
    xb_got = lax.ppermute(edge_hi, "gx", up_x)
    xa_got = lax.ppermute(edge_lo, "gx", down_x)
    second_got = lax.ppermute(second, "gz", cross_pairs)

    PAIRS = ((0, 3), (1, 2))
    DRIFT = (-1.5 * FREQUENCY_STEP, -0.5 * FREQUENCY_STEP)

    def entries(t, p, q, r, s):
        return t, q, p + r, p - r, q + s, s - q, t + p, t - p

    def couple(acc, ent, vec):
        t, q, pr, pmr, qs, sq, tp, tmp = ent
        out = []
        for i in range(2):
            a, e, b, g = (vec[j][i] for j in range(4))
            out.append(
                (
                    acc[0][i] + t * a + pr * b + sq * g,
                    acc[1][i] + t * e + qs * b + pmr * g,
                    acc[2][i] + pr * a + qs * e + tp * b + q * g,
                    acc[3][i] + sq * a + pmr * e + q * b + tmp * g,
                )
            )
        return [(out[0][j], out[1][j]) for j in range(4)]

    def harmonics_of(acc, scale):
        out = [None] * 4
        for at, (lo, hi) in enumerate(PAIRS):
            (ar, ai), (er, ei) = acc[2 * at], acc[2 * at + 1]
            out[lo] = ((ar + ei) * scale, (ai - er) * scale)
            out[hi] = ((ar - ei) * scale, (ai + er) * scale)
        return out

    def basis_of(values):
        out = []
        for lo, hi in PAIRS:
            (lr, li), (hr, hi_) = values[lo], values[hi]
            out += [(lr + hr, li + hi_), (hi_ - li, lr - hr)]
        return out

    def rhs(ref, fields):
        cols = [ref[f] for f in fields]
        return cols[0] if len(cols) == 1 else jnp.concatenate(cols, axis=1)

    def dot(a, b):
        return jnp.dot(a, b, preferred_element_type=f32)

    def resident_slopes(pert_ref, grads, plain, lin, rows_ref, walls_ref):
        me_h = place()[0]
        row, column = iotas(own, own)
        to_z, to_x = column_cells(column, nz, nx)
        for i in range(3):
            rows_ref[i * own : (i + 1) * own] = slope_matrix(i, row >> nx.bit_length() - 1, row & (nx - 1), to_z, to_x).astype(bf16)
        store_walls(walls_ref, ny)
        mean_freq = 12.0 * FREQUENCY_STEP * (me_h * per + 1.5 - per * harms / 2).astype(f32)

        for at, (lo, hi) in enumerate(PAIRS):
            for i in range(2):
                fl, fr = lo * 8 + i * 4 + 3, hi * 8 + i * 4 + 3
                got = dot(rows_ref[: 2 * own], rhs(pert_ref, (fl, fr)))
                wall = dot(rhs(pert_ref, (fl, fr)), walls_ref[:, : 2 * ny])
                for d in range(3):
                    if d == 1:
                        total, diff = wall[:, :ny], wall[:, ny:]
                    else:
                        span = slice(0, own) if d == 0 else slice(own, 2 * own)
                        total, diff = got[span, :ny] + got[span, ny:], got[span, :ny] - got[span, ny:]
                    lin[2 * at, i, d] = total
                    lin[2 * at + 1, 1 - i, d] = diff if i == 0 else -diff
        for at, (lo, hi) in enumerate(PAIRS):
            for c in range(3):
                for i in range(2):
                    sign = 1.0 if i == 0 else -1.0
                    fl, fr = lo * 8 + i * 4 + c, hi * 8 + i * 4 + c
                    got = dot(rows_ref[...], rhs(pert_ref, (fl, fr)))
                    xl, xr = pert_ref[fl].astype(f32), pert_ref[fr].astype(f32)
                    wall = dot(rhs(pert_ref, (fl, fr)), walls_ref[...])
                    total, diff = xl + xr, xl - xr
                    plain[2 * at, i, c] = total
                    plain[2 * at + 1, 1 - i, c] = sign * diff
                    for d in range(3):
                        if d == 1:
                            gt, gd = wall[:, :ny], wall[:, ny : 2 * ny]
                        else:
                            span = slice(0, own) if d == 0 else slice(own, 2 * own)
                            gt, gd = got[span, :ny] + got[span, ny:], got[span, :ny] - got[span, ny:]
                        gd = sign * gd
                        grads[2 * at, i, c, d] = gt
                        grads[2 * at + 1, 1 - i, c, d] = gd
                        if d == c:
                            if c == 0:
                                lin[2 * at, i, 3] = gt
                                lin[2 * at + 1, 1 - i, 3] = gd
                            else:
                                lin[2 * at, i, 3] = lin[2 * at, i, 3] + gt
                                lin[2 * at + 1, 1 - i, 3] = lin[2 * at + 1, 1 - i, 3] + gd
                    lt = got[2 * own :, :ny] + got[2 * own :, ny:] + wall[:, 2 * ny : 3 * ny]
                    ld = got[2 * own :, :ny] - got[2 * own :, ny:] + wall[:, 3 * ny :]
                    drift = 12.0 * DRIFT[at]
                    lin[2 * at, i, c] = lin[2 * at, i, c] - VISCOSITY * lt
                    lin[2 * at + 1, 1 - i, c] = lin[2 * at + 1, 1 - i, c] - sign * VISCOSITY * ld
                    lin[2 * at, 1 - i, c] = lin[2 * at, 1 - i, c] + sign * (mean_freq * total + drift * diff)
                    lin[2 * at + 1, i, c] = lin[2 * at + 1, i, c] - (mean_freq * diff + drift * total)

    def resident(mean_ref, mode_ref, grads, plain, lin, out_ref, ents, rows_ref, walls_ref):
        row, column = iotas(own, own)
        to_z, to_x = column_cells(column, nz, nx)
        for i in range(2):
            rows_ref[i * own : (i + 1) * own] = slope_matrix(i, row >> nx.bit_length() - 1, row & (nx - 1), to_z, to_x).astype(bf16)
        store_walls(walls_ref, ny)
        for c in range(3):
            picked = [mean_ref[c].astype(f32)] + [mode_ref[3 * i + c].astype(f32) for i in range(4)]
            for n, ent in enumerate(entries(*picked)):
                ents[c, n] = ent
            mean_at = dot(rows_ref[...], rhs(mean_ref, (c,)))
            mean_wall = dot(mean_ref[c], walls_ref[:ny, :ny])
            real = dot(rows_ref[...], rhs(mode_ref, (c, 6 + c)))
            imag = dot(rows_ref[...], rhs(mode_ref, (3 + c, 9 + c)))
            wall_real = dot(rhs(mode_ref, (c, 6 + c)), walls_ref[:, : 2 * ny])
            wall_imag = dot(rhs(mode_ref, (3 + c, 9 + c)), walls_ref[:, : 2 * ny])
            for d in range(3):
                if d == 1:
                    pr, pmr = wall_real[:, :ny], wall_real[:, ny:]
                    qs, qms = wall_imag[:, :ny], wall_imag[:, ny:]
                    t, p, q = mean_wall, 0.5 * (pr + pmr), 0.5 * (qs + qms)
                    values = (t, q, pr, pmr, qs, -qms, t + p, t - p)
                else:
                    span = slice(0, own) if d == 0 else slice(own, 2 * own)
                    values = entries(mean_at[span], real[span, :ny], imag[span, :ny], real[span, ny:], imag[span, ny:])
                for n, ent in enumerate(values):
                    ents[3 + 3 * d + c, n] = ent

        def block(b, carry):
            rows = pl.ds(pl.multiple_of(b * 8, 8), 8)
            accs = [[(lin[j, 0, c, rows], lin[j, 1, c, rows]) for j in range(4)] for c in range(4)]
            for d in range(3):
                flow = [ents[d, n, rows] for n in range(8)]
                for c in range(3):
                    accs[c] = couple(accs[c], flow, [(grads[j, 0, c, d, rows], grads[j, 1, c, d, rows]) for j in range(4)])
                along = [(plain[j, 0, d, rows], plain[j, 1, d, rows]) for j in range(4)]
                for c in range(3):
                    slope = [ents[3 + 3 * d + c, n, rows] for n in range(8)]
                    accs[c] = couple(accs[c], slope, along)
            for c in range(4):
                for k, (re, im) in enumerate(harmonics_of(accs[c], 1.0 / 24.0)):
                    out_ref[k * 8 + c, rows] = re
                    out_ref[k * 8 + 4 + c, rows] = im
            return carry

        lax.fori_loop(0, own // 8, block, 0, unroll=2)

    flat = lambda a: a.reshape(a.shape[0], -1, ny)
    with jax.named_scope("resident_slopes"):
        slopes = pl.pallas_call(
            resident_slopes,
            out_shape=tuple(jax.ShapeDtypeStruct(n + (own, ny), f32) for n in ((4, 2, 3, 3), (4, 2, 3), (4, 2, 4))),
            scratch_shapes=[pltpu.VMEM((3 * own, own), bf16), pltpu.VMEM((2 * ny, 4 * ny), bf16)],
            compiler_params=pltpu.CompilerParams(vmem_limit_bytes=20 * 1024 * 1024),
        )(flat(pert))
    with jax.named_scope("resident"):
        whole = pl.pallas_call(
            resident,
            out_shape=jax.ShapeDtypeStruct((n_pert, own, ny), f32),
            scratch_shapes=[
                pltpu.VMEM((12, 8, own, ny), f32),
                pltpu.VMEM((2 * own, own), bf16),
                pltpu.VMEM((2 * ny, 2 * ny), bf16),
            ],
            compiler_params=roomy,
        )(flat(mean), flat(mode), *slopes)

    base_modes_at = n_pert + n_mean
    ends = 16 * nz

    def edge_taps(tables):
        row, column = iotas(ends, own + 2 * HALO_X)
        last = row >= 8 * nz
        row = jnp.where(last, row - 8 * nz, row)
        to_z, to_x = column_cells(column, nz, nx)
        dz, dx = to_z - (row >> 3), to_x - (row & 7) - jnp.where(last, nx - 8, 0)
        return jnp.concatenate([jnp.where(dz == 0, taps(dx, table), 0.0)[:, own:] for table in tables], axis=0).astype(bf16)

    def add_edges(pert_ref, mean_ref, mode_ref, xb_ref, xa_ref, _, out_ref, vecs, lins, bends):
        taps_of = edge_taps((FIRST, SECOND))

        def bent(fields, lap):
            cols = [jnp.concatenate([edge_tile(xb_ref, f), edge_tile(xa_ref, f)], axis=0) for f in fields]
            both = cols[0] if len(cols) == 1 else jnp.concatenate(cols, axis=1)
            got = jnp.dot(taps_of if lap else taps_of[:ends], both, preferred_element_type=f32)
            return [(got[:ends, i * ny : (i + 1) * ny], got[ends:, i * ny : (i + 1) * ny]) for i in range(len(fields))]

        for at, (lo, hi) in enumerate(PAIRS):
            for i in range(2):
                sign = 1.0 if i == 0 else -1.0
                for c in range(4):
                    (gl, ll), (gr, lr) = bent((lo * 8 + 4 * i + c, hi * 8 + 4 * i + c), c < 3)
                    if c < 3:
                        vecs[2 * at, i, c] = gl + gr
                        vecs[2 * at + 1, 1 - i, c] = sign * (gl - gr)
                        lins[2 * at, i, c] = -VISCOSITY * (ll + lr)
                        lins[2 * at + 1, 1 - i, c] = (-VISCOSITY * sign) * (ll - lr)
                    else:
                        lins[2 * at, i, 0] = lins[2 * at, i, 0] + (gl + gr)
                        lins[2 * at + 1, 1 - i, 0] = lins[2 * at + 1, 1 - i, 0] + sign * (gl - gr)
        for c in range(3):
            at = base_modes_at + c
            (t, _), = bent((n_pert + c,), False)
            (p, _), (r, _) = bent((at, at + 6), False)
            (q, _), (s_, _) = bent((at + 3, at + 9), False)
            for n, ent in enumerate(entries(t, p, q, r, s_)):
                bends[c, n] = ent

        def layer_ends(z, carry):
            for end in range(2):
                strip = pl.ds(pl.multiple_of(z * nx + end * (nx // 2), 16), 16)
                keep = slice(8 * end, 8 * end + 8)
                mine = pl.ds(pl.multiple_of((end * nz + z) * 8, 8), 8)

                def read(ref, f):
                    return ref[f, strip].astype(f32)[keep]

                flow = entries(read(mean_ref, 0), *[read(mode_ref, 3 * i) for i in range(4)])
                along = basis_of([(read(pert_ref, l * 8), read(pert_ref, l * 8 + 4)) for l in range(per)])
                for c in range(4):
                    if c < 3:
                        acc = [(lins[j, 0, c, mine], lins[j, 1, c, mine]) for j in range(4)]
                        acc = couple(acc, flow, [(vecs[j, 0, c, mine], vecs[j, 1, c, mine]) for j in range(4)])
                        acc = couple(acc, [bends[c, n, mine] for n in range(8)], along)
                    else:
                        acc = [(vecs[j, 0, 0, mine], vecs[j, 1, 0, mine]) for j in range(4)]
                    for k, parts in enumerate(harmonics_of(acc, 1.0 / 24.0)):
                        for i in range(2):
                            out_ref[k * 8 + 4 * i + c, mine] = parts[i]
            return carry

        lax.fori_loop(0, nz, layer_ends, 0)

    with jax.named_scope("edges"):
        edged = pl.pallas_call(
            add_edges,
            out_shape=jax.ShapeDtypeStruct((n_pert, ends, ny), f32),
            in_specs=[VMEM] * 5 + [ANY],
            scratch_shapes=[
                pltpu.VMEM((4, 2, 3, ends, ny), f32),
                pltpu.VMEM((4, 2, 3, ends, ny), f32),
                pltpu.VMEM((3, 8, ends, ny), f32),
            ],
            compiler_params=roomy,
        )(flat(pert), flat(mean), flat(mode), xb_got, xa_got, whole)

    faces_deep = n_nb * 2 * nx
    nb_tiles = 3 * n_nb // 4
    deep = faces_deep + 2 * nb_tiles * HALO_X

    def nb_tile(ref, after, f):
        group, i = divmod(f, 4)
        at = [faces_deep + (after * nb_tiles + 3 * group + j) * HALO_X for j in range(3)]
        if i < 3:
            return ref[at[i] : at[i] + HALO_X]
        parts = [ref[row : row + HALO_X].astype(f32)[used:] for row in at]
        return jnp.concatenate(parts + [jnp.zeros((spare, ny), f32)], axis=0).astype(bf16)

    def pack_relay(first_ref, xb_ref, xa_ref, _, *outs):
        scal = place()
        for s, out in enumerate(outs):
            for i in range(modes * 2):
                group = sent(s, scal) * 2 + i
                for c in range(3):
                    at = (3 * i + c) * 2 * nx
                    out[at : at + 2 * nx] = first_ref[group * 4 + c].reshape(2 * nx, ny)
            for after, ref in enumerate((xb_ref, xa_ref)):
                for group in range(n_nb // 4):
                    rows = []
                    for f in range(4 * group, 4 * group + 4):
                        rows.append(ref[(sent(s, scal) * 2 + f // 3) * 3 + f % 3].astype(f32))
                    for i in range(3):
                        at = faces_deep + (after * nb_tiles + 3 * group + i) * HALO_X
                        tile = jnp.concatenate([rows[i][:used], rows[3][spare * i : spare * (i + 1)]], axis=0)
                        out[at : at + HALO_X] = tile.astype(bf16)

    with jax.named_scope("pack_relay"):
        relay = pl.pallas_call(
            pack_relay,
            out_shape=tuple(jax.ShapeDtypeStruct((deep, ny), bf16) for _ in range(sides)),
            in_specs=[VMEM] * 3 + [ANY],
            compiler_params=roomy,
        )(first_got, xb_got, xa_got, edged)
    relay_got = [lax.ppermute(b, "harm", p) for b, p in zip(relay, harm_perms)]

    def pack_near(pert_ref, mean_ref, mode_ref, *rest):
        out = rest[-1]
        z = pl.ds(place()[3], 2)
        out[:n_pert] = pert_ref[:, z]
        out[n_pert : n_pert + n_mean] = mean_ref[:, z]
        out[n_pert + n_mean : n_res] = mode_ref[:, z]
        for s in range(sides):
            out[n_res + s * n_nb : n_res + (s + 1) * n_nb] = rest[s][:, z]

    with jax.named_scope("pack_near"):
        near = pl.pallas_call(
            pack_near,
            out_shape=face(n_all),
            in_specs=[VMEM] * (3 + sides) + [ANY],
            compiler_params=roomy,
        )(pert, mean, mode, *nb_got, relay[0])
    near_got = lax.ppermute(near, "gz", near_pairs)

    below, above = [], []
    for k in range(per):
        for m in range(-modes, modes + 1):
            l = k - m
            if l < 0:
                below.append((k, m, 0, (l + modes) * 6))
            elif l >= per:
                above.append((k, m, sides - 1, (l - per) * 6))

    def on_sides(work):
        me_h = lax.axis_index("harm")
        pl.when(me_h > 0)(lambda: work(below))
        pl.when(me_h < harms - 1)(lambda: work(above))

    def product(acc, flow, value, m):
        (fr, fi), (vr, vi) = flow, value
        if m > 0:
            return acc[0] + fr * vr - fi * vi, acc[1] + fr * vi + fi * vr
        return acc[0] + fr * vr + fi * vi, acc[1] + fr * vi - fi * vr


    def face_place(cross, step):
        odd = place()[1]
        before = (odd == 0) if cross else (odd == 1)
        return before, jnp.where(before, step, nz - 1 - step), jnp.where(before, 1, 0)

    def faces(out_ref, mean_ref, mode_ref, pert_ref, nb_refs, first_ref, second_ref, near_ref, relay_refs, step, lowest=0):
        cross = near_ref is None
        before, layer, near_at = face_place(cross, step)
        turn = jnp.where(before, 1.0, -1.0)

        def mix(pair):
            return pair[1] - 8.0 * pair[0] if step == 0 else pair[0]

        def mix_lap(pair):
            return pair[1] - 16.0 * pair[0] if step == 0 else pair[0]

        def chunk_work(chunk, carry):
            rows = pl.ds(pl.multiple_of(layer * nx + chunk * 16, 16), 16)
            out_rows = pl.ds(pl.multiple_of((layer - lowest) * nx + chunk * 16, 16), 16)
            strip = pl.ds(pl.multiple_of(chunk * 16, 16), 16)

            def halos(f):
                if not cross:
                    ref, at = near_ref, f
                elif f < n_pert:
                    ref, at = first_ref, f
                else:
                    ref, at = second_ref, f - n_pert
                return ref[at, near_at, strip].astype(f32), (ref[at, 1 - near_at, strip].astype(f32) if step == 0 else None)

            def nb_halos(s, f):
                if not cross:
                    return halos(n_res + s * n_nb + f)
                at = [pl.ds(pl.multiple_of((2 * f + j) * nx + chunk * 16, 16), 16) for j in (near_at, 1 - near_at)]
                return tuple(relay_refs[s][r].astype(f32) for r in at)

            velocity, base = first_ref is not None or not cross, second_ref is not None or not cross
            if velocity:
                flow = entries(mean_ref[2, rows].astype(f32), *[mode_ref[3 * i + 2, rows].astype(f32) for i in range(4)])
            if base:
                along = basis_of([(pert_ref[l * 8 + 2, rows].astype(f32), pert_ref[l * 8 + 6, rows].astype(f32)) for l in range(per)])
            for c in range(4 if velocity else 3):
                acc = [(0.0, 0.0)] * 4
                if velocity and c < 3:
                    got = [[halos(l * 8 + 4 * i + c) for i in range(2)] for l in range(per)]
                    vec = basis_of([(mix(g[0]), mix(g[1])) for g in got])
                    lap = basis_of([(mix_lap(g[0]), mix_lap(g[1])) for g in got])
                    if c == 2:
                        acc = basis_of([(mix(halos(l * 8 + 3)), mix(halos(l * 8 + 7))) for l in range(per)])
                    acc = couple(acc, flow, vec)
                if base and c < 3:
                    bend = entries(mix(halos(n_pert + c)), *[mix(halos(base_modes_at + 3 * i + c)) for i in range(4)])
                    acc = couple(acc, bend, along)
                if c == 3:
                    acc = vec
                if velocity and c < 3:
                    acc = [tuple(turn * a + VISCOSITY * v for a, v in zip(*pair)) for pair in zip(acc, lap)]
                else:
                    acc = [tuple(turn * a for a in pair) for pair in acc]
                for k, parts in enumerate(harmonics_of(acc, 1.0 / 24.0)):
                    for i in range(2):
                        at = k * 8 + 4 * i + c
                        out_ref[at, out_rows] = out_ref[at, out_rows] + parts[i]

            def nb_work(pairs):
                for k in sorted({p[0] for p in pairs}):
                    zero = jnp.zeros((16, ny), f32)
                    for c in range(3):
                        acc = (zero, zero)
                        for _, m, s, f in [p for p in pairs if p[0] == k]:
                            at = (abs(m) - 1) * 6
                            mine = tuple(mode_ref[at + 3 * i + 2, rows].astype(f32) for i in range(2))
                            acc = product(acc, mine, tuple(mix(nb_halos(s, f + 3 * i + c)) for i in range(2)), m)
                            bent = tuple(mix(halos(base_modes_at + at + 3 * i + c)) for i in range(2))
                            carried = tuple(nb_refs[s][f + 3 * i + 2, rows].astype(f32) for i in range(2))
                            acc = product(acc, bent, carried, m)
                        for i in range(2):
                            at = k * 8 + 4 * i + c
                            out_ref[at, out_rows] = out_ref[at, out_rows] + (turn * (1.0 / 12.0)) * acc[i]

            if base:
                on_sides(nb_work)
            return carry

        lax.fori_loop(0, nx // 16, chunk_work, 0)

    def neighbours(mask_ref, pert_ref, mean_ref, mode_ref, xb_ref, xa_ref, whole_ref, edged_ref, first_ref, near_ref, *rest):
        nb_refs = rest[:sides]
        out_any, out_ref, grads, plain, stencil_ref, walls_ref, sems = rest[-7:]
        row, column = iotas(own, own + 2 * HALO_X)
        to_z, to_x = column_cells(column, nz, nx)
        for i in range(2):
            stencil_ref[i * own : (i + 1) * own] = slope_matrix(i, row >> nx.bit_length() - 1, row & (nx - 1), to_z, to_x).astype(bf16)
        store_walls(walls_ref, ny)

        def slopes(at, mine, halo):
            both = jnp.concatenate(mine, axis=1)
            rows = both if halo is None else jnp.concatenate([both, halo], axis=0)
            got = jnp.dot(stencil_ref[:, : rows.shape[0]], rows, preferred_element_type=f32)
            wall = [jnp.dot(x, walls_ref[:ny, :ny], preferred_element_type=f32) for x in mine]
            for i in range(2):
                lanes = slice(i * ny, (i + 1) * ny)
                grads[at + i, 0] = got[:own, lanes]
                grads[at + i, 2] = got[own:, lanes]
                grads[at + i, 1] = wall[i]
                plain[at + i] = mine[i].astype(f32)

        for f in range(0, n_modes, 2):
            at = base_modes_at + f
            halo = [jnp.concatenate([edge_tile(ref, at), edge_tile(ref, at + 1)], axis=1) for ref in (xb_ref, xa_ref)]
            slopes(f, [mode_ref[f], mode_ref[f + 1]], jnp.concatenate(halo, axis=0))
        for s in range(sides):
            for f in range(0, n_nb, 2):
                slopes(n_modes + s * n_nb + f, [nb_refs[s][f], nb_refs[s][f + 1]], None)

        for z in range(nz):
            rows = slice(z * nx, (z + 1) * nx)
            solid = PENALTY * mask_ref[rows].astype(f32)
            for f in range(n_pert):
                if f % 4 < 3:
                    out_ref[f, rows] = whole_ref[f, rows] + solid * pert_ref[f, rows].astype(f32)
                else:
                    out_ref[f, rows] = whole_ref[f, rows]
            for end in range(2):
                rows = slice(z * nx + end * (nx - 8), z * nx + end * (nx - 8) + 8)
                mine = slice((end * nz + z) * 8, (end * nz + z + 1) * 8)
                out_ref[:, rows] = out_ref[:, rows] + edged_ref[:, mine]

        def work(pairs):
            def block(b, carry):
                rows = pl.ds(pl.multiple_of(b * 8, 8), 8)
                for k in sorted({p[0] for p in pairs}):
                    zero = jnp.zeros((8, ny), f32)
                    acc = [(zero, zero)] * 3
                    for _, m, s, f in [p for p in pairs if p[0] == k]:
                        at, base = n_modes + s * n_nb + f, (abs(m) - 1) * 6
                        for d in range(3):
                            flow = plain[base + d, rows], plain[base + 3 + d, rows]
                            along = plain[at + d, rows], plain[at + 3 + d, rows]
                            for c in range(3):
                                slope = grads[base + c, d, rows], grads[base + 3 + c, d, rows]
                                grad = grads[at + c, d, rows], grads[at + 3 + c, d, rows]
                                acc[c] = product(acc[c], flow, grad, m)
                                acc[c] = product(acc[c], slope, along, m)
                    for c in range(3):
                        for i in range(2):
                            at = k * 8 + 4 * i + c
                            out_ref[at, rows] = out_ref[at, rows] + acc[c][i] * (1.0 / 12.0)
                return carry

            lax.fori_loop(0, own // 8, block, 0)

        on_sides(work)
        sends = []

        def send(layer):
            rows = pl.ds(pl.multiple_of(layer * nx, nx), nx)
            sends.append(pltpu.make_async_copy(out_ref.at[:, rows], out_any.at[:, rows], sems.at[len(sends)]))
            sends[-1].start()

        for layer in range(2, nz - 2):
            send(layer)
        for step in range(2):
            faces(out_ref, mean_ref, mode_ref, pert_ref, nb_refs, None, None, near_ref, None, step)
            send(face_place(False, step)[1])
        for step in range(2):
            faces(out_ref, mean_ref, mode_ref, pert_ref, nb_refs, first_ref, None, None, None, step)
        for copy in sends:
            copy.wait()

    n_ext = n_modes + sides * n_nb
    with jax.named_scope("neighbours"):
        result, inner = pl.pallas_call(
            neighbours,
            out_shape=(jax.ShapeDtypeStruct((n_pert, own, ny), f32),) * 2,
            out_specs=(HBM, VMEM),
            scratch_shapes=[
                pltpu.VMEM((n_ext, 3, own, ny), f32),
                pltpu.VMEM((n_ext, own, ny), f32),
                pltpu.VMEM((2 * own, own + 2 * HALO_X), bf16),
                pltpu.VMEM((ny, ny), bf16),
                pltpu.SemaphoreType.DMA((nz - 2,)),
            ],
            compiler_params=roomy,
        )(mask, flat(pert), flat(mean), flat(mode), xb_got, xa_got, whole, edged, first_got, near_got, *[flat(b) for b in nb_got])

    n_keys = n_pert // 2 if swap else n_pert

    def finish(pert_ref, mean_ref, mode_ref, inner_ref, second_ref, _, *rest):
        relay_refs, nb_refs = rest[:sides], rest[sides : 2 * sides]
        out_any, done, fringe, bends, sems = rest[2 * sides :]
        half = nx // 2
        keys = jnp.where(lax.axis_index("harm") == 0, n_pert - n_keys, 0) if swap else 0
        inner_layer = jnp.where(face_place(True, 0)[0], 2, 0)
        taps_of = edge_taps((FIRST,))
        sends = []

        def send(src, dst):
            sends.append(pltpu.make_async_copy(src, dst, sems.at[len(sends)]))
            sends[-1].start()

        for s in range(sides):
            for f in range(0, n_nb, 2):
                both = [jnp.concatenate([nb_tile(relay_refs[s], after, f + i) for after in range(2)], axis=0) for i in range(2)]
                both = jnp.concatenate(both, axis=1)
                got = jnp.dot(taps_of, both, preferred_element_type=f32)
                for i in range(2):
                    bends[s * n_nb + f + i] = got[:, i * ny : (i + 1) * ny]

        def edge_terms(pairs, z, end, add):
            strip = pl.ds(pl.multiple_of(z * nx + end * half, 16), 16)
            keep = slice(8 * end, 8 * end + 8)
            bent = pl.ds(pl.multiple_of((end * nz + z) * 8, 8), 8)
            for k in sorted({p[0] for p in pairs}):
                zero = jnp.zeros((8, ny), f32)
                acc = [(zero, zero)] * 3
                for _, m, s, f in [p for p in pairs if p[0] == k]:
                    base = (abs(m) - 1) * 6
                    flow = tuple(mode_ref[base + 3 * i, strip].astype(f32)[keep] for i in range(2))
                    for c in range(3):
                        at = s * n_nb + f + c
                        acc[c] = product(acc[c], flow, (bends[at, bent], bends[at + 3, bent]), m)
                for c in range(3):
                    for i in range(2):
                        add(k, 4 * i + c, acc[c][i] * (1.0 / 12.0))

        def end_rows(z, end):
            return pl.ds(pl.multiple_of(z * nx + end * (nx - 8), 8), 8)

        def other_edges(pairs):
            lowest = min(p[0] for p in pairs) * 8 if swap else 0

            def at_layer(j, carry):
                for end in range(2):

                    def add(k, part, value):
                        at = k * 8 + part - lowest
                        fringe[end, at, j] = fringe[end, at, j] + value

                    edge_terms(pairs, inner_layer + j, end, add)
                return carry

            lax.fori_loop(0, nz - 2, at_layer, 0)

        for j in range(nz - 2):
            for end in range(2):
                fringe[end, :, j] = inner_ref[pl.ds(keys, n_keys), end_rows(inner_layer + j, end)]
        on_sides(other_edges)
        for j in range(nz - 2):
            for end in range(2):
                send(fringe.at[end, :, j], out_any.at[pl.ds(keys, n_keys), end_rows(inner_layer + j, end)])

        first_row = pl.multiple_of(jnp.where(face_place(True, 0)[0], 0, (nz - 2) * nx), nx)
        done[...] = inner_ref[:, pl.ds(first_row, 2 * nx)]
        cross_layer = first_row // nx

        def cross_edges(pairs):
            def at_layer(j, carry):
                for end in range(2):
                    rows = end_rows(j, end)

                    def add(k, part, value):
                        done[k * 8 + part, rows] = done[k * 8 + part, rows] + value

                    edge_terms(pairs, cross_layer + j, end, add)
                return carry

            lax.fori_loop(0, 2, at_layer, 0)

        on_sides(cross_edges)
        for step in range(2):
            faces(done, mean_ref, mode_ref, pert_ref, nb_refs, None, second_ref, None, relay_refs, step, cross_layer)
            layer = face_place(True, step)[1]
            here = pl.ds(pl.multiple_of((layer - cross_layer) * nx, nx), nx)
            send(done.at[:, here], out_any.at[:, pl.ds(pl.multiple_of(layer * nx, nx), nx)])
        for copy in sends:
            copy.wait()

    with jax.named_scope("finish"):
        out = pl.pallas_call(
            finish,
            out_shape=jax.ShapeDtypeStruct((n_pert, own, ny), f32),
            in_specs=[VMEM] * 5 + [HBM] + [VMEM] * (2 * sides),
            out_specs=HBM,
            input_output_aliases={5: 0},
            scratch_shapes=[
                pltpu.VMEM((n_pert, 2 * nx, ny), f32),
                pltpu.VMEM((2, n_keys, nz - 2, 8, ny), f32),
                pltpu.VMEM((sides * n_nb, ends, ny), f32),
                pltpu.SemaphoreType.DMA((2 + 2 * (nz - 2),)),
            ],
            compiler_params=roomy,
        )(
            flat(pert), flat(mean), flat(mode), inner, second_got, result,
            *relay_got, *[flat(b) for b in nb_got],
        )
    return jnp.swapaxes(out.reshape(per, 2, 4, nz, nx, ny), 3, 4)


def solution(mesh):
    return jax.shard_map(
        shards,
        mesh=mesh,
        in_specs=(
            P("harm", None, None, "gx", "gz", None),
            P(None, "gx", "gz", None),
            P(None, None, None, "gx", "gz", None),
            P("gx", "gz", None),
        ),
        out_specs=P("harm", None, None, "gx", "gz", None),
        check_vma=False,
    )
```

```python
import jax
import jax.numpy as jnp
from jax import lax
from jax.experimental import pallas as pl
from jax.experimental.pallas import tpu as pltpu
from jax.sharding import PartitionSpec as P

FREQUENCY_STEP = 0.2
VISCOSITY = 0.05
PENALTY = 4.0
FIRST = {-2: 1.0, -1: -8.0, 1: 8.0, 2: -1.0}
SECOND = {-2: -1.0, -1: 16.0, 0: -30.0, 1: 16.0, 2: -1.0}
HALO_X = 16
VMEM_BYTES = 58 * 1024 * 1024
ANY = pl.BlockSpec(memory_space=pl.ANY)
VMEM = pl.BlockSpec(memory_space=pltpu.VMEM)
HBM = pl.BlockSpec(memory_space=pltpu.HBM)


def taps(delta, table):
    out = jnp.zeros(delta.shape, jnp.float32)
    for step, weight in table.items():
        out = jnp.where(delta == step, weight, out)
    return out


def iotas(rows, columns):
    return lax.broadcasted_iota(jnp.int32, (rows, 1), 0), lax.broadcasted_iota(jnp.int32, (1, columns), 1)


def column_cells(column, nz, nx):
    shift, own = nx.bit_length() - 1, nz * nx
    halo = column - own
    after = halo >= HALO_X
    edge = jnp.where(after, halo - HALO_X, halo)
    inside = column < own
    z = jnp.where(inside, column >> shift, edge >> 1)
    x = jnp.where(inside, column & (nx - 1), (edge & 1) + jnp.where(after, nx, -2))
    return z, x


def slope_matrix(part, z, x, to_z, to_x):
    dz, dx = to_z - z, to_x - x
    if part == 0:
        return jnp.where(dz == 0, taps(dx, FIRST), 0.0)
    if part == 1:
        return jnp.where(dx == 0, taps(dz, FIRST), 0.0)
    return jnp.where(dz == 0, taps(dx, SECOND), 0.0) + jnp.where(dx == 0, taps(dz, SECOND), 0.0)


def store_walls(walls_ref, ny):
    row, column = iotas(ny, ny)
    first, second = (taps(row - column, table).astype(jnp.bfloat16) for table in (FIRST, SECOND))
    for i, (block, sign) in enumerate(((first, 1), (first, -1), (second, 1), (second, -1))):
        if i * ny < walls_ref.shape[1]:
            walls_ref[:ny, i * ny : (i + 1) * ny] = block
            if walls_ref.shape[0] > ny:
                walls_ref[ny:, i * ny : (i + 1) * ny] = block if sign > 0 else -block


def run_copies(copies, sems):
    started = [pltpu.make_async_copy(src, dst, sems.at[i]) for i, (src, dst) in enumerate(copies)]
    for copy in started:
        copy.start()
    for copy in started:
        copy.wait()


def shards(perturbation, base_mean, base_modes, solid_mask):
    per, modes = perturbation.shape[0], base_modes.shape[0]
    nx, nz, ny = perturbation.shape[3], perturbation.shape[4], perturbation.shape[5]
    own = nz * nx
    bf16, f32 = jnp.bfloat16, jnp.float32
    harms, size_x, size_z = (lax.axis_size(a) for a in ("harm", "gx", "gz"))
    swap = harms == 2
    sides = 1 if swap else 2
    n_pert, n_mean, n_modes = per * 8, 3, modes * 6
    n_base = n_mean + n_modes
    n_res = n_pert + n_base
    n_nb = modes * 6
    n_all = n_res + sides * n_nb

    pert = jnp.swapaxes(perturbation, 3, 4).reshape(n_pert, nz, nx, ny)
    mean = jnp.swapaxes(base_mean, 1, 2)
    mode = jnp.swapaxes(base_modes, 3, 4).reshape(n_modes, nz, nx, ny)
    mask = jnp.swapaxes(solid_mask, 0, 1).reshape(own, ny)

    def place():
        me_h, odd = lax.axis_index("harm"), lax.rem(lax.axis_index("gz"), 2)
        shared = jnp.where(me_h == 0, per - modes, 0) if swap else 0
        return me_h, odd, odd * (nz - 2), (1 - odd) * (nz - 2), shared

    cross_pairs = [(i, (i + 1) % size_z if i % 2 else (i - 1) % size_z) for i in range(size_z)]
    near_pairs = [(i, i + 1 if i % 2 == 0 else i - 1) for i in range(size_z)]
    up_x = [(i, (i + 1) % size_x) for i in range(size_x)]
    down_x = [(j, i) for i, j in up_x]
    if swap:
        harm_perms = [[(0, 1), (1, 0)]]
    else:
        up_h = [(i, i + 1) for i in range(harms - 1)]
        harm_perms = [up_h, [(j, i) for i, j in up_h]]
    def sent(s, scal):
        return scal[4] if swap else (per - modes if s == 0 else 0)

    face = lambda n: jax.ShapeDtypeStruct((n, 2, nx, ny), bf16)
    roomy = pltpu.CompilerParams(vmem_limit_bytes=32 * 1024 * 1024)

    used = 2 * nz
    spare = HALO_X - used
    tiles = 3 * (-(-n_res // 4))

    def edge_tile(ref, f):
        group, i = divmod(f, 4)
        if i < 3:
            return ref[3 * group + i]
        parts = [ref[3 * group + j].astype(f32)[used:] for j in range(3)]
        return jnp.concatenate(parts + [jnp.zeros((spare, ny), f32)], axis=0).astype(bf16)

    def pack(pert_any, mean_any, mode_any, first_any, second_any, lo_any, hi_any, *rest):
        nb_anys = rest[:sides]
        pert_ref, mean_ref, mode_ref, lo_ref, hi_ref, in_sems, out_sems = rest[sides:]
        scal = place()
        z = pl.ds(scal[2], 2)
        loads = [(pert_any.at[pl.ds(8 * l, 8)], pert_ref.at[pl.ds(8 * l, 8)]) for l in range(per)]
        loads += [(mean_any, mean_ref), (mode_any, mode_ref)]
        loads = [pltpu.make_async_copy(src, dst, in_sems.at[i]) for i, (src, dst) in enumerate(loads)]
        for copy in loads:
            copy.start()
        out = []

        def send(src, dst):
            out.append(pltpu.make_async_copy(src, dst, out_sems.at[len(out)]))
            out[-1].start()

        row, column = iotas(2 * HALO_X, own)
        low = row < HALO_X
        row = jnp.where(low, row, row - HALO_X)
        target = (row >> 1) * nx + (row & 1) + jnp.where(low, 0, nx - 2)
        pick = jnp.where(column == target, 1.0, 0.0).astype(bf16)
        where = [(pert_ref, f) for f in range(n_pert)] + [(mean_ref, f) for f in range(n_mean)] + [(mode_ref, f) for f in range(n_modes)]

        def edges(group):
            got = []
            for f in range(4 * group, min(4 * group + 4, n_res), 2):
                mine = [ref[i].reshape(own, ny) for ref, i in where[f : min(f + 2, n_res)]]
                both = jnp.concatenate(mine, axis=1) if len(mine) == 2 else mine[0]
                both = jnp.dot(pick, both, preferred_element_type=f32)
                got += [both[:, i * ny : (i + 1) * ny] for i in range(len(mine))]
            if len(got) == 3:
                got.append(jnp.zeros((2 * HALO_X, ny), f32))
            for i in range(3):
                for ref, at in ((lo_ref, 0), (hi_ref, HALO_X)):
                    extra = got[3][at + spare * i : at + spare * (i + 1)]
                    ref[3 * group + i] = jnp.concatenate([got[i][at : at + used], extra], axis=0).astype(bf16)

        for l in range(per):
            loads[l].wait()
            mine = pl.ds(8 * l, 8)
            send(pert_ref.at[mine, z], first_any.at[mine])
        for s, nb_any in enumerate(nb_anys):
            for i in range(modes * 2):
                send(pert_ref.at[pl.ds(sent(s, scal) * 8 + 4 * i, 3)], nb_any.at[pl.ds(3 * i, 3)])
        for group in range(n_pert // 4):
            edges(group)
        loads[per].wait()
        loads[per + 1].wait()
        send(mean_ref.at[:, z], second_any.at[pl.ds(0, n_mean)])
        send(mode_ref.at[:, z], second_any.at[pl.ds(n_mean, n_modes)])
        for group in range(n_pert // 4, tiles // 3):
            edges(group)
        send(lo_ref, lo_any)
        send(hi_ref, hi_any)
        for copy in out:
            copy.wait()

    edge = jax.ShapeDtypeStruct((tiles, HALO_X, ny), bf16)
    with jax.named_scope("pack"):
        first, second, edge_lo, edge_hi, *nb_send = pl.pallas_call(
            pack,
            out_shape=(face(n_pert), face(n_base), edge, edge) + tuple(jax.ShapeDtypeStruct((n_nb, nz, nx, ny), bf16) for _ in range(sides)),
            in_specs=[HBM] * 3,
            out_specs=(ANY,) * (4 + sides),
            scratch_shapes=[
                pltpu.VMEM((n_pert, nz, nx, ny), bf16),
                pltpu.VMEM((n_mean, nz, nx, ny), bf16),
                pltpu.VMEM((n_modes, nz, nx, ny), bf16),
                pltpu.VMEM((tiles, HALO_X, ny), bf16),
                pltpu.VMEM((tiles, HALO_X, ny), bf16),
                pltpu.SemaphoreType.DMA((per + 2,)),
                pltpu.SemaphoreType.DMA((per + sides * modes * 2 + 4,)),
            ],
            compiler_params=pltpu.CompilerParams(vmem_limit_bytes=VMEM_BYTES),
        )(pert, mean, mode)
    first_got = lax.ppermute(first, "gz", cross_pairs)
    nb_got = [lax.ppermute(b, "harm", p) for b, p in zip(nb_send, harm_perms)]
    xb_got = lax.ppermute(edge_hi, "gx", up_x)
    xa_got = lax.ppermute(edge_lo, "gx", down_x)
    second_got = lax.ppermute(second, "gz", cross_pairs)

    PAIRS = ((0, 3), (1, 2))
    DRIFT = (-1.5 * FREQUENCY_STEP, -0.5 * FREQUENCY_STEP)

    def entries(t, p, q, r, s):
        return t, q, p + r, p - r, q + s, s - q, t + p, t - p

    def couple(acc, ent, vec):
        t, q, pr, pmr, qs, sq, tp, tmp = ent
        out = []
        for i in range(2):
            a, e, b, g = (vec[j][i] for j in range(4))
            out.append(
                (
                    acc[0][i] + t * a + pr * b + sq * g,
                    acc[1][i] + t * e + qs * b + pmr * g,
                    acc[2][i] + pr * a + qs * e + tp * b + q * g,
                    acc[3][i] + sq * a + pmr * e + q * b + tmp * g,
                )
            )
        return [(out[0][j], out[1][j]) for j in range(4)]

    def harmonics_of(acc, scale):
        out = [None] * 4
        for at, (lo, hi) in enumerate(PAIRS):
            (ar, ai), (er, ei) = acc[2 * at], acc[2 * at + 1]
            out[lo] = ((ar + ei) * scale, (ai - er) * scale)
            out[hi] = ((ar - ei) * scale, (ai + er) * scale)
        return out

    def basis_of(values):
        out = []
        for lo, hi in PAIRS:
            (lr, li), (hr, hi_) = values[lo], values[hi]
            out += [(lr + hr, li + hi_), (hi_ - li, lr - hr)]
        return out

    def rhs(ref, fields):
        cols = [ref[f] for f in fields]
        return cols[0] if len(cols) == 1 else jnp.concatenate(cols, axis=1)

    def dot(a, b):
        return jnp.dot(a, b, preferred_element_type=f32)

    def resident_slopes(pert_ref, grads, plain, lin, rows_ref, walls_ref):
        me_h = place()[0]
        row, column = iotas(own, own)
        to_z, to_x = column_cells(column, nz, nx)
        for i in range(3):
            rows_ref[i * own : (i + 1) * own] = slope_matrix(i, row >> nx.bit_length() - 1, row & (nx - 1), to_z, to_x).astype(bf16)
        store_walls(walls_ref, ny)
        mean_freq = 12.0 * FREQUENCY_STEP * (me_h * per + 1.5 - per * harms / 2).astype(f32)

        for at, (lo, hi) in enumerate(PAIRS):
            for i in range(2):
                fl, fr = lo * 8 + i * 4 + 3, hi * 8 + i * 4 + 3
                got = dot(rows_ref[: 2 * own], rhs(pert_ref, (fl, fr)))
                wall = dot(rhs(pert_ref, (fl, fr)), walls_ref[:, : 2 * ny])
                for d in range(3):
                    if d == 1:
                        total, diff = wall[:, :ny], wall[:, ny:]
                    else:
                        span = slice(0, own) if d == 0 else slice(own, 2 * own)
                        total, diff = got[span, :ny] + got[span, ny:], got[span, :ny] - got[span, ny:]
                    lin[2 * at, i, d] = total
                    lin[2 * at + 1, 1 - i, d] = diff if i == 0 else -diff
        for at, (lo, hi) in enumerate(PAIRS):
            for c in range(3):
                for i in range(2):
                    sign = 1.0 if i == 0 else -1.0
                    fl, fr = lo * 8 + i * 4 + c, hi * 8 + i * 4 + c
                    got = dot(rows_ref[...], rhs(pert_ref, (fl, fr)))
                    xl, xr = pert_ref[fl].astype(f32), pert_ref[fr].astype(f32)
                    wall = dot(rhs(pert_ref, (fl, fr)), walls_ref[...])
                    total, diff = xl + xr, xl - xr
                    plain[2 * at, i, c] = total
                    plain[2 * at + 1, 1 - i, c] = sign * diff
                    for d in range(3):
                        if d == 1:
                            gt, gd = wall[:, :ny], wall[:, ny : 2 * ny]
                        else:
                            span = slice(0, own) if d == 0 else slice(own, 2 * own)
                            gt, gd = got[span, :ny] + got[span, ny:], got[span, :ny] - got[span, ny:]
                        gd = sign * gd
                        grads[2 * at, i, c, d] = gt
                        grads[2 * at + 1, 1 - i, c, d] = gd
                        if d == c:
                            if c == 0:
                                lin[2 * at, i, 3] = gt
                                lin[2 * at + 1, 1 - i, 3] = gd
                            else:
                                lin[2 * at, i, 3] = lin[2 * at, i, 3] + gt
                                lin[2 * at + 1, 1 - i, 3] = lin[2 * at + 1, 1 - i, 3] + gd
                    lt = got[2 * own :, :ny] + got[2 * own :, ny:] + wall[:, 2 * ny : 3 * ny]
                    ld = got[2 * own :, :ny] - got[2 * own :, ny:] + wall[:, 3 * ny :]
                    drift = 12.0 * DRIFT[at]
                    lin[2 * at, i, c] = lin[2 * at, i, c] - VISCOSITY * lt
                    lin[2 * at + 1, 1 - i, c] = lin[2 * at + 1, 1 - i, c] - sign * VISCOSITY * ld
                    lin[2 * at, 1 - i, c] = lin[2 * at, 1 - i, c] + sign * (mean_freq * total + drift * diff)
                    lin[2 * at + 1, i, c] = lin[2 * at + 1, i, c] - (mean_freq * diff + drift * total)

    def resident(mean_ref, mode_ref, grads, plain, lin, out_ref, ents, rows_ref, walls_ref):
        row, column = iotas(own, own)
        to_z, to_x = column_cells(column, nz, nx)
        for i in range(2):
            rows_ref[i * own : (i + 1) * own] = slope_matrix(i, row >> nx.bit_length() - 1, row & (nx - 1), to_z, to_x).astype(bf16)
        store_walls(walls_ref, ny)
        for c in range(3):
            picked = [mean_ref[c].astype(f32)] + [mode_ref[3 * i + c].astype(f32) for i in range(4)]
            for n, ent in enumerate(entries(*picked)):
                ents[c, n] = ent
            mean_at = dot(rows_ref[...], rhs(mean_ref, (c,)))
            mean_wall = dot(mean_ref[c], walls_ref[:ny, :ny])
            real = dot(rows_ref[...], rhs(mode_ref, (c, 6 + c)))
            imag = dot(rows_ref[...], rhs(mode_ref, (3 + c, 9 + c)))
            wall_real = dot(rhs(mode_ref, (c, 6 + c)), walls_ref[:, : 2 * ny])
            wall_imag = dot(rhs(mode_ref, (3 + c, 9 + c)), walls_ref[:, : 2 * ny])
            for d in range(3):
                if d == 1:
                    pr, pmr = wall_real[:, :ny], wall_real[:, ny:]
                    qs, qms = wall_imag[:, :ny], wall_imag[:, ny:]
                    t, p, q = mean_wall, 0.5 * (pr + pmr), 0.5 * (qs + qms)
                    values = (t, q, pr, pmr, qs, -qms, t + p, t - p)
                else:
                    span = slice(0, own) if d == 0 else slice(own, 2 * own)
                    values = entries(mean_at[span], real[span, :ny], imag[span, :ny], real[span, ny:], imag[span, ny:])
                for n, ent in enumerate(values):
                    ents[3 + 3 * d + c, n] = ent

        def block(b, carry):
            rows = pl.ds(pl.multiple_of(b * 8, 8), 8)
            accs = [[(lin[j, 0, c, rows], lin[j, 1, c, rows]) for j in range(4)] for c in range(4)]
            for d in range(3):
                flow = [ents[d, n, rows] for n in range(8)]
                for c in range(3):
                    accs[c] = couple(accs[c], flow, [(grads[j, 0, c, d, rows], grads[j, 1, c, d, rows]) for j in range(4)])
                along = [(plain[j, 0, d, rows], plain[j, 1, d, rows]) for j in range(4)]
                for c in range(3):
                    slope = [ents[3 + 3 * d + c, n, rows] for n in range(8)]
                    accs[c] = couple(accs[c], slope, along)
            for c in range(4):
                for k, (re, im) in enumerate(harmonics_of(accs[c], 1.0 / 24.0)):
                    out_ref[k * 8 + c, rows] = re
                    out_ref[k * 8 + 4 + c, rows] = im
            return carry

        lax.fori_loop(0, own // 8, block, 0, unroll=4)

    flat = lambda a: a.reshape(a.shape[0], -1, ny)
    with jax.named_scope("resident_slopes"):
        slopes = pl.pallas_call(
            resident_slopes,
            out_shape=tuple(jax.ShapeDtypeStruct(n + (own, ny), f32) for n in ((4, 2, 3, 3), (4, 2, 3), (4, 2, 4))),
            scratch_shapes=[pltpu.VMEM((3 * own, own), bf16), pltpu.VMEM((2 * ny, 4 * ny), bf16)],
            compiler_params=pltpu.CompilerParams(vmem_limit_bytes=20 * 1024 * 1024),
        )(flat(pert))
    with jax.named_scope("resident"):
        whole = pl.pallas_call(
            resident,
            out_shape=jax.ShapeDtypeStruct((n_pert, own, ny), f32),
            scratch_shapes=[
                pltpu.VMEM((12, 8, own, ny), f32),
                pltpu.VMEM((2 * own, own), bf16),
                pltpu.VMEM((2 * ny, 2 * ny), bf16),
            ],
            compiler_params=roomy,
        )(flat(mean), flat(mode), *slopes)

    base_modes_at = n_pert + n_mean
    ends = 16 * nz

    def edge_taps(tables):
        row, column = iotas(ends, own + 2 * HALO_X)
        last = row >= 8 * nz
        row = jnp.where(last, row - 8 * nz, row)
        to_z, to_x = column_cells(column, nz, nx)
        dz, dx = to_z - (row >> 3), to_x - (row & 7) - jnp.where(last, nx - 8, 0)
        return jnp.concatenate([jnp.where(dz == 0, taps(dx, table), 0.0)[:, own:] for table in tables], axis=0).astype(bf16)

    def add_edges(pert_ref, mean_ref, mode_ref, xb_ref, xa_ref, _, out_ref, vecs, lins, bends):
        taps_of = edge_taps((FIRST, SECOND))

        def bent(fields, lap):
            cols = [jnp.concatenate([edge_tile(xb_ref, f), edge_tile(xa_ref, f)], axis=0) for f in fields]
            both = cols[0] if len(cols) == 1 else jnp.concatenate(cols, axis=1)
            got = jnp.dot(taps_of if lap else taps_of[:ends], both, preferred_element_type=f32)
            return [(got[:ends, i * ny : (i + 1) * ny], got[ends:, i * ny : (i + 1) * ny]) for i in range(len(fields))]

        for at, (lo, hi) in enumerate(PAIRS):
            for i in range(2):
                sign = 1.0 if i == 0 else -1.0
                for c in range(4):
                    (gl, ll), (gr, lr) = bent((lo * 8 + 4 * i + c, hi * 8 + 4 * i + c), c < 3)
                    if c < 3:
                        vecs[2 * at, i, c] = gl + gr
                        vecs[2 * at + 1, 1 - i, c] = sign * (gl - gr)
                        lins[2 * at, i, c] = -VISCOSITY * (ll + lr)
                        lins[2 * at + 1, 1 - i, c] = (-VISCOSITY * sign) * (ll - lr)
                    else:
                        lins[2 * at, i, 0] = lins[2 * at, i, 0] + (gl + gr)
                        lins[2 * at + 1, 1 - i, 0] = lins[2 * at + 1, 1 - i, 0] + sign * (gl - gr)
        for c in range(3):
            at = base_modes_at + c
            (t, _), = bent((n_pert + c,), False)
            (p, _), (r, _) = bent((at, at + 6), False)
            (q, _), (s_, _) = bent((at + 3, at + 9), False)
            for n, ent in enumerate(entries(t, p, q, r, s_)):
                bends[c, n] = ent

        def layer_ends(z, carry):
            for end in range(2):
                strip = pl.ds(pl.multiple_of(z * nx + end * (nx // 2), 16), 16)
                keep = slice(8 * end, 8 * end + 8)
                mine = pl.ds(pl.multiple_of((end * nz + z) * 8, 8), 8)

                def read(ref, f):
                    return ref[f, strip].astype(f32)[keep]

                flow = entries(read(mean_ref, 0), *[read(mode_ref, 3 * i) for i in range(4)])
                along = basis_of([(read(pert_ref, l * 8), read(pert_ref, l * 8 + 4)) for l in range(per)])
                for c in range(4):
                    if c < 3:
                        acc = [(lins[j, 0, c, mine], lins[j, 1, c, mine]) for j in range(4)]
                        acc = couple(acc, flow, [(vecs[j, 0, c, mine], vecs[j, 1, c, mine]) for j in range(4)])
                        acc = couple(acc, [bends[c, n, mine] for n in range(8)], along)
                    else:
                        acc = [(vecs[j, 0, 0, mine], vecs[j, 1, 0, mine]) for j in range(4)]
                    for k, parts in enumerate(harmonics_of(acc, 1.0 / 24.0)):
                        for i in range(2):
                            out_ref[k * 8 + 4 * i + c, mine] = parts[i]
            return carry

        lax.fori_loop(0, nz, layer_ends, 0, unroll=2)

    with jax.named_scope("edges"):
        edged = pl.pallas_call(
            add_edges,
            out_shape=jax.ShapeDtypeStruct((n_pert, ends, ny), f32),
            in_specs=[VMEM] * 5 + [ANY],
            scratch_shapes=[
                pltpu.VMEM((4, 2, 3, ends, ny), f32),
                pltpu.VMEM((4, 2, 3, ends, ny), f32),
                pltpu.VMEM((3, 8, ends, ny), f32),
            ],
            compiler_params=roomy,
        )(flat(pert), flat(mean), flat(mode), xb_got, xa_got, whole)

    faces_deep = n_nb * 2 * nx
    nb_tiles = 3 * n_nb // 4
    deep = faces_deep + 2 * nb_tiles * HALO_X

    def nb_tile(ref, after, f):
        group, i = divmod(f, 4)
        at = [faces_deep + (after * nb_tiles + 3 * group + j) * HALO_X for j in range(3)]
        if i < 3:
            return ref[at[i] : at[i] + HALO_X]
        parts = [ref[row : row + HALO_X].astype(f32)[used:] for row in at]
        return jnp.concatenate(parts + [jnp.zeros((spare, ny), f32)], axis=0).astype(bf16)

    def pack_relay(first_ref, xb_ref, xa_ref, _, *outs):
        scal = place()
        for s, out in enumerate(outs):
            for i in range(modes * 2):
                group = sent(s, scal) * 2 + i
                for c in range(3):
                    at = (3 * i + c) * 2 * nx
                    out[at : at + 2 * nx] = first_ref[group * 4 + c].reshape(2 * nx, ny)
            for after, ref in enumerate((xb_ref, xa_ref)):
                for group in range(n_nb // 4):
                    rows = []
                    for f in range(4 * group, 4 * group + 4):
                        rows.append(ref[(sent(s, scal) * 2 + f // 3) * 3 + f % 3].astype(f32))
                    for i in range(3):
                        at = faces_deep + (after * nb_tiles + 3 * group + i) * HALO_X
                        tile = jnp.concatenate([rows[i][:used], rows[3][spare * i : spare * (i + 1)]], axis=0)
                        out[at : at + HALO_X] = tile.astype(bf16)

    with jax.named_scope("pack_relay"):
        relay = pl.pallas_call(
            pack_relay,
            out_shape=tuple(jax.ShapeDtypeStruct((deep, ny), bf16) for _ in range(sides)),
            in_specs=[VMEM] * 3 + [ANY],
            compiler_params=roomy,
        )(first_got, xb_got, xa_got, edged)
    relay_got = [lax.ppermute(b, "harm", p) for b, p in zip(relay, harm_perms)]

    def pack_near(pert_ref, mean_ref, mode_ref, *rest):
        out = rest[-1]
        z = pl.ds(place()[3], 2)
        out[:n_pert] = pert_ref[:, z]
        out[n_pert : n_pert + n_mean] = mean_ref[:, z]
        out[n_pert + n_mean : n_res] = mode_ref[:, z]
        for s in range(sides):
            out[n_res + s * n_nb : n_res + (s + 1) * n_nb] = rest[s][:, z]

    with jax.named_scope("pack_near"):
        near = pl.pallas_call(
            pack_near,
            out_shape=face(n_all),
            in_specs=[VMEM] * (3 + sides) + [ANY],
            compiler_params=roomy,
        )(pert, mean, mode, *nb_got, relay[0])
    near_got = lax.ppermute(near, "gz", near_pairs)

    below, above = [], []
    for k in range(per):
        for m in range(-modes, modes + 1):
            l = k - m
            if l < 0:
                below.append((k, m, 0, (l + modes) * 6))
            elif l >= per:
                above.append((k, m, sides - 1, (l - per) * 6))

    def on_sides(work):
        me_h = lax.axis_index("harm")
        pl.when(me_h > 0)(lambda: work(below))
        pl.when(me_h < harms - 1)(lambda: work(above))

    def product(acc, flow, value, m):
        (fr, fi), (vr, vi) = flow, value
        if m > 0:
            return acc[0] + fr * vr - fi * vi, acc[1] + fr * vi + fi * vr
        return acc[0] + fr * vr + fi * vi, acc[1] + fr * vi - fi * vr


    def face_place(cross, step):
        odd = place()[1]
        before = (odd == 0) if cross else (odd == 1)
        return before, jnp.where(before, step, nz - 1 - step), jnp.where(before, 1, 0)

    def faces(out_ref, mean_ref, mode_ref, pert_ref, nb_refs, first_ref, second_ref, near_ref, relay_refs, step, lowest=0):
        cross = near_ref is None
        before, layer, near_at = face_place(cross, step)
        turn = jnp.where(before, 1.0, -1.0)

        def mix(pair):
            return pair[1] - 8.0 * pair[0] if step == 0 else pair[0]

        def mix_lap(pair):
            return pair[1] - 16.0 * pair[0] if step == 0 else pair[0]

        def chunk_work(chunk, carry):
            rows = pl.ds(pl.multiple_of(layer * nx + chunk * 16, 16), 16)
            out_rows = pl.ds(pl.multiple_of((layer - lowest) * nx + chunk * 16, 16), 16)
            strip = pl.ds(pl.multiple_of(chunk * 16, 16), 16)

            def halos(f):
                if not cross:
                    ref, at = near_ref, f
                elif f < n_pert:
                    ref, at = first_ref, f
                else:
                    ref, at = second_ref, f - n_pert
                return ref[at, near_at, strip].astype(f32), (ref[at, 1 - near_at, strip].astype(f32) if step == 0 else None)

            def nb_halos(s, f):
                if not cross:
                    return halos(n_res + s * n_nb + f)
                at = [pl.ds(pl.multiple_of((2 * f + j) * nx + chunk * 16, 16), 16) for j in (near_at, 1 - near_at)]
                return tuple(relay_refs[s][r].astype(f32) for r in at)

            velocity, base = first_ref is not None or not cross, second_ref is not None or not cross
            if velocity:
                flow = entries(mean_ref[2, rows].astype(f32), *[mode_ref[3 * i + 2, rows].astype(f32) for i in range(4)])
            if base:
                along = basis_of([(pert_ref[l * 8 + 2, rows].astype(f32), pert_ref[l * 8 + 6, rows].astype(f32)) for l in range(per)])
            for c in range(4 if velocity else 3):
                acc = [(0.0, 0.0)] * 4
                if velocity and c < 3:
                    got = [[halos(l * 8 + 4 * i + c) for i in range(2)] for l in range(per)]
                    vec = basis_of([(mix(g[0]), mix(g[1])) for g in got])
                    lap = basis_of([(mix_lap(g[0]), mix_lap(g[1])) for g in got])
                    if c == 2:
                        acc = basis_of([(mix(halos(l * 8 + 3)), mix(halos(l * 8 + 7))) for l in range(per)])
                    acc = couple(acc, flow, vec)
                if base and c < 3:
                    bend = entries(mix(halos(n_pert + c)), *[mix(halos(base_modes_at + 3 * i + c)) for i in range(4)])
                    acc = couple(acc, bend, along)
                if c == 3:
                    acc = vec
                if velocity and c < 3:
                    acc = [tuple(turn * a + VISCOSITY * v for a, v in zip(*pair)) for pair in zip(acc, lap)]
                else:
                    acc = [tuple(turn * a for a in pair) for pair in acc]
                for k, parts in enumerate(harmonics_of(acc, 1.0 / 24.0)):
                    for i in range(2):
                        at = k * 8 + 4 * i + c
                        out_ref[at, out_rows] = out_ref[at, out_rows] + parts[i]

            def nb_work(pairs):
                for k in sorted({p[0] for p in pairs}):
                    zero = jnp.zeros((16, ny), f32)
                    for c in range(3):
                        acc = (zero, zero)
                        for _, m, s, f in [p for p in pairs if p[0] == k]:
                            at = (abs(m) - 1) * 6
                            mine = tuple(mode_ref[at + 3 * i + 2, rows].astype(f32) for i in range(2))
                            acc = product(acc, mine, tuple(mix(nb_halos(s, f + 3 * i + c)) for i in range(2)), m)
                            bent = tuple(mix(halos(base_modes_at + at + 3 * i + c)) for i in range(2))
                            carried = tuple(nb_refs[s][f + 3 * i + 2, rows].astype(f32) for i in range(2))
                            acc = product(acc, bent, carried, m)
                        for i in range(2):
                            at = k * 8 + 4 * i + c
                            out_ref[at, out_rows] = out_ref[at, out_rows] + (turn * (1.0 / 12.0)) * acc[i]

            if base:
                on_sides(nb_work)
            return carry

        lax.fori_loop(0, nx // 16, chunk_work, 0, unroll=True)

    def neighbours(mask_ref, pert_ref, mean_ref, mode_ref, xb_ref, xa_ref, whole_ref, edged_ref, first_ref, near_ref, *rest):
        nb_refs = rest[:sides]
        out_any, out_ref, grads, plain, stencil_ref, walls_ref, sems = rest[-7:]
        row, column = iotas(own, own + 2 * HALO_X)
        to_z, to_x = column_cells(column, nz, nx)
        for i in range(2):
            stencil_ref[i * own : (i + 1) * own] = slope_matrix(i, row >> nx.bit_length() - 1, row & (nx - 1), to_z, to_x).astype(bf16)
        store_walls(walls_ref, ny)

        def slopes(at, mine, halo):
            both = jnp.concatenate(mine, axis=1)
            rows = both if halo is None else jnp.concatenate([both, halo], axis=0)
            got = jnp.dot(stencil_ref[:, : rows.shape[0]], rows, preferred_element_type=f32)
            wall = [jnp.dot(x, walls_ref[:ny, :ny], preferred_element_type=f32) for x in mine]
            for i in range(2):
                lanes = slice(i * ny, (i + 1) * ny)
                grads[at + i, 0] = got[:own, lanes]
                grads[at + i, 2] = got[own:, lanes]
                grads[at + i, 1] = wall[i]
                plain[at + i] = mine[i].astype(f32)

        for f in range(0, n_modes, 2):
            at = base_modes_at + f
            halo = [jnp.concatenate([edge_tile(ref, at), edge_tile(ref, at + 1)], axis=1) for ref in (xb_ref, xa_ref)]
            slopes(f, [mode_ref[f], mode_ref[f + 1]], jnp.concatenate(halo, axis=0))
        for s in range(sides):
            for f in range(0, n_nb, 2):
                slopes(n_modes + s * n_nb + f, [nb_refs[s][f], nb_refs[s][f + 1]], None)

        for z in range(nz):
            rows = slice(z * nx, (z + 1) * nx)
            solid = PENALTY * mask_ref[rows].astype(f32)
            for f in range(n_pert):
                if f % 4 < 3:
                    out_ref[f, rows] = whole_ref[f, rows] + solid * pert_ref[f, rows].astype(f32)
                else:
                    out_ref[f, rows] = whole_ref[f, rows]
            for end in range(2):
                rows = slice(z * nx + end * (nx - 8), z * nx + end * (nx - 8) + 8)
                mine = slice((end * nz + z) * 8, (end * nz + z + 1) * 8)
                out_ref[:, rows] = out_ref[:, rows] + edged_ref[:, mine]

        def work(pairs):
            def block(b, carry):
                rows = pl.ds(pl.multiple_of(b * 8, 8), 8)
                for k in sorted({p[0] for p in pairs}):
                    zero = jnp.zeros((8, ny), f32)
                    acc = [(zero, zero)] * 3
                    for _, m, s, f in [p for p in pairs if p[0] == k]:
                        at, base = n_modes + s * n_nb + f, (abs(m) - 1) * 6
                        for d in range(3):
                            flow = plain[base + d, rows], plain[base + 3 + d, rows]
                            along = plain[at + d, rows], plain[at + 3 + d, rows]
                            for c in range(3):
                                slope = grads[base + c, d, rows], grads[base + 3 + c, d, rows]
                                grad = grads[at + c, d, rows], grads[at + 3 + c, d, rows]
                                acc[c] = product(acc[c], flow, grad, m)
                                acc[c] = product(acc[c], slope, along, m)
                    for c in range(3):
                        for i in range(2):
                            at = k * 8 + 4 * i + c
                            out_ref[at, rows] = out_ref[at, rows] + acc[c][i] * (1.0 / 12.0)
                return carry

            lax.fori_loop(0, own // 8, block, 0, unroll=2)

        on_sides(work)
        sends = []

        def send(layer):
            rows = pl.ds(pl.multiple_of(layer * nx, nx), nx)
            sends.append(pltpu.make_async_copy(out_ref.at[:, rows], out_any.at[:, rows], sems.at[len(sends)]))
            sends[-1].start()

        for layer in range(2, nz - 2):
            send(layer)
        for step in range(2):
            faces(out_ref, mean_ref, mode_ref, pert_ref, nb_refs, None, None, near_ref, None, step)
            send(face_place(False, step)[1])
        for step in range(2):
            faces(out_ref, mean_ref, mode_ref, pert_ref, nb_refs, first_ref, None, None, None, step)
        for copy in sends:
            copy.wait()

    n_ext = n_modes + sides * n_nb
    with jax.named_scope("neighbours"):
        result, inner = pl.pallas_call(
            neighbours,
            out_shape=(jax.ShapeDtypeStruct((n_pert, own, ny), f32),) * 2,
            out_specs=(HBM, VMEM),
            scratch_shapes=[
                pltpu.VMEM((n_ext, 3, own, ny), f32),
                pltpu.VMEM((n_ext, own, ny), f32),
                pltpu.VMEM((2 * own, own + 2 * HALO_X), bf16),
                pltpu.VMEM((ny, ny), bf16),
                pltpu.SemaphoreType.DMA((nz - 2,)),
            ],
            compiler_params=roomy,
        )(mask, flat(pert), flat(mean), flat(mode), xb_got, xa_got, whole, edged, first_got, near_got, *[flat(b) for b in nb_got])

    n_keys = n_pert // 2 if swap else n_pert

    def finish(pert_ref, mean_ref, mode_ref, inner_ref, second_ref, _, *rest):
        relay_refs, nb_refs = rest[:sides], rest[sides : 2 * sides]
        out_any, done, fringe, bends, sems = rest[2 * sides :]
        half = nx // 2
        keys = jnp.where(lax.axis_index("harm") == 0, n_pert - n_keys, 0) if swap else 0
        inner_layer = jnp.where(face_place(True, 0)[0], 2, 0)
        taps_of = edge_taps((FIRST,))
        sends = []

        def send(src, dst):
            sends.append(pltpu.make_async_copy(src, dst, sems.at[len(sends)]))
            sends[-1].start()

        for s in range(sides):
            for f in range(0, n_nb, 2):
                both = [jnp.concatenate([nb_tile(relay_refs[s], after, f + i) for after in range(2)], axis=0) for i in range(2)]
                both = jnp.concatenate(both, axis=1)
                got = jnp.dot(taps_of, both, preferred_element_type=f32)
                for i in range(2):
                    bends[s * n_nb + f + i] = got[:, i * ny : (i + 1) * ny]

        def edge_terms(pairs, z, end, add):
            strip = pl.ds(pl.multiple_of(z * nx + end * half, 16), 16)
            keep = slice(8 * end, 8 * end + 8)
            bent = pl.ds(pl.multiple_of((end * nz + z) * 8, 8), 8)
            for k in sorted({p[0] for p in pairs}):
                zero = jnp.zeros((8, ny), f32)
                acc = [(zero, zero)] * 3
                for _, m, s, f in [p for p in pairs if p[0] == k]:
                    base = (abs(m) - 1) * 6
                    flow = tuple(mode_ref[base + 3 * i, strip].astype(f32)[keep] for i in range(2))
                    for c in range(3):
                        at = s * n_nb + f + c
                        acc[c] = product(acc[c], flow, (bends[at, bent], bends[at + 3, bent]), m)
                for c in range(3):
                    for i in range(2):
                        add(k, 4 * i + c, acc[c][i] * (1.0 / 12.0))

        def end_rows(z, end):
            return pl.ds(pl.multiple_of(z * nx + end * (nx - 8), 8), 8)

        def other_edges(pairs):
            lowest = min(p[0] for p in pairs) * 8 if swap else 0

            def at_layer(j, carry):
                for end in range(2):

                    def add(k, part, value):
                        at = k * 8 + part - lowest
                        fringe[end, at, j] = fringe[end, at, j] + value

                    edge_terms(pairs, inner_layer + j, end, add)
                return carry

            lax.fori_loop(0, nz - 2, at_layer, 0, unroll=2)

        for j in range(nz - 2):
            for end in range(2):
                fringe[end, :, j] = inner_ref[pl.ds(keys, n_keys), end_rows(inner_layer + j, end)]
        on_sides(other_edges)
        for j in range(nz - 2):
            for end in range(2):
                send(fringe.at[end, :, j], out_any.at[pl.ds(keys, n_keys), end_rows(inner_layer + j, end)])

        first_row = pl.multiple_of(jnp.where(face_place(True, 0)[0], 0, (nz - 2) * nx), nx)
        done[...] = inner_ref[:, pl.ds(first_row, 2 * nx)]
        cross_layer = first_row // nx

        def cross_edges(pairs):
            def at_layer(j, carry):
                for end in range(2):
                    rows = end_rows(j, end)

                    def add(k, part, value):
                        done[k * 8 + part, rows] = done[k * 8 + part, rows] + value

                    edge_terms(pairs, cross_layer + j, end, add)
                return carry

            lax.fori_loop(0, 2, at_layer, 0, unroll=True)

        on_sides(cross_edges)
        for step in range(2):
            faces(done, mean_ref, mode_ref, pert_ref, nb_refs, None, second_ref, None, relay_refs, step, cross_layer)
            layer = face_place(True, step)[1]
            here = pl.ds(pl.multiple_of((layer - cross_layer) * nx, nx), nx)
            send(done.at[:, here], out_any.at[:, pl.ds(pl.multiple_of(layer * nx, nx), nx)])
        for copy in sends:
            copy.wait()

    with jax.named_scope("finish"):
        out = pl.pallas_call(
            finish,
            out_shape=jax.ShapeDtypeStruct((n_pert, own, ny), f32),
            in_specs=[VMEM] * 5 + [HBM] + [VMEM] * (2 * sides),
            out_specs=HBM,
            input_output_aliases={5: 0},
            scratch_shapes=[
                pltpu.VMEM((n_pert, 2 * nx, ny), f32),
                pltpu.VMEM((2, n_keys, nz - 2, 8, ny), f32),
                pltpu.VMEM((sides * n_nb, ends, ny), f32),
                pltpu.SemaphoreType.DMA((2 + 2 * (nz - 2),)),
            ],
            compiler_params=roomy,
        )(
            flat(pert), flat(mean), flat(mode), inner, second_got, result,
            *relay_got, *[flat(b) for b in nb_got],
        )
    return jnp.swapaxes(out.reshape(per, 2, 4, nz, nx, ny), 3, 4)


def solution(mesh):
    return jax.shard_map(
        shards,
        mesh=mesh,
        in_specs=(
            P("harm", None, None, "gx", "gz", None),
            P(None, "gx", "gz", None),
            P(None, None, None, "gx", "gz", None),
            P("gx", "gz", None),
        ),
        out_specs=P("harm", None, None, "gx", "gz", None),
        check_vma=False,
    )
```

```python
import jax
import jax.numpy as jnp
from jax import lax
from jax.experimental import pallas as pl
from jax.experimental.pallas import tpu as pltpu
from jax.sharding import PartitionSpec as P

FREQUENCY_STEP = 0.2
VISCOSITY = 0.05
PENALTY = 4.0
FIRST = {-2: 1.0, -1: -8.0, 1: 8.0, 2: -1.0}
SECOND = {-2: -1.0, -1: 16.0, 0: -30.0, 1: 16.0, 2: -1.0}
HALO_X = 16
VMEM_BYTES = 58 * 1024 * 1024
ANY = pl.BlockSpec(memory_space=pl.ANY)
VMEM = pl.BlockSpec(memory_space=pltpu.VMEM)
HBM = pl.BlockSpec(memory_space=pltpu.HBM)


def taps(delta, table):
    out = jnp.zeros(delta.shape, jnp.float32)
    for step, weight in table.items():
        out = jnp.where(delta == step, weight, out)
    return out


def iotas(rows, columns):
    return lax.broadcasted_iota(jnp.int32, (rows, 1), 0), lax.broadcasted_iota(jnp.int32, (1, columns), 1)


def column_cells(column, nz, nx):
    shift, own = nx.bit_length() - 1, nz * nx
    halo = column - own
    after = halo >= HALO_X
    edge = jnp.where(after, halo - HALO_X, halo)
    inside = column < own
    z = jnp.where(inside, column >> shift, edge >> 1)
    x = jnp.where(inside, column & (nx - 1), (edge & 1) + jnp.where(after, nx, -2))
    return z, x


def slope_matrix(part, z, x, to_z, to_x):
    dz, dx = to_z - z, to_x - x
    if part == 0:
        return jnp.where(dz == 0, taps(dx, FIRST), 0.0)
    if part == 1:
        return jnp.where(dx == 0, taps(dz, FIRST), 0.0)
    return jnp.where(dz == 0, taps(dx, SECOND), 0.0) + jnp.where(dx == 0, taps(dz, SECOND), 0.0)


def store_walls(walls_ref, ny):
    row, column = iotas(ny, ny)
    first, second = (taps(row - column, table).astype(jnp.bfloat16) for table in (FIRST, SECOND))
    for i, (block, sign) in enumerate(((first, 1), (first, -1), (second, 1), (second, -1))):
        if i * ny < walls_ref.shape[1]:
            walls_ref[:ny, i * ny : (i + 1) * ny] = block
            if walls_ref.shape[0] > ny:
                walls_ref[ny:, i * ny : (i + 1) * ny] = block if sign > 0 else -block


def run_copies(copies, sems):
    started = [pltpu.make_async_copy(src, dst, sems.at[i]) for i, (src, dst) in enumerate(copies)]
    for copy in started:
        copy.start()
    for copy in started:
        copy.wait()


def shards(perturbation, base_mean, base_modes, solid_mask):
    per, modes = perturbation.shape[0], base_modes.shape[0]
    nx, nz, ny = perturbation.shape[3], perturbation.shape[4], perturbation.shape[5]
    own = nz * nx
    bf16, f32 = jnp.bfloat16, jnp.float32
    harms, size_x, size_z = (lax.axis_size(a) for a in ("harm", "gx", "gz"))
    swap = harms == 2
    sides = 1 if swap else 2
    n_pert, n_mean, n_modes = per * 8, 3, modes * 6
    n_base = n_mean + n_modes
    n_res = n_pert + n_base
    n_nb = modes * 6
    n_all = n_res + sides * n_nb

    pert = jnp.swapaxes(perturbation, 3, 4).reshape(n_pert, nz, nx, ny)
    mean = jnp.swapaxes(base_mean, 1, 2)
    mode = jnp.swapaxes(base_modes, 3, 4).reshape(n_modes, nz, nx, ny)
    mask = jnp.swapaxes(solid_mask, 0, 1).reshape(own, ny)

    def place():
        me_h, odd = lax.axis_index("harm"), lax.rem(lax.axis_index("gz"), 2)
        shared = jnp.where(me_h == 0, per - modes, 0) if swap else 0
        return me_h, odd, odd * (nz - 2), (1 - odd) * (nz - 2), shared

    cross_pairs = [(i, (i + 1) % size_z if i % 2 else (i - 1) % size_z) for i in range(size_z)]
    near_pairs = [(i, i + 1 if i % 2 == 0 else i - 1) for i in range(size_z)]
    up_x = [(i, (i + 1) % size_x) for i in range(size_x)]
    down_x = [(j, i) for i, j in up_x]
    if swap:
        harm_perms = [[(0, 1), (1, 0)]]
    else:
        up_h = [(i, i + 1) for i in range(harms - 1)]
        harm_perms = [up_h, [(j, i) for i, j in up_h]]
    def sent(s, scal):
        return scal[4] if swap else (per - modes if s == 0 else 0)

    face = lambda n: jax.ShapeDtypeStruct((n, 2, nx, ny), bf16)
    roomy = pltpu.CompilerParams(vmem_limit_bytes=32 * 1024 * 1024)

    used = 2 * nz
    spare = HALO_X - used
    tiles = 3 * (-(-n_res // 4))

    def edge_tile(ref, f):
        group, i = divmod(f, 4)
        if i < 3:
            return ref[3 * group + i]
        parts = [ref[3 * group + j].astype(f32)[used:] for j in range(3)]
        return jnp.concatenate(parts + [jnp.zeros((spare, ny), f32)], axis=0).astype(bf16)

    def pack(pert_any, mean_any, mode_any, first_any, second_any, lo_any, hi_any, *rest):
        nb_anys = rest[:sides]
        pert_ref, mean_ref, mode_ref, lo_ref, hi_ref, in_sems, out_sems = rest[sides:]
        scal = place()
        z = pl.ds(scal[2], 2)
        loads = [(pert_any.at[pl.ds(8 * l, 8)], pert_ref.at[pl.ds(8 * l, 8)]) for l in range(per)]
        loads += [(mean_any, mean_ref), (mode_any, mode_ref)]
        loads = [pltpu.make_async_copy(src, dst, in_sems.at[i]) for i, (src, dst) in enumerate(loads)]
        for copy in loads:
            copy.start()
        out = []

        def send(src, dst):
            out.append(pltpu.make_async_copy(src, dst, out_sems.at[len(out)]))
            out[-1].start()

        row, column = iotas(2 * HALO_X, own)
        low = row < HALO_X
        row = jnp.where(low, row, row - HALO_X)
        target = (row >> 1) * nx + (row & 1) + jnp.where(low, 0, nx - 2)
        pick = jnp.where(column == target, 1.0, 0.0).astype(bf16)
        where = [(pert_ref, f) for f in range(n_pert)] + [(mean_ref, f) for f in range(n_mean)] + [(mode_ref, f) for f in range(n_modes)]

        def edges(group):
            got = []
            for f in range(4 * group, min(4 * group + 4, n_res), 2):
                mine = [ref[i].reshape(own, ny) for ref, i in where[f : min(f + 2, n_res)]]
                both = jnp.concatenate(mine, axis=1) if len(mine) == 2 else mine[0]
                both = jnp.dot(pick, both, preferred_element_type=f32)
                got += [both[:, i * ny : (i + 1) * ny] for i in range(len(mine))]
            if len(got) == 3:
                got.append(jnp.zeros((2 * HALO_X, ny), f32))
            for i in range(3):
                for ref, at in ((lo_ref, 0), (hi_ref, HALO_X)):
                    extra = got[3][at + spare * i : at + spare * (i + 1)]
                    ref[3 * group + i] = jnp.concatenate([got[i][at : at + used], extra], axis=0).astype(bf16)

        for l in range(per):
            loads[l].wait()
            mine = pl.ds(8 * l, 8)
            send(pert_ref.at[mine, z], first_any.at[mine])
        for s, nb_any in enumerate(nb_anys):
            for i in range(modes * 2):
                send(pert_ref.at[pl.ds(sent(s, scal) * 8 + 4 * i, 3)], nb_any.at[pl.ds(3 * i, 3)])
        for group in range(n_pert // 4):
            edges(group)
        loads[per].wait()
        loads[per + 1].wait()
        send(mean_ref.at[:, z], second_any.at[pl.ds(0, n_mean)])
        send(mode_ref.at[:, z], second_any.at[pl.ds(n_mean, n_modes)])
        for group in range(n_pert // 4, tiles // 3):
            edges(group)
        send(lo_ref, lo_any)
        send(hi_ref, hi_any)
        for copy in out:
            copy.wait()

    edge = jax.ShapeDtypeStruct((tiles, HALO_X, ny), bf16)
    with jax.named_scope("pack"):
        first, second, edge_lo, edge_hi, *nb_send = pl.pallas_call(
            pack,
            out_shape=(face(n_pert), face(n_base), edge, edge) + tuple(jax.ShapeDtypeStruct((n_nb, nz, nx, ny), bf16) for _ in range(sides)),
            in_specs=[HBM] * 3,
            out_specs=(ANY,) * (4 + sides),
            scratch_shapes=[
                pltpu.VMEM((n_pert, nz, nx, ny), bf16),
                pltpu.VMEM((n_mean, nz, nx, ny), bf16),
                pltpu.VMEM((n_modes, nz, nx, ny), bf16),
                pltpu.VMEM((tiles, HALO_X, ny), bf16),
                pltpu.VMEM((tiles, HALO_X, ny), bf16),
                pltpu.SemaphoreType.DMA((per + 2,)),
                pltpu.SemaphoreType.DMA((per + sides * modes * 2 + 4,)),
            ],
            compiler_params=pltpu.CompilerParams(vmem_limit_bytes=VMEM_BYTES),
        )(pert, mean, mode)
    first_got = lax.ppermute(first, "gz", cross_pairs)
    nb_got = [lax.ppermute(b, "harm", p) for b, p in zip(nb_send, harm_perms)]
    xb_got = lax.ppermute(edge_hi, "gx", up_x)
    xa_got = lax.ppermute(edge_lo, "gx", down_x)
    second_got = lax.ppermute(second, "gz", cross_pairs)

    PAIRS = ((0, 3), (1, 2))
    DRIFT = (-1.5 * FREQUENCY_STEP, -0.5 * FREQUENCY_STEP)

    def entries(t, p, q, r, s):
        return t, q, p + r, p - r, q + s, s - q, t + p, t - p

    def couple(acc, ent, vec):
        t, q, pr, pmr, qs, sq, tp, tmp = ent
        out = []
        for i in range(2):
            a, e, b, g = (vec[j][i] for j in range(4))
            out.append(
                (
                    acc[0][i] + t * a + pr * b + sq * g,
                    acc[1][i] + t * e + qs * b + pmr * g,
                    acc[2][i] + pr * a + qs * e + tp * b + q * g,
                    acc[3][i] + sq * a + pmr * e + q * b + tmp * g,
                )
            )
        return [(out[0][j], out[1][j]) for j in range(4)]

    def harmonics_of(acc, scale):
        out = [None] * 4
        for at, (lo, hi) in enumerate(PAIRS):
            (ar, ai), (er, ei) = acc[2 * at], acc[2 * at + 1]
            out[lo] = ((ar + ei) * scale, (ai - er) * scale)
            out[hi] = ((ar - ei) * scale, (ai + er) * scale)
        return out

    def basis_of(values):
        out = []
        for lo, hi in PAIRS:
            (lr, li), (hr, hi_) = values[lo], values[hi]
            out += [(lr + hr, li + hi_), (hi_ - li, lr - hr)]
        return out

    def rhs(ref, fields):
        cols = [ref[f] for f in fields]
        return cols[0] if len(cols) == 1 else jnp.concatenate(cols, axis=1)

    def dot(a, b):
        return jnp.dot(a, b, preferred_element_type=f32)

    def resident_slopes(pert_ref, grads, plain, lin, rows_ref, walls_ref):
        me_h = place()[0]
        row, column = iotas(own, own)
        to_z, to_x = column_cells(column, nz, nx)
        for i in range(3):
            rows_ref[i * own : (i + 1) * own] = slope_matrix(i, row >> nx.bit_length() - 1, row & (nx - 1), to_z, to_x).astype(bf16)
        store_walls(walls_ref, ny)
        mean_freq = 12.0 * FREQUENCY_STEP * (me_h * per + 1.5 - per * harms / 2).astype(f32)

        for at, (lo, hi) in enumerate(PAIRS):
            for i in range(2):
                fl, fr = lo * 8 + i * 4 + 3, hi * 8 + i * 4 + 3
                got = dot(rows_ref[: 2 * own], rhs(pert_ref, (fl, fr)))
                wall = dot(rhs(pert_ref, (fl, fr)), walls_ref[:, : 2 * ny])
                for d in range(3):
                    if d == 1:
                        total, diff = wall[:, :ny], wall[:, ny:]
                    else:
                        span = slice(0, own) if d == 0 else slice(own, 2 * own)
                        total, diff = got[span, :ny] + got[span, ny:], got[span, :ny] - got[span, ny:]
                    lin[2 * at, i, d] = total
                    lin[2 * at + 1, 1 - i, d] = diff if i == 0 else -diff
        for at, (lo, hi) in enumerate(PAIRS):
            for c in range(3):
                for i in range(2):
                    sign = 1.0 if i == 0 else -1.0
                    fl, fr = lo * 8 + i * 4 + c, hi * 8 + i * 4 + c
                    got = dot(rows_ref[...], rhs(pert_ref, (fl, fr)))
                    xl, xr = pert_ref[fl].astype(f32), pert_ref[fr].astype(f32)
                    wall = dot(rhs(pert_ref, (fl, fr)), walls_ref[...])
                    total, diff = xl + xr, xl - xr
                    plain[2 * at, i, c] = total
                    plain[2 * at + 1, 1 - i, c] = sign * diff
                    for d in range(3):
                        if d == 1:
                            gt, gd = wall[:, :ny], wall[:, ny : 2 * ny]
                        else:
                            span = slice(0, own) if d == 0 else slice(own, 2 * own)
                            gt, gd = got[span, :ny] + got[span, ny:], got[span, :ny] - got[span, ny:]
                        gd = sign * gd
                        grads[2 * at, i, c, d] = gt
                        grads[2 * at + 1, 1 - i, c, d] = gd
                        if d == c:
                            if c == 0:
                                lin[2 * at, i, 3] = gt
                                lin[2 * at + 1, 1 - i, 3] = gd
                            else:
                                lin[2 * at, i, 3] = lin[2 * at, i, 3] + gt
                                lin[2 * at + 1, 1 - i, 3] = lin[2 * at + 1, 1 - i, 3] + gd
                    lt = got[2 * own :, :ny] + got[2 * own :, ny:] + wall[:, 2 * ny : 3 * ny]
                    ld = got[2 * own :, :ny] - got[2 * own :, ny:] + wall[:, 3 * ny :]
                    drift = 12.0 * DRIFT[at]
                    lin[2 * at, i, c] = lin[2 * at, i, c] - VISCOSITY * lt
                    lin[2 * at + 1, 1 - i, c] = lin[2 * at + 1, 1 - i, c] - sign * VISCOSITY * ld
                    lin[2 * at, 1 - i, c] = lin[2 * at, 1 - i, c] + sign * (mean_freq * total + drift * diff)
                    lin[2 * at + 1, i, c] = lin[2 * at + 1, i, c] - (mean_freq * diff + drift * total)

    def resident(mean_ref, mode_ref, grads, plain, lin, out_ref, ents, rows_ref, walls_ref):
        row, column = iotas(own, own)
        to_z, to_x = column_cells(column, nz, nx)
        for i in range(2):
            rows_ref[i * own : (i + 1) * own] = slope_matrix(i, row >> nx.bit_length() - 1, row & (nx - 1), to_z, to_x).astype(bf16)
        store_walls(walls_ref, ny)
        for c in range(3):
            picked = [mean_ref[c].astype(f32)] + [mode_ref[3 * i + c].astype(f32) for i in range(4)]
            for n, ent in enumerate(entries(*picked)):
                ents[c, n] = ent
            mean_at = dot(rows_ref[...], rhs(mean_ref, (c,)))
            mean_wall = dot(mean_ref[c], walls_ref[:ny, :ny])
            real = dot(rows_ref[...], rhs(mode_ref, (c, 6 + c)))
            imag = dot(rows_ref[...], rhs(mode_ref, (3 + c, 9 + c)))
            wall_real = dot(rhs(mode_ref, (c, 6 + c)), walls_ref[:, : 2 * ny])
            wall_imag = dot(rhs(mode_ref, (3 + c, 9 + c)), walls_ref[:, : 2 * ny])
            for d in range(3):
                if d == 1:
                    pr, pmr = wall_real[:, :ny], wall_real[:, ny:]
                    qs, qms = wall_imag[:, :ny], wall_imag[:, ny:]
                    t, p, q = mean_wall, 0.5 * (pr + pmr), 0.5 * (qs + qms)
                    values = (t, q, pr, pmr, qs, -qms, t + p, t - p)
                else:
                    span = slice(0, own) if d == 0 else slice(own, 2 * own)
                    values = entries(mean_at[span], real[span, :ny], imag[span, :ny], real[span, ny:], imag[span, ny:])
                for n, ent in enumerate(values):
                    ents[3 + 3 * d + c, n] = ent

        def block(b, carry):
            rows = pl.ds(pl.multiple_of(b * 8, 8), 8)
            accs = [[(lin[j, 0, c, rows], lin[j, 1, c, rows]) for j in range(4)] for c in range(4)]
            for d in range(3):
                flow = [ents[d, n, rows] for n in range(8)]
                for c in range(3):
                    accs[c] = couple(accs[c], flow, [(grads[j, 0, c, d, rows], grads[j, 1, c, d, rows]) for j in range(4)])
                along = [(plain[j, 0, d, rows], plain[j, 1, d, rows]) for j in range(4)]
                for c in range(3):
                    slope = [ents[3 + 3 * d + c, n, rows] for n in range(8)]
                    accs[c] = couple(accs[c], slope, along)
            for c in range(4):
                for k, (re, im) in enumerate(harmonics_of(accs[c], 1.0 / 24.0)):
                    out_ref[k * 8 + c, rows] = re
                    out_ref[k * 8 + 4 + c, rows] = im
            return carry

        lax.fori_loop(0, own // 8, block, 0, unroll=4)

    flat = lambda a: a.reshape(a.shape[0], -1, ny)
    with jax.named_scope("resident_slopes"):
        slopes = pl.pallas_call(
            resident_slopes,
            out_shape=tuple(jax.ShapeDtypeStruct(n + (own, ny), f32) for n in ((4, 2, 3, 3), (4, 2, 3), (4, 2, 4))),
            scratch_shapes=[pltpu.VMEM((3 * own, own), bf16), pltpu.VMEM((2 * ny, 4 * ny), bf16)],
            compiler_params=pltpu.CompilerParams(vmem_limit_bytes=20 * 1024 * 1024),
        )(flat(pert))
    with jax.named_scope("resident"):
        whole = pl.pallas_call(
            resident,
            out_shape=jax.ShapeDtypeStruct((n_pert, own, ny), f32),
            scratch_shapes=[
                pltpu.VMEM((12, 8, own, ny), f32),
                pltpu.VMEM((2 * own, own), bf16),
                pltpu.VMEM((2 * ny, 2 * ny), bf16),
            ],
            compiler_params=roomy,
        )(flat(mean), flat(mode), *slopes)

    base_modes_at = n_pert + n_mean
    ends = 16 * nz

    def edge_taps(tables):
        row, column = iotas(ends, own + 2 * HALO_X)
        last = row >= 8 * nz
        row = jnp.where(last, row - 8 * nz, row)
        to_z, to_x = column_cells(column, nz, nx)
        dz, dx = to_z - (row >> 3), to_x - (row & 7) - jnp.where(last, nx - 8, 0)
        return jnp.concatenate([jnp.where(dz == 0, taps(dx, table), 0.0)[:, own:] for table in tables], axis=0).astype(bf16)

    def add_edges(pert_ref, mean_ref, mode_ref, xb_ref, xa_ref, _, out_ref, vecs, lins, bends):
        taps_of = edge_taps((FIRST, SECOND))

        def bent(fields, lap):
            cols = [jnp.concatenate([edge_tile(xb_ref, f), edge_tile(xa_ref, f)], axis=0) for f in fields]
            both = cols[0] if len(cols) == 1 else jnp.concatenate(cols, axis=1)
            got = jnp.dot(taps_of if lap else taps_of[:ends], both, preferred_element_type=f32)
            return [(got[:ends, i * ny : (i + 1) * ny], got[ends:, i * ny : (i + 1) * ny]) for i in range(len(fields))]

        for at, (lo, hi) in enumerate(PAIRS):
            for i in range(2):
                sign = 1.0 if i == 0 else -1.0
                for c in range(4):
                    (gl, ll), (gr, lr) = bent((lo * 8 + 4 * i + c, hi * 8 + 4 * i + c), c < 3)
                    if c < 3:
                        vecs[2 * at, i, c] = gl + gr
                        vecs[2 * at + 1, 1 - i, c] = sign * (gl - gr)
                        lins[2 * at, i, c] = -VISCOSITY * (ll + lr)
                        lins[2 * at + 1, 1 - i, c] = (-VISCOSITY * sign) * (ll - lr)
                    else:
                        lins[2 * at, i, 0] = lins[2 * at, i, 0] + (gl + gr)
                        lins[2 * at + 1, 1 - i, 0] = lins[2 * at + 1, 1 - i, 0] + sign * (gl - gr)
        for c in range(3):
            at = base_modes_at + c
            (t, _), = bent((n_pert + c,), False)
            (p, _), (r, _) = bent((at, at + 6), False)
            (q, _), (s_, _) = bent((at + 3, at + 9), False)
            for n, ent in enumerate(entries(t, p, q, r, s_)):
                bends[c, n] = ent

        def layer_ends(z, carry):
            for end in range(2):
                strip = pl.ds(pl.multiple_of(z * nx + end * (nx // 2), 16), 16)
                keep = slice(8 * end, 8 * end + 8)
                mine = pl.ds(pl.multiple_of((end * nz + z) * 8, 8), 8)

                def read(ref, f):
                    return ref[f, strip].astype(f32)[keep]

                flow = entries(read(mean_ref, 0), *[read(mode_ref, 3 * i) for i in range(4)])
                along = basis_of([(read(pert_ref, l * 8), read(pert_ref, l * 8 + 4)) for l in range(per)])
                for c in range(4):
                    if c < 3:
                        acc = [(lins[j, 0, c, mine], lins[j, 1, c, mine]) for j in range(4)]
                        acc = couple(acc, flow, [(vecs[j, 0, c, mine], vecs[j, 1, c, mine]) for j in range(4)])
                        acc = couple(acc, [bends[c, n, mine] for n in range(8)], along)
                    else:
                        acc = [(vecs[j, 0, 0, mine], vecs[j, 1, 0, mine]) for j in range(4)]
                    for k, parts in enumerate(harmonics_of(acc, 1.0 / 24.0)):
                        for i in range(2):
                            out_ref[k * 8 + 4 * i + c, mine] = parts[i]
            return carry

        lax.fori_loop(0, nz, layer_ends, 0, unroll=2)

    with jax.named_scope("edges"):
        edged = pl.pallas_call(
            add_edges,
            out_shape=jax.ShapeDtypeStruct((n_pert, ends, ny), f32),
            in_specs=[VMEM] * 5 + [ANY],
            scratch_shapes=[
                pltpu.VMEM((4, 2, 3, ends, ny), f32),
                pltpu.VMEM((4, 2, 3, ends, ny), f32),
                pltpu.VMEM((3, 8, ends, ny), f32),
            ],
            compiler_params=roomy,
        )(flat(pert), flat(mean), flat(mode), xb_got, xa_got, whole)

    faces_deep = n_nb * 2 * nx
    nb_tiles = 3 * n_nb // 4
    deep = faces_deep + 2 * nb_tiles * HALO_X

    def nb_tile(ref, after, f):
        group, i = divmod(f, 4)
        at = [faces_deep + (after * nb_tiles + 3 * group + j) * HALO_X for j in range(3)]
        if i < 3:
            return ref[at[i] : at[i] + HALO_X]
        parts = [ref[row : row + HALO_X].astype(f32)[used:] for row in at]
        return jnp.concatenate(parts + [jnp.zeros((spare, ny), f32)], axis=0).astype(bf16)

    def pack_relay(first_ref, xb_ref, xa_ref, _, *outs):
        scal = place()
        for s, out in enumerate(outs):
            for i in range(modes * 2):
                group = sent(s, scal) * 2 + i
                for c in range(3):
                    at = (3 * i + c) * 2 * nx
                    out[at : at + 2 * nx] = first_ref[group * 4 + c].reshape(2 * nx, ny)
            for after, ref in enumerate((xb_ref, xa_ref)):
                for group in range(n_nb // 4):
                    rows = []
                    for f in range(4 * group, 4 * group + 4):
                        rows.append(ref[(sent(s, scal) * 2 + f // 3) * 3 + f % 3].astype(f32))
                    for i in range(3):
                        at = faces_deep + (after * nb_tiles + 3 * group + i) * HALO_X
                        tile = jnp.concatenate([rows[i][:used], rows[3][spare * i : spare * (i + 1)]], axis=0)
                        out[at : at + HALO_X] = tile.astype(bf16)

    with jax.named_scope("pack_relay"):
        relay = pl.pallas_call(
            pack_relay,
            out_shape=tuple(jax.ShapeDtypeStruct((deep, ny), bf16) for _ in range(sides)),
            in_specs=[VMEM] * 3 + [ANY],
            compiler_params=roomy,
        )(first_got, xb_got, xa_got, edged)
    relay_got = [lax.ppermute(b, "harm", p) for b, p in zip(relay, harm_perms)]

    def pack_near(pert_ref, mean_ref, mode_ref, *rest):
        out = rest[-1]
        z = pl.ds(place()[3], 2)
        out[:n_pert] = pert_ref[:, z]
        out[n_pert : n_pert + n_mean] = mean_ref[:, z]
        out[n_pert + n_mean : n_res] = mode_ref[:, z]
        for s in range(sides):
            out[n_res + s * n_nb : n_res + (s + 1) * n_nb] = rest[s][:, z]

    with jax.named_scope("pack_near"):
        near = pl.pallas_call(
            pack_near,
            out_shape=face(n_all),
            in_specs=[VMEM] * (3 + sides) + [ANY],
            compiler_params=roomy,
        )(pert, mean, mode, *nb_got, relay[0])
    near_got = lax.ppermute(near, "gz", near_pairs)

    below, above = [], []
    for k in range(per):
        for m in range(-modes, modes + 1):
            l = k - m
            if l < 0:
                below.append((k, m, 0, (l + modes) * 6))
            elif l >= per:
                above.append((k, m, sides - 1, (l - per) * 6))

    def on_sides(work):
        me_h = lax.axis_index("harm")
        pl.when(me_h > 0)(lambda: work(below))
        pl.when(me_h < harms - 1)(lambda: work(above))

    def product(acc, flow, value, m):
        (fr, fi), (vr, vi) = flow, value
        if m > 0:
            return acc[0] + fr * vr - fi * vi, acc[1] + fr * vi + fi * vr
        return acc[0] + fr * vr + fi * vi, acc[1] + fr * vi - fi * vr


    def face_place(cross, step):
        odd = place()[1]
        before = (odd == 0) if cross else (odd == 1)
        return before, jnp.where(before, step, nz - 1 - step), jnp.where(before, 1, 0)

    def faces(out_ref, mean_ref, mode_ref, pert_ref, nb_refs, first_ref, second_ref, near_ref, relay_refs, step, lowest=0, after=None):
        cross = near_ref is None
        before, layer, near_at = face_place(cross, step)
        turn = jnp.where(before, 1.0, -1.0)

        def mix(pair):
            return pair[1] - 8.0 * pair[0] if step == 0 else pair[0]

        def mix_lap(pair):
            return pair[1] - 16.0 * pair[0] if step == 0 else pair[0]

        def chunk_work(chunk, carry):
            rows = pl.ds(pl.multiple_of(layer * nx + chunk * 16, 16), 16)
            out_rows = pl.ds(pl.multiple_of((layer - lowest) * nx + chunk * 16, 16), 16)
            strip = pl.ds(chunk * 16 if isinstance(chunk, int) else pl.multiple_of(chunk * 16, 16), 16)

            def halos(f):
                if not cross:
                    ref, at = near_ref, f
                elif f < n_pert:
                    ref, at = first_ref, f
                else:
                    ref, at = second_ref, f - n_pert
                return ref[at, near_at, strip].astype(f32), (ref[at, 1 - near_at, strip].astype(f32) if step == 0 else None)

            def nb_halos(s, f):
                if not cross:
                    return halos(n_res + s * n_nb + f)
                at = [pl.ds(pl.multiple_of((2 * f + j) * nx + chunk * 16, 16), 16) for j in (near_at, 1 - near_at)]
                return tuple(relay_refs[s][r].astype(f32) for r in at)

            velocity, base = first_ref is not None or not cross, second_ref is not None or not cross
            if velocity:
                flow = entries(mean_ref[2, rows].astype(f32), *[mode_ref[3 * i + 2, rows].astype(f32) for i in range(4)])
            if base:
                along = basis_of([(pert_ref[l * 8 + 2, rows].astype(f32), pert_ref[l * 8 + 6, rows].astype(f32)) for l in range(per)])
            for c in range(4 if velocity else 3):
                acc = [(0.0, 0.0)] * 4
                if velocity and c < 3:
                    got = [[halos(l * 8 + 4 * i + c) for i in range(2)] for l in range(per)]
                    vec = basis_of([(mix(g[0]), mix(g[1])) for g in got])
                    lap = basis_of([(mix_lap(g[0]), mix_lap(g[1])) for g in got])
                    if c == 2:
                        acc = basis_of([(mix(halos(l * 8 + 3)), mix(halos(l * 8 + 7))) for l in range(per)])
                    acc = couple(acc, flow, vec)
                if base and c < 3:
                    bend = entries(mix(halos(n_pert + c)), *[mix(halos(base_modes_at + 3 * i + c)) for i in range(4)])
                    acc = couple(acc, bend, along)
                if c == 3:
                    acc = vec
                if velocity and c < 3:
                    acc = [tuple(turn * a + VISCOSITY * v for a, v in zip(*pair)) for pair in zip(acc, lap)]
                else:
                    acc = [tuple(turn * a for a in pair) for pair in acc]
                for k, parts in enumerate(harmonics_of(acc, 1.0 / 24.0)):
                    for i in range(2):
                        at = k * 8 + 4 * i + c
                        out_ref[at, out_rows] = out_ref[at, out_rows] + parts[i]

            def nb_work(pairs):
                for k in sorted({p[0] for p in pairs}):
                    zero = jnp.zeros((16, ny), f32)
                    for c in range(3):
                        acc = (zero, zero)
                        for _, m, s, f in [p for p in pairs if p[0] == k]:
                            at = (abs(m) - 1) * 6
                            mine = tuple(mode_ref[at + 3 * i + 2, rows].astype(f32) for i in range(2))
                            acc = product(acc, mine, tuple(mix(nb_halos(s, f + 3 * i + c)) for i in range(2)), m)
                            bent = tuple(mix(halos(base_modes_at + at + 3 * i + c)) for i in range(2))
                            carried = tuple(nb_refs[s][f + 3 * i + 2, rows].astype(f32) for i in range(2))
                            acc = product(acc, bent, carried, m)
                        for i in range(2):
                            at = k * 8 + 4 * i + c
                            out_ref[at, out_rows] = out_ref[at, out_rows] + (turn * (1.0 / 12.0)) * acc[i]

            if base:
                on_sides(nb_work)
            return carry

        if after is None:
            lax.fori_loop(0, nx // 16, chunk_work, 0, unroll=True)
        else:
            for chunk in range(nx // 16):
                chunk_work(chunk, 0)
                after(layer, chunk)

    def neighbours(mask_ref, pert_ref, mean_ref, mode_ref, xb_ref, xa_ref, whole_ref, edged_ref, first_ref, near_ref, *rest):
        nb_refs = rest[:sides]
        out_any, out_ref, grads, plain, stencil_ref, walls_ref, sems = rest[-7:]
        row, column = iotas(own, own + 2 * HALO_X)
        to_z, to_x = column_cells(column, nz, nx)
        for i in range(2):
            stencil_ref[i * own : (i + 1) * own] = slope_matrix(i, row >> nx.bit_length() - 1, row & (nx - 1), to_z, to_x).astype(bf16)
        store_walls(walls_ref, ny)

        def slopes(at, mine, halo):
            both = jnp.concatenate(mine, axis=1)
            rows = both if halo is None else jnp.concatenate([both, halo], axis=0)
            got = jnp.dot(stencil_ref[:, : rows.shape[0]], rows, preferred_element_type=f32)
            wall = [jnp.dot(x, walls_ref[:ny, :ny], preferred_element_type=f32) for x in mine]
            for i in range(2):
                lanes = slice(i * ny, (i + 1) * ny)
                grads[at + i, 0] = got[:own, lanes]
                grads[at + i, 2] = got[own:, lanes]
                grads[at + i, 1] = wall[i]
                plain[at + i] = mine[i].astype(f32)

        for f in range(0, n_modes, 2):
            at = base_modes_at + f
            halo = [jnp.concatenate([edge_tile(ref, at), edge_tile(ref, at + 1)], axis=1) for ref in (xb_ref, xa_ref)]
            slopes(f, [mode_ref[f], mode_ref[f + 1]], jnp.concatenate(halo, axis=0))
        for s in range(sides):
            for f in range(0, n_nb, 2):
                slopes(n_modes + s * n_nb + f, [nb_refs[s][f], nb_refs[s][f + 1]], None)

        for z in range(nz):
            rows = slice(z * nx, (z + 1) * nx)
            solid = PENALTY * mask_ref[rows].astype(f32)
            for f in range(n_pert):
                if f % 4 < 3:
                    out_ref[f, rows] = whole_ref[f, rows] + solid * pert_ref[f, rows].astype(f32)
                else:
                    out_ref[f, rows] = whole_ref[f, rows]
            for end in range(2):
                rows = slice(z * nx + end * (nx - 8), z * nx + end * (nx - 8) + 8)
                mine = slice((end * nz + z) * 8, (end * nz + z + 1) * 8)
                out_ref[:, rows] = out_ref[:, rows] + edged_ref[:, mine]

        def work(pairs):
            def block(b, carry):
                rows = pl.ds(pl.multiple_of(b * 8, 8), 8)
                for k in sorted({p[0] for p in pairs}):
                    zero = jnp.zeros((8, ny), f32)
                    acc = [(zero, zero)] * 3
                    for _, m, s, f in [p for p in pairs if p[0] == k]:
                        at, base = n_modes + s * n_nb + f, (abs(m) - 1) * 6
                        for d in range(3):
                            flow = plain[base + d, rows], plain[base + 3 + d, rows]
                            along = plain[at + d, rows], plain[at + 3 + d, rows]
                            for c in range(3):
                                slope = grads[base + c, d, rows], grads[base + 3 + c, d, rows]
                                grad = grads[at + c, d, rows], grads[at + 3 + c, d, rows]
                                acc[c] = product(acc[c], flow, grad, m)
                                acc[c] = product(acc[c], slope, along, m)
                    for c in range(3):
                        for i in range(2):
                            at = k * 8 + 4 * i + c
                            out_ref[at, rows] = out_ref[at, rows] + acc[c][i] * (1.0 / 12.0)
                return carry

            lax.fori_loop(0, own // 8, block, 0, unroll=2)

        on_sides(work)
        sends = []

        def send(layer):
            rows = pl.ds(pl.multiple_of(layer * nx, nx), nx)
            sends.append(pltpu.make_async_copy(out_ref.at[:, rows], out_any.at[:, rows], sems.at[len(sends)]))
            sends[-1].start()

        for layer in range(2, nz - 2):
            send(layer)
        for step in range(2):
            faces(out_ref, mean_ref, mode_ref, pert_ref, nb_refs, None, None, near_ref, None, step)
            send(face_place(False, step)[1])
        for step in range(2):
            faces(out_ref, mean_ref, mode_ref, pert_ref, nb_refs, first_ref, None, None, None, step)
        for copy in sends:
            copy.wait()

    n_ext = n_modes + sides * n_nb
    with jax.named_scope("neighbours"):
        result, inner = pl.pallas_call(
            neighbours,
            out_shape=(jax.ShapeDtypeStruct((n_pert, own, ny), f32),) * 2,
            out_specs=(HBM, VMEM),
            scratch_shapes=[
                pltpu.VMEM((n_ext, 3, own, ny), f32),
                pltpu.VMEM((n_ext, own, ny), f32),
                pltpu.VMEM((2 * own, own + 2 * HALO_X), bf16),
                pltpu.VMEM((ny, ny), bf16),
                pltpu.SemaphoreType.DMA((nz - 2,)),
            ],
            compiler_params=roomy,
        )(mask, flat(pert), flat(mean), flat(mode), xb_got, xa_got, whole, edged, first_got, near_got, *[flat(b) for b in nb_got])

    n_keys = n_pert // 2 if swap else n_pert

    def finish(pert_ref, mean_ref, mode_ref, inner_ref, second_ref, _, *rest):
        relay_refs, nb_refs = rest[:sides], rest[sides : 2 * sides]
        out_any, done, fringe, bends, sems = rest[2 * sides :]
        half = nx // 2
        keys = jnp.where(lax.axis_index("harm") == 0, n_pert - n_keys, 0) if swap else 0
        inner_layer = jnp.where(face_place(True, 0)[0], 2, 0)
        taps_of = edge_taps((FIRST,))
        sends = []

        def send(src, dst):
            sends.append(pltpu.make_async_copy(src, dst, sems.at[len(sends)]))
            sends[-1].start()

        for s in range(sides):
            for f in range(0, n_nb, 2):
                both = [jnp.concatenate([nb_tile(relay_refs[s], after, f + i) for after in range(2)], axis=0) for i in range(2)]
                both = jnp.concatenate(both, axis=1)
                got = jnp.dot(taps_of, both, preferred_element_type=f32)
                for i in range(2):
                    bends[s * n_nb + f + i] = got[:, i * ny : (i + 1) * ny]

        def edge_terms(pairs, z, end, add):
            strip = pl.ds(pl.multiple_of(z * nx + end * half, 16), 16)
            keep = slice(8 * end, 8 * end + 8)
            bent = pl.ds(pl.multiple_of((end * nz + z) * 8, 8), 8)
            for k in sorted({p[0] for p in pairs}):
                zero = jnp.zeros((8, ny), f32)
                acc = [(zero, zero)] * 3
                for _, m, s, f in [p for p in pairs if p[0] == k]:
                    base = (abs(m) - 1) * 6
                    flow = tuple(mode_ref[base + 3 * i, strip].astype(f32)[keep] for i in range(2))
                    for c in range(3):
                        at = s * n_nb + f + c
                        acc[c] = product(acc[c], flow, (bends[at, bent], bends[at + 3, bent]), m)
                for c in range(3):
                    for i in range(2):
                        add(k, 4 * i + c, acc[c][i] * (1.0 / 12.0))

        def end_rows(z, end):
            return pl.ds(pl.multiple_of(z * nx + end * (nx - 8), 8), 8)

        def other_edges(pairs):
            lowest = min(p[0] for p in pairs) * 8 if swap else 0

            def at_layer(j, carry):
                for end in range(2):

                    def add(k, part, value):
                        at = k * 8 + part - lowest
                        fringe[end, at, j] = fringe[end, at, j] + value

                    edge_terms(pairs, inner_layer + j, end, add)
                return carry

            lax.fori_loop(0, nz - 2, at_layer, 0, unroll=2)

        for j in range(nz - 2):
            for end in range(2):
                fringe[end, :, j] = inner_ref[pl.ds(keys, n_keys), end_rows(inner_layer + j, end)]
        on_sides(other_edges)
        for j in range(nz - 2):
            for end in range(2):
                send(fringe.at[end, :, j], out_any.at[pl.ds(keys, n_keys), end_rows(inner_layer + j, end)])

        first_row = pl.multiple_of(jnp.where(face_place(True, 0)[0], 0, (nz - 2) * nx), nx)
        done[...] = inner_ref[:, pl.ds(first_row, 2 * nx)]
        cross_layer = first_row // nx

        def cross_edges(pairs):
            def at_layer(j, carry):
                for end in range(2):
                    rows = end_rows(j, end)

                    def add(k, part, value):
                        done[k * 8 + part, rows] = done[k * 8 + part, rows] + value

                    edge_terms(pairs, cross_layer + j, end, add)
                return carry

            lax.fori_loop(0, 2, at_layer, 0, unroll=True)

        on_sides(cross_edges)
        def send_chunk(layer, chunk):
            here = pl.ds(pl.multiple_of((layer - cross_layer) * nx + chunk * 16, 16), 16)
            send(done.at[:, here], out_any.at[:, pl.ds(pl.multiple_of(layer * nx + chunk * 16, 16), 16)])

        for step in range(2):
            faces(done, mean_ref, mode_ref, pert_ref, nb_refs, None, second_ref, None, relay_refs, step, cross_layer, send_chunk)
        for copy in sends:
            copy.wait()

    with jax.named_scope("finish"):
        out = pl.pallas_call(
            finish,
            out_shape=jax.ShapeDtypeStruct((n_pert, own, ny), f32),
            in_specs=[VMEM] * 5 + [HBM] + [VMEM] * (2 * sides),
            out_specs=HBM,
            input_output_aliases={5: 0},
            scratch_shapes=[
                pltpu.VMEM((n_pert, 2 * nx, ny), f32),
                pltpu.VMEM((2, n_keys, nz - 2, 8, ny), f32),
                pltpu.VMEM((sides * n_nb, ends, ny), f32),
                pltpu.SemaphoreType.DMA((nx // 8 + 2 * (nz - 2),)),
            ],
            compiler_params=roomy,
        )(
            flat(pert), flat(mean), flat(mode), inner, second_got, result,
            *relay_got, *[flat(b) for b in nb_got],
        )
    return jnp.swapaxes(out.reshape(per, 2, 4, nz, nx, ny), 3, 4)


def solution(mesh):
    return jax.shard_map(
        shards,
        mesh=mesh,
        in_specs=(
            P("harm", None, None, "gx", "gz", None),
            P(None, "gx", "gz", None),
            P(None, None, None, "gx", "gz", None),
            P("gx", "gz", None),
        ),
        out_specs=P("harm", None, None, "gx", "gz", None),
        check_vma=False,
    )
```

```python
import jax
import jax.numpy as jnp
from jax import lax
from jax.experimental import pallas as pl
from jax.experimental.pallas import tpu as pltpu
from jax.sharding import PartitionSpec as P

FREQUENCY_STEP = 0.2
VISCOSITY = 0.05
PENALTY = 4.0
FIRST = {-2: 1.0, -1: -8.0, 1: 8.0, 2: -1.0}
SECOND = {-2: -1.0, -1: 16.0, 0: -30.0, 1: 16.0, 2: -1.0}
HALO_X = 16
VMEM_BYTES = 58 * 1024 * 1024
ANY = pl.BlockSpec(memory_space=pl.ANY)
VMEM = pl.BlockSpec(memory_space=pltpu.VMEM)
HBM = pl.BlockSpec(memory_space=pltpu.HBM)


def taps(delta, table):
    out = jnp.zeros(delta.shape, jnp.float32)
    for step, weight in table.items():
        out = jnp.where(delta == step, weight, out)
    return out


def iotas(rows, columns):
    return lax.broadcasted_iota(jnp.int32, (rows, 1), 0), lax.broadcasted_iota(jnp.int32, (1, columns), 1)


def column_cells(column, nz, nx):
    shift, own = nx.bit_length() - 1, nz * nx
    halo = column - own
    after = halo >= HALO_X
    edge = jnp.where(after, halo - HALO_X, halo)
    inside = column < own
    z = jnp.where(inside, column >> shift, edge >> 1)
    x = jnp.where(inside, column & (nx - 1), (edge & 1) + jnp.where(after, nx, -2))
    return z, x


def slope_matrix(part, z, x, to_z, to_x):
    dz, dx = to_z - z, to_x - x
    if part == 0:
        return jnp.where(dz == 0, taps(dx, FIRST), 0.0)
    if part == 1:
        return jnp.where(dx == 0, taps(dz, FIRST), 0.0)
    return jnp.where(dz == 0, taps(dx, SECOND), 0.0) + jnp.where(dx == 0, taps(dz, SECOND), 0.0)


def store_walls(walls_ref, ny):
    row, column = iotas(ny, ny)
    first, second = (taps(row - column, table).astype(jnp.bfloat16) for table in (FIRST, SECOND))
    for i, (block, sign) in enumerate(((first, 1), (first, -1), (second, 1), (second, -1))):
        if i * ny < walls_ref.shape[1]:
            walls_ref[:ny, i * ny : (i + 1) * ny] = block
            if walls_ref.shape[0] > ny:
                walls_ref[ny:, i * ny : (i + 1) * ny] = block if sign > 0 else -block


def run_copies(copies, sems):
    started = [pltpu.make_async_copy(src, dst, sems.at[i]) for i, (src, dst) in enumerate(copies)]
    for copy in started:
        copy.start()
    for copy in started:
        copy.wait()


def shards(perturbation, base_mean, base_modes, solid_mask):
    per, modes = perturbation.shape[0], base_modes.shape[0]
    nx, nz, ny = perturbation.shape[3], perturbation.shape[4], perturbation.shape[5]
    own = nz * nx
    bf16, f32 = jnp.bfloat16, jnp.float32
    harms, size_x, size_z = (lax.axis_size(a) for a in ("harm", "gx", "gz"))
    swap = harms == 2
    sides = 1 if swap else 2
    n_pert, n_mean, n_modes = per * 8, 3, modes * 6
    n_base = n_mean + n_modes
    n_res = n_pert + n_base
    n_nb = modes * 6
    n_all = n_res + sides * n_nb

    pert = jnp.swapaxes(perturbation, 3, 4).reshape(n_pert, nz, nx, ny)
    mean = jnp.swapaxes(base_mean, 1, 2)
    mode = jnp.swapaxes(base_modes, 3, 4).reshape(n_modes, nz, nx, ny)
    mask = jnp.swapaxes(solid_mask, 0, 1).reshape(own, ny)

    def place():
        me_h, odd = lax.axis_index("harm"), lax.rem(lax.axis_index("gz"), 2)
        shared = jnp.where(me_h == 0, per - modes, 0) if swap else 0
        return me_h, odd, odd * (nz - 2), (1 - odd) * (nz - 2), shared

    cross_pairs = [(i, (i + 1) % size_z if i % 2 else (i - 1) % size_z) for i in range(size_z)]
    near_pairs = [(i, i + 1 if i % 2 == 0 else i - 1) for i in range(size_z)]
    up_x = [(i, (i + 1) % size_x) for i in range(size_x)]
    down_x = [(j, i) for i, j in up_x]
    if swap:
        harm_perms = [[(0, 1), (1, 0)]]
    else:
        up_h = [(i, i + 1) for i in range(harms - 1)]
        harm_perms = [up_h, [(j, i) for i, j in up_h]]
    def sent(s, scal):
        return scal[4] if swap else (per - modes if s == 0 else 0)

    face = lambda n: jax.ShapeDtypeStruct((n, 2, nx, ny), bf16)
    roomy = pltpu.CompilerParams(vmem_limit_bytes=32 * 1024 * 1024)

    used = 2 * nz
    spare = HALO_X - used
    tiles = 3 * (-(-n_res // 4))

    def edge_tile(ref, f):
        group, i = divmod(f, 4)
        if i < 3:
            return ref[3 * group + i]
        parts = [ref[3 * group + j].astype(f32)[used:] for j in range(3)]
        return jnp.concatenate(parts + [jnp.zeros((spare, ny), f32)], axis=0).astype(bf16)

    def pack(pert_any, mean_any, mode_any, first_any, second_any, lo_any, hi_any, *rest):
        nb_anys = rest[:sides]
        pert_ref, mean_ref, mode_ref, lo_ref, hi_ref, in_sems, out_sems = rest[sides:]
        scal = place()
        z = pl.ds(scal[2], 2)
        loads = [(pert_any.at[pl.ds(8 * l, 8)], pert_ref.at[pl.ds(8 * l, 8)]) for l in range(per)]
        loads += [(mean_any, mean_ref), (mode_any, mode_ref)]
        loads = [pltpu.make_async_copy(src, dst, in_sems.at[i]) for i, (src, dst) in enumerate(loads)]
        for copy in loads:
            copy.start()
        out = []

        def send(src, dst):
            out.append(pltpu.make_async_copy(src, dst, out_sems.at[len(out)]))
            out[-1].start()

        row, column = iotas(2 * HALO_X, own)
        low = row < HALO_X
        row = jnp.where(low, row, row - HALO_X)
        target = (row >> 1) * nx + (row & 1) + jnp.where(low, 0, nx - 2)
        pick = jnp.where(column == target, 1.0, 0.0).astype(bf16)
        where = [(pert_ref, f) for f in range(n_pert)] + [(mean_ref, f) for f in range(n_mean)] + [(mode_ref, f) for f in range(n_modes)]

        def edges(group):
            got = []
            for f in range(4 * group, min(4 * group + 4, n_res), 2):
                mine = [ref[i].reshape(own, ny) for ref, i in where[f : min(f + 2, n_res)]]
                both = jnp.concatenate(mine, axis=1) if len(mine) == 2 else mine[0]
                both = jnp.dot(pick, both, preferred_element_type=f32)
                got += [both[:, i * ny : (i + 1) * ny] for i in range(len(mine))]
            if len(got) == 3:
                got.append(jnp.zeros((2 * HALO_X, ny), f32))
            for i in range(3):
                for ref, at in ((lo_ref, 0), (hi_ref, HALO_X)):
                    extra = got[3][at + spare * i : at + spare * (i + 1)]
                    ref[3 * group + i] = jnp.concatenate([got[i][at : at + used], extra], axis=0).astype(bf16)

        for l in range(per):
            loads[l].wait()
            mine = pl.ds(8 * l, 8)
            send(pert_ref.at[mine, z], first_any.at[mine])
        for s, nb_any in enumerate(nb_anys):
            for i in range(modes * 2):
                send(pert_ref.at[pl.ds(sent(s, scal) * 8 + 4 * i, 3)], nb_any.at[pl.ds(3 * i, 3)])
        for group in range(n_pert // 4):
            edges(group)
        early = pl.ds(0, 3 * n_pert // 4)
        send(lo_ref.at[early], lo_any.at[early])
        send(hi_ref.at[early], hi_any.at[early])
        loads[per].wait()
        loads[per + 1].wait()
        send(mean_ref.at[:, z], second_any.at[pl.ds(0, n_mean)])
        send(mode_ref.at[:, z], second_any.at[pl.ds(n_mean, n_modes)])
        for group in range(n_pert // 4, tiles // 3):
            edges(group)
        late = pl.ds(3 * n_pert // 4, tiles - 3 * n_pert // 4)
        send(lo_ref.at[late], lo_any.at[late])
        send(hi_ref.at[late], hi_any.at[late])
        for copy in out:
            copy.wait()

    edge = jax.ShapeDtypeStruct((tiles, HALO_X, ny), bf16)
    with jax.named_scope("pack"):
        first, second, edge_lo, edge_hi, *nb_send = pl.pallas_call(
            pack,
            out_shape=(face(n_pert), face(n_base), edge, edge) + tuple(jax.ShapeDtypeStruct((n_nb, nz, nx, ny), bf16) for _ in range(sides)),
            in_specs=[HBM] * 3,
            out_specs=(ANY,) * (4 + sides),
            scratch_shapes=[
                pltpu.VMEM((n_pert, nz, nx, ny), bf16),
                pltpu.VMEM((n_mean, nz, nx, ny), bf16),
                pltpu.VMEM((n_modes, nz, nx, ny), bf16),
                pltpu.VMEM((tiles, HALO_X, ny), bf16),
                pltpu.VMEM((tiles, HALO_X, ny), bf16),
                pltpu.SemaphoreType.DMA((per + 2,)),
                pltpu.SemaphoreType.DMA((per + sides * modes * 2 + 6,)),
            ],
            compiler_params=pltpu.CompilerParams(vmem_limit_bytes=VMEM_BYTES),
        )(pert, mean, mode)
    first_got = lax.ppermute(first, "gz", cross_pairs)
    nb_got = [lax.ppermute(b, "harm", p) for b, p in zip(nb_send, harm_perms)]
    xb_got = lax.ppermute(edge_hi, "gx", up_x)
    xa_got = lax.ppermute(edge_lo, "gx", down_x)
    second_got = lax.ppermute(second, "gz", cross_pairs)

    PAIRS = ((0, 3), (1, 2))
    DRIFT = (-1.5 * FREQUENCY_STEP, -0.5 * FREQUENCY_STEP)

    def entries(t, p, q, r, s):
        return t, q, p + r, p - r, q + s, s - q, t + p, t - p

    def couple(acc, ent, vec):
        t, q, pr, pmr, qs, sq, tp, tmp = ent
        out = []
        for i in range(2):
            a, e, b, g = (vec[j][i] for j in range(4))
            out.append(
                (
                    acc[0][i] + t * a + pr * b + sq * g,
                    acc[1][i] + t * e + qs * b + pmr * g,
                    acc[2][i] + pr * a + qs * e + tp * b + q * g,
                    acc[3][i] + sq * a + pmr * e + q * b + tmp * g,
                )
            )
        return [(out[0][j], out[1][j]) for j in range(4)]

    def harmonics_of(acc, scale):
        out = [None] * 4
        for at, (lo, hi) in enumerate(PAIRS):
            (ar, ai), (er, ei) = acc[2 * at], acc[2 * at + 1]
            out[lo] = ((ar + ei) * scale, (ai - er) * scale)
            out[hi] = ((ar - ei) * scale, (ai + er) * scale)
        return out

    def basis_of(values):
        out = []
        for lo, hi in PAIRS:
            (lr, li), (hr, hi_) = values[lo], values[hi]
            out += [(lr + hr, li + hi_), (hi_ - li, lr - hr)]
        return out

    def rhs(ref, fields):
        cols = [ref[f] for f in fields]
        return cols[0] if len(cols) == 1 else jnp.concatenate(cols, axis=1)

    def dot(a, b):
        return jnp.dot(a, b, preferred_element_type=f32)

    def resident_slopes(pert_ref, grads, plain, lin, rows_ref, walls_ref):
        me_h = place()[0]
        row, column = iotas(own, own)
        to_z, to_x = column_cells(column, nz, nx)
        for i in range(3):
            rows_ref[i * own : (i + 1) * own] = slope_matrix(i, row >> nx.bit_length() - 1, row & (nx - 1), to_z, to_x).astype(bf16)
        store_walls(walls_ref, ny)
        mean_freq = 12.0 * FREQUENCY_STEP * (me_h * per + 1.5 - per * harms / 2).astype(f32)

        for at, (lo, hi) in enumerate(PAIRS):
            for i in range(2):
                fl, fr = lo * 8 + i * 4 + 3, hi * 8 + i * 4 + 3
                got = dot(rows_ref[: 2 * own], rhs(pert_ref, (fl, fr)))
                wall = dot(rhs(pert_ref, (fl, fr)), walls_ref[:, : 2 * ny])
                for d in range(3):
                    if d == 1:
                        total, diff = wall[:, :ny], wall[:, ny:]
                    else:
                        span = slice(0, own) if d == 0 else slice(own, 2 * own)
                        total, diff = got[span, :ny] + got[span, ny:], got[span, :ny] - got[span, ny:]
                    lin[2 * at, i, d] = total
                    lin[2 * at + 1, 1 - i, d] = diff if i == 0 else -diff
        for at, (lo, hi) in enumerate(PAIRS):
            for c in range(3):
                for i in range(2):
                    sign = 1.0 if i == 0 else -1.0
                    fl, fr = lo * 8 + i * 4 + c, hi * 8 + i * 4 + c
                    got = dot(rows_ref[...], rhs(pert_ref, (fl, fr)))
                    xl, xr = pert_ref[fl].astype(f32), pert_ref[fr].astype(f32)
                    wall = dot(rhs(pert_ref, (fl, fr)), walls_ref[...])
                    total, diff = xl + xr, xl - xr
                    plain[2 * at, i, c] = total
                    plain[2 * at + 1, 1 - i, c] = sign * diff
                    for d in range(3):
                        if d == 1:
                            gt, gd = wall[:, :ny], wall[:, ny : 2 * ny]
                        else:
                            span = slice(0, own) if d == 0 else slice(own, 2 * own)
                            gt, gd = got[span, :ny] + got[span, ny:], got[span, :ny] - got[span, ny:]
                        gd = sign * gd
                        grads[2 * at, i, c, d] = gt
                        grads[2 * at + 1, 1 - i, c, d] = gd
                        if d == c:
                            if c == 0:
                                lin[2 * at, i, 3] = gt
                                lin[2 * at + 1, 1 - i, 3] = gd
                            else:
                                lin[2 * at, i, 3] = lin[2 * at, i, 3] + gt
                                lin[2 * at + 1, 1 - i, 3] = lin[2 * at + 1, 1 - i, 3] + gd
                    lt = got[2 * own :, :ny] + got[2 * own :, ny:] + wall[:, 2 * ny : 3 * ny]
                    ld = got[2 * own :, :ny] - got[2 * own :, ny:] + wall[:, 3 * ny :]
                    drift = 12.0 * DRIFT[at]
                    lin[2 * at, i, c] = lin[2 * at, i, c] - VISCOSITY * lt
                    lin[2 * at + 1, 1 - i, c] = lin[2 * at + 1, 1 - i, c] - sign * VISCOSITY * ld
                    lin[2 * at, 1 - i, c] = lin[2 * at, 1 - i, c] + sign * (mean_freq * total + drift * diff)
                    lin[2 * at + 1, i, c] = lin[2 * at + 1, i, c] - (mean_freq * diff + drift * total)

    def resident(mean_ref, mode_ref, grads, plain, lin, out_ref, ents, rows_ref, walls_ref):
        row, column = iotas(own, own)
        to_z, to_x = column_cells(column, nz, nx)
        for i in range(2):
            rows_ref[i * own : (i + 1) * own] = slope_matrix(i, row >> nx.bit_length() - 1, row & (nx - 1), to_z, to_x).astype(bf16)
        store_walls(walls_ref, ny)
        for c in range(3):
            picked = [mean_ref[c].astype(f32)] + [mode_ref[3 * i + c].astype(f32) for i in range(4)]
            for n, ent in enumerate(entries(*picked)):
                ents[c, n] = ent
            mean_at = dot(rows_ref[...], rhs(mean_ref, (c,)))
            mean_wall = dot(mean_ref[c], walls_ref[:ny, :ny])
            real = dot(rows_ref[...], rhs(mode_ref, (c, 6 + c)))
            imag = dot(rows_ref[...], rhs(mode_ref, (3 + c, 9 + c)))
            wall_real = dot(rhs(mode_ref, (c, 6 + c)), walls_ref[:, : 2 * ny])
            wall_imag = dot(rhs(mode_ref, (3 + c, 9 + c)), walls_ref[:, : 2 * ny])
            for d in range(3):
                if d == 1:
                    pr, pmr = wall_real[:, :ny], wall_real[:, ny:]
                    qs, qms = wall_imag[:, :ny], wall_imag[:, ny:]
                    t, p, q = mean_wall, 0.5 * (pr + pmr), 0.5 * (qs + qms)
                    values = (t, q, pr, pmr, qs, -qms, t + p, t - p)
                else:
                    span = slice(0, own) if d == 0 else slice(own, 2 * own)
                    values = entries(mean_at[span], real[span, :ny], imag[span, :ny], real[span, ny:], imag[span, ny:])
                for n, ent in enumerate(values):
                    ents[3 + 3 * d + c, n] = ent

        def block(b, carry):
            rows = pl.ds(pl.multiple_of(b * 8, 8), 8)
            accs = [[(lin[j, 0, c, rows], lin[j, 1, c, rows]) for j in range(4)] for c in range(4)]
            for d in range(3):
                flow = [ents[d, n, rows] for n in range(8)]
                for c in range(3):
                    accs[c] = couple(accs[c], flow, [(grads[j, 0, c, d, rows], grads[j, 1, c, d, rows]) for j in range(4)])
                along = [(plain[j, 0, d, rows], plain[j, 1, d, rows]) for j in range(4)]
                for c in range(3):
                    slope = [ents[3 + 3 * d + c, n, rows] for n in range(8)]
                    accs[c] = couple(accs[c], slope, along)
            for c in range(4):
                for k, (re, im) in enumerate(harmonics_of(accs[c], 1.0 / 24.0)):
                    out_ref[k * 8 + c, rows] = re
                    out_ref[k * 8 + 4 + c, rows] = im
            return carry

        lax.fori_loop(0, own // 8, block, 0, unroll=4)

    flat = lambda a: a.reshape(a.shape[0], -1, ny)
    with jax.named_scope("resident_slopes"):
        slopes = pl.pallas_call(
            resident_slopes,
            out_shape=tuple(jax.ShapeDtypeStruct(n + (own, ny), f32) for n in ((4, 2, 3, 3), (4, 2, 3), (4, 2, 4))),
            scratch_shapes=[pltpu.VMEM((3 * own, own), bf16), pltpu.VMEM((2 * ny, 4 * ny), bf16)],
            compiler_params=pltpu.CompilerParams(vmem_limit_bytes=20 * 1024 * 1024),
        )(flat(pert))
    with jax.named_scope("resident"):
        whole = pl.pallas_call(
            resident,
            out_shape=jax.ShapeDtypeStruct((n_pert, own, ny), f32),
            scratch_shapes=[
                pltpu.VMEM((12, 8, own, ny), f32),
                pltpu.VMEM((2 * own, own), bf16),
                pltpu.VMEM((2 * ny, 2 * ny), bf16),
            ],
            compiler_params=roomy,
        )(flat(mean), flat(mode), *slopes)

    base_modes_at = n_pert + n_mean
    ends = 16 * nz

    def edge_taps(tables):
        row, column = iotas(ends, own + 2 * HALO_X)
        last = row >= 8 * nz
        row = jnp.where(last, row - 8 * nz, row)
        to_z, to_x = column_cells(column, nz, nx)
        dz, dx = to_z - (row >> 3), to_x - (row & 7) - jnp.where(last, nx - 8, 0)
        return jnp.concatenate([jnp.where(dz == 0, taps(dx, table), 0.0)[:, own:] for table in tables], axis=0).astype(bf16)

    def add_edges(pert_ref, mean_ref, mode_ref, xb_ref, xa_ref, _, out_ref, vecs, lins, bends):
        taps_of = edge_taps((FIRST, SECOND))

        def bent(fields, lap):
            cols = [jnp.concatenate([edge_tile(xb_ref, f), edge_tile(xa_ref, f)], axis=0) for f in fields]
            both = cols[0] if len(cols) == 1 else jnp.concatenate(cols, axis=1)
            got = jnp.dot(taps_of if lap else taps_of[:ends], both, preferred_element_type=f32)
            return [(got[:ends, i * ny : (i + 1) * ny], got[ends:, i * ny : (i + 1) * ny]) for i in range(len(fields))]

        for at, (lo, hi) in enumerate(PAIRS):
            for i in range(2):
                sign = 1.0 if i == 0 else -1.0
                for c in range(4):
                    (gl, ll), (gr, lr) = bent((lo * 8 + 4 * i + c, hi * 8 + 4 * i + c), c < 3)
                    if c < 3:
                        vecs[2 * at, i, c] = gl + gr
                        vecs[2 * at + 1, 1 - i, c] = sign * (gl - gr)
                        lins[2 * at, i, c] = -VISCOSITY * (ll + lr)
                        lins[2 * at + 1, 1 - i, c] = (-VISCOSITY * sign) * (ll - lr)
                    else:
                        lins[2 * at, i, 0] = lins[2 * at, i, 0] + (gl + gr)
                        lins[2 * at + 1, 1 - i, 0] = lins[2 * at + 1, 1 - i, 0] + sign * (gl - gr)
        for c in range(3):
            at = base_modes_at + c
            (t, _), = bent((n_pert + c,), False)
            (p, _), (r, _) = bent((at, at + 6), False)
            (q, _), (s_, _) = bent((at + 3, at + 9), False)
            for n, ent in enumerate(entries(t, p, q, r, s_)):
                bends[c, n] = ent

        def layer_ends(z, carry):
            for end in range(2):
                strip = pl.ds(pl.multiple_of(z * nx + end * (nx // 2), 16), 16)
                keep = slice(8 * end, 8 * end + 8)
                mine = pl.ds(pl.multiple_of((end * nz + z) * 8, 8), 8)

                def read(ref, f):
                    return ref[f, strip].astype(f32)[keep]

                flow = entries(read(mean_ref, 0), *[read(mode_ref, 3 * i) for i in range(4)])
                along = basis_of([(read(pert_ref, l * 8), read(pert_ref, l * 8 + 4)) for l in range(per)])
                for c in range(4):
                    if c < 3:
                        acc = [(lins[j, 0, c, mine], lins[j, 1, c, mine]) for j in range(4)]
                        acc = couple(acc, flow, [(vecs[j, 0, c, mine], vecs[j, 1, c, mine]) for j in range(4)])
                        acc = couple(acc, [bends[c, n, mine] for n in range(8)], along)
                    else:
                        acc = [(vecs[j, 0, 0, mine], vecs[j, 1, 0, mine]) for j in range(4)]
                    for k, parts in enumerate(harmonics_of(acc, 1.0 / 24.0)):
                        for i in range(2):
                            out_ref[k * 8 + 4 * i + c, mine] = parts[i]
            return carry

        lax.fori_loop(0, nz, layer_ends, 0, unroll=2)

    with jax.named_scope("edges"):
        edged = pl.pallas_call(
            add_edges,
            out_shape=jax.ShapeDtypeStruct((n_pert, ends, ny), f32),
            in_specs=[VMEM] * 5 + [ANY],
            scratch_shapes=[
                pltpu.VMEM((4, 2, 3, ends, ny), f32),
                pltpu.VMEM((4, 2, 3, ends, ny), f32),
                pltpu.VMEM((3, 8, ends, ny), f32),
            ],
            compiler_params=roomy,
        )(flat(pert), flat(mean), flat(mode), xb_got, xa_got, whole)

    faces_deep = n_nb * 2 * nx
    nb_tiles = 3 * n_nb // 4
    deep = faces_deep + 2 * nb_tiles * HALO_X

    def nb_tile(ref, after, f):
        group, i = divmod(f, 4)
        at = [faces_deep + (after * nb_tiles + 3 * group + j) * HALO_X for j in range(3)]
        if i < 3:
            return ref[at[i] : at[i] + HALO_X]
        parts = [ref[row : row + HALO_X].astype(f32)[used:] for row in at]
        return jnp.concatenate(parts + [jnp.zeros((spare, ny), f32)], axis=0).astype(bf16)

    def pack_relay(first_ref, xb_ref, xa_ref, _, *outs):
        scal = place()
        for s, out in enumerate(outs):
            for i in range(modes * 2):
                group = sent(s, scal) * 2 + i
                for c in range(3):
                    at = (3 * i + c) * 2 * nx
                    out[at : at + 2 * nx] = first_ref[group * 4 + c].reshape(2 * nx, ny)
            for after, ref in enumerate((xb_ref, xa_ref)):
                for group in range(n_nb // 4):
                    rows = []
                    for f in range(4 * group, 4 * group + 4):
                        rows.append(ref[(sent(s, scal) * 2 + f // 3) * 3 + f % 3].astype(f32))
                    for i in range(3):
                        at = faces_deep + (after * nb_tiles + 3 * group + i) * HALO_X
                        tile = jnp.concatenate([rows[i][:used], rows[3][spare * i : spare * (i + 1)]], axis=0)
                        out[at : at + HALO_X] = tile.astype(bf16)

    with jax.named_scope("pack_relay"):
        relay = pl.pallas_call(
            pack_relay,
            out_shape=tuple(jax.ShapeDtypeStruct((deep, ny), bf16) for _ in range(sides)),
            in_specs=[VMEM] * 3 + [ANY],
            compiler_params=roomy,
        )(first_got, xb_got, xa_got, edged)
    relay_got = [lax.ppermute(b, "harm", p) for b, p in zip(relay, harm_perms)]

    def pack_near(pert_ref, mean_ref, mode_ref, *rest):
        out = rest[-1]
        z = pl.ds(place()[3], 2)
        out[:n_pert] = pert_ref[:, z]
        out[n_pert : n_pert + n_mean] = mean_ref[:, z]
        out[n_pert + n_mean : n_res] = mode_ref[:, z]
        for s in range(sides):
            out[n_res + s * n_nb : n_res + (s + 1) * n_nb] = rest[s][:, z]

    with jax.named_scope("pack_near"):
        near = pl.pallas_call(
            pack_near,
            out_shape=face(n_all),
            in_specs=[VMEM] * (3 + sides) + [ANY],
            compiler_params=roomy,
        )(pert, mean, mode, *nb_got, relay[0])
    near_got = lax.ppermute(near, "gz", near_pairs)

    below, above = [], []
    for k in range(per):
        for m in range(-modes, modes + 1):
            l = k - m
            if l < 0:
                below.append((k, m, 0, (l + modes) * 6))
            elif l >= per:
                above.append((k, m, sides - 1, (l - per) * 6))

    def on_sides(work):
        me_h = lax.axis_index("harm")
        pl.when(me_h > 0)(lambda: work(below))
        pl.when(me_h < harms - 1)(lambda: work(above))

    def product(acc, flow, value, m):
        (fr, fi), (vr, vi) = flow, value
        if m > 0:
            return acc[0] + fr * vr - fi * vi, acc[1] + fr * vi + fi * vr
        return acc[0] + fr * vr + fi * vi, acc[1] + fr * vi - fi * vr


    def face_place(cross, step):
        odd = place()[1]
        before = (odd == 0) if cross else (odd == 1)
        return before, jnp.where(before, step, nz - 1 - step), jnp.where(before, 1, 0)

    def faces(out_ref, mean_ref, mode_ref, pert_ref, nb_refs, first_ref, second_ref, near_ref, relay_refs, step, lowest=0, after=None):
        cross = near_ref is None
        before, layer, near_at = face_place(cross, step)
        turn = jnp.where(before, 1.0, -1.0)

        def mix(pair):
            return pair[1] - 8.0 * pair[0] if step == 0 else pair[0]

        def mix_lap(pair):
            return pair[1] - 16.0 * pair[0] if step == 0 else pair[0]

        def chunk_work(chunk, carry):
            rows = pl.ds(pl.multiple_of(layer * nx + chunk * 16, 16), 16)
            out_rows = pl.ds(pl.multiple_of((layer - lowest) * nx + chunk * 16, 16), 16)
            strip = pl.ds(chunk * 16 if isinstance(chunk, int) else pl.multiple_of(chunk * 16, 16), 16)

            def halos(f):
                if not cross:
                    ref, at = near_ref, f
                elif f < n_pert:
                    ref, at = first_ref, f
                else:
                    ref, at = second_ref, f - n_pert
                return ref[at, near_at, strip].astype(f32), (ref[at, 1 - near_at, strip].astype(f32) if step == 0 else None)

            def nb_halos(s, f):
                if not cross:
                    return halos(n_res + s * n_nb + f)
                at = [pl.ds(pl.multiple_of((2 * f + j) * nx + chunk * 16, 16), 16) for j in (near_at, 1 - near_at)]
                return tuple(relay_refs[s][r].astype(f32) for r in at)

            velocity, base = first_ref is not None or not cross, second_ref is not None or not cross
            if velocity:
                flow = entries(mean_ref[2, rows].astype(f32), *[mode_ref[3 * i + 2, rows].astype(f32) for i in range(4)])
            if base:
                along = basis_of([(pert_ref[l * 8 + 2, rows].astype(f32), pert_ref[l * 8 + 6, rows].astype(f32)) for l in range(per)])
            for c in range(4 if velocity else 3):
                acc = [(0.0, 0.0)] * 4
                if velocity and c < 3:
                    got = [[halos(l * 8 + 4 * i + c) for i in range(2)] for l in range(per)]
                    vec = basis_of([(mix(g[0]), mix(g[1])) for g in got])
                    lap = basis_of([(mix_lap(g[0]), mix_lap(g[1])) for g in got])
                    if c == 2:
                        acc = basis_of([(mix(halos(l * 8 + 3)), mix(halos(l * 8 + 7))) for l in range(per)])
                    acc = couple(acc, flow, vec)
                if base and c < 3:
                    bend = entries(mix(halos(n_pert + c)), *[mix(halos(base_modes_at + 3 * i + c)) for i in range(4)])
                    acc = couple(acc, bend, along)
                if c == 3:
                    acc = vec
                if velocity and c < 3:
                    acc = [tuple(turn * a + VISCOSITY * v for a, v in zip(*pair)) for pair in zip(acc, lap)]
                else:
                    acc = [tuple(turn * a for a in pair) for pair in acc]
                for k, parts in enumerate(harmonics_of(acc, 1.0 / 24.0)):
                    for i in range(2):
                        at = k * 8 + 4 * i + c
                        out_ref[at, out_rows] = out_ref[at, out_rows] + parts[i]

            def nb_work(pairs):
                for k in sorted({p[0] for p in pairs}):
                    zero = jnp.zeros((16, ny), f32)
                    for c in range(3):
                        acc = (zero, zero)
                        for _, m, s, f in [p for p in pairs if p[0] == k]:
                            at = (abs(m) - 1) * 6
                            mine = tuple(mode_ref[at + 3 * i + 2, rows].astype(f32) for i in range(2))
                            acc = product(acc, mine, tuple(mix(nb_halos(s, f + 3 * i + c)) for i in range(2)), m)
                            bent = tuple(mix(halos(base_modes_at + at + 3 * i + c)) for i in range(2))
                            carried = tuple(nb_refs[s][f + 3 * i + 2, rows].astype(f32) for i in range(2))
                            acc = product(acc, bent, carried, m)
                        for i in range(2):
                            at = k * 8 + 4 * i + c
                            out_ref[at, out_rows] = out_ref[at, out_rows] + (turn * (1.0 / 12.0)) * acc[i]

            if base:
                on_sides(nb_work)
            return carry

        if after is None:
            lax.fori_loop(0, nx // 16, chunk_work, 0, unroll=True)
        else:
            for chunk in range(nx // 16):
                chunk_work(chunk, 0)
                after(layer, chunk)

    def neighbours(mask_ref, pert_ref, mean_ref, mode_ref, xb_ref, xa_ref, whole_ref, edged_ref, first_ref, near_ref, *rest):
        nb_refs = rest[:sides]
        out_any, out_ref, grads, plain, stencil_ref, walls_ref, sems = rest[-7:]
        row, column = iotas(own, own + 2 * HALO_X)
        to_z, to_x = column_cells(column, nz, nx)
        for i in range(2):
            stencil_ref[i * own : (i + 1) * own] = slope_matrix(i, row >> nx.bit_length() - 1, row & (nx - 1), to_z, to_x).astype(bf16)
        store_walls(walls_ref, ny)

        def slopes(at, mine, halo):
            both = jnp.concatenate(mine, axis=1)
            rows = both if halo is None else jnp.concatenate([both, halo], axis=0)
            got = jnp.dot(stencil_ref[:, : rows.shape[0]], rows, preferred_element_type=f32)
            wall = [jnp.dot(x, walls_ref[:ny, :ny], preferred_element_type=f32) for x in mine]
            for i in range(2):
                lanes = slice(i * ny, (i + 1) * ny)
                grads[at + i, 0] = got[:own, lanes]
                grads[at + i, 2] = got[own:, lanes]
                grads[at + i, 1] = wall[i]
                plain[at + i] = mine[i].astype(f32)

        for f in range(0, n_modes, 2):
            at = base_modes_at + f
            halo = [jnp.concatenate([edge_tile(ref, at), edge_tile(ref, at + 1)], axis=1) for ref in (xb_ref, xa_ref)]
            slopes(f, [mode_ref[f], mode_ref[f + 1]], jnp.concatenate(halo, axis=0))
        for s in range(sides):
            for f in range(0, n_nb, 2):
                slopes(n_modes + s * n_nb + f, [nb_refs[s][f], nb_refs[s][f + 1]], None)

        for z in range(nz):
            rows = slice(z * nx, (z + 1) * nx)
            solid = PENALTY * mask_ref[rows].astype(f32)
            for f in range(n_pert):
                if f % 4 < 3:
                    out_ref[f, rows] = whole_ref[f, rows] + solid * pert_ref[f, rows].astype(f32)
                else:
                    out_ref[f, rows] = whole_ref[f, rows]
            for end in range(2):
                rows = slice(z * nx + end * (nx - 8), z * nx + end * (nx - 8) + 8)
                mine = slice((end * nz + z) * 8, (end * nz + z + 1) * 8)
                out_ref[:, rows] = out_ref[:, rows] + edged_ref[:, mine]

        def work(pairs):
            def block(b, carry):
                rows = pl.ds(pl.multiple_of(b * 8, 8), 8)
                for k in sorted({p[0] for p in pairs}):
                    zero = jnp.zeros((8, ny), f32)
                    acc = [(zero, zero)] * 3
                    for _, m, s, f in [p for p in pairs if p[0] == k]:
                        at, base = n_modes + s * n_nb + f, (abs(m) - 1) * 6
                        for d in range(3):
                            flow = plain[base + d, rows], plain[base + 3 + d, rows]
                            along = plain[at + d, rows], plain[at + 3 + d, rows]
                            for c in range(3):
                                slope = grads[base + c, d, rows], grads[base + 3 + c, d, rows]
                                grad = grads[at + c, d, rows], grads[at + 3 + c, d, rows]
                                acc[c] = product(acc[c], flow, grad, m)
                                acc[c] = product(acc[c], slope, along, m)
                    for c in range(3):
                        for i in range(2):
                            at = k * 8 + 4 * i + c
                            out_ref[at, rows] = out_ref[at, rows] + acc[c][i] * (1.0 / 12.0)
                return carry

            lax.fori_loop(0, own // 8, block, 0, unroll=2)

        on_sides(work)
        sends = []

        def send(layer):
            rows = pl.ds(pl.multiple_of(layer * nx, nx), nx)
            sends.append(pltpu.make_async_copy(out_ref.at[:, rows], out_any.at[:, rows], sems.at[len(sends)]))
            sends[-1].start()

        for layer in range(2, nz - 2):
            send(layer)
        for step in range(2):
            faces(out_ref, mean_ref, mode_ref, pert_ref, nb_refs, None, None, near_ref, None, step)
            send(face_place(False, step)[1])
        for step in range(2):
            faces(out_ref, mean_ref, mode_ref, pert_ref, nb_refs, first_ref, None, None, None, step)
        for copy in sends:
            copy.wait()

    n_ext = n_modes + sides * n_nb
    with jax.named_scope("neighbours"):
        result, inner = pl.pallas_call(
            neighbours,
            out_shape=(jax.ShapeDtypeStruct((n_pert, own, ny), f32),) * 2,
            out_specs=(HBM, VMEM),
            scratch_shapes=[
                pltpu.VMEM((n_ext, 3, own, ny), f32),
                pltpu.VMEM((n_ext, own, ny), f32),
                pltpu.VMEM((2 * own, own + 2 * HALO_X), bf16),
                pltpu.VMEM((ny, ny), bf16),
                pltpu.SemaphoreType.DMA((nz - 2,)),
            ],
            compiler_params=roomy,
        )(mask, flat(pert), flat(mean), flat(mode), xb_got, xa_got, whole, edged, first_got, near_got, *[flat(b) for b in nb_got])

    n_keys = n_pert // 2 if swap else n_pert

    def finish(pert_ref, mean_ref, mode_ref, inner_ref, second_ref, _, *rest):
        relay_refs, nb_refs = rest[:sides], rest[sides : 2 * sides]
        out_any, done, fringe, bends, sems = rest[2 * sides :]
        half = nx // 2
        keys = jnp.where(lax.axis_index("harm") == 0, n_pert - n_keys, 0) if swap else 0
        inner_layer = jnp.where(face_place(True, 0)[0], 2, 0)
        taps_of = edge_taps((FIRST,))
        sends = []

        def send(src, dst):
            sends.append(pltpu.make_async_copy(src, dst, sems.at[len(sends)]))
            sends[-1].start()

        for s in range(sides):
            for f in range(0, n_nb, 2):
                both = [jnp.concatenate([nb_tile(relay_refs[s], after, f + i) for after in range(2)], axis=0) for i in range(2)]
                both = jnp.concatenate(both, axis=1)
                got = jnp.dot(taps_of, both, preferred_element_type=f32)
                for i in range(2):
                    bends[s * n_nb + f + i] = got[:, i * ny : (i + 1) * ny]

        def edge_terms(pairs, z, end, add):
            strip = pl.ds(pl.multiple_of(z * nx + end * half, 16), 16)
            keep = slice(8 * end, 8 * end + 8)
            bent = pl.ds(pl.multiple_of((end * nz + z) * 8, 8), 8)
            for k in sorted({p[0] for p in pairs}):
                zero = jnp.zeros((8, ny), f32)
                acc = [(zero, zero)] * 3
                for _, m, s, f in [p for p in pairs if p[0] == k]:
                    base = (abs(m) - 1) * 6
                    flow = tuple(mode_ref[base + 3 * i, strip].astype(f32)[keep] for i in range(2))
                    for c in range(3):
                        at = s * n_nb + f + c
                        acc[c] = product(acc[c], flow, (bends[at, bent], bends[at + 3, bent]), m)
                for c in range(3):
                    for i in range(2):
                        add(k, 4 * i + c, acc[c][i] * (1.0 / 12.0))

        def end_rows(z, end):
            return pl.ds(pl.multiple_of(z * nx + end * (nx - 8), 8), 8)

        def other_edges(pairs):
            lowest = min(p[0] for p in pairs) * 8 if swap else 0

            def at_layer(j, carry):
                for end in range(2):

                    def add(k, part, value):
                        at = k * 8 + part - lowest
                        fringe[end, at, j] = fringe[end, at, j] + value

                    edge_terms(pairs, inner_layer + j, end, add)
                return carry

            lax.fori_loop(0, nz - 2, at_layer, 0, unroll=2)

        for j in range(nz - 2):
            for end in range(2):
                fringe[end, :, j] = inner_ref[pl.ds(keys, n_keys), end_rows(inner_layer + j, end)]
        on_sides(other_edges)
        for j in range(nz - 2):
            for end in range(2):
                send(fringe.at[end, :, j], out_any.at[pl.ds(keys, n_keys), end_rows(inner_layer + j, end)])

        first_row = pl.multiple_of(jnp.where(face_place(True, 0)[0], 0, (nz - 2) * nx), nx)
        done[...] = inner_ref[:, pl.ds(first_row, 2 * nx)]
        cross_layer = first_row // nx

        def cross_edges(pairs):
            def at_layer(j, carry):
                for end in range(2):
                    rows = end_rows(j, end)

                    def add(k, part, value):
                        done[k * 8 + part, rows] = done[k * 8 + part, rows] + value

                    edge_terms(pairs, cross_layer + j, end, add)
                return carry

            lax.fori_loop(0, 2, at_layer, 0, unroll=True)

        on_sides(cross_edges)
        def send_chunk(layer, chunk):
            here = pl.ds(pl.multiple_of((layer - cross_layer) * nx + chunk * 16, 16), 16)
            send(done.at[:, here], out_any.at[:, pl.ds(pl.multiple_of(layer * nx + chunk * 16, 16), 16)])

        for step in range(2):
            faces(done, mean_ref, mode_ref, pert_ref, nb_refs, None, second_ref, None, relay_refs, step, cross_layer, send_chunk)
        for copy in sends:
            copy.wait()

    with jax.named_scope("finish"):
        out = pl.pallas_call(
            finish,
            out_shape=jax.ShapeDtypeStruct((n_pert, own, ny), f32),
            in_specs=[VMEM] * 5 + [HBM] + [VMEM] * (2 * sides),
            out_specs=HBM,
            input_output_aliases={5: 0},
            scratch_shapes=[
                pltpu.VMEM((n_pert, 2 * nx, ny), f32),
                pltpu.VMEM((2, n_keys, nz - 2, 8, ny), f32),
                pltpu.VMEM((sides * n_nb, ends, ny), f32),
                pltpu.SemaphoreType.DMA((nx // 8 + 2 * (nz - 2),)),
            ],
            compiler_params=roomy,
        )(
            flat(pert), flat(mean), flat(mode), inner, second_got, result,
            *relay_got, *[flat(b) for b in nb_got],
        )
    return jnp.swapaxes(out.reshape(per, 2, 4, nz, nx, ny), 3, 4)


def solution(mesh):
    return jax.shard_map(
        shards,
        mesh=mesh,
        in_specs=(
            P("harm", None, None, "gx", "gz", None),
            P(None, "gx", "gz", None),
            P(None, None, None, "gx", "gz", None),
            P("gx", "gz", None),
        ),
        out_specs=P("harm", None, None, "gx", "gz", None),
        check_vma=False,
    )
```
